32 devices in a mesh: fsdp: 2 (over x), ctx: 4 (over z), tp: 4 (over y, core).
Axes of the slice: x: 2, y: 2, z: 4, core: 2. Of those that a mesh axis runs over, the one named last changes fastest.
Arguments:
- inputs: bfloat16 [4, 736, 1152], P('fsdp', 'ctx'), may hold values from -6 to 6
- cotangent: bfloat16 [4, 736, 1152], P('fsdp', 'ctx'), may hold values from -6 to 6
- valid_count: int32 [4], P('fsdp'), may hold values from 369 to 736, as said below
- norm_gain: float32 [2, 2, 1152], replicated, may hold values from 0.5 to 1.5
- norm_bias: float32 [2, 2, 1152], replicated, may hold values from -1.8 to 1.8
- w_qkv: bfloat16 [2, 1152, 3, 1152], P(None, ('fsdp', 'ctx'), None, 'tp'), may hold values from -0.25 to 0.25
- bias_qv: float32 [2, 2, 1152], P(None, None, 'tp'), may hold values from -3 to 3
- w_out: bfloat16 [2, 1152, 1152], P(None, ('fsdp', 'ctx'), 'tp'), may hold values from -1.5 to 1.5
- w_up: bfloat16 [2, 1152, 4304], P(None, ('fsdp', 'ctx'), 'tp'), may hold values from -0.1875 to 0.1875
- bias_up: float32 [2, 4304], P(None, 'tp'), may hold values from -3 to 3
- w_down: bfloat16 [2, 1152, 4304], P(None, ('fsdp', 'ctx'), 'tp'), may hold values from -0.09375 to 0.09375
- bias_resid: float32 [2, 2, 1152], replicated, may hold values from -1.8 to 1.8
Outputs:
- output: bfloat16 [4, 736, 1152], P('fsdp', 'ctx')
- grad_inputs: float32 [4, 736, 1152], P('fsdp', 'ctx')
- grad_norm_gain: float32 [2, 2, 1152], replicated
- grad_norm_bias: float32 [2, 2, 1152], replicated
- grad_qkv: float32 [2, 1152, 3, 1152], P(None, ('fsdp', 'ctx'), None, 'tp')
- grad_bias_qv: float32 [2, 2, 1152], P(None, None, 'tp')
- grad_out: float32 [2, 1152, 1152], P(None, ('fsdp', 'ctx'), 'tp')
- grad_up: float32 [2, 1152, 4304], P(None, ('fsdp', 'ctx'), 'tp')
- grad_bias_up: float32 [2, 4304], P(None, 'tp')
- grad_down: float32 [2, 1152, 4304], P(None, ('fsdp', 'ctx'), 'tp')
- grad_bias_resid: float32 [2, 2, 1152], replicated
The draws below stay inside these ranges and needn't reach their ends.
Inputs may be any that keep to these rules, and one draw needn't show every extreme that they name: `valid_count`: some image has no padding.
All inputs are finite; a program needn't handle non-finite values.
Results may differ from the reference program's by a relative error of at most 0.028.
The reference program's roundings to bfloat16 on the way count: a program that leaves them out, or rounds other values in their place, can miss the bound.
Values may be sent and summed in bfloat16 or wider, within the bound.
A program may use at most 192 MiB of HBM per device.

```python
import jax
import jax.numpy as jnp
from jax import lax

D = 1152
HEAD_DIM = 72
FF = 4304
S = 736
L = 2
IMG_DEV = 2
IMAGES = 4


def draw_valid_count(key, part):
    key = jax.random.fold_in(key, 7)
    count_key = jax.random.fold_in(key, 11)
    pick_key = jax.random.fold_in(key, 13)
    lowest = S // 2 + 1
    counts = jax.random.randint(count_key, (IMAGES,), lowest, S + 1)
    full_image = jax.random.randint(pick_key, (), 0, IMAGES)
    counts = counts.at[full_image].set(S)
    return counts.astype(jnp.int32)


def steps_of(stream_key, extent, shards, least, high):
    loudness, own = 1.0, jax.random.fold_in(stream_key, 6)
    for dim, blocks in shards:
        heights = jnp.exp(jax.random.uniform(jax.random.fold_in(own, dim), (blocks,), jnp.float32, least / len(shards), high / len(shards)))
        loudness = loudness * jnp.repeat(heights, extent[dim] // blocks).reshape([-1 if axis == dim else 1 for axis in range(len(extent))])
    return loudness


def gaussian(key, shape, scale, reach, split=(), held_as=jnp.bfloat16):
    entries = jax.random.normal(key, shape, jnp.float32) * scale
    if len(split) > 0:
        entries = steps_of(key, shape, split, -0.22, 0.18) * entries
    return jnp.clip(entries, min=-reach, max=reach).astype(held_as)


def setup_inputs(seed: int = 0) -> dict:
    keys = jax.random.split(jax.random.key(seed), 13)
    return {
        "inputs": gaussian(keys[0], (IMAGES, S, D), 1.0, 6.0, ((0, 2), (1, 4))),
        "cotangent": gaussian(keys[1], (IMAGES, S, D), 1.0, 6.0, ((0, 2), (1, 4))),
        "valid_count": draw_valid_count(jax.random.fold_in(keys[12], 71), 0),
        "norm_gain": jnp.clip(1.0 + 0.1 * jax.random.normal(keys[3], (L, 2, D), jnp.float32), 0.5, 1.5),
        "norm_bias": gaussian(keys[4], (L, 2, D), 0.3, 1.8, (), jnp.float32),
        "w_qkv": gaussian(keys[5], (L, D, 3, D), (D // 2) ** -0.5, 0.25, ((1, 8), (3, 4))),
        "bias_qv": gaussian(keys[6], (L, 2, D), 0.5, 3.0, ((2, 4),), jnp.float32),
        "w_out": gaussian(keys[7], (L, D, D), (max(D // 64, 1)) ** -0.5, 1.5, ((1, 8), (2, 4))),
        "w_up": gaussian(keys[8], (L, D, FF), D ** -0.5, 0.1875, ((1, 8), (2, 4))),
        "bias_up": gaussian(keys[9], (L, FF), 0.5, 3.0, ((1, 4),), jnp.float32),
        "w_down": gaussian(keys[10], (L, D, FF), FF ** -0.5, 0.09375, ((1, 8), (2, 4))),
        "bias_resid": gaussian(keys[11], (L, 2, D), 0.3, 1.8, (), jnp.float32),
    }


norm_eps = 1e-06
gelu_root = 0.7978845608028654
gelu_cubic = 0.044715
masked_score = -1e+30

@jax.custom_vjp
def low(v):
    return lax.optimization_barrier(v.astype(jnp.bfloat16)).astype(jnp.float32)

@jax.custom_vjp
def low_back(v):
    return v

def low_keep(v):
    return (low(v), None)

def low_pass(kept, grad):
    return (grad,)

def back_keep(v):
    return (v, None)

def back_low(kept, grad):
    return (low(grad),)
low.defvjp(low_keep, low_pass)
low_back.defvjp(back_keep, back_low)

def layer_norm(values, scale_vec, shift_vec):
    centre = lax.optimization_barrier(jnp.mean(values, axis=-1, keepdims=True))
    centred = values - centre
    spread = lax.optimization_barrier(jnp.mean(centred * centred, axis=-1, keepdims=True))
    return centred * lax.rsqrt(spread + norm_eps) * scale_vec + shift_vec

def gelu_tanh(values):
    return 0.5 * values * (1.0 + jnp.tanh(gelu_root * (values + gelu_cubic * values * values * values)))

def attend_one(packed):
    queries, own_keys, own_values, key_valid = packed
    seq_rows, head_width = queries.shape
    head_count = head_width // HEAD_DIM
    query_heads = queries.reshape(seq_rows, head_count, HEAD_DIM)
    key_heads = own_keys.reshape(seq_rows, head_count, HEAD_DIM)
    value_heads = own_values.reshape(seq_rows, head_count, HEAD_DIM)
    scores = low_back(HEAD_DIM ** (-0.5) * jnp.einsum('qhe,khe->hqk', query_heads, key_heads, precision=lax.Precision.HIGHEST))
    scores = jnp.where(key_valid[None, None, :], scores, masked_score)
    attn_probs = low(jax.nn.softmax(scores, axis=-1))
    mixed = jnp.einsum('hqk,khe->qhe', attn_probs, value_heads, precision=lax.Precision.HIGHEST)
    return low(low_back(mixed.reshape(seq_rows, head_width)))

def block(stream, params, key_valid):
    gains, shifts, qkv_full, qv_bias, out_full, up_full, up_bias, down_full, resid_bias = params
    highest = lax.Precision.HIGHEST
    low_first = low(layer_norm(stream, gains[0], shifts[0]))
    projected = jnp.einsum('bsd,dkt->bskt', low_first, qkv_full, precision=highest)
    queries = low(low_back(projected[:, :, 0] + qv_bias[0]))
    own_keys = low(low_back(projected[:, :, 1]))
    own_values = low(low_back(projected[:, :, 2] + qv_bias[1]))
    mixed = lax.map(jax.checkpoint(attend_one), (queries, own_keys, own_values, key_valid))
    middle = stream + low_back(jnp.einsum('bst,dt->bsd', mixed, out_full, precision=highest) + resid_bias[0])
    low_second = low(layer_norm(middle, gains[1], shifts[1]))
    pre_act = low_back(jnp.einsum('bsd,df->bsf', low_second, up_full, precision=highest) + up_bias)
    hidden = low(gelu_tanh(pre_act))
    return middle + low_back(jnp.einsum('bsf,df->bsd', hidden, down_full, precision=highest) + resid_bias[1])

def forward(stream, params, key_valid):
    for layer_at in range(params[0].shape[0]):
        stream = block(stream, tuple((stacked_param[layer_at] for stacked_param in params)), key_valid)
    return stream

def reference(inputs, cotangent, valid_count, norm_gain, norm_bias, w_qkv, bias_qv, w_out, w_up, bias_up, w_down, bias_resid):
    params = tuple((stacked_param.astype(jnp.float32) for stacked_param in (norm_gain, norm_bias, w_qkv, bias_qv, w_out, w_up, bias_up, w_down, bias_resid)))
    group_count = inputs.shape[0] // IMG_DEV
    positions = jnp.arange(S, dtype=jnp.int32)

    def regroup(array_in):
        return array_in.reshape((group_count, IMG_DEV) + array_in.shape[1:])

    def step(totals, packed):
        input_group, cot_group, count_group = packed
        key_valid = positions[None, :] < count_group[:, None]

        def run_all(stream, weights):
            return forward(stream, weights, key_valid)
        result, pull = jax.vjp(run_all, input_group.astype(jnp.float32), params)
        cot_valid = cot_group.astype(jnp.float32) * key_valid[:, :, None].astype(jnp.float32)
        input_grad, param_grads = pull(cot_valid)
        totals = tuple((total_now + grad_now for total_now, grad_now in zip(totals, param_grads)))
        return (totals, (result.astype(jnp.bfloat16), input_grad))
    zeros_init = tuple((jnp.zeros(stacked_param.shape, jnp.float32) for stacked_param in params))
    totals, (results, input_grads) = lax.scan(step, zeros_init, (regroup(inputs), regroup(cotangent), regroup(valid_count)))
    output = results.reshape(inputs.shape)
    grad_inputs = input_grads.reshape(inputs.shape)
    return (output, grad_inputs, totals[0], totals[1], totals[2], totals[3], totals[4], totals[5], totals[6], totals[7], totals[8])
```

```python
import functools

import jax
import jax.numpy as jnp
from jax import lax
from jax.experimental import pallas as pl
from jax.experimental.pallas import tpu as pltpu
from jax.sharding import PartitionSpec as P

HEAD_DIM = 72
norm_eps = 1e-06
gelu_root = 0.7978845608028654
gelu_cubic = 0.044715
masked_score = -1e30

MESH = pl.DeviceIdType.MESH
f32 = jnp.float32
bf16 = jnp.bfloat16
VMEM = pltpu.VMEM
DMA = pltpu.SemaphoreType.DMA


def up_to(value, unit):
    return (value + unit - 1) // unit * unit


def dot(a, b, over):
    return lax.dot_general(a, b, (((over[0],), (over[1],)), ((), ())), preferred_element_type=f32)


class Sizes:
    def __init__(self, mesh, inputs, w_qkv, w_up):
        self.fsdp, self.ctx, self.tp = mesh.shape["fsdp"], mesh.shape["ctx"], mesh.shape["tp"]
        self.images, self.rows, self.d = inputs.shape
        self.layers, self.wrows = w_qkv.shape[0], w_qkv.shape[1]
        self.zl = self.ctx // self.images
        self.chips_y = self.tp // 2
        self.chips = self.zl * self.chips_y
        self.team = self.chips * 2
        self.part = up_to(-(-self.rows // self.tp), 16)
        self.block = self.images * self.part
        self.tile = 2 * self.block
        self.keys = self.chips * self.tile
        self.wide = w_qkv.shape[3] // self.zl
        self.heads = self.wide // HEAD_DIM
        self.ff = w_up.shape[2] // self.zl
        self.ffp = up_to(self.ff, 128)
        self.headp = up_to(self.wide, 128)
        self.qkvp = up_to(3 * self.wide, 128)
        self.attnp = up_to(4 * self.wide, 128)
        self.cols = self.attnp + 2 * self.ffp
        self.wrowsp = up_to(self.wrows, 16)
        self.groups = self.fsdp * self.ctx


class Place:
    def __init__(self, sz):
        self.sz = sz
        self.f, self.c, self.t = lax.axis_index("fsdp"), lax.axis_index("ctx"), lax.axis_index("tp")
        self.zh, self.zl = self.c // sz.zl, self.c % sz.zl
        self.y, self.k = self.t // 2, self.t % 2
        self.chip = self.zl * sz.chips_y + self.y
        self.slot = 2 * self.chip + self.k

    def chip_at(self, step):
        sz = self.sz
        zl = (self.zl + step // sz.chips_y) % sz.zl
        y = (self.y + step % sz.chips_y) % sz.chips_y
        return zl, y

    def chip_back(self, step):
        sz = self.sz
        zl = (self.zl + sz.zl - step // sz.chips_y) % sz.zl
        y = (self.y + sz.chips_y - step % sz.chips_y) % sz.chips_y
        return zl, y

    def index(self, chip):
        return chip[0] * self.sz.chips_y + chip[1]

    def device(self, chip):
        return (self.f, self.zh * self.sz.zl + chip[0], 2 * chip[1] + self.k)

    @property
    def twin(self):
        return (self.f, self.c, self.t + 1 - 2 * self.k)


def greet(others):
    barrier = pltpu.get_barrier_semaphore()
    for other in others:
        pl.semaphore_signal(barrier, inc=1, device_id=other, device_id_type=MESH)
    pl.semaphore_wait(barrier, len(others))


def send(src, dst, send_sem, recv_sem, device):
    return pltpu.make_async_remote_copy(
        src_ref=src, dst_ref=dst, send_sem=send_sem, recv_sem=recv_sem, device_id=device, device_id_type=MESH
    )


def team_peers(pc):
    return [pc.device(pc.chip_at(step)) for step in range(1, pc.sz.chips)] + [pc.twin]


class Gather:
    def __init__(self, pc, buf, sems, at):
        self.pc, self.buf, self.sems, self.at = pc, buf, sems, at

    def far(self, step, slot, device):
        return send(self.buf.at[slot], self.buf.at[slot], self.sems.at[self.at, 0, step],
                    self.sems.at[self.at, 1, step], device)

    def near(self, step, slot):
        return send(self.buf.at[slot], self.buf.at[slot], self.sems.at[self.at, 2, step],
                    self.sems.at[self.at, 3, step], self.pc.twin)

    def start(self):
        pc = self.pc
        for step in range(1, pc.sz.chips):
            self.far(step, pc.slot, pc.device(pc.chip_at(step))).start()
        self.near(0, pc.slot).start()

    def arrive(self, step):
        pc = self.pc
        chip = pc.chip_back(step)
        at = pc.index(chip)

        @pl.when(step > 0)
        def _():
            self.far(step, 2 * at + pc.k, pc.device(chip)).wait_recv()
            self.near(step, 2 * at + pc.k).start()

        self.near(step, 2 * at + 1 - pc.k).wait_recv()
        return at

    def finish(self):
        pc = self.pc
        for step in range(pc.sz.chips):
            if step:
                self.far(step, pc.slot, pc.device(pc.chip_at(step))).wait_send()
            self.near(step, pc.slot).wait_send()


class Scatter:
    def __init__(self, pc, bufs, sems, at):
        self.pc, self.sems, self.at = pc, sems, at
        self.both, self.keep, self.tsend, self.trecv, self.rsend, self.rrecv = bufs

    def near(self, step):
        return send(self.tsend.at[step], self.trecv.at[step], self.sems.at[self.at, 0, step],
                    self.sems.at[self.at, 1, step], self.pc.twin)

    def far(self, step):
        return send(self.rsend.at[step], self.rrecv.at[step], self.sems.at[self.at, 2, step],
                    self.sems.at[self.at, 3, step], self.pc.device(self.pc.chip_back(step)))

    def push(self, step, partial):
        pc, block = self.pc, self.pc.sz.block
        self.both[...] = partial.reshape(2, block, partial.shape[-1])
        self.tsend[step] = self.both[1 - pc.k].astype(bf16)
        self.near(step).start()
        self.keep[step] = self.both[pc.k]

        @pl.when(step > 0)
        def _():
            self.relay(step - 1)

    def relay(self, step):
        self.near(step).wait_recv()
        total = self.keep[step] + self.trecv[step].astype(f32)

        def own():
            self.keep[0] = total

        def other():
            self.rsend[step] = total.astype(bf16)
            self.far(step).start()

        if isinstance(step, int):
            own() if step == 0 else other()
        else:
            pl.when(step == 0)(own)
            pl.when(step > 0)(other)

    def flush(self):
        self.relay(self.pc.sz.chips - 1)

    def finish(self):
        total = self.keep[0]
        for step in range(1, self.pc.sz.chips):
            self.far(step).wait_recv()
            total = total + self.rrecv[step].astype(f32)
        for step in range(self.pc.sz.chips):
            self.near(step).wait_send()
            if step:
                self.far(step).wait_send()
        return total


def team_scratch(sz, gathers, scatters):
    n = sz.chips
    return [
        VMEM((2, sz.block, sz.d), f32),
        VMEM((n, sz.block, sz.d), f32),
        VMEM((n, sz.block, sz.d), bf16),
        VMEM((n, sz.block, sz.d), bf16),
        VMEM((n, sz.block, sz.d), bf16),
        VMEM((n, sz.block, sz.d), bf16),
        DMA((gathers, 4, n)),
        DMA((scatters, 4, n)),
    ]


def normalised(values):
    centre = jnp.mean(values, axis=-1, keepdims=True)
    centred = values - centre
    spread = jnp.mean(centred * centred, axis=-1, keepdims=True)
    inverse = lax.rsqrt(spread + norm_eps)
    return centred * inverse, inverse


def norm_back(values, gain, grad):
    high, inverse = normalised(values)
    scaled = grad * gain
    term = inverse * (
        scaled
        - jnp.mean(scaled, axis=-1, keepdims=True)
        - high * jnp.mean(scaled * high, axis=-1, keepdims=True)
    )
    return term, jnp.sum(grad * high, axis=0, keepdims=True), jnp.sum(grad, axis=0, keepdims=True)


def lanes_of(shape):
    return lax.broadcasted_iota(jnp.int32, shape, len(shape) - 1)


def unpack_out(sz, w_ref, o_ref):
    at = 3 * sz.wide // 128 * 128
    shift = 3 * sz.wide - at

    def step(i, carry):
        rows = pl.ds(pl.multiple_of(i * 128, 128), 128)
        piece = pltpu.roll(w_ref[rows, at:at + sz.headp].astype(f32), sz.headp - shift, 1)
        o_ref[rows, :] = jnp.where(lanes_of(piece.shape) < sz.wide, piece, 0.0).astype(bf16)
        return carry

    lax.fori_loop(0, sz.d // 128, step, 0)


def take(sz, values, kind):
    at = kind * sz.wide // 128 * 128
    shift = kind * sz.wide - at
    piece = values[:, at:at + sz.headp]
    if shift:
        piece = pltpu.roll(piece, sz.headp - shift, 1)
    return jnp.where(lanes_of(piece.shape) < sz.wide, piece, 0.0)


def head_of(values, head):
    lanes = lanes_of(values.shape)
    mine = (lanes >= head * HEAD_DIM) & (lanes < (head + 1) * HEAD_DIM)
    return jnp.where(mine, values, jnp.zeros_like(values))


def probabilities(q_head, keys, valid):
    scores = dot(q_head, keys, (1, 1)) * HEAD_DIM ** (-0.5)
    scores = jnp.where(valid > 0.0, scores, masked_score)
    weights = jnp.exp(scores - jnp.max(scores, axis=-1, keepdims=True))
    return weights / jnp.sum(weights, axis=-1, keepdims=True)


def forward_kernel(
    sz, stream_ref, w_ref, gain_ref, shift_ref, qv_ref, upb_ref, resid_ref, valid_ref,
    out_ref, middle_ref, n1_ref, n2_ref, q_ref, k_ref, v_ref, mixed_ref, pre_ref, hidden_ref,
    o_ref, both, keep, tsend, trecv, rsend, rrecv, gsems, ssems,
):
    pc = Place(sz)
    bufs = (both, keep, tsend, trecv, rsend, rrecv)
    greet(team_peers(pc))
    gather = Gather(pc, n1_ref, gsems, 0)
    high, _ = normalised(stream_ref[...])
    n1_ref[pc.slot] = (high * gain_ref[0:1, :] + shift_ref[0:1, :]).astype(bf16)
    gather.start()
    unpack_out(sz, w_ref, o_ref)

    def project(step, carry):
        at = gather.arrive(step)
        tokens = n1_ref[pl.ds(2 * at, 2)].reshape(sz.tile, sz.d)
        both3 = dot(tokens, w_ref[:, 0:sz.qkvp], (1, 0))
        q_ref[at] = (take(sz, both3, 0) + qv_ref[0:1, :]).astype(bf16)
        k_ref[at] = take(sz, both3, 1).astype(bf16)
        v_ref[at] = (take(sz, both3, 2) + qv_ref[1:2, :]).astype(bf16)
        return carry

    lax.fori_loop(0, sz.chips, project, 0)
    gather.finish()
    scatter = Scatter(pc, bufs, ssems, 0)

    def attend(step, carry):
        at = pc.index(pc.chip_back(step))
        keys = k_ref[...].reshape(sz.keys, sz.headp)
        values = v_ref[...].reshape(sz.keys, sz.headp)
        queries = q_ref[at]
        total = jnp.zeros((sz.tile, sz.headp), f32)
        for head in range(sz.heads):
            probs = probabilities(head_of(queries, head), keys, valid_ref[...])
            total = total + dot(probs.astype(bf16), head_of(values, head), (1, 0))
        mixed = total.astype(bf16)
        mixed_ref[at] = mixed
        scatter.push(step, dot(mixed, o_ref[...], (1, 1)))
        return carry

    lax.fori_loop(0, sz.chips, attend, 0)
    scatter.flush()
    middle = stream_ref[...] + (scatter.finish() + resid_ref[0:1, :])
    middle_ref[...] = middle
    gather = Gather(pc, n2_ref, gsems, 1)
    high, _ = normalised(middle)
    n2_ref[pc.slot] = (high * gain_ref[1:2, :] + shift_ref[1:2, :]).astype(bf16)
    gather.start()
    scatter2 = Scatter(pc, bufs, ssems, 1)

    def feed(step, carry):
        at = gather.arrive(step)
        tokens = n2_ref[pl.ds(2 * at, 2)].reshape(sz.tile, sz.d)
        pre = dot(tokens, w_ref[:, sz.attnp:sz.attnp + sz.ffp], (1, 0)) + upb_ref[...]
        pre_ref[at] = pre
        hidden = (0.5 * pre * (1.0 + jnp.tanh(gelu_root * (pre + gelu_cubic * pre * pre * pre)))).astype(bf16)
        hidden_ref[at] = hidden
        scatter2.push(step, dot(hidden, w_ref[:, sz.attnp + sz.ffp:], (1, 1)))
        return carry

    lax.fori_loop(0, sz.chips, feed, 0)
    scatter2.flush()
    gather.finish()
    out_ref[...] = middle_ref[...] + (scatter2.finish() + resid_ref[1:2, :])


def backward_kernel(
    sz, grad_ref, stream_ref, middle_ref, n1_ref, n2_ref, q_ref, k_ref, v_ref, mixed_ref, pre_ref, hidden_ref,
    w_ref, gain_ref, valid_ref,
    below_ref, dw_ref, vec_ref, dqv_ref, dup_ref,
    o_ref, gl_ref, ml_ref, pg_ref, mg_ref, dk_ref, dv_ref, stack_ref, gmid_ref,
    both, keep, tsend, trecv, rsend, rrecv, gsems, ssems,
):
    pc = Place(sz)
    bufs = (both, keep, tsend, trecv, rsend, rrecv)
    greet(team_peers(pc))
    up_at, down_at = sz.attnp, sz.attnp + sz.ffp
    span = 384 if sz.d % 384 == 0 else 128

    gather = Gather(pc, gl_ref, gsems, 0)
    grad_low = grad_ref[...].astype(bf16)
    gl_ref[pc.slot] = grad_low
    gather.start()
    vec_ref[5:6, :] = jnp.sum(grad_low.astype(f32), axis=0, keepdims=True)
    unpack_out(sz, w_ref, o_ref)
    scatter = Scatter(pc, bufs, ssems, 0)
    dup_ref[...] = jnp.zeros_like(dup_ref)

    def feed(step, carry):
        at = gather.arrive(step)
        grads = gl_ref[pl.ds(2 * at, 2)].reshape(sz.tile, sz.d)
        back = dot(grads, w_ref[:, down_at:], (1, 0))
        pre = pre_ref[at]
        bent = jnp.tanh(gelu_root * (pre + gelu_cubic * pre * pre * pre))
        slope = 0.5 * (1.0 + bent) + 0.5 * pre * (1.0 - bent * bent) * (
            gelu_root * (1.0 + 3.0 * gelu_cubic * pre * pre)
        )
        pre_grad = (back * slope).astype(bf16)
        pg_ref[at] = pre_grad
        dup_ref[...] += jnp.sum(pre_grad.astype(f32), axis=0, keepdims=True)
        scatter.push(step, dot(pre_grad, w_ref[:, up_at:down_at], (1, 1)))
        return carry

    lax.fori_loop(0, sz.chips, feed, 0)
    scatter.flush()

    def grads_ff(i, carry):
        lanes = pl.ds(pl.multiple_of(i * span, 128), span)
        hidden = hidden_ref[...].reshape(sz.keys, sz.ffp)
        dw_ref[lanes, down_at:] = dot(gl_ref[:, :, lanes].reshape(sz.keys, span), hidden, (0, 0)).astype(bf16)
        pre_grad = pg_ref[...].reshape(sz.keys, sz.ffp)
        dw_ref[lanes, up_at:down_at] = dot(n2_ref[:, :, lanes].reshape(sz.keys, span), pre_grad, (0, 0)).astype(bf16)
        return carry

    lax.fori_loop(0, sz.d // span, grads_ff, 0)
    gather.finish()
    second = scatter.finish()
    term, dgain, dshift = norm_back(middle_ref[...], gain_ref[1:2, :], second)
    vec_ref[1:2, :] = dgain
    vec_ref[3:4, :] = dshift
    grad_mid = grad_ref[...] + term
    gmid_ref[...] = grad_mid
    mid_low = grad_mid.astype(bf16)
    gather2 = Gather(pc, ml_ref, gsems, 1)
    ml_ref[pc.slot] = mid_low
    gather2.start()
    vec_ref[4:5, :] = jnp.sum(mid_low.astype(f32), axis=0, keepdims=True)

    def mix(step, carry):
        at = gather2.arrive(step)
        grads = ml_ref[pl.ds(2 * at, 2)].reshape(sz.tile, sz.d)
        mg_ref[at] = dot(grads, o_ref[...], (1, 0)).astype(bf16)
        return carry

    lax.fori_loop(0, sz.chips, mix, 0)
    gather2.finish()
    dk_ref[...] = jnp.zeros_like(dk_ref)
    dv_ref[...] = jnp.zeros_like(dv_ref)
    dqv_ref[...] = jnp.zeros_like(dqv_ref)
    scale = HEAD_DIM ** (-0.5)

    def attend(at, carry):
        keys = k_ref[...].reshape(sz.keys, sz.headp)
        values = v_ref[...].reshape(sz.keys, sz.headp)
        total = jnp.zeros((sz.tile, sz.headp), f32)
        for head in range(sz.heads):
            q_head = head_of(q_ref[at], head)
            g_head = head_of(mg_ref[at], head)
            probs = probabilities(q_head, keys, valid_ref[...])
            dprobs = dot(g_head, values, (1, 1))
            inner = jnp.sum(probs * dprobs, axis=-1, keepdims=True)
            dscores = (probs * (dprobs - inner)).astype(bf16)
            total = total + dot(dscores, head_of(keys, head), (1, 0))
            dk_ref[...] += dot(dscores, q_head, (0, 0))
            dv_ref[...] += dot(probs.astype(bf16), g_head, (0, 0))
        dq = (scale * total).astype(bf16).astype(f32)
        dqv_ref[0:1, :] += jnp.sum(dq, axis=0, keepdims=True)
        stack_ref[at, :, 0:sz.headp] = dq.astype(bf16)
        return carry

    lax.fori_loop(0, sz.chips, attend, 0)
    scatter2 = Scatter(pc, bufs, ssems, 1)

    def back_project(step, carry):
        at = pc.index(pc.chip_back(step))
        rows = pl.ds(pl.multiple_of(at * sz.tile, sz.tile), sz.tile)
        dk = (scale * dk_ref[rows, :]).astype(bf16).astype(f32)
        dv = dv_ref[rows, :].astype(bf16).astype(f32)
        dqv_ref[1:2, :] += jnp.sum(dv, axis=0, keepdims=True)
        dq = stack_ref[at, :, 0:sz.headp].astype(f32)
        total = jnp.pad(dq, ((0, 0), (0, sz.qkvp - sz.headp)))
        for kind, piece in ((1, dk), (2, dv)):
            start = kind * sz.wide // 128 * 128
            shift = kind * sz.wide - start
            moved = pltpu.roll(piece, shift, 1) if shift else piece
            total = total + jnp.pad(moved, ((0, 0), (start, sz.qkvp - start - sz.headp)))
        stacked = total.astype(bf16)
        stack_ref[at] = stacked
        scatter2.push(step, dot(stacked, w_ref[:, 0:sz.qkvp], (1, 1)))
        return carry

    lax.fori_loop(0, sz.chips, back_project, 0)
    scatter2.flush()
    o_at = 3 * sz.wide // 128 * 128
    o_shift = 3 * sz.wide - o_at

    def grads_attn(i, carry):
        lanes = pl.ds(pl.multiple_of(i * span, 128), span)
        stacked = stack_ref[...].reshape(sz.keys, sz.qkvp)
        dqkv = dot(n1_ref[:, :, lanes].reshape(sz.keys, span), stacked, (0, 0))
        mixed = mixed_ref[...].reshape(sz.keys, sz.headp)
        dout = dot(ml_ref[:, :, lanes].reshape(sz.keys, span), mixed, (0, 0))
        if o_shift:
            dout = pltpu.roll(dout, o_shift, 1)
        total = jnp.pad(dqkv, ((0, 0), (0, sz.attnp - sz.qkvp))) + jnp.pad(
            dout, ((0, 0), (o_at, sz.attnp - o_at - sz.headp))
        )
        dw_ref[lanes, 0:sz.attnp] = total.astype(bf16)
        return carry

    lax.fori_loop(0, sz.d // span, grads_attn, 0)
    first = scatter2.finish()
    term, dgain, dshift = norm_back(stream_ref[...], gain_ref[0:1, :], first)
    vec_ref[0:1, :] = dgain
    vec_ref[2:3, :] = dshift
    vec_ref[6:8, :] = jnp.zeros_like(vec_ref[6:8, :])
    below_ref[...] = gmid_ref[...] + term


def whole(ref_count):
    return [pl.BlockSpec(memory_space=pltpu.VMEM)] * ref_count


def params(collective_id):
    return pltpu.CompilerParams(
        collective_id=collective_id, has_side_effects=True, vmem_limit_bytes=60 * 1024 * 1024
    )


def forward(sz, stream, w, gains, shifts, qv, upb, resid, valid):
    shapes = [
        ((sz.block, sz.d), f32), ((sz.block, sz.d), f32),
        ((sz.team, sz.block, sz.d), bf16), ((sz.team, sz.block, sz.d), bf16),
        ((sz.chips, sz.tile, sz.headp), bf16), ((sz.chips, sz.tile, sz.headp), bf16),
        ((sz.chips, sz.tile, sz.headp), bf16), ((sz.chips, sz.tile, sz.headp), bf16),
        ((sz.chips, sz.tile, sz.ffp), f32), ((sz.chips, sz.tile, sz.ffp), bf16),
    ]
    return pl.pallas_call(
        functools.partial(forward_kernel, sz),
        out_shape=[jax.ShapeDtypeStruct(*s) for s in shapes],
        in_specs=whole(8),
        out_specs=whole(len(shapes)),
        scratch_shapes=[VMEM((sz.d, sz.headp), bf16)] + team_scratch(sz, 2, 2),
        compiler_params=params(1),
        name="layer_forward",
    )(stream, w, gains, shifts, qv, upb, resid, valid)


def backward(sz, grad, stream, saved, w, gains, valid):
    shapes = [
        ((sz.block, sz.d), f32), ((sz.d, sz.cols), bf16), ((8, sz.d), f32),
        ((2, sz.headp), f32), ((1, sz.ffp), f32),
    ]
    return pl.pallas_call(
        functools.partial(backward_kernel, sz),
        out_shape=[jax.ShapeDtypeStruct(*s) for s in shapes],
        in_specs=whole(14),
        out_specs=whole(len(shapes)),
        scratch_shapes=[
            VMEM((sz.d, sz.headp), bf16),
            VMEM((sz.team, sz.block, sz.d), bf16),
            VMEM((sz.team, sz.block, sz.d), bf16),
            VMEM((sz.chips, sz.tile, sz.ffp), bf16),
            VMEM((sz.chips, sz.tile, sz.headp), bf16),
            VMEM((sz.keys, sz.headp), f32),
            VMEM((sz.keys, sz.headp), f32),
            VMEM((sz.chips, sz.tile, sz.qkvp), bf16),
            VMEM((sz.block, sz.d), f32),
        ]
        + team_scratch(sz, 2, 2),
        compiler_params=params(2),
        name="layer_backward",
    )(grad, stream, *saved, w, gains, valid)


class Weights:
    def __init__(self, pc, own_ref, all_ref, sems):
        self.pc, self.own, self.all, self.sems = pc, own_ref, all_ref, sems

    def along_ctx(self, step):
        pc, sz = self.pc, self.pc.sz
        c = (pc.c + step) % sz.ctx
        return send(self.own.at[c % sz.zl], self.all.at[pc.f * sz.ctx + pc.c], self.sems.at[0, 0, step],
                    self.sems.at[0, 1, step], (pc.f, c, pc.t))

    def own_copy(self):
        pc, sz = self.pc, self.pc.sz
        return pltpu.make_async_copy(self.own.at[pc.zl], self.all.at[pc.f * sz.ctx + pc.c], self.sems.at[0, 0, 0])

    def along_fsdp(self, jump, step):
        pc, sz = self.pc, self.pc.sz
        at = pc.f * sz.ctx + (pc.c + sz.ctx - step) % sz.ctx
        return send(self.all.at[at], self.all.at[at], self.sems.at[jump, 0, step], self.sems.at[jump, 1, step],
                    ((pc.f + jump) % sz.fsdp, pc.c, pc.t))

    def start(self):
        for step in range(1, self.pc.sz.ctx):
            self.along_ctx(step).start()
        self.own_copy().start()

    def forward(self):
        sz = self.pc.sz
        for step in range(sz.ctx):
            if step:
                self.along_ctx(step).wait_recv()
            else:
                self.own_copy().wait()
            for jump in range(1, sz.fsdp):
                self.along_fsdp(jump, step).start()

    def finish(self):
        sz = self.pc.sz
        for step in range(sz.ctx):
            if step:
                self.along_ctx(step).wait_send()
            for jump in range(1, sz.fsdp):
                self.along_fsdp(jump, step).wait()


def weight_peers(pc):
    sz = pc.sz
    return [(pc.f, (pc.c + step) % sz.ctx, pc.t) for step in range(1, sz.ctx)] + [
        ((pc.f + jump) % sz.fsdp, pc.c, pc.t) for jump in range(1, sz.fsdp)
    ]


def fetch_kernel(sz, *refs):
    own_refs, tokens_ref = refs[:sz.layers], refs[sz.layers]
    all_refs, mine_ref = refs[sz.layers + 1:2 * sz.layers + 1], refs[2 * sz.layers + 1]
    wsems, tsems = refs[2 * sz.layers + 2:]
    pc = Place(sz)
    greet(weight_peers(pc))

    def swap(step):
        zh = (pc.zh + step) % sz.images
        return send(tokens_ref.at[zh], mine_ref.at[pc.zh], tsems.at[0, step], tsems.at[1, step],
                    (pc.f, zh * sz.zl + pc.zl, pc.t))

    for step in range(1, sz.images):
        swap(step).start()
    moves = [Weights(pc, own_refs[l], all_refs[l], wsems.at[l]) for l in range(sz.layers)]
    for move in moves:
        move.start()
    mine_ref[pc.zh] = tokens_ref[pc.zh]
    for move in moves:
        move.forward()
    for move in moves:
        move.finish()
    for step in range(1, sz.images):
        swap(step).wait()


def fetch(sz, packs, tokens):
    shapes = [((sz.groups, sz.wrowsp, sz.cols), bf16)] * sz.layers + [(tokens.shape, bf16)]
    return pl.pallas_call(
        functools.partial(fetch_kernel, sz),
        out_shape=[jax.ShapeDtypeStruct(*s) for s in shapes],
        in_specs=whole(sz.layers + 1),
        out_specs=whole(len(shapes)),
        scratch_shapes=[DMA((sz.layers, sz.fsdp, 2, sz.ctx)), DMA((2, sz.images))],
        compiler_params=params(3),
        name="fetch_weights",
    )(*packs, tokens)


class Reduce:
    def __init__(self, pc, dw_ref, out_ref, got, total, recv, sems):
        self.pc, self.dw, self.out = pc, dw_ref, out_ref
        self.got, self.total, self.recv, self.sems = got, total, recv, sems

    def along_fsdp(self, jump, step):
        pc, sz = self.pc, self.pc.sz
        f = (pc.f + jump) % sz.fsdp
        return send(self.dw.at[f * sz.ctx + (pc.c + step) % sz.ctx], self.got.at[jump - 1, step],
                    self.sems.at[jump, 0, step], self.sems.at[jump, 1, step], (f, pc.c, pc.t))

    def along_ctx(self, step):
        pc, sz = self.pc, self.pc.sz
        c = (pc.c + step) % sz.ctx
        return send(self.total.at[step], self.recv.at[step], self.sems.at[0, 0, step], self.sems.at[0, 1, step],
                    (pc.f, c, pc.t))

    def order(self):
        return list(range(1, self.pc.sz.ctx)) + [0]

    def start(self):
        for step in self.order():
            for jump in range(1, self.pc.sz.fsdp):
                self.along_fsdp(jump, step).start()

    def forward(self):
        pc, sz = self.pc, self.pc.sz
        for step in self.order():
            for jump in range(1, sz.fsdp):
                self.along_fsdp(jump, step).wait_recv()
            at = pc.f * sz.ctx + (pc.c + step) % sz.ctx
            total = self.dw[at].astype(f32)
            for jump in range(1, sz.fsdp):
                total = total + self.got[jump - 1, step].astype(f32)
            self.total[step] = total.astype(bf16)
            if step:
                self.along_ctx(step).start()

    def finish(self):
        pc, sz = self.pc, self.pc.sz
        for step in range(1, sz.ctx):
            self.along_ctx(step).wait_recv()
        for j in range(sz.zl):
            total = None
            for zh in range(sz.images):
                step = (pc.c + sz.ctx - (zh * sz.zl + j)) % sz.ctx
                piece = self.recv[step].astype(f32)
                total = piece if total is None else total + piece
            self.out[j] = total
        for step in range(sz.ctx):
            if step:
                self.along_ctx(step).wait_send()
            for jump in range(1, sz.fsdp):
                self.along_fsdp(jump, step).wait_send()


def give_kernel(sz, *refs):
    n = sz.layers
    dw_refs, ends_ref, small_ref, share_ref = refs[:n], refs[n], refs[n + 1], refs[n + 2]
    out_refs, whole_ref, small_out, share_out = refs[n + 3:2 * n + 3], *refs[2 * n + 3:2 * n + 6]
    got, total, recv, rsems, esems, ysems, ssems, from_tp, from_ctx, from_fsdp, sum_tp, sum_ctx = refs[2 * n + 6:]
    pc = Place(sz)
    peers = [(pc.f, (pc.c + s) % sz.ctx, pc.t) for s in range(1, sz.ctx)]
    peers += [((pc.f + s) % sz.fsdp, pc.c, pc.t) for s in range(1, sz.fsdp)]
    peers += [(pc.f, pc.c, (pc.t + s) % sz.tp) for s in range(1, sz.tp)]
    greet(peers)
    moves = [Reduce(pc, dw_refs[l], out_refs[l], got.at[l], total.at[l], recv.at[l], rsems.at[l]) for l in range(n)]

    def swap(step):
        zh = (pc.zh + step) % sz.images
        return send(ends_ref.at[zh], whole_ref.at[pc.t, pc.zh], esems.at[0, step], esems.at[1, step],
                    (pc.f, zh * sz.zl + pc.zl, pc.t))

    def spread(step):
        return send(whole_ref.at[pc.t], whole_ref.at[pc.t], ysems.at[0, step], ysems.at[1, step],
                    (pc.f, pc.c, (pc.t + step) % sz.tp))

    def spread_wait(step):
        back = (pc.t + sz.tp - step) % sz.tp
        return send(whole_ref.at[back], whole_ref.at[back], ysems.at[0, step], ysems.at[1, step],
                    (pc.f, pc.c, back))

    for step in range(1, sz.images):
        swap(step).start()
    whole_ref[pc.t, pc.zh] = ends_ref[pc.zh]
    for move in moves:
        move.start()
    for step in range(1, sz.images):
        swap(step).wait()
    for step in range(1, sz.tp):
        spread(step).start()

    def over_tp(step):
        return send(small_ref, from_tp.at[step], ssems.at[0, 0, step], ssems.at[0, 1, step],
                    (pc.f, pc.c, (pc.t + step) % sz.tp))

    def over_ctx(step):
        return send(sum_tp, from_ctx.at[step], ssems.at[1, 0, step], ssems.at[1, 1, step],
                    (pc.f, (pc.c + step) % sz.ctx, pc.t))

    def over_fsdp(step):
        return send(sum_ctx, from_fsdp.at[step], ssems.at[2, 0, step], ssems.at[2, 1, step],
                    ((pc.f + step) % sz.fsdp, pc.c, pc.t))

    rows = small_ref.shape[0]
    for step in range(1, sz.tp):
        over_tp(step).start()
    for move in moves:
        move.forward()
    value = small_ref[...]
    for step in range(1, sz.tp):
        over_tp(step).wait()
        value = value + from_tp[step]
    sum_tp[0:rows, :] = value
    sum_tp[rows:, :] = share_ref[...]
    for step in range(1, sz.ctx):
        over_ctx(step).start()
    value = sum_tp[...]
    for step in range(1, sz.ctx):
        over_ctx(step).wait()
        value = value + from_ctx[step]
    sum_ctx[...] = value
    for step in range(1, sz.fsdp):
        over_fsdp(step).start()
    for step in range(1, sz.fsdp):
        over_fsdp(step).wait()
        value = value + from_fsdp[step]
    small_out[...] = value[0:rows, :]
    share_out[...] = value[rows:, :]
    for step in range(1, sz.tp):
        spread_wait(step).wait_recv()
        spread(step).wait_send()
    for move in moves:
        move.recv[0] = move.total[0]
        move.finish()


def give(sz, dws, ends, small, share):
    rows = small.shape[0] + share.shape[0]
    shapes = [((sz.zl, sz.wrowsp, sz.cols), f32)] * sz.layers + [
        ((sz.tp,) + ends.shape, bf16), (small.shape, f32), (share.shape, f32),
    ]
    n, far = sz.layers, max(sz.tp, sz.ctx, sz.fsdp)
    return pl.pallas_call(
        functools.partial(give_kernel, sz),
        out_shape=[jax.ShapeDtypeStruct(*s) for s in shapes],
        in_specs=whole(n + 3),
        out_specs=whole(len(shapes)),
        scratch_shapes=[
            VMEM((n, max(sz.fsdp - 1, 1), sz.ctx, sz.wrowsp, sz.cols), bf16),
            VMEM((n, sz.ctx, sz.wrowsp, sz.cols), bf16),
            VMEM((n, sz.ctx, sz.wrowsp, sz.cols), bf16),
            DMA((n, sz.fsdp, 2, sz.ctx)),
            DMA((2, sz.images)),
            DMA((2, sz.tp)),
            DMA((3, 2, far)),
            VMEM((sz.tp,) + small.shape, f32),
            VMEM((sz.ctx, rows, sz.d), f32),
            VMEM((sz.fsdp, rows, sz.d), f32),
            VMEM((rows, sz.d), f32),
            VMEM((rows, sz.d), f32),
        ],
        compiler_params=params(4),
        name="give_gradients",
    )(*dws, ends, small, share)


def pack_weights(sz, w_qkv, w_out, w_up, w_down):
    def split(a, to):
        a = a.reshape(sz.wrows, -1, sz.zl, a.shape[-1] // sz.zl)
        a = jnp.moveaxis(a, 2, 0).reshape(sz.zl, sz.wrows, -1)
        return jnp.pad(a, ((0, 0), (0, sz.wrowsp - sz.wrows), (0, to - a.shape[2])))

    attn = jnp.concatenate([w_qkv, w_out[:, None]], axis=1)
    return jnp.concatenate([split(attn, sz.attnp), split(w_up, sz.ffp), split(w_down, sz.ffp)], axis=2)


def unpack_grads(sz, sums):
    sums = sums[:, :sz.wrows]

    def join(a, kinds):
        a = a.reshape(sz.zl, sz.wrows, kinds, -1)
        return jnp.moveaxis(a, 0, 2).reshape(sz.wrows, kinds, -1)

    attn = join(sums[:, :, :4 * sz.wide], 4)
    up = join(sums[:, :, sz.attnp:sz.attnp + sz.ff], 1)[:, 0]
    down = join(sums[:, :, sz.attnp + sz.ffp:sz.attnp + sz.ffp + sz.ff], 1)[:, 0]
    return attn[:, :3], attn[:, 3], up, down


def per_device(mesh, inputs, cotangent, valid_count, norm_gain, norm_bias, w_qkv, bias_qv, w_out, w_up, bias_up,
               w_down, bias_resid):
    sz = Sizes(mesh, inputs, w_qkv, w_up)
    c, t = lax.axis_index("ctx"), lax.axis_index("tp")
    zh, zl = c // sz.zl, c % sz.zl
    slot = zl * sz.tp + t

    def pieces(a):
        a = jnp.pad(a, ((0, 0), (0, sz.tp * sz.part - sz.rows), (0, 0)))
        return lax.dynamic_slice_in_dim(a, t * sz.part, sz.part, axis=1)

    tokens = jnp.stack([pieces(inputs), pieces(cotangent)], axis=1)

    row = jnp.arange(sz.keys, dtype=jnp.int32)
    of_slot, within = row // sz.block, row % sz.block
    token = (of_slot % sz.tp) * sz.part + within % sz.part
    source = (within // sz.part) * sz.zl + of_slot // sz.tp
    position = source * sz.rows + token
    count = lax.dynamic_index_in_dim(valid_count, zh, keepdims=False)
    valid = ((token < sz.rows) & (position < count)).astype(f32)
    own_valid = lax.dynamic_slice_in_dim(valid, slot * sz.block, sz.block)

    packs = [pack_weights(sz, w_qkv[l], w_out[l], w_up[l], w_down[l]) for l in range(sz.layers)]
    *fetched, mine = fetch(sz, packs, tokens)
    weights = [w[:, :sz.wrows].reshape(sz.d, sz.cols) for w in fetched]
    valid = valid[None, :]

    def half(a, to):
        a = lax.dynamic_index_in_dim(a.reshape(a.shape[0], sz.zl, -1), zl, axis=1, keepdims=False)
        return jnp.pad(a, ((0, 0), (0, to - a.shape[1])))

    stream = mine[:, 0].reshape(sz.block, sz.d).astype(f32)
    streams, kept = [], []
    for l in range(sz.layers):
        streams.append(stream)
        stream, *saved = forward(
            sz, stream, weights[l], norm_gain[l], norm_bias[l], half(bias_qv[l], sz.headp),
            half(bias_up[l][None], sz.ffp), bias_resid[l], valid,
        )
        kept.append(saved)
    output = stream.astype(bf16)

    grad = mine[:, 1].reshape(sz.block, sz.d).astype(f32) * own_valid[:, None]
    dws, vecs, dqvs, dups = [[None] * sz.layers for _ in range(4)]
    for l in reversed(range(sz.layers)):
        grad, dws[l], vecs[l], dqvs[l], dups[l] = backward(
            sz, grad, streams[l], kept[l], weights[l], norm_gain[l], valid
        )
    ends = jnp.stack(
        [output.reshape(sz.images, sz.part, sz.d), grad.astype(bf16).reshape(sz.images, sz.part, sz.d)], axis=1
    )
    blocks = [
        jnp.pad(dw.reshape(sz.groups, sz.wrows, sz.cols), ((0, 0), (0, sz.wrowsp - sz.wrows), (0, 0))) for dw in dws
    ]
    small = jnp.concatenate(vecs, axis=0)
    mine_now = (jnp.arange(sz.zl) == zl).astype(f32)[:, None, None]

    def wide(a):
        return jnp.pad(a, ((0, 0), (0, sz.d - a.shape[1])))

    share = jnp.concatenate([jnp.concatenate([wide(dqvs[l]), wide(dups[l])], axis=0) for l in range(sz.layers)], axis=0)
    share = (share[None] * mine_now).reshape(-1, sz.d)
    share = jnp.pad(share, ((0, up_to(share.shape[0], 8) - share.shape[0]), (0, 0)))
    *sums, ends, small, share = give(sz, blocks, ends, small, share)

    ends = jnp.moveaxis(ends, (2, 1), (0, 1))
    ends = ends.reshape(2, sz.images, sz.tp * sz.part, sz.d)[:, :, :sz.rows]
    small = small.reshape(sz.layers, 8, sz.d)
    share = share[:sz.zl * sz.layers * 3].reshape(sz.zl, sz.layers, 3, sz.d)
    grad_qv = jnp.moveaxis(share[:, :, 0:2, :sz.wide], 0, 2).reshape(sz.layers, 2, -1)
    grad_up_bias = jnp.moveaxis(share[:, :, 2, :sz.ff], 0, 1).reshape(sz.layers, -1)
    large = [unpack_grads(sz, s) for s in sums]
    stack = lambda i: jnp.stack([g[i] for g in large])
    return (
        ends[0], ends[1].astype(f32), small[:, 0:2], small[:, 2:4], stack(0), grad_qv, stack(1), stack(2),
        grad_up_bias, stack(3), small[:, 4:6],
    )


def solution(mesh):
    tokens, rows = P("fsdp", "ctx", None), P(None, ("fsdp", "ctx"), "tp")
    qkv = P(None, ("fsdp", "ctx"), None, "tp")
    qv, up = P(None, None, "tp"), P(None, "tp")
    return jax.shard_map(
        functools.partial(per_device, mesh),
        mesh=mesh,
        in_specs=(tokens, tokens, P("fsdp"), P(), P(), qkv, qv, rows, rows, up, rows, P()),
        out_specs=(tokens, tokens, P(), P(), qkv, qv, rows, rows, up, rows, P()),
        check_vma=False,
    )
```

```python
import functools

import jax
import jax.numpy as jnp
from jax import lax
from jax.experimental import pallas as pl
from jax.experimental.pallas import tpu as pltpu
from jax.sharding import PartitionSpec as P

HEAD_DIM = 72
norm_eps = 1e-06
gelu_root = 0.7978845608028654
gelu_cubic = 0.044715
masked_score = -1e30

MESH = pl.DeviceIdType.MESH
f32 = jnp.float32
bf16 = jnp.bfloat16
VMEM = pltpu.VMEM
DMA = pltpu.SemaphoreType.DMA


def up_to(value, unit):
    return (value + unit - 1) // unit * unit


def dot(a, b, over):
    return lax.dot_general(a, b, (((over[0],), (over[1],)), ((), ())), preferred_element_type=f32)


class Sizes:
    def __init__(self, mesh, inputs, w_qkv, w_up):
        self.fsdp, self.ctx, self.tp = mesh.shape["fsdp"], mesh.shape["ctx"], mesh.shape["tp"]
        self.images, self.rows, self.d = inputs.shape
        self.layers, self.wrows = w_qkv.shape[0], w_qkv.shape[1]
        self.zl = self.ctx // self.images
        self.chips_y = self.tp // 2
        self.chips = self.zl * self.chips_y
        self.team = self.chips * 2
        self.part = up_to(-(-self.rows // self.tp), 16)
        self.block = self.images * self.part
        self.tile = 2 * self.block
        self.keys = self.chips * self.tile
        self.wide = w_qkv.shape[3] // self.zl
        self.heads = self.wide // HEAD_DIM
        self.ff = w_up.shape[2] // self.zl
        self.ffw = up_to(2 * self.ff, 128)
        self.down_at = self.ff // 128 * 128
        self.down_shift = self.ff - self.down_at
        self.ffp = self.ffw - self.down_at
        self.headp = up_to(self.wide, 128)
        self.qkvp = up_to(3 * self.wide, 128)
        self.attnp = up_to(4 * self.wide, 128)
        self.wrowsp = up_to(self.wrows, 16)
        self.groups = self.fsdp * self.ctx


class Place:
    def __init__(self, sz):
        self.sz = sz
        self.f, self.c, self.t = lax.axis_index("fsdp"), lax.axis_index("ctx"), lax.axis_index("tp")
        self.zh, self.zl = self.c // sz.zl, self.c % sz.zl
        self.y, self.k = self.t // 2, self.t % 2
        self.chip = self.zl * sz.chips_y + self.y
        self.slot = 2 * self.chip + self.k

    def chip_at(self, step):
        sz = self.sz
        zl = (self.zl + step // sz.chips_y) % sz.zl
        y = (self.y + step % sz.chips_y) % sz.chips_y
        return zl, y

    def chip_back(self, step):
        sz = self.sz
        zl = (self.zl + sz.zl - step // sz.chips_y) % sz.zl
        y = (self.y + sz.chips_y - step % sz.chips_y) % sz.chips_y
        return zl, y

    def index(self, chip):
        return chip[0] * self.sz.chips_y + chip[1]

    def device(self, chip):
        return (self.f, self.zh * self.sz.zl + chip[0], 2 * chip[1] + self.k)

    @property
    def twin(self):
        return (self.f, self.c, self.t + 1 - 2 * self.k)


    def ctx_ahead(self, step):
        sz = self.sz
        return (self.zh + step // sz.zl) % sz.images * sz.zl + (self.zl + step % sz.zl) % sz.zl

    def ctx_back(self, step):
        sz = self.sz
        zh = (self.zh + sz.images - step // sz.zl) % sz.images
        return zh * sz.zl + (self.zl + sz.zl - step % sz.zl) % sz.zl


def greet(others):
    barrier = pltpu.get_barrier_semaphore()
    for other in others:
        pl.semaphore_signal(barrier, inc=1, device_id=other, device_id_type=MESH)
    pl.semaphore_wait(barrier, len(others))


def send(src, dst, send_sem, recv_sem, device):
    return pltpu.make_async_remote_copy(
        src_ref=src, dst_ref=dst, send_sem=send_sem, recv_sem=recv_sem, device_id=device, device_id_type=MESH
    )


def team_peers(pc):
    return [pc.device(pc.chip_at(step)) for step in range(1, pc.sz.chips)] + [pc.twin]


def weight_peers(pc, team=False):
    sz = pc.sz
    first = sz.zl if team else 1
    return [(pc.f, pc.ctx_ahead(step), pc.t) for step in range(first, sz.ctx)] + [
        ((pc.f + jump) % sz.fsdp, pc.c, pc.t) for jump in range(1, sz.fsdp)
    ]


class Gather:
    def __init__(self, pc, buf, sems, at):
        self.pc, self.buf, self.sems, self.at = pc, buf, sems, at

    def far(self, step, slot, device):
        return send(self.buf.at[slot], self.buf.at[slot], self.sems.at[self.at, 0, step],
                    self.sems.at[self.at, 1, step], device)

    def near(self, step, slot):
        return send(self.buf.at[slot], self.buf.at[slot], self.sems.at[self.at, 2, step],
                    self.sems.at[self.at, 3, step], self.pc.twin)

    def start(self):
        pc = self.pc
        for step in range(1, pc.sz.chips):
            self.far(step, pc.slot, pc.device(pc.chip_at(step))).start()
        self.near(0, pc.slot).start()

    def arrive(self, step):
        pc = self.pc
        chip = pc.chip_back(step)
        at = pc.index(chip)

        @pl.when(step > 0)
        def _():
            self.far(step, 2 * at + pc.k, pc.device(chip)).wait_recv()
            self.near(step, 2 * at + pc.k).start()

        self.near(step, 2 * at + 1 - pc.k).wait_recv()
        return at

    def finish(self):
        pc = self.pc
        for step in range(pc.sz.chips):
            if step:
                self.far(step, pc.slot, pc.device(pc.chip_at(step))).wait_send()
            self.near(step, pc.slot).wait_send()


class Scatter:
    def __init__(self, pc, bufs, sems, at):
        self.pc, self.sems, self.at = pc, sems, at
        self.both, self.keep, self.tsend, self.trecv, self.rsend, self.rrecv = bufs

    def near(self, step):
        return send(self.tsend.at[step], self.trecv.at[step], self.sems.at[self.at, 0, step],
                    self.sems.at[self.at, 1, step], self.pc.twin)

    def far(self, step):
        return send(self.rsend.at[step], self.rrecv.at[step], self.sems.at[self.at, 2, step],
                    self.sems.at[self.at, 3, step], self.pc.device(self.pc.chip_back(step)))

    def push(self, step, partial):
        pc, block = self.pc, self.pc.sz.block
        self.both[...] = partial.reshape(2, block, partial.shape[-1])
        self.tsend[step] = self.both[1 - pc.k].astype(bf16)
        self.near(step).start()
        self.keep[step] = self.both[pc.k]

        @pl.when(step > 0)
        def _():
            self.relay(step - 1)

    def relay(self, step):
        self.near(step).wait_recv()
        total = self.keep[step] + self.trecv[step].astype(f32)

        def own():
            self.keep[0] = total

        def other():
            self.rsend[step] = total.astype(bf16)
            self.far(step).start()

        if isinstance(step, int):
            own() if step == 0 else other()
        else:
            pl.when(step == 0)(own)
            pl.when(step > 0)(other)

    def flush(self):
        self.relay(self.pc.sz.chips - 1)

    def finish(self):
        total = self.keep[0]
        for step in range(1, self.pc.sz.chips):
            self.far(step).wait_recv()
            total = total + self.rrecv[step].astype(f32)
        for step in range(self.pc.sz.chips):
            self.near(step).wait_send()
            if step:
                self.far(step).wait_send()
        return total


def team_scratch(sz, gathers, scatters):
    n = sz.chips
    return [
        VMEM((2, sz.block, sz.d), f32),
        VMEM((n, sz.block, sz.d), f32),
        VMEM((n, sz.block, sz.d), bf16),
        VMEM((n, sz.block, sz.d), bf16),
        VMEM((n, sz.block, sz.d), bf16),
        VMEM((n, sz.block, sz.d), bf16),
        DMA((gathers, 4, n)),
        DMA((scatters, 4, n)),
    ]


def normalised(values):
    centre = jnp.mean(values, axis=-1, keepdims=True)
    centred = values - centre
    spread = jnp.mean(centred * centred, axis=-1, keepdims=True)
    inverse = lax.rsqrt(spread + norm_eps)
    return centred * inverse, inverse


def norm_back(values, gain, grad):
    high, inverse = normalised(values)
    scaled = grad * gain
    term = inverse * (
        scaled
        - jnp.mean(scaled, axis=-1, keepdims=True)
        - high * jnp.mean(scaled * high, axis=-1, keepdims=True)
    )
    return term, jnp.sum(grad * high, axis=0, keepdims=True), jnp.sum(grad, axis=0, keepdims=True)


def lanes_of(shape):
    return lax.broadcasted_iota(jnp.int32, shape, len(shape) - 1)


def unpack_out(sz, w_ref, o_ref):
    at = 3 * sz.wide // 128 * 128
    shift = 3 * sz.wide - at

    def step(i, carry):
        rows = pl.ds(pl.multiple_of(i * 128, 128), 128)
        piece = pltpu.roll(w_ref[rows, at:at + sz.headp].astype(f32), sz.headp - shift, 1)
        o_ref[rows, :] = jnp.where(lanes_of(piece.shape) < sz.wide, piece, 0.0).astype(bf16)
        return carry

    lax.fori_loop(0, sz.d // 128, step, 0)


def take(sz, values, kind):
    at = kind * sz.wide // 128 * 128
    shift = kind * sz.wide - at
    piece = values[:, at:at + sz.headp]
    if shift:
        piece = pltpu.roll(piece, sz.headp - shift, 1)
    return jnp.where(lanes_of(piece.shape) < sz.wide, piece, 0.0)


def head_of(values, head):
    lanes = lanes_of(values.shape)
    mine = (lanes >= head * HEAD_DIM) & (lanes < (head + 1) * HEAD_DIM)
    return jnp.where(mine, values, jnp.zeros_like(values))


def probabilities(q_head, keys, valid):
    scores = dot(q_head, keys, (1, 1)) * HEAD_DIM ** (-0.5)
    scores = jnp.where(valid > 0.0, scores, masked_score)
    weights = jnp.exp(scores - jnp.max(scores, axis=-1, keepdims=True))
    return weights / jnp.sum(weights, axis=-1, keepdims=True)


class Fetch:
    def __init__(self, pc, own, everything, sems):
        self.pc, self.own, self.all, self.sems = pc, own, everything, sems
        self.parts = [self.start, self.pass_own] + [
            functools.partial(self.pass_on, step) for step in range(1, pc.sz.ctx)
        ]

    def along_ctx(self, step):
        pc = self.pc
        c = pc.ctx_ahead(step)
        return send(self.own.at[c % pc.sz.zl], self.all.at[pc.f * pc.sz.ctx + pc.c], self.sems.at[0, 0, step],
                    self.sems.at[0, 1, step], (pc.f, c, pc.t))

    def own_copy(self):
        pc = self.pc
        return pltpu.make_async_copy(self.own.at[pc.zl], self.all.at[pc.f * pc.sz.ctx + pc.c], self.sems.at[0, 0, 0])

    def along_fsdp(self, jump, step):
        pc, sz = self.pc, self.pc.sz
        at = pc.f * sz.ctx + pc.ctx_back(step)
        return send(self.all.at[at], self.all.at[at], self.sems.at[jump, 0, step], self.sems.at[jump, 1, step],
                    ((pc.f + jump) % sz.fsdp, pc.c, pc.t))

    def start(self):
        self.own_copy().start()
        for step in range(1, self.pc.sz.ctx):
            self.along_ctx(step).start()

    def pass_own(self):
        self.own_copy().wait()
        for jump in range(1, self.pc.sz.fsdp):
            self.along_fsdp(jump, 0).start()

    def pass_on(self, step):
        self.along_ctx(step).wait_recv()
        for jump in range(1, self.pc.sz.fsdp):
            self.along_fsdp(jump, step).start()

    def finish(self):
        sz = self.pc.sz
        for step in range(sz.ctx):
            if step:
                self.along_ctx(step).wait_send()
            for jump in range(1, sz.fsdp):
                self.along_fsdp(jump, step).wait()

    @staticmethod
    def result(sz, cols):
        return [((sz.groups, sz.wrowsp, cols), bf16)]

    @staticmethod
    def scratch(sz, cols):
        return [DMA((sz.fsdp, 2, sz.ctx))]


class Give:
    def __init__(self, pc, dw, out, got, total, recv, sems):
        self.pc, self.dw, self.out = pc, dw, out
        self.got, self.total, self.recv, self.sems = got, total, recv, sems
        self.order = list(range(pc.sz.ctx - 1, -1, -1))
        self.parts = [self.start] + [functools.partial(self.pass_on, step) for step in self.order]

    def along_fsdp(self, jump, step):
        pc, sz = self.pc, self.pc.sz
        f = (pc.f + jump) % sz.fsdp
        return send(self.dw.at[f * sz.ctx + pc.ctx_ahead(step)], self.got.at[jump - 1, step],
                    self.sems.at[jump, 0, step], self.sems.at[jump, 1, step], (f, pc.c, pc.t))

    def along_ctx(self, step):
        pc = self.pc
        return send(self.total.at[step], self.recv.at[pc.c], self.sems.at[0, 0, step], self.sems.at[0, 1, step],
                    (pc.f, pc.ctx_ahead(step), pc.t))

    def from_ctx(self, step):
        pc = self.pc
        return send(self.total.at[step], self.recv.at[pc.ctx_back(step)], self.sems.at[0, 0, step],
                    self.sems.at[0, 1, step], (pc.f, pc.ctx_back(step), pc.t))

    def start(self):
        for step in self.order:
            for jump in range(1, self.pc.sz.fsdp):
                self.along_fsdp(jump, step).start()

    def pass_on(self, step):
        pc, sz = self.pc, self.pc.sz
        for jump in range(1, sz.fsdp):
            self.along_fsdp(jump, step).wait_recv()
        total = self.dw[pc.f * sz.ctx + pc.ctx_ahead(step)].astype(f32)
        for jump in range(1, sz.fsdp):
            total = total + self.got[jump - 1, step].astype(f32)
        if step:
            self.total[step] = total.astype(bf16)
            self.along_ctx(step).start()
        else:
            self.recv[pc.c] = total.astype(bf16)

    def finish(self):
        pc, sz = self.pc, self.pc.sz
        for step in range(1, sz.ctx):
            self.from_ctx(step).wait_recv()
        for j in range(sz.zl):
            total = self.recv[j].astype(f32)
            for zh in range(1, sz.images):
                total = total + self.recv[zh * sz.zl + j].astype(f32)
            self.out[j] = total
        for step in range(sz.ctx):
            if step:
                self.along_ctx(step).wait_send()
            for jump in range(1, sz.fsdp):
                self.along_fsdp(jump, step).wait_send()

    @staticmethod
    def result(sz, cols):
        return [((sz.zl, sz.wrowsp, cols), f32)]

    @staticmethod
    def scratch(sz, cols):
        return [
            VMEM((max(sz.fsdp - 1, 1), sz.ctx, sz.wrowsp, cols), bf16),
            VMEM((sz.ctx, sz.wrowsp, cols), bf16),
            VMEM((sz.ctx, sz.wrowsp, cols), bf16),
            DMA((sz.fsdp, 2, sz.ctx)),
        ]


class Beside:
    def __init__(self, pc, mover, refs):
        self.mover = mover(pc, *refs) if mover else None

    def part(self, index):
        if self.mover:
            self.mover.parts[index]()

    def rest(self, first):
        if self.mover:
            for part in self.mover.parts[first:]:
                part()

    def at(self, step, places):
        if self.mover:
            for when, index in places.items():
                pl.when(step == when)(functools.partial(self.part, index))

    def finish(self):
        if self.mover:
            self.mover.finish()


def split_refs(refs, *counts):
    out, at = [], 0
    for count in counts:
        out.append(refs[at:at + count])
        at += count
    assert at == len(refs)
    return out


def layer_kernel(body, ins, outs, scratch, gathers, scatters, mover, sz, *refs):
    m = 1 if mover else 0
    own, team = len(scratch), 8
    rest = len(refs) - ins - m - outs - m - own - team
    a, ma, b, mb, s, t, ms = split_refs(refs, ins, m, outs, m, own, team, rest)
    pc = Place(sz)
    greet(team_peers(pc) + (weight_peers(pc, True) if mover else []))
    body(sz, pc, Beside(pc, mover, (*ma, *mb, *ms)), *a, *b, *s, t[:6], t[6], t[7])


def layer_call(sz, name, ident, body, operands, shapes, scratch, gathers, scatters, mover=None, extra=None):
    cols = extra.shape[-1] if mover else 0
    results = list(shapes) + (mover.result(sz, cols) if mover else [])
    n_in = len(operands) + (1 if mover else 0)
    return pl.pallas_call(
        functools.partial(layer_kernel, body, len(operands), len(shapes), scratch, gathers, scatters, mover, sz),
        out_shape=[jax.ShapeDtypeStruct(*s) for s in results],
        in_specs=whole(n_in),
        out_specs=whole(len(results)),
        scratch_shapes=scratch + team_scratch(sz, gathers, scatters) + (mover.scratch(sz, cols) if mover else []),
        compiler_params=params(ident),
        name=name,
    )(*operands, *([extra] if mover else []))


def whole(ref_count):
    return [pl.BlockSpec(memory_space=pltpu.VMEM)] * ref_count


def params(collective_id):
    return pltpu.CompilerParams(
        collective_id=collective_id, has_side_effects=True, vmem_limit_bytes=60 * 1024 * 1024
    )


def attn_forward(sz, pc, beside, stream_ref, w_ref, gain_ref, shift_ref, qv_ref, resid_ref, valid_ref,
                 middle_ref, n1_ref, q_ref, k_ref, v_ref, mixed_ref, o_ref, bufs, gsems, ssems):
    gather = Gather(pc, n1_ref, gsems, 0)
    high, _ = normalised(stream_ref[...])
    n1_ref[pc.slot] = (high * gain_ref[0:1, :] + shift_ref[0:1, :]).astype(bf16)
    gather.start()
    beside.part(0)
    unpack_out(sz, w_ref, o_ref)
    beside.part(1)

    def project(step, carry):
        at = gather.arrive(step)
        tokens = n1_ref[pl.ds(2 * at, 2)].reshape(sz.tile, sz.d)
        both3 = dot(tokens, w_ref[:, 0:sz.qkvp], (1, 0))
        q_ref[at] = (take(sz, both3, 0) + qv_ref[0:1, :]).astype(bf16)
        k_ref[at] = take(sz, both3, 1).astype(bf16)
        v_ref[at] = (take(sz, both3, 2) + qv_ref[1:2, :]).astype(bf16)
        return carry

    lax.fori_loop(0, sz.chips, project, 0)
    gather.finish()
    scatter = Scatter(pc, bufs, ssems, 0)

    def attend(step, carry):
        at = pc.index(pc.chip_back(step))
        keys = k_ref[...].reshape(sz.keys, sz.headp)
        values = v_ref[...].reshape(sz.keys, sz.headp)
        queries = q_ref[at]
        total = jnp.zeros((sz.tile, sz.headp), f32)
        for head in range(sz.heads):
            probs = probabilities(head_of(queries, head), keys, valid_ref[...])
            total = total + dot(probs.astype(bf16), head_of(values, head), (1, 0))
        mixed = total.astype(bf16)
        mixed_ref[at] = mixed
        scatter.push(step, dot(mixed, o_ref[...], (1, 1)))
        beside.at(step, {sz.chips - 1: 2})
        return carry

    lax.fori_loop(0, sz.chips, attend, 0)
    scatter.flush()
    beside.rest(3)
    middle_ref[...] = stream_ref[...] + (scatter.finish() + resid_ref[0:1, :])
    beside.finish()


def ff_forward(sz, pc, beside, middle_ref, w_ref, gain_ref, shift_ref, upb_ref, resid_ref,
               out_ref, n2_ref, pre_ref, hidden_ref, bufs, gsems, ssems):
    gather = Gather(pc, n2_ref, gsems, 0)
    high, _ = normalised(middle_ref[...])
    n2_ref[pc.slot] = (high * gain_ref[1:2, :] + shift_ref[1:2, :]).astype(bf16)
    gather.start()
    beside.part(0)
    beside.part(1)
    scatter = Scatter(pc, bufs, ssems, 0)

    def feed(step, carry):
        at = gather.arrive(step)
        tokens = n2_ref[pl.ds(2 * at, 2)].reshape(sz.tile, sz.d)
        pre = dot(tokens, w_ref[:, 0:sz.ffp], (1, 0)) + upb_ref[...]
        pre_ref[at] = pre
        hidden = 0.5 * pre * (1.0 + jnp.tanh(gelu_root * (pre + gelu_cubic * pre * pre * pre)))
        hidden = jnp.where(lanes_of(hidden.shape) < sz.ff, hidden, 0.0)
        if sz.down_shift:
            hidden = pltpu.roll(hidden, sz.down_shift, 1)
        hidden = hidden.astype(bf16)
        hidden_ref[at] = hidden
        scatter.push(step, dot(hidden, w_ref[:, sz.down_at:], (1, 1)))
        beside.at(step, {sz.chips - 1: 2})
        return carry

    lax.fori_loop(0, sz.chips, feed, 0)
    scatter.flush()
    gather.finish()
    beside.rest(3)
    out_ref[...] = middle_ref[...] + (scatter.finish() + resid_ref[1:2, :])
    beside.finish()


def ff_backward(sz, pc, beside, grad_ref, middle_ref, n2_ref, pre_ref, hidden_ref, w_ref, gain_ref,
                gmid_ref, dw_ref, vec_ref, dup_ref, gl_ref, pg_ref, bufs, gsems, ssems):
    span = 384 if sz.d % 384 == 0 else 128
    gather = Gather(pc, gl_ref, gsems, 0)
    grad_low = grad_ref[...].astype(bf16)
    gl_ref[pc.slot] = grad_low
    gather.start()
    beside.part(0)
    vec_ref[...] = jnp.zeros_like(vec_ref)
    vec_ref[2:3, :] = jnp.sum(grad_low.astype(f32), axis=0, keepdims=True)
    scatter = Scatter(pc, bufs, ssems, 0)
    dup_ref[...] = jnp.zeros_like(dup_ref)

    def feed(step, carry):
        at = gather.arrive(step)
        grads = gl_ref[pl.ds(2 * at, 2)].reshape(sz.tile, sz.d)
        back = dot(grads, w_ref[:, sz.down_at:], (1, 0))
        if sz.down_shift:
            back = pltpu.roll(back, sz.ffp - sz.down_shift, 1)
        pre = pre_ref[at]
        bent = jnp.tanh(gelu_root * (pre + gelu_cubic * pre * pre * pre))
        slope = 0.5 * (1.0 + bent) + 0.5 * pre * (1.0 - bent * bent) * (
            gelu_root * (1.0 + 3.0 * gelu_cubic * pre * pre)
        )
        pre_grad = jnp.where(lanes_of(back.shape) < sz.ff, back * slope, 0.0).astype(bf16)
        pg_ref[at] = pre_grad
        dup_ref[...] += jnp.sum(pre_grad.astype(f32), axis=0, keepdims=True)
        scatter.push(step, dot(pre_grad, w_ref[:, 0:sz.ffp], (1, 1)))
        beside.at(step, {sz.chips - 2: 1, sz.chips - 1: 2})
        return carry

    lax.fori_loop(0, sz.chips, feed, 0)
    scatter.flush()
    beside.rest(3)

    def grads_ff(i, carry):
        lanes = pl.ds(pl.multiple_of(i * span, 128), span)
        hidden = hidden_ref[...].reshape(sz.keys, sz.ffp)
        down = dot(gl_ref[:, :, lanes].reshape(sz.keys, span), hidden, (0, 0))
        pre_grad = pg_ref[...].reshape(sz.keys, sz.ffp)
        up = dot(n2_ref[:, :, lanes].reshape(sz.keys, span), pre_grad, (0, 0))
        dw_ref[lanes, 0:sz.down_at] = up[:, 0:sz.down_at].astype(bf16)
        over = sz.ffp - sz.down_at
        if over:
            dw_ref[lanes, sz.down_at:sz.ffp] = (up[:, sz.down_at:] + down[:, 0:over]).astype(bf16)
        dw_ref[lanes, sz.ffp:] = down[:, over:].astype(bf16)
        return carry

    lax.fori_loop(0, sz.d // span, grads_ff, 0)
    gather.finish()
    second = scatter.finish()
    term, dgain, dshift = norm_back(middle_ref[...], gain_ref[1:2, :], second)
    vec_ref[0:1, :] = dgain
    vec_ref[1:2, :] = dshift
    gmid_ref[...] = grad_ref[...] + term
    beside.finish()


def attn_backward(sz, pc, beside, gmid_ref, stream_ref, n1_ref, q_ref, k_ref, v_ref, mixed_ref, w_ref, gain_ref,
                  valid_ref, below_ref, dw_ref, vec_ref, dqv_ref,
                  o_ref, ml_ref, mg_ref, dk_ref, dv_ref, stack_ref, bufs, gsems, ssems):
    span = 384 if sz.d % 384 == 0 else 128
    gather = Gather(pc, ml_ref, gsems, 0)
    mid_low = gmid_ref[...].astype(bf16)
    ml_ref[pc.slot] = mid_low
    gather.start()
    beside.part(0)
    vec_ref[...] = jnp.zeros_like(vec_ref)
    vec_ref[2:3, :] = jnp.sum(mid_low.astype(f32), axis=0, keepdims=True)
    unpack_out(sz, w_ref, o_ref)

    def mix(step, carry):
        at = gather.arrive(step)
        grads = ml_ref[pl.ds(2 * at, 2)].reshape(sz.tile, sz.d)
        mg_ref[at] = dot(grads, o_ref[...], (1, 0)).astype(bf16)
        return carry

    lax.fori_loop(0, sz.chips, mix, 0)
    gather.finish()
    beside.part(1)
    dk_ref[...] = jnp.zeros_like(dk_ref)
    dv_ref[...] = jnp.zeros_like(dv_ref)
    dqv_ref[...] = jnp.zeros_like(dqv_ref)
    scale = HEAD_DIM ** (-0.5)

    def attend(at, carry):
        keys = k_ref[...].reshape(sz.keys, sz.headp)
        values = v_ref[...].reshape(sz.keys, sz.headp)
        total = jnp.zeros((sz.tile, sz.headp), f32)
        for head in range(sz.heads):
            q_head = head_of(q_ref[at], head)
            g_head = head_of(mg_ref[at], head)
            probs = probabilities(q_head, keys, valid_ref[...])
            dprobs = dot(g_head, values, (1, 1))
            inner = jnp.sum(probs * dprobs, axis=-1, keepdims=True)
            dscores = (probs * (dprobs - inner)).astype(bf16)
            total = total + dot(dscores, head_of(keys, head), (1, 0))
            dk_ref[...] += dot(dscores, q_head, (0, 0))
            dv_ref[...] += dot(probs.astype(bf16), g_head, (0, 0))
        dq = (scale * total).astype(bf16).astype(f32)
        dqv_ref[0:1, :] += jnp.sum(dq, axis=0, keepdims=True)
        stack_ref[at, :, 0:sz.headp] = dq.astype(bf16)
        beside.at(at, {1: 2, 3: 3})
        return carry

    lax.fori_loop(0, sz.chips, attend, 0)
    beside.rest(4)
    scatter = Scatter(pc, bufs, ssems, 0)

    def back_project(step, carry):
        at = pc.index(pc.chip_back(step))
        rows = pl.ds(pl.multiple_of(at * sz.tile, sz.tile), sz.tile)
        dk = (scale * dk_ref[rows, :]).astype(bf16).astype(f32)
        dv = dv_ref[rows, :].astype(bf16).astype(f32)
        dqv_ref[1:2, :] += jnp.sum(dv, axis=0, keepdims=True)
        dq = stack_ref[at, :, 0:sz.headp].astype(f32)
        total = jnp.pad(dq, ((0, 0), (0, sz.qkvp - sz.headp)))
        for kind, piece in ((1, dk), (2, dv)):
            start = kind * sz.wide // 128 * 128
            shift = kind * sz.wide - start
            moved = pltpu.roll(piece, shift, 1) if shift else piece
            total = total + jnp.pad(moved, ((0, 0), (start, sz.qkvp - start - sz.headp)))
        stacked = total.astype(bf16)
        stack_ref[at] = stacked
        scatter.push(step, dot(stacked, w_ref[:, 0:sz.qkvp], (1, 1)))
        return carry

    lax.fori_loop(0, sz.chips, back_project, 0)
    scatter.flush()
    o_at = 3 * sz.wide // 128 * 128
    o_shift = 3 * sz.wide - o_at

    def grads_attn(i, carry):
        lanes = pl.ds(pl.multiple_of(i * span, 128), span)
        stacked = stack_ref[...].reshape(sz.keys, sz.qkvp)
        dqkv = dot(n1_ref[:, :, lanes].reshape(sz.keys, span), stacked, (0, 0))
        mixed = mixed_ref[...].reshape(sz.keys, sz.headp)
        dout = dot(ml_ref[:, :, lanes].reshape(sz.keys, span), mixed, (0, 0))
        if o_shift:
            dout = pltpu.roll(dout, o_shift, 1)
        total = jnp.pad(dqkv, ((0, 0), (0, sz.attnp - sz.qkvp))) + jnp.pad(
            dout, ((0, 0), (o_at, sz.attnp - o_at - sz.headp))
        )
        dw_ref[lanes, 0:sz.attnp] = total.astype(bf16)
        return carry

    lax.fori_loop(0, sz.d // span, grads_attn, 0)
    first = scatter.finish()
    term, dgain, dshift = norm_back(stream_ref[...], gain_ref[0:1, :], first)
    vec_ref[0:1, :] = dgain
    vec_ref[1:2, :] = dshift
    below_ref[...] = gmid_ref[...] + term
    beside.finish()


def shift_lanes(values, start, count, at, width):
    have = values.shape[-1]
    first, last = start // 128 * 128, up_to(start + count, 128)
    to = at // 128 * 128
    span = max(last - first, up_to(at + count, 128) - to)
    piece = values[:, first:min(last, have)].astype(f32)
    if piece.shape[-1] < span:
        piece = jnp.pad(piece, ((0, 0), (0, span - piece.shape[-1])))
    turn = ((at - to) - (start - first)) % span
    if turn:
        piece = pltpu.roll(piece, turn, 1)
    lanes = lanes_of(piece.shape)
    piece = jnp.where((lanes >= at - to) & (lanes < at - to + count), piece, 0.0)
    piece = piece[:, 0:min(span, width - to)]
    return jnp.pad(piece, ((0, 0), (to, width - to - piece.shape[-1])))


def open_kernel(sz, wqkv_ref, wout_ref, wup_ref, wdown_ref, tokens_ref, valid_ref, *refs):
    n = sz.layers
    everything, attn_refs, ff_refs, (stream_ref, grad_ref), (attn0_ref, mine_ref, tsems, wsems) = split_refs(
        refs, 1, n - 1, n, 2, 4
    )
    attn_refs = [attn0_ref] + list(attn_refs)
    pc = Place(sz)
    greet(weight_peers(pc))

    def swap(step):
        zh = (pc.zh + step) % sz.images
        return send(tokens_ref.at[zh], mine_ref.at[pc.zh], tsems.at[0, step], tsems.at[1, step],
                    (pc.f, zh * sz.zl + pc.zl, pc.t))

    def pack(ref, half, pieces):
        total = None
        for values, start, count, at in pieces:
            piece = shift_lanes(values, start, count, at, ref.shape[-1])
            total = piece if total is None else total + piece
        ref[half, 0:sz.wrows, :] = total.astype(bf16)
        if sz.wrowsp > sz.wrows:
            ref[half, sz.wrows:, :] = jnp.zeros((sz.wrowsp - sz.wrows, ref.shape[-1]), bf16)

    def pack_attn(layer):
        full = sz.wide * sz.zl
        for half in range(sz.zl):
            pieces = [(wqkv_ref[layer], kind * full + half * sz.wide, sz.wide, kind * sz.wide) for kind in range(3)]
            pack(attn_refs[layer], half, pieces + [(wout_ref[layer], half * sz.wide, sz.wide, 3 * sz.wide)])

    pack_attn(0)
    move = Fetch(pc, attn0_ref, everything[0], wsems)
    move.parts[0]()
    for step in range(1, sz.images):
        swap(step).start()
    move.parts[1]()
    mine_ref[pc.zh] = tokens_ref[pc.zh]
    for layer in range(n):
        if layer:
            pack_attn(layer)
        for half in range(sz.zl):
            pack(ff_refs[layer], half, [(wup_ref[layer], half * sz.ff, sz.ff, 0),
                                        (wdown_ref[layer], half * sz.ff, sz.ff, sz.ff)])
    for step in range(1, sz.images):
        swap(step).wait()
    stream_ref[...] = mine_ref[:, 0].reshape(sz.block, sz.d).astype(f32)
    grad_ref[...] = mine_ref[:, 1].reshape(sz.block, sz.d).astype(f32) * valid_ref[...]
    for part in move.parts[2:]:
        part()
    move.finish()


def open_call(sz, w_qkv, w_out, w_up, w_down, tokens, own_valid):
    attn, ff = ((sz.zl, sz.wrowsp, sz.attnp), bf16), ((sz.zl, sz.wrowsp, sz.ffw), bf16)
    own = ((sz.block, sz.d), f32)
    shapes = Fetch.result(sz, sz.attnp) + [attn] * (sz.layers - 1) + [ff] * sz.layers + [own, own]
    operands = (w_qkv.reshape(sz.layers, sz.wrows, -1), w_out, w_up, w_down, tokens, own_valid)
    return pl.pallas_call(
        functools.partial(open_kernel, sz),
        out_shape=[jax.ShapeDtypeStruct(*s) for s in shapes],
        in_specs=whole(len(operands)),
        out_specs=whole(len(shapes)),
        scratch_shapes=[VMEM(*attn), VMEM(tokens.shape, bf16), DMA((2, sz.images))] + Fetch.scratch(sz, 0),
        compiler_params=params(9),
        name="open",
    )(*operands)


def give_kernel(sz, dw_ref, stream_ref, grad_ref, *refs):
    n = sz.layers
    ff_vecs, attn_vecs, dqvs, dups, (sum_ref, whole_ref, small_ref), own, give_refs = split_refs(
        refs, n, n, n, n, 3, 10, 4
    )
    ends_ref, esems, ysems, ssems, first, from_tp, from_ctx, from_fsdp, sum_tp, sum_ctx = own
    pc = Place(sz)
    greet(weight_peers(pc) + [(pc.f, pc.c, (pc.t + s) % sz.tp) for s in range(1, sz.tp)])
    move = Give(pc, dw_ref, sum_ref, *give_refs)
    move.parts[0]()

    def swap(step):
        zh = (pc.zh + step) % sz.images
        return send(ends_ref.at[zh], whole_ref.at[pc.t, pc.zh], esems.at[0, step], esems.at[1, step],
                    (pc.f, zh * sz.zl + pc.zl, pc.t))

    def spread(step):
        return send(whole_ref.at[pc.t], whole_ref.at[pc.t], ysems.at[0, step], ysems.at[1, step],
                    (pc.f, pc.c, (pc.t + step) % sz.tp))

    def spread_wait(step):
        back = (pc.t + sz.tp - step) % sz.tp
        return send(whole_ref.at[back], whole_ref.at[back], ysems.at[0, step], ysems.at[1, step],
                    (pc.f, pc.c, back))

    for kind, ref in enumerate((stream_ref, grad_ref)):
        ends_ref[:, kind] = ref[...].reshape(sz.images, sz.part, sz.d).astype(bf16)
    for step in range(1, sz.images):
        swap(step).start()
    whole_ref[pc.t, pc.zh] = ends_ref[pc.zh]

    def over_tp(step):
        return send(first, from_tp.at[step], ssems.at[0, 0, step], ssems.at[0, 1, step],
                    (pc.f, pc.c, (pc.t + step) % sz.tp))

    def over_ctx(step):
        return send(sum_tp, from_ctx.at[step], ssems.at[1, 0, step], ssems.at[1, 1, step],
                    (pc.f, pc.ctx_ahead(step), pc.t))

    def over_fsdp(step):
        return send(sum_ctx, from_fsdp.at[step], ssems.at[2, 0, step], ssems.at[2, 1, step],
                    ((pc.f + step) % sz.fsdp, pc.c, pc.t))

    sum_tp[...] = jnp.zeros_like(sum_tp)
    for layer in range(n):
        first[layer] = jnp.zeros_like(first[layer])
        for kind in range(3):
            first[layer, 2 * kind:2 * kind + 1, :] = attn_vecs[layer][kind:kind + 1, :]
            first[layer, 2 * kind + 1:2 * kind + 2, :] = ff_vecs[layer][kind:kind + 1, :]
        sum_tp[n + pc.zl, 3 * layer:3 * layer + 2, 0:sz.headp] = dqvs[layer][...]
        sum_tp[n + pc.zl, 3 * layer + 2:3 * layer + 3, 0:sz.ffp] = dups[layer][...]
    for step in range(1, sz.tp):
        over_tp(step).start()
    for step in range(1, sz.images):
        swap(step).wait()
    for step in range(1, sz.tp):
        spread(step).start()
    move.parts[1]()
    value = first[...]
    for step in range(1, sz.tp):
        over_tp(step).wait()
        value = value + from_tp[step]
    sum_tp[0:n] = value
    for step in range(1, sz.ctx):
        over_ctx(step).start()
    move.parts[2]()
    value = sum_tp[...]
    for step in range(1, sz.ctx):
        over_ctx(step).wait()
        value = value + from_ctx[step]
    sum_ctx[...] = value
    for step in range(1, sz.fsdp):
        over_fsdp(step).start()
    for part in move.parts[3:]:
        part()
    value = sum_ctx[...]
    for step in range(1, sz.fsdp):
        over_fsdp(step).wait()
        value = value + from_fsdp[step]
    small_ref[...] = value
    for step in range(1, sz.tp):
        spread_wait(step).wait_recv()
        spread(step).wait_send()
    move.finish()


def give_call(sz, dw, stream, grad, ff_vecs, attn_vecs, dqvs, dups):
    n, far = sz.layers, max(sz.tp, sz.ctx, sz.fsdp)
    deep = up_to(max(6, 3 * n), 8)
    small = (n + sz.zl, deep, sz.d)
    ends = (sz.images, 2, sz.part, sz.d)
    shapes = Give.result(sz, sz.attnp) + [((sz.tp,) + ends, bf16), (small, f32)]
    operands = (dw, stream, grad, *ff_vecs, *attn_vecs, *dqvs, *dups)
    return pl.pallas_call(
        functools.partial(give_kernel, sz),
        out_shape=[jax.ShapeDtypeStruct(*s) for s in shapes],
        in_specs=whole(len(operands)),
        out_specs=whole(len(shapes)),
        scratch_shapes=[
            VMEM(ends, bf16), DMA((2, sz.images)), DMA((2, sz.tp)), DMA((3, 2, far)),
            VMEM((n, deep, sz.d), f32),
            VMEM((sz.tp, n, deep, sz.d), f32),
            VMEM((sz.ctx,) + small, f32),
            VMEM((sz.fsdp,) + small, f32),
            VMEM(small, f32),
            VMEM(small, f32),
        ]
        + Give.scratch(sz, sz.attnp),
        compiler_params=params(10),
        name="give_rest",
    )(*operands)


def close_kernel(sz, *refs):
    n = sz.layers
    attn_refs, ff_refs, (whole_ref, small_ref), outs = split_refs(refs, n, n, 2, 11)
    out_ref, gin_ref, gain_ref, bias_ref, qkv_ref, qv_ref, wout_ref, up_ref, upb_ref, down_ref, resid_ref = outs
    full, ff = sz.wide * sz.zl, sz.ff * sz.zl

    def join(ref, start, count, width):
        total = None
        for half in range(sz.zl):
            piece = shift_lanes(ref[half], start, count, half * count, up_to(width, 128))
            total = piece if total is None else total + piece
        return total[0:sz.wrows, 0:width]

    for layer in range(n):
        for kind in range(3):
            at = kind * full
            qkv_ref[layer, :, at:at + full] = join(attn_refs[layer], kind * sz.wide, sz.wide, full)
        wout_ref[layer] = join(attn_refs[layer], 3 * sz.wide, sz.wide, full)
        up_ref[layer] = join(ff_refs[layer], 0, sz.ff, ff)
        down_ref[layer] = join(ff_refs[layer], sz.ff, sz.ff, ff)
        values = small_ref[layer]
        gain_ref[layer] = values[0:2]
        bias_ref[layer] = values[2:4]
        resid_ref[layer] = values[4:6]
        total_qv, total_up = None, None
        for half in range(sz.zl):
            values = small_ref[n + half]
            qv = shift_lanes(values, 0, sz.wide, half * sz.wide, up_to(full, 128))
            up = shift_lanes(values, 0, sz.ff, half * sz.ff, up_to(ff, 128))
            total_qv = qv if total_qv is None else total_qv + qv
            total_up = up if total_up is None else total_up + up
        qv_ref[layer] = total_qv[3 * layer:3 * layer + 2, 0:full]
        upb_ref[layer:layer + 1, :] = total_up[3 * layer + 2:3 * layer + 3, 0:ff]
    for image in range(sz.images):
        rows = whole_ref[:, image, 0].reshape(sz.tp * sz.part, sz.d)
        out_ref[image] = rows[0:sz.rows]
        rows = whole_ref[:, image, 1].reshape(sz.tp * sz.part, sz.d)
        gin_ref[image] = rows.astype(f32)[0:sz.rows]


def close_call(sz, attn_sums, ff_sums, ends, small):
    n, full, ff = sz.layers, sz.wide * sz.zl, sz.ff * sz.zl
    tokens = (sz.images, sz.rows, sz.d)
    vec, up = ((n, 2, sz.d), f32), ((n, sz.wrows, ff), f32)
    shapes = [
        (tokens, bf16), (tokens, f32), vec, vec, ((n, sz.wrows, 3 * full), f32), ((n, 2, full), f32),
        ((n, sz.wrows, full), f32), up, ((n, ff), f32), up, vec,
    ]
    results = pl.pallas_call(
        functools.partial(close_kernel, sz),
        out_shape=[jax.ShapeDtypeStruct(*s) for s in shapes],
        in_specs=whole(2 * n + 2),
        out_specs=whole(len(shapes)),
        compiler_params=pltpu.CompilerParams(vmem_limit_bytes=60 * 1024 * 1024),
        name="close",
    )(*attn_sums, *ff_sums, ends, small)
    results = list(results)
    results[4] = results[4].reshape(n, sz.wrows, 3, full)
    return tuple(results)


def per_device(mesh, inputs, cotangent, valid_count, norm_gain, norm_bias, w_qkv, bias_qv, w_out, w_up, bias_up,
               w_down, bias_resid):
    sz = Sizes(mesh, inputs, w_qkv, w_up)
    n = sz.layers
    c, t = lax.axis_index("ctx"), lax.axis_index("tp")
    zh, zl = c // sz.zl, c % sz.zl
    slot = zl * sz.tp + t

    def pieces(a):
        a = jnp.pad(a, ((0, 0), (0, sz.tp * sz.part - sz.rows), (0, 0)))
        return lax.dynamic_slice_in_dim(a, t * sz.part, sz.part, axis=1)

    tokens = jnp.stack([pieces(inputs), pieces(cotangent)], axis=1)

    row = jnp.arange(sz.keys, dtype=jnp.int32)
    of_slot, within = row // sz.block, row % sz.block
    token = (of_slot % sz.tp) * sz.part + within % sz.part
    source = (within // sz.part) * sz.zl + of_slot // sz.tp
    position = source * sz.rows + token
    count = lax.dynamic_index_in_dim(valid_count, zh, keepdims=False)
    valid = ((token < sz.rows) & (position < count)).astype(f32)
    own_valid = lax.dynamic_slice_in_dim(valid, slot * sz.block, sz.block)[:, None]
    valid = valid[None, :]

    attn0, *rest = open_call(sz, w_qkv, w_out, w_up, w_down, tokens, own_valid)
    own_attn, own_ff, (stream, grad) = split_refs(rest, n - 1, n, 2)
    own_attn = [None] + list(own_attn)

    def half(a, to):
        a = lax.dynamic_index_in_dim(a.reshape(a.shape[0], sz.zl, -1), zl, axis=1, keepdims=False)
        return jnp.pad(a, ((0, 0), (0, to - a.shape[1])))

    def joined(w):
        return w[:, :sz.wrows].reshape(sz.d, w.shape[-1])

    def blocks(dw):
        dw = dw.reshape(sz.groups, sz.wrows, dw.shape[-1])
        return jnp.pad(dw, ((0, 0), (0, sz.wrowsp - sz.wrows), (0, 0)))

    own = ((sz.block, sz.d), f32)
    team = ((sz.team, sz.block, sz.d), bf16)
    head = ((sz.chips, sz.tile, sz.headp), bf16)
    hidden = (sz.chips, sz.tile, sz.ffp)
    vec = ((8, sz.d), f32)
    o_scratch = VMEM((sz.d, sz.headp), bf16)

    w_attn, w_ff = [joined(attn0)] + [None] * (n - 1), [None] * n
    streams, attn_kept, ff_kept, middles = [], [], [], []
    for l in range(n):
        streams.append(stream)
        middle, *kept, fetched = layer_call(
            sz, "attn_forward", 1, attn_forward,
            (stream, w_attn[l], norm_gain[l], norm_bias[l], half(bias_qv[l], sz.headp), bias_resid[l], valid),
            [own, team] + [head] * 4, [o_scratch], 1, 1, Fetch, own_ff[l],
        )
        w_ff[l] = joined(fetched)
        middles.append(middle)
        attn_kept.append(kept)
        last = l == n - 1
        stream, *kept = layer_call(
            sz, "ff_forward_last" if last else "ff_forward", 3 if last else 2, ff_forward,
            (middle, w_ff[l], norm_gain[l], norm_bias[l], half(bias_up[l][None], sz.ffp), bias_resid[l]),
            [own, team, (hidden, f32), (hidden, bf16)], [], 1, 1,
            *(() if last else (Fetch, own_attn[l + 1])),
        )
        if not last:
            w_attn[l + 1] = joined(kept.pop())
        ff_kept.append(kept)

    attn_sums, ff_sums, ff_vecs, attn_vecs, dqvs, dups = [[None] * n for _ in range(6)]
    pending = None
    for l in reversed(range(n)):
        last = l == n - 1
        gmid, dw_ff, ff_vecs[l], dups[l], *summed = layer_call(
            sz, "ff_backward_last" if last else "ff_backward", 5 if last else 4, ff_backward,
            (grad, middles[l], *ff_kept[l], w_ff[l], norm_gain[l]),
            [own, ((sz.d, sz.ffw), bf16), vec, ((1, sz.ffp), f32)],
            [VMEM(*team), VMEM(hidden, bf16)], 1, 1, *(() if last else (Give, blocks(pending))),
        )
        if not last:
            attn_sums[l + 1] = summed[0]
        grad, pending, attn_vecs[l], dqvs[l], ff_sums[l] = layer_call(
            sz, "attn_backward", 6, attn_backward,
            (gmid, streams[l], *attn_kept[l], w_attn[l], norm_gain[l], valid),
            [own, ((sz.d, sz.attnp), bf16), vec, ((2, sz.headp), f32)],
            [o_scratch, VMEM(*team), VMEM(*head), VMEM((sz.keys, sz.headp), f32), VMEM((sz.keys, sz.headp), f32),
             VMEM((sz.chips, sz.tile, sz.qkvp), bf16)],
            1, 1, Give, blocks(dw_ff),
        )
    attn_sums[0], ends, small = give_call(sz, blocks(pending), stream, grad, ff_vecs, attn_vecs, dqvs, dups)
    return close_call(sz, attn_sums, ff_sums, ends, small)


def solution(mesh):
    tokens, rows = P("fsdp", "ctx", None), P(None, ("fsdp", "ctx"), "tp")
    qkv = P(None, ("fsdp", "ctx"), None, "tp")
    qv, up = P(None, None, "tp"), P(None, "tp")
    return jax.shard_map(
        functools.partial(per_device, mesh),
        mesh=mesh,
        in_specs=(tokens, tokens, P("fsdp"), P(), P(), qkv, qv, rows, rows, up, rows, P()),
        out_specs=(tokens, tokens, P(), P(), qkv, qv, rows, rows, up, rows, P()),
        check_vma=False,
    )
```

```python
import functools

import jax
import jax.numpy as jnp
from jax import lax
from jax.experimental import pallas as pl
from jax.experimental.pallas import tpu as pltpu
from jax.sharding import PartitionSpec as P

HEAD_DIM = 72
norm_eps = 1e-06
gelu_root = 0.7978845608028654
gelu_cubic = 0.044715
masked_score = -1e30

MESH = pl.DeviceIdType.MESH
f32 = jnp.float32
bf16 = jnp.bfloat16
VMEM = pltpu.VMEM
DMA = pltpu.SemaphoreType.DMA


def up_to(value, unit):
    return (value + unit - 1) // unit * unit


def dot(a, b, over):
    return lax.dot_general(a, b, (((over[0],), (over[1],)), ((), ())), preferred_element_type=f32)


class Sizes:
    def __init__(self, mesh, inputs, w_qkv, w_up):
        self.fsdp, self.ctx, self.tp = mesh.shape["fsdp"], mesh.shape["ctx"], mesh.shape["tp"]
        self.images, self.rows, self.d = inputs.shape
        self.layers, self.wrows = w_qkv.shape[0], w_qkv.shape[1]
        self.zl = self.ctx // self.images
        self.chips_y = self.tp // 2
        self.chips = self.zl * self.chips_y
        self.team = self.chips * 2
        self.part = up_to(-(-self.rows // self.tp), 16)
        self.block = self.images * self.part
        self.units = self.chips * self.images
        self.tile = 2 * self.part
        self.keys = self.units * self.tile
        self.wide = w_qkv.shape[3] // self.zl
        self.heads = self.wide // HEAD_DIM
        self.ff = w_up.shape[2] // self.zl
        self.ffw = up_to(2 * self.ff, 128)
        self.down_at = self.ff // 128 * 128
        self.down_shift = self.ff - self.down_at
        self.ffp = self.ffw - self.down_at
        self.headp = up_to(self.wide, 128)
        self.qkvp = up_to(3 * self.wide, 128)
        self.attnp = up_to(4 * self.wide, 128)
        self.wrowsp = up_to(self.wrows, 16)
        self.groups = self.fsdp * self.ctx


class Place:
    def __init__(self, sz):
        self.sz = sz
        self.f, self.c, self.t = lax.axis_index("fsdp"), lax.axis_index("ctx"), lax.axis_index("tp")
        self.zh, self.zl = self.c // sz.zl, self.c % sz.zl
        self.y, self.k = self.t // 2, self.t % 2
        self.chip = self.zl * sz.chips_y + self.y
        self.slot = 2 * self.chip + self.k

    def chip_at(self, step):
        sz = self.sz
        zl = (self.zl + step // sz.chips_y) % sz.zl
        y = (self.y + step % sz.chips_y) % sz.chips_y
        return zl, y

    def chip_back(self, step):
        sz = self.sz
        zl = (self.zl + sz.zl - step // sz.chips_y) % sz.zl
        y = (self.y + sz.chips_y - step % sz.chips_y) % sz.chips_y
        return zl, y

    def index(self, chip):
        return chip[0] * self.sz.chips_y + chip[1]

    def device(self, chip):
        return (self.f, self.zh * self.sz.zl + chip[0], 2 * chip[1] + self.k)

    @property
    def twin(self):
        return (self.f, self.c, self.t + 1 - 2 * self.k)


    def ctx_ahead(self, step):
        sz = self.sz
        return (self.zh + step // sz.zl) % sz.images * sz.zl + (self.zl + step % sz.zl) % sz.zl

    def ctx_back(self, step):
        sz = self.sz
        zh = (self.zh + sz.images - step // sz.zl) % sz.images
        return zh * sz.zl + (self.zl + sz.zl - step % sz.zl) % sz.zl


class Greeting:
    def __init__(self, others):
        self.count = len(others)
        self.barrier = pltpu.get_barrier_semaphore()
        for other in others:
            pl.semaphore_signal(self.barrier, inc=1, device_id=other, device_id_type=MESH)

    def wait(self):
        pl.semaphore_wait(self.barrier, self.count)


def greet(others):
    Greeting(others).wait()


def send(src, dst, send_sem, recv_sem, device):
    return pltpu.make_async_remote_copy(
        src_ref=src, dst_ref=dst, send_sem=send_sem, recv_sem=recv_sem, device_id=device, device_id_type=MESH
    )


def team_peers(pc):
    return [pc.device(pc.chip_at(step)) for step in range(1, pc.sz.chips)] + [pc.twin]


def weight_peers(pc, team=False):
    sz = pc.sz
    first = sz.zl if team else 1
    return [(pc.f, pc.ctx_ahead(step), pc.t) for step in range(first, sz.ctx)] + [
        ((pc.f + jump) % sz.fsdp, pc.c, pc.t) for jump in range(1, sz.fsdp)
    ]


def pick(step, values):
    if isinstance(step, int):
        return values[step]
    out = jnp.int32(values[0])
    for i in range(1, len(values)):
        out = jnp.where(step == i, jnp.int32(values[i]), out)
    return out


def when(condition, run):
    if isinstance(condition, (bool, int)):
        if condition:
            run()
    else:
        pl.when(condition)(run)


class Routes:
    def __init__(self, sz):
        self.sz = sz
        pieces = range(sz.images)
        z = [dz * sz.chips_y for dz in range(1, sz.zl)]
        y = list(range(1, sz.chips_y))
        self.straight = z + y
        self.turned = [dz + dy for dz in z for dy in y]
        own = [(0, p) for p in pieces]
        near = [(b, p) for p in pieces for b in self.straight]
        far = [(b, p) for p in pieces for b in self.turned]
        self.arriving = own + near + far
        self.leaving = far + [(b, p) for b in z for p in pieces] + [(b, p) for b in y for p in pieces] + own


def backs(order):
    return [b for b, _ in order]


def pieces_of(order):
    return [p for _, p in order]


class Gather:
    def __init__(self, pc, buf, sems, turn_z=()):
        self.pc, self.buf, self.sems = pc, buf, sems
        self.routes = Routes(pc.sz)
        self.order = self.routes.arriving
        self.turn_z = turn_z

    def move(self, kind, back, piece, slot, device):
        return send(self.buf.at[slot, piece], self.buf.at[slot, piece], self.sems.at[kind, back, piece],
                    self.sems.at[kind + 1, back, piece], device)

    def near(self, back, piece, slot):
        return self.move(2, back, piece, slot, self.pc.twin)

    def start(self):
        pc = self.pc
        for piece in range(pc.sz.images):
            for step in self.routes.straight:
                self.move(0, step, piece, pc.slot, pc.device(pc.chip_at(step))).start()
            self.near(0, piece, pc.slot).start()

    def relays(self, back, piece):
        sz = self.pc.sz
        if back == 0 or back in self.routes.turned:
            return []
        if back % sz.chips_y == 0:
            return [] if piece in self.turn_z else [(back + dy, dy) for dy in range(1, sz.chips_y)]
        return [(back + dz * sz.chips_y, dz * sz.chips_y) for dz in range(1, sz.zl)] if piece in self.turn_z else []

    def forward(self, step):
        pc, order = self.pc, self.order
        back, piece = pick(step, backs(order)), pick(step, pieces_of(order))
        slot = 2 * pc.index(pc.chip_back(back)) + pc.k

        def other():
            self.move(0, back, piece, slot, pc.twin).wait_recv()
            self.near(back, piece, slot).start()

        when(back > 0, other)
        for at, (b, p) in enumerate(order):
            for seen, ahead in self.relays(b, p):
                when(step == at, self.move(0, seen, p, slot, pc.device(pc.chip_at(ahead))).start)

    def ready(self, step):
        pc = self.pc
        back, piece = pick(step, backs(self.order)), pick(step, pieces_of(self.order))
        at = pc.index(pc.chip_back(back))
        self.near(back, piece, 2 * at + 1 - pc.k).wait_recv()
        return at * pc.sz.images + piece, at, piece

    def ahead(self, step):
        if isinstance(step, int):
            if step + 1 < len(self.order):
                self.forward(step + 1)
        else:
            pl.when(step + 1 < len(self.order))(lambda: self.forward(step + 1))

    def tokens(self, at, piece):
        sz = self.pc.sz
        return self.buf[pl.ds(2 * at, 2), piece].reshape(sz.tile, sz.d)

    def finish(self):
        pc = self.pc
        for b, p in self.order:
            if b:
                self.move(0, b, p, pc.slot, pc.twin).wait_send()
            self.near(b, p, pc.slot).wait_send()


class Scatter:
    def __init__(self, pc, bufs, sems, turn):
        self.pc, self.sems, self.turn = pc, sems, turn
        self.both, self.keep, self.tsend, self.trecv, self.rsend, self.rrecv = bufs
        self.routes = Routes(pc.sz)
        self.order = self.routes.leaving if turn else self.routes.arriving

    def near(self, back, piece):
        return send(self.tsend.at[back, piece], self.trecv.at[back, piece], self.sems.at[0, back, piece],
                    self.sems.at[1, back, piece], self.pc.twin)

    def far(self, back, piece):
        pc, sz = self.pc, self.pc.sz
        to = back
        if self.turn:
            if isinstance(back, int):
                to = back % sz.chips_y or back
            else:
                dy = lax.rem(back, jnp.int32(sz.chips_y))
                to = jnp.where(dy > 0, dy, back)
        return send(self.rsend.at[back, piece], self.rrecv.at[back, piece], self.sems.at[2, back, piece],
                    self.sems.at[3, back, piece], pc.device(pc.chip_back(to)))

    def at(self, step):
        return pick(step, backs(self.order)), pick(step, pieces_of(self.order))

    def unit(self, step):
        back, piece = self.at(step)
        return self.pc.index(self.pc.chip_back(back)) * self.pc.sz.images + piece

    def push(self, step, partial):
        pc = self.pc
        back, piece = self.at(step)
        self.both[...] = partial.reshape(2, pc.sz.part, partial.shape[-1])
        self.tsend[back, piece] = self.both[1 - pc.k].astype(bf16)
        self.near(back, piece).start()
        self.keep[back, piece] = self.both[pc.k]
        pl.when(step > 0)(lambda: self.relay(step - 1))

    def relay(self, step):
        sz = self.pc.sz
        back, piece = self.at(step)
        self.near(back, piece).wait_recv()
        self.keep[back, piece] += self.trecv[back, piece].astype(f32)
        if self.turn:
            for at, (b, p) in enumerate(self.order):
                if b and b % sz.chips_y == 0:

                    def extra(b=b, p=p):
                        for dy in range(1, sz.chips_y):
                            self.far(b + dy, p).wait_recv()
                            self.keep[b, p] += self.rrecv[b + dy, p].astype(f32)

                    when(step == at, extra)

        def leave():
            self.rsend[back, piece] = self.keep[back, piece].astype(bf16)
            self.far(back, piece).start()

        when(back > 0, leave)

    def flush(self):
        self.relay(self.pc.sz.units - 1)

    def finish(self):
        sz = self.pc.sz
        total = self.keep[0]
        for back in range(1, sz.chips):
            if self.turn and back in self.routes.turned:
                continue
            for piece in range(sz.images):
                self.far(back, piece).wait_recv()
            total = total + self.rrecv[back].astype(f32)
        for back, piece in self.order:
            self.near(back, piece).wait_send()
            if back:
                self.far(back, piece).wait_send()
        return total.reshape(sz.block, sz.d)


def team_scratch(sz):
    n = (sz.chips, sz.images)
    return [
        VMEM((2, sz.part, sz.d), f32),
        VMEM(n + (sz.part, sz.d), f32),
        VMEM(n + (sz.part, sz.d), bf16),
        VMEM(n + (sz.part, sz.d), bf16),
        VMEM(n + (sz.part, sz.d), bf16),
        VMEM(n + (sz.part, sz.d), bf16),
        DMA((4,) + n),
        DMA((4,) + n),
    ]


def normalised(values):
    centre = jnp.mean(values, axis=-1, keepdims=True)
    centred = values - centre
    spread = jnp.mean(centred * centred, axis=-1, keepdims=True)
    inverse = lax.rsqrt(spread + norm_eps)
    return centred * inverse, inverse


def norm_back(values, gain, grad):
    high, inverse = normalised(values)
    scaled = grad * gain
    term = inverse * (
        scaled
        - jnp.mean(scaled, axis=-1, keepdims=True)
        - high * jnp.mean(scaled * high, axis=-1, keepdims=True)
    )
    return term, jnp.sum(grad * high, axis=0, keepdims=True), jnp.sum(grad, axis=0, keepdims=True)


def lanes_of(shape):
    return lax.broadcasted_iota(jnp.int32, shape, len(shape) - 1)


def unpack_out(sz, w_ref, o_ref):
    at = 3 * sz.wide // 128 * 128
    shift = 3 * sz.wide - at

    def step(i, carry):
        rows = pl.ds(pl.multiple_of(i * 128, 128), 128)
        piece = pltpu.roll(w_ref[rows, at:at + sz.headp].astype(f32), sz.headp - shift, 1)
        o_ref[rows, :] = jnp.where(lanes_of(piece.shape) < sz.wide, piece, 0.0).astype(bf16)
        return carry

    lax.fori_loop(0, sz.d // 128, step, 0)


def take(sz, values, kind):
    at = kind * sz.wide // 128 * 128
    shift = kind * sz.wide - at
    piece = values[:, at:at + sz.headp]
    if shift:
        piece = pltpu.roll(piece, sz.headp - shift, 1)
    return jnp.where(lanes_of(piece.shape) < sz.wide, piece, 0.0)


def head_of(values, head):
    lanes = lanes_of(values.shape)
    mine = (lanes >= head * HEAD_DIM) & (lanes < (head + 1) * HEAD_DIM)
    return jnp.where(mine, values, jnp.zeros_like(values))


def probabilities(q_head, keys, valid):
    scores = dot(q_head, keys, (1, 1)) * HEAD_DIM ** (-0.5)
    scores = jnp.where(valid > 0.0, scores, masked_score)
    weights = jnp.exp(scores - jnp.max(scores, axis=-1, keepdims=True))
    return weights / jnp.sum(weights, axis=-1, keepdims=True)


FF_TURN = (1,)

class Fetch:
    def __init__(self, pc, own, everything, sems):
        self.pc, self.own, self.all, self.sems = pc, own, everything, sems
        self.parts = [self.start, self.pass_own] + [
            functools.partial(self.pass_on, step) for step in range(1, pc.sz.ctx)
        ]

    def along_ctx(self, step):
        pc = self.pc
        c = pc.ctx_ahead(step)
        return send(self.own.at[c % pc.sz.zl], self.all.at[pc.f * pc.sz.ctx + pc.c], self.sems.at[0, 0, step],
                    self.sems.at[0, 1, step], (pc.f, c, pc.t))

    def own_copy(self):
        pc = self.pc
        return pltpu.make_async_copy(self.own.at[pc.zl], self.all.at[pc.f * pc.sz.ctx + pc.c], self.sems.at[0, 0, 0])

    def along_fsdp(self, jump, step):
        pc, sz = self.pc, self.pc.sz
        at = pc.f * sz.ctx + pc.ctx_back(step)
        return send(self.all.at[at], self.all.at[at], self.sems.at[jump, 0, step], self.sems.at[jump, 1, step],
                    ((pc.f + jump) % sz.fsdp, pc.c, pc.t))

    def start(self):
        self.own_copy().start()
        for step in range(1, min(3, self.pc.sz.ctx)):
            self.along_ctx(step).start()

    def pass_own(self):
        self.own_copy().wait()
        for jump in range(1, self.pc.sz.fsdp):
            self.along_fsdp(jump, 0).start()

    def pass_on(self, step):
        self.along_ctx(step).wait_recv()
        if step + 2 < self.pc.sz.ctx:
            self.along_ctx(step + 2).start()
        for jump in range(1, self.pc.sz.fsdp):
            self.along_fsdp(jump, step).start()

    def finish(self):
        sz = self.pc.sz
        for step in range(sz.ctx):
            if step:
                self.along_ctx(step).wait_send()
            for jump in range(1, sz.fsdp):
                self.along_fsdp(jump, step).wait()

    @staticmethod
    def result(sz, cols):
        return [((sz.groups, sz.wrowsp, cols), bf16)]

    @staticmethod
    def scratch(sz, cols):
        return [DMA((sz.fsdp, 2, sz.ctx))]


class Give:
    def __init__(self, pc, dw, out, got, total, recv, sems):
        self.pc, self.dw, self.out = pc, dw, out
        self.got, self.total, self.recv, self.sems = got, total, recv, sems
        self.order = list(range(pc.sz.ctx - 1, -1, -1))
        self.parts = [self.start] + [functools.partial(self.pass_on, step) for step in self.order]

    def along_fsdp(self, jump, step):
        pc, sz = self.pc, self.pc.sz
        f = (pc.f + jump) % sz.fsdp
        return send(self.dw.at[f * sz.ctx + pc.ctx_ahead(step)], self.got.at[jump - 1, step],
                    self.sems.at[jump, 0, step], self.sems.at[jump, 1, step], (f, pc.c, pc.t))

    def along_ctx(self, step):
        pc = self.pc
        return send(self.total.at[step], self.recv.at[pc.c], self.sems.at[0, 0, step], self.sems.at[0, 1, step],
                    (pc.f, pc.ctx_ahead(step), pc.t))

    def from_ctx(self, step):
        pc = self.pc
        return send(self.total.at[step], self.recv.at[pc.ctx_back(step)], self.sems.at[0, 0, step],
                    self.sems.at[0, 1, step], (pc.f, pc.ctx_back(step), pc.t))

    def start(self):
        for step in self.order[:2]:
            for jump in range(1, self.pc.sz.fsdp):
                self.along_fsdp(jump, step).start()

    def pass_on(self, step):
        pc, sz = self.pc, self.pc.sz
        for jump in range(1, sz.fsdp):
            self.along_fsdp(jump, step).wait_recv()
            if step >= 2:
                self.along_fsdp(jump, step - 2).start()
        total = self.dw[pc.f * sz.ctx + pc.ctx_ahead(step)].astype(f32)
        for jump in range(1, sz.fsdp):
            total = total + self.got[jump - 1, step].astype(f32)
        if step:
            self.total[step] = total.astype(bf16)
            self.along_ctx(step).start()
        else:
            self.recv[pc.c] = total.astype(bf16)

    def finish(self):
        pc, sz = self.pc, self.pc.sz
        for step in range(1, sz.ctx):
            self.from_ctx(step).wait_recv()
        for j in range(sz.zl):
            total = self.recv[j].astype(f32)
            for zh in range(1, sz.images):
                total = total + self.recv[zh * sz.zl + j].astype(f32)
            self.out[j] = total
        for step in range(sz.ctx):
            if step:
                self.along_ctx(step).wait_send()
            for jump in range(1, sz.fsdp):
                self.along_fsdp(jump, step).wait_send()

    @staticmethod
    def result(sz, cols):
        return [((sz.zl, sz.wrowsp, cols), f32)]

    @staticmethod
    def scratch(sz, cols):
        return [
            VMEM((max(sz.fsdp - 1, 1), sz.ctx, sz.wrowsp, cols), bf16),
            VMEM((sz.ctx, sz.wrowsp, cols), bf16),
            VMEM((sz.ctx, sz.wrowsp, cols), bf16),
            DMA((sz.fsdp, 2, sz.ctx)),
        ]


class Beside:
    def __init__(self, pc, mover, refs):
        self.mover = mover(pc, *refs) if mover else None

    def part(self, index):
        if self.mover:
            self.mover.parts[index]()

    def rest(self, first):
        if self.mover:
            for part in self.mover.parts[first:]:
                part()

    def at(self, step, places):
        if self.mover:
            for when, index in places.items():
                pl.when(step == when)(functools.partial(self.part, index))

    def finish(self):
        if self.mover:
            self.mover.finish()


def by_unit(sz, values):
    values = values.reshape(sz.chips, 2, sz.images, sz.part, values.shape[-1])
    return jnp.swapaxes(values, 1, 2).reshape(sz.keys, values.shape[-1])


def gather_norm(pc, greeting, gather, values, gain, shift):
    high, _ = normalised(values)
    low = (high * gain + shift).astype(bf16)
    gather.buf[pc.slot] = low.reshape(pc.sz.images, pc.sz.part, pc.sz.d)
    if greeting:
        greeting.wait()
    gather.start()


def split_refs(refs, *counts):
    out, at = [], 0
    for count in counts:
        out.append(refs[at:at + count])
        at += count
    assert at == len(refs)
    return out


def layer_kernel(body, ins, outs, scratch, mover, sz, *refs):
    m = 1 if mover else 0
    own, team = len(scratch), 8
    rest = len(refs) - ins - m - outs - m - own - team
    a, ma, b, mb, s, t, ms = split_refs(refs, ins, m, outs, m, own, team, rest)
    pc = Place(sz)
    greeting = Greeting(team_peers(pc) + (weight_peers(pc, True) if mover else []))
    body(sz, pc, greeting, Beside(pc, mover, (*ma, *mb, *ms)), *a, *b, *s, t[:6], t[6], t[7])


def layer_call(sz, name, ident, body, operands, shapes, scratch, mover=None, extra=None):
    cols = extra.shape[-1] if mover else 0
    results = list(shapes) + (mover.result(sz, cols) if mover else [])
    n_in = len(operands) + (1 if mover else 0)
    return pl.pallas_call(
        functools.partial(layer_kernel, body, len(operands), len(shapes), scratch, mover, sz),
        out_shape=[jax.ShapeDtypeStruct(*s) for s in results],
        in_specs=whole(n_in),
        out_specs=whole(len(results)),
        scratch_shapes=scratch + team_scratch(sz) + (mover.scratch(sz, cols) if mover else []),
        compiler_params=params(ident),
        name=name,
    )(*operands, *([extra] if mover else []))


def whole(ref_count):
    return [pl.BlockSpec(memory_space=pltpu.VMEM)] * ref_count


def params(collective_id):
    return pltpu.CompilerParams(
        collective_id=collective_id, has_side_effects=True, vmem_limit_bytes=60 * 1024 * 1024
    )


def attn_forward(first, sz, pc, greeting, beside, stream_ref, w_ref, gain_ref, shift_ref, qv_ref, resid_ref, valid_ref, *refs):
    given, (middle_ref,), made, (q_ref, k_ref, v_ref, mixed_ref, o_ref, bufs, gsems, ssems) = split_refs(
        refs, 1 if first else 0, 1, 0 if first else 1, 8
    )
    gather = Gather(pc, given[0] if first else made[0], gsems)
    if first:
        greeting.wait()
    else:
        gather_norm(pc, greeting, gather, stream_ref[...], gain_ref[0:1, :], shift_ref[0:1, :])
    beside.part(0)
    unpack_out(sz, w_ref, o_ref)
    beside.part(1)

    def project(step, carry):
        if first:
            at, piece = lax.div(step, sz.images), lax.rem(step, sz.images)
            unit = step
        else:
            unit, at, piece = gather.ready(step)
        both3 = dot(gather.tokens(at, piece), w_ref[:, 0:sz.qkvp], (1, 0))
        if not first:
            gather.ahead(step)
        q_ref[unit] = (take(sz, both3, 0) + qv_ref[0:1, :]).astype(bf16)
        k_ref[unit] = take(sz, both3, 1).astype(bf16)
        v_ref[unit] = (take(sz, both3, 2) + qv_ref[1:2, :]).astype(bf16)
        return carry

    lax.fori_loop(0, sz.units, project, 0)
    if not first:
        gather.finish()
    scatter = Scatter(pc, bufs, ssems, True)

    def attend(step, carry):
        unit = scatter.unit(step)
        keys = k_ref[...].reshape(sz.keys, sz.headp)
        values = v_ref[...].reshape(sz.keys, sz.headp)
        queries = q_ref[unit]
        total = jnp.zeros((sz.tile, sz.headp), f32)
        for head in range(sz.heads):
            probs = probabilities(head_of(queries, head), keys, valid_ref[...])
            total = total + dot(probs.astype(bf16), head_of(values, head), (1, 0))
        mixed = total.astype(bf16)
        mixed_ref[unit] = mixed
        scatter.push(step, dot(mixed, o_ref[...], (1, 1)))
        beside.at(step, {1: 2, 3: 3})
        return carry

    lax.fori_loop(0, sz.units, attend, 0)
    scatter.flush()
    beside.rest(4)
    middle_ref[...] = stream_ref[...] + (scatter.finish() + resid_ref[0:1, :])
    beside.finish()


def ff_forward(sz, pc, greeting, beside, middle_ref, w_ref, gain_ref, shift_ref, upb_ref, resid_ref,
               out_ref, n2_ref, pre_ref, hidden_ref, bufs, gsems, ssems):
    gather = Gather(pc, n2_ref, gsems, FF_TURN)
    gather_norm(pc, greeting, gather, middle_ref[...], gain_ref[1:2, :], shift_ref[1:2, :])
    beside.part(0)
    beside.part(1)
    scatter = Scatter(pc, bufs, ssems, False)

    def feed(step, carry):
        unit, at, piece = gather.ready(step)
        pre = dot(gather.tokens(at, piece), w_ref[:, 0:sz.ffp], (1, 0)) + upb_ref[...]
        gather.ahead(step)
        pre_ref[unit] = pre
        hidden = 0.5 * pre * (1.0 + jnp.tanh(gelu_root * (pre + gelu_cubic * pre * pre * pre)))
        hidden = jnp.where(lanes_of(hidden.shape) < sz.ff, hidden, 0.0)
        if sz.down_shift:
            hidden = pltpu.roll(hidden, sz.down_shift, 1)
        hidden = hidden.astype(bf16)
        hidden_ref[unit] = hidden
        scatter.push(step, dot(hidden, w_ref[:, sz.down_at:], (1, 1)))
        beside.at(step, {4: 2, 6: 3})
        return carry

    lax.fori_loop(0, sz.units, feed, 0)
    scatter.flush()
    gather.finish()
    beside.rest(4)
    out_ref[...] = middle_ref[...] + (scatter.finish() + resid_ref[1:2, :])
    beside.finish()


def ff_backward(sz, pc, greeting, beside, grad_ref, middle_ref, n2_ref, pre_ref, hidden_ref, w_ref, gain_ref,
                gmid_ref, dw_ref, vec_ref, dup_ref, gl_ref, pg_ref, bufs, gsems, ssems):
    span = 384 if sz.d % 384 == 0 else 128
    gather = Gather(pc, gl_ref, gsems, FF_TURN)
    grad_low = grad_ref[...].astype(bf16)
    gl_ref[pc.slot] = grad_low.reshape(sz.images, sz.part, sz.d)
    greeting.wait()
    gather.start()
    beside.part(0)
    vec_ref[...] = jnp.zeros_like(vec_ref)
    vec_ref[2:3, :] = jnp.sum(grad_low.astype(f32), axis=0, keepdims=True)
    scatter = Scatter(pc, bufs, ssems, False)
    dup_ref[...] = jnp.zeros_like(dup_ref)

    def feed(step, carry):
        unit, at, piece = gather.ready(step)
        back = dot(gather.tokens(at, piece), w_ref[:, sz.down_at:], (1, 0))
        gather.ahead(step)
        if sz.down_shift:
            back = pltpu.roll(back, sz.ffp - sz.down_shift, 1)
        pre = pre_ref[unit]
        bent = jnp.tanh(gelu_root * (pre + gelu_cubic * pre * pre * pre))
        slope = 0.5 * (1.0 + bent) + 0.5 * pre * (1.0 - bent * bent) * (
            gelu_root * (1.0 + 3.0 * gelu_cubic * pre * pre)
        )
        pre_grad = jnp.where(lanes_of(back.shape) < sz.ff, back * slope, 0.0).astype(bf16)
        pg_ref[unit] = pre_grad
        dup_ref[...] += jnp.sum(pre_grad.astype(f32), axis=0, keepdims=True)
        scatter.push(step, dot(pre_grad, w_ref[:, 0:sz.ffp], (1, 1)))
        beside.at(step, {3: 1, 5: 2, 7: 3})
        return carry

    lax.fori_loop(0, sz.units, feed, 0)
    scatter.flush()
    beside.rest(4)

    def grads_ff(i, carry):
        lanes = pl.ds(pl.multiple_of(i * span, 128), span)
        hidden = hidden_ref[...].reshape(sz.keys, sz.ffp)
        down = dot(by_unit(sz, gl_ref[:, :, :, lanes]), hidden, (0, 0))
        pre_grad = pg_ref[...].reshape(sz.keys, sz.ffp)
        up = dot(by_unit(sz, n2_ref[:, :, :, lanes]), pre_grad, (0, 0))
        dw_ref[lanes, 0:sz.down_at] = up[:, 0:sz.down_at].astype(bf16)
        over = sz.ffp - sz.down_at
        if over:
            dw_ref[lanes, sz.down_at:sz.ffp] = (up[:, sz.down_at:] + down[:, 0:over]).astype(bf16)
        dw_ref[lanes, sz.ffp:] = down[:, over:].astype(bf16)
        return carry

    lax.fori_loop(0, sz.d // span, grads_ff, 0)
    gather.finish()
    second = scatter.finish()
    term, dgain, dshift = norm_back(middle_ref[...], gain_ref[1:2, :], second)
    vec_ref[0:1, :] = dgain
    vec_ref[1:2, :] = dshift
    gmid_ref[...] = grad_ref[...] + term
    beside.finish()


def attn_backward(sz, pc, greeting, beside, gmid_ref, stream_ref, n1_ref, q_ref, k_ref, v_ref, mixed_ref, w_ref, gain_ref,
                  valid_ref, below_ref, dw_ref, vec_ref, dqv_ref,
                  o_ref, ml_ref, dk_ref, dv_ref, stack_ref, bufs, gsems, ssems):
    span = 384 if sz.d % 384 == 0 else 128
    gather = Gather(pc, ml_ref, gsems)
    mid_low = gmid_ref[...].astype(bf16)
    ml_ref[pc.slot] = mid_low.reshape(sz.images, sz.part, sz.d)
    greeting.wait()
    gather.start()
    beside.part(0)
    vec_ref[...] = jnp.zeros_like(vec_ref)
    vec_ref[2:3, :] = jnp.sum(mid_low.astype(f32), axis=0, keepdims=True)
    unpack_out(sz, w_ref, o_ref)
    dk_ref[...] = jnp.zeros_like(dk_ref)
    dv_ref[...] = jnp.zeros_like(dv_ref)
    dqv_ref[...] = jnp.zeros_like(dqv_ref)
    scale = HEAD_DIM ** (-0.5)

    def attend(step, carry):
        unit, at, piece = gather.ready(step)
        mixed_grad = dot(gather.tokens(at, piece), o_ref[...], (1, 0)).astype(bf16)
        gather.ahead(step)
        keys = k_ref[...].reshape(sz.keys, sz.headp)
        values = v_ref[...].reshape(sz.keys, sz.headp)
        total = jnp.zeros((sz.tile, sz.headp), f32)
        for head in range(sz.heads):
            q_head = head_of(q_ref[unit], head)
            g_head = head_of(mixed_grad, head)
            probs = probabilities(q_head, keys, valid_ref[...])
            dprobs = dot(g_head, values, (1, 1))
            inner = jnp.sum(probs * dprobs, axis=-1, keepdims=True)
            dscores = (probs * (dprobs - inner)).astype(bf16)
            total = total + dot(dscores, head_of(keys, head), (1, 0))
            dk_ref[...] += dot(dscores, q_head, (0, 0))
            dv_ref[...] += dot(probs.astype(bf16), g_head, (0, 0))
        dq = (scale * total).astype(bf16).astype(f32)
        dqv_ref[0:1, :] += jnp.sum(dq, axis=0, keepdims=True)
        stack_ref[unit, :, 0:sz.headp] = dq.astype(bf16)
        beside.at(step, {2: 1, 4: 2, 6: 3})
        return carry

    lax.fori_loop(0, sz.units, attend, 0)
    gather.finish()
    beside.rest(4)
    scatter = Scatter(pc, bufs, ssems, True)

    def back_project(step, carry):
        unit = scatter.unit(step)
        rows = pl.ds(pl.multiple_of(unit * sz.tile, sz.tile), sz.tile)
        dk = (scale * dk_ref[rows, :]).astype(bf16).astype(f32)
        dv = dv_ref[rows, :].astype(bf16).astype(f32)
        dqv_ref[1:2, :] += jnp.sum(dv, axis=0, keepdims=True)
        dq = stack_ref[unit, :, 0:sz.headp].astype(f32)
        total = jnp.pad(dq, ((0, 0), (0, sz.qkvp - sz.headp)))
        for kind, piece in ((1, dk), (2, dv)):
            start = kind * sz.wide // 128 * 128
            shift = kind * sz.wide - start
            moved = pltpu.roll(piece, shift, 1) if shift else piece
            total = total + jnp.pad(moved, ((0, 0), (start, sz.qkvp - start - sz.headp)))
        stacked = total.astype(bf16)
        stack_ref[unit] = stacked
        scatter.push(step, dot(stacked, w_ref[:, 0:sz.qkvp], (1, 1)))
        return carry

    lax.fori_loop(0, sz.units, back_project, 0)
    scatter.flush()
    o_at = 3 * sz.wide // 128 * 128
    o_shift = 3 * sz.wide - o_at

    def grads_attn(i, carry):
        lanes = pl.ds(pl.multiple_of(i * span, 128), span)
        stacked = stack_ref[...].reshape(sz.keys, sz.qkvp)
        dqkv = dot(by_unit(sz, n1_ref[:, :, :, lanes]), stacked, (0, 0))
        mixed = mixed_ref[...].reshape(sz.keys, sz.headp)
        dout = dot(by_unit(sz, ml_ref[:, :, :, lanes]), mixed, (0, 0))
        if o_shift:
            dout = pltpu.roll(dout, o_shift, 1)
        total = jnp.pad(dqkv, ((0, 0), (0, sz.attnp - sz.qkvp))) + jnp.pad(
            dout, ((0, 0), (o_at, sz.attnp - o_at - sz.headp))
        )
        dw_ref[lanes, 0:sz.attnp] = total.astype(bf16)
        return carry

    lax.fori_loop(0, sz.d // span, grads_attn, 0)
    first = scatter.finish()
    term, dgain, dshift = norm_back(stream_ref[...], gain_ref[0:1, :], first)
    vec_ref[0:1, :] = dgain
    vec_ref[1:2, :] = dshift
    below_ref[...] = gmid_ref[...] + term
    beside.finish()


def shift_lanes(values, start, count, at, width):
    have = values.shape[-1]
    first, last = start // 128 * 128, up_to(start + count, 128)
    to = at // 128 * 128
    span = max(last - first, up_to(at + count, 128) - to)
    piece = values[:, first:min(last, have)].astype(f32)
    if piece.shape[-1] < span:
        piece = jnp.pad(piece, ((0, 0), (0, span - piece.shape[-1])))
    turn = ((at - to) - (start - first)) % span
    if turn:
        piece = pltpu.roll(piece, turn, 1)
    lanes = lanes_of(piece.shape)
    piece = jnp.where((lanes >= at - to) & (lanes < at - to + count), piece, 0.0)
    piece = piece[:, 0:min(span, width - to)]
    return jnp.pad(piece, ((0, 0), (to, width - to - piece.shape[-1])))


def open_kernel(sz, wqkv_ref, wout_ref, wup_ref, wdown_ref, tokens_ref, valid_ref, gain_ref, shift_ref, *refs):
    n = sz.layers
    everything, attn_refs, ff_refs, (stream_ref, grad_ref, n1_ref), own = split_refs(refs, 1, n - 1, n, 3, 5)
    attn0_ref, mine_ref, tsems, gsems, wsems = own
    attn_refs = [attn0_ref] + list(attn_refs)
    pc = Place(sz)
    greet(team_peers(pc) + weight_peers(pc, True))

    def swap(step):
        zh = (pc.zh + step) % sz.images
        return send(tokens_ref.at[zh], mine_ref.at[pc.zh], tsems.at[0, step], tsems.at[1, step],
                    (pc.f, zh * sz.zl + pc.zl, pc.t))

    def pack(ref, half, pieces):
        total = None
        for values, start, count, at in pieces:
            piece = shift_lanes(values, start, count, at, ref.shape[-1])
            total = piece if total is None else total + piece
        ref[half, 0:sz.wrows, :] = total.astype(bf16)
        if sz.wrowsp > sz.wrows:
            ref[half, sz.wrows:, :] = jnp.zeros((sz.wrowsp - sz.wrows, ref.shape[-1]), bf16)

    def pack_attn(layer):
        full = sz.wide * sz.zl
        for half in range(sz.zl):
            pieces = [(wqkv_ref[layer], kind * full + half * sz.wide, sz.wide, kind * sz.wide) for kind in range(3)]
            pack(attn_refs[layer], half, pieces + [(wout_ref[layer], half * sz.wide, sz.wide, 3 * sz.wide)])

    for step in range(1, sz.images):
        swap(step).start()
    pack_attn(0)
    move = Fetch(pc, attn0_ref, everything[0], wsems)
    move.parts[0]()
    mine_ref[pc.zh] = tokens_ref[pc.zh]
    for step in range(1, sz.images):
        swap(step).wait()
    move.parts[1]()
    stream = mine_ref[:, 0].reshape(sz.block, sz.d).astype(f32)
    stream_ref[...] = stream
    gather = Gather(pc, n1_ref, gsems, FF_TURN)
    gather_norm(pc, None, gather, stream, gain_ref[0:1, :], shift_ref[0:1, :])
    grad_ref[...] = mine_ref[:, 1].reshape(sz.block, sz.d).astype(f32) * valid_ref[...]
    move.parts[2]()
    for layer in range(1, n):
        pack_attn(layer)
    move.parts[3]()
    for layer in range(n):
        for half in range(sz.zl):
            pack(ff_refs[layer], half, [(wup_ref[layer], half * sz.ff, sz.ff, 0),
                                        (wdown_ref[layer], half * sz.ff, sz.ff, sz.ff)])
    for step in range(sz.units):
        gather.forward(step)
        gather.ready(step)
    for part in move.parts[4:]:
        part()
    gather.finish()
    move.finish()


def open_call(sz, w_qkv, w_out, w_up, w_down, tokens, own_valid, gains, shifts):
    attn, ff = ((sz.zl, sz.wrowsp, sz.attnp), bf16), ((sz.zl, sz.wrowsp, sz.ffw), bf16)
    own = ((sz.block, sz.d), f32)
    team = ((sz.team, sz.images, sz.part, sz.d), bf16)
    shapes = Fetch.result(sz, sz.attnp) + [attn] * (sz.layers - 1) + [ff] * sz.layers + [own, own, team]
    operands = (w_qkv.reshape(sz.layers, sz.wrows, -1), w_out, w_up, w_down, tokens, own_valid, gains, shifts)
    return pl.pallas_call(
        functools.partial(open_kernel, sz),
        out_shape=[jax.ShapeDtypeStruct(*s) for s in shapes],
        in_specs=whole(len(operands)),
        out_specs=whole(len(shapes)),
        scratch_shapes=[VMEM(*attn), VMEM(tokens.shape, bf16), DMA((2, sz.images)), DMA((4, sz.chips, sz.images))]
        + Fetch.scratch(sz, 0),
        compiler_params=params(9),
        name="open",
    )(*operands)


def give_kernel(sz, dw_ref, stream_ref, grad_ref, *refs):
    n = sz.layers
    ff_vecs, attn_vecs, dqvs, dups, (sum_ref, whole_ref, small_ref), own, give_refs = split_refs(
        refs, n, n, n, n, 3, 10, 4
    )
    ends_ref, esems, ysems, ssems, first, from_tp, from_ctx, from_fsdp, sum_tp, sum_ctx = own
    pc = Place(sz)
    greet(weight_peers(pc) + [(pc.f, pc.c, (pc.t + s) % sz.tp) for s in range(1, sz.tp)])
    move = Give(pc, dw_ref, sum_ref, *give_refs)
    move.parts[0]()

    def swap(step):
        zh = (pc.zh + step) % sz.images
        return send(ends_ref.at[zh], whole_ref.at[pc.t, pc.zh], esems.at[0, step], esems.at[1, step],
                    (pc.f, zh * sz.zl + pc.zl, pc.t))

    def spread(step):
        return send(whole_ref.at[pc.t], whole_ref.at[pc.t], ysems.at[0, step], ysems.at[1, step],
                    (pc.f, pc.c, (pc.t + step) % sz.tp))

    def spread_wait(step):
        back = (pc.t + sz.tp - step) % sz.tp
        return send(whole_ref.at[back], whole_ref.at[back], ysems.at[0, step], ysems.at[1, step],
                    (pc.f, pc.c, back))

    for kind, ref in enumerate((stream_ref, grad_ref)):
        ends_ref[:, kind] = ref[...].reshape(sz.images, sz.part, sz.d).astype(bf16)
    for step in range(1, sz.images):
        swap(step).start()
    whole_ref[pc.t, pc.zh] = ends_ref[pc.zh]

    def over_tp(step):
        return send(first, from_tp.at[step], ssems.at[0, 0, step], ssems.at[0, 1, step],
                    (pc.f, pc.c, (pc.t + step) % sz.tp))

    def over_ctx(step):
        return send(sum_tp, from_ctx.at[step], ssems.at[1, 0, step], ssems.at[1, 1, step],
                    (pc.f, pc.ctx_ahead(step), pc.t))

    def over_fsdp(step):
        return send(sum_ctx, from_fsdp.at[step], ssems.at[2, 0, step], ssems.at[2, 1, step],
                    ((pc.f + step) % sz.fsdp, pc.c, pc.t))

    sum_tp[...] = jnp.zeros_like(sum_tp)
    for layer in range(n):
        first[layer] = jnp.zeros_like(first[layer])
        for kind in range(3):
            first[layer, 2 * kind:2 * kind + 1, :] = attn_vecs[layer][kind:kind + 1, :]
            first[layer, 2 * kind + 1:2 * kind + 2, :] = ff_vecs[layer][kind:kind + 1, :]
        sum_tp[n + pc.zl, 3 * layer:3 * layer + 2, 0:sz.headp] = dqvs[layer][...]
        sum_tp[n + pc.zl, 3 * layer + 2:3 * layer + 3, 0:sz.ffp] = dups[layer][...]
    for step in range(1, sz.tp):
        over_tp(step).start()
    for step in range(1, sz.images):
        swap(step).wait()
    for step in range(1, sz.tp):
        spread(step).start()
    move.parts[1]()
    value = first[...]
    for step in range(1, sz.tp):
        over_tp(step).wait()
        value = value + from_tp[step]
    sum_tp[0:n] = value
    for step in range(1, sz.ctx):
        over_ctx(step).start()
    move.parts[2]()
    value = sum_tp[...]
    for step in range(1, sz.ctx):
        over_ctx(step).wait()
        value = value + from_ctx[step]
    sum_ctx[...] = value
    for step in range(1, sz.fsdp):
        over_fsdp(step).start()
    for part in move.parts[3:]:
        part()
    value = sum_ctx[...]
    for step in range(1, sz.fsdp):
        over_fsdp(step).wait()
        value = value + from_fsdp[step]
    small_ref[...] = value
    for step in range(1, sz.tp):
        spread_wait(step).wait_recv()
        spread(step).wait_send()
    move.finish()


def give_call(sz, dw, stream, grad, ff_vecs, attn_vecs, dqvs, dups):
    n, far = sz.layers, max(sz.tp, sz.ctx, sz.fsdp)
    deep = up_to(max(6, 3 * n), 8)
    small = (n + sz.zl, deep, sz.d)
    ends = (sz.images, 2, sz.part, sz.d)
    shapes = Give.result(sz, sz.attnp) + [((sz.tp,) + ends, bf16), (small, f32)]
    operands = (dw, stream, grad, *ff_vecs, *attn_vecs, *dqvs, *dups)
    return pl.pallas_call(
        functools.partial(give_kernel, sz),
        out_shape=[jax.ShapeDtypeStruct(*s) for s in shapes],
        in_specs=whole(len(operands)),
        out_specs=whole(len(shapes)),
        scratch_shapes=[
            VMEM(ends, bf16), DMA((2, sz.images)), DMA((2, sz.tp)), DMA((3, 2, far)),
            VMEM((n, deep, sz.d), f32),
            VMEM((sz.tp, n, deep, sz.d), f32),
            VMEM((sz.ctx,) + small, f32),
            VMEM((sz.fsdp,) + small, f32),
            VMEM(small, f32),
            VMEM(small, f32),
        ]
        + Give.scratch(sz, sz.attnp),
        compiler_params=params(10),
        name="give_rest",
    )(*operands)


def close_kernel(sz, *refs):
    n = sz.layers
    attn_refs, ff_refs, (whole_ref, small_ref), outs = split_refs(refs, n, n, 2, 11)
    out_ref, gin_ref, gain_ref, bias_ref, qkv_ref, qv_ref, wout_ref, up_ref, upb_ref, down_ref, resid_ref = outs
    full, ff = sz.wide * sz.zl, sz.ff * sz.zl

    def join(ref, start, count, width):
        total = None
        for half in range(sz.zl):
            piece = shift_lanes(ref[half], start, count, half * count, up_to(width, 128))
            total = piece if total is None else total + piece
        return total[0:sz.wrows, 0:width]

    for layer in range(n):
        for kind in range(3):
            at = kind * full
            qkv_ref[layer, :, at:at + full] = join(attn_refs[layer], kind * sz.wide, sz.wide, full)
        wout_ref[layer] = join(attn_refs[layer], 3 * sz.wide, sz.wide, full)
        up_ref[layer] = join(ff_refs[layer], 0, sz.ff, ff)
        down_ref[layer] = join(ff_refs[layer], sz.ff, sz.ff, ff)
        values = small_ref[layer]
        gain_ref[layer] = values[0:2]
        bias_ref[layer] = values[2:4]
        resid_ref[layer] = values[4:6]
        total_qv, total_up = None, None
        for half in range(sz.zl):
            values = small_ref[n + half]
            qv = shift_lanes(values, 0, sz.wide, half * sz.wide, up_to(full, 128))
            up = shift_lanes(values, 0, sz.ff, half * sz.ff, up_to(ff, 128))
            total_qv = qv if total_qv is None else total_qv + qv
            total_up = up if total_up is None else total_up + up
        qv_ref[layer] = total_qv[3 * layer:3 * layer + 2, 0:full]
        upb_ref[layer:layer + 1, :] = total_up[3 * layer + 2:3 * layer + 3, 0:ff]
    for image in range(sz.images):
        rows = whole_ref[:, image, 0].reshape(sz.tp * sz.part, sz.d)
        out_ref[image] = rows[0:sz.rows]
        rows = whole_ref[:, image, 1].reshape(sz.tp * sz.part, sz.d)
        gin_ref[image] = rows.astype(f32)[0:sz.rows]


def close_call(sz, attn_sums, ff_sums, ends, small):
    n, full, ff = sz.layers, sz.wide * sz.zl, sz.ff * sz.zl
    tokens = (sz.images, sz.rows, sz.d)
    vec, up = ((n, 2, sz.d), f32), ((n, sz.wrows, ff), f32)
    shapes = [
        (tokens, bf16), (tokens, f32), vec, vec, ((n, sz.wrows, 3 * full), f32), ((n, 2, full), f32),
        ((n, sz.wrows, full), f32), up, ((n, ff), f32), up, vec,
    ]
    results = pl.pallas_call(
        functools.partial(close_kernel, sz),
        out_shape=[jax.ShapeDtypeStruct(*s) for s in shapes],
        in_specs=whole(2 * n + 2),
        out_specs=whole(len(shapes)),
        compiler_params=pltpu.CompilerParams(vmem_limit_bytes=60 * 1024 * 1024),
        name="close",
    )(*attn_sums, *ff_sums, ends, small)
    results = list(results)
    results[4] = results[4].reshape(n, sz.wrows, 3, full)
    return tuple(results)


def per_device(mesh, inputs, cotangent, valid_count, norm_gain, norm_bias, w_qkv, bias_qv, w_out, w_up, bias_up,
               w_down, bias_resid):
    sz = Sizes(mesh, inputs, w_qkv, w_up)
    n = sz.layers
    c, t = lax.axis_index("ctx"), lax.axis_index("tp")
    zh, zl = c // sz.zl, c % sz.zl
    slot = zl * sz.tp + t

    def pieces(a):
        a = jnp.pad(a, ((0, 0), (0, sz.tp * sz.part - sz.rows), (0, 0)))
        return lax.dynamic_slice_in_dim(a, t * sz.part, sz.part, axis=1)

    tokens = jnp.stack([pieces(inputs), pieces(cotangent)], axis=1)

    row = jnp.arange(sz.keys, dtype=jnp.int32)
    unit, within = row // sz.tile, row % sz.tile
    of_slot = unit // sz.images * 2 + within // sz.part
    count = lax.dynamic_index_in_dim(valid_count, zh, keepdims=False)

    def valid_at(slots, piece, place):
        token = slots % sz.tp * sz.part + place
        position = (piece * sz.zl + slots // sz.tp) * sz.rows + token
        return ((token < sz.rows) & (position < count)).astype(f32)

    valid = valid_at(of_slot, unit % sz.images, within % sz.part)[None, :]
    mine = jnp.arange(sz.block, dtype=jnp.int32)
    own_valid = valid_at(slot, mine // sz.part, mine % sz.part)[:, None]

    attn0, *rest = open_call(sz, w_qkv, w_out, w_up, w_down, tokens, own_valid, norm_gain[0], norm_bias[0])
    own_attn, own_ff, (stream, grad, normed) = split_refs(rest, n - 1, n, 3)
    own_attn = [None] + list(own_attn)

    def half(a, to):
        a = lax.dynamic_index_in_dim(a.reshape(a.shape[0], sz.zl, -1), zl, axis=1, keepdims=False)
        return jnp.pad(a, ((0, 0), (0, to - a.shape[1])))

    def joined(w):
        return w[:, :sz.wrows].reshape(sz.d, w.shape[-1])

    def blocks(dw):
        dw = dw.reshape(sz.groups, sz.wrows, dw.shape[-1])
        return jnp.pad(dw, ((0, 0), (0, sz.wrowsp - sz.wrows), (0, 0)))

    own = ((sz.block, sz.d), f32)
    team = ((sz.team, sz.images, sz.part, sz.d), bf16)
    head = ((sz.units, sz.tile, sz.headp), bf16)
    hidden = (sz.units, sz.tile, sz.ffp)
    vec = ((8, sz.d), f32)
    o_scratch = VMEM((sz.d, sz.headp), bf16)

    w_attn, w_ff = [joined(attn0)] + [None] * (n - 1), [None] * n
    streams, attn_kept, ff_kept, middles = [], [], [], []
    for l in range(n):
        streams.append(stream)
        operands = (stream, w_attn[l], norm_gain[l], norm_bias[l], half(bias_qv[l], sz.headp), bias_resid[l], valid)
        if l == 0:
            middle, *kept, fetched = layer_call(
                sz, "attn_forward_first", 7, functools.partial(attn_forward, True), operands + (normed,),
                [own] + [head] * 4, [o_scratch], Fetch, own_ff[l],
            )
            kept = [normed] + kept
        else:
            middle, *kept, fetched = layer_call(
                sz, "attn_forward", 1, functools.partial(attn_forward, False), operands,
                [own, team] + [head] * 4, [o_scratch], Fetch, own_ff[l],
            )
        w_ff[l] = joined(fetched)
        middles.append(middle)
        attn_kept.append(kept)
        last = l == n - 1
        stream, *kept = layer_call(
            sz, "ff_forward_last" if last else "ff_forward", 3 if last else 2, ff_forward,
            (middle, w_ff[l], norm_gain[l], norm_bias[l], half(bias_up[l][None], sz.ffp), bias_resid[l]),
            [own, team, (hidden, f32), (hidden, bf16)], [],
            *(() if last else (Fetch, own_attn[l + 1])),
        )
        if not last:
            w_attn[l + 1] = joined(kept.pop())
        ff_kept.append(kept)

    attn_sums, ff_sums, ff_vecs, attn_vecs, dqvs, dups = [[None] * n for _ in range(6)]
    pending = None
    for l in reversed(range(n)):
        last = l == n - 1
        gmid, dw_ff, ff_vecs[l], dups[l], *summed = layer_call(
            sz, "ff_backward_last" if last else "ff_backward", 5 if last else 4, ff_backward,
            (grad, middles[l], *ff_kept[l], w_ff[l], norm_gain[l]),
            [own, ((sz.d, sz.ffw), bf16), vec, ((1, sz.ffp), f32)],
            [VMEM(*team), VMEM(hidden, bf16)], *(() if last else (Give, blocks(pending))),
        )
        if not last:
            attn_sums[l + 1] = summed[0]
        grad, pending, attn_vecs[l], dqvs[l], ff_sums[l] = layer_call(
            sz, "attn_backward", 6, attn_backward,
            (gmid, streams[l], *attn_kept[l], w_attn[l], norm_gain[l], valid),
            [own, ((sz.d, sz.attnp), bf16), vec, ((2, sz.headp), f32)],
            [o_scratch, VMEM(*team), VMEM((sz.keys, sz.headp), f32), VMEM((sz.keys, sz.headp), f32),
             VMEM((sz.units, sz.tile, sz.qkvp), bf16)],
            Give, blocks(dw_ff),
        )
    attn_sums[0], ends, small = give_call(sz, blocks(pending), stream, grad, ff_vecs, attn_vecs, dqvs, dups)
    return close_call(sz, attn_sums, ff_sums, ends, small)


def solution(mesh):
    tokens, rows = P("fsdp", "ctx", None), P(None, ("fsdp", "ctx"), "tp")
    qkv = P(None, ("fsdp", "ctx"), None, "tp")
    qv, up = P(None, None, "tp"), P(None, "tp")
    return jax.shard_map(
        functools.partial(per_device, mesh),
        mesh=mesh,
        in_specs=(tokens, tokens, P("fsdp"), P(), P(), qkv, qv, rows, rows, up, rows, P()),
        out_specs=(tokens, tokens, P(), P(), qkv, qv, rows, rows, up, rows, P()),
        check_vma=False,
    )
```

```python
import functools

import jax
import jax.numpy as jnp
from jax import lax
from jax.experimental import pallas as pl
from jax.experimental.pallas import tpu as pltpu
from jax.sharding import PartitionSpec as P

HEAD_DIM = 72
norm_eps = 1e-06
gelu_root = 0.7978845608028654
gelu_cubic = 0.044715
masked_score = -1e30

MESH = pl.DeviceIdType.MESH
f32 = jnp.float32
bf16 = jnp.bfloat16
VMEM = pltpu.VMEM
DMA = pltpu.SemaphoreType.DMA


def up_to(value, unit):
    return (value + unit - 1) // unit * unit


def dot(a, b, over):
    return lax.dot_general(a, b, (((over[0],), (over[1],)), ((), ())), preferred_element_type=f32)


class Sizes:
    def __init__(self, mesh, inputs, w_qkv, w_up):
        self.fsdp, self.ctx, self.tp = mesh.shape["fsdp"], mesh.shape["ctx"], mesh.shape["tp"]
        self.images, self.rows, self.d = inputs.shape
        self.layers, self.wrows = w_qkv.shape[0], w_qkv.shape[1]
        self.zl = self.ctx // self.images
        self.chips_y = self.tp // 2
        self.chips = self.zl * self.chips_y
        self.team = self.chips * 2
        self.part = up_to(-(-self.rows // self.tp), 16)
        self.block = self.images * self.part
        self.units = self.chips * self.images
        self.tile = 2 * self.part
        self.keys = self.units * self.tile
        self.wide = w_qkv.shape[3] // self.zl
        self.heads = self.wide // HEAD_DIM
        self.ff = w_up.shape[2] // self.zl
        self.ffw = up_to(2 * self.ff, 128)
        self.down_at = self.ff // 128 * 128
        self.down_shift = self.ff - self.down_at
        self.ffp = self.ffw - self.down_at
        self.headp = up_to(self.wide, 128)
        self.qkvp = up_to(3 * self.wide, 128)
        self.attnp = up_to(4 * self.wide, 128)
        self.wrowsp = up_to(self.wrows, 16)
        self.groups = self.fsdp * self.ctx


class Place:
    def __init__(self, sz):
        self.sz = sz
        self.f, self.c, self.t = lax.axis_index("fsdp"), lax.axis_index("ctx"), lax.axis_index("tp")
        self.zh, self.zl = self.c // sz.zl, self.c % sz.zl
        self.y, self.k = self.t // 2, self.t % 2
        self.chip = self.zl * sz.chips_y + self.y
        self.slot = 2 * self.chip + self.k

    def chip_at(self, step):
        sz = self.sz
        zl = (self.zl + step // sz.chips_y) % sz.zl
        y = (self.y + step % sz.chips_y) % sz.chips_y
        return zl, y

    def chip_back(self, step):
        sz = self.sz
        zl = (self.zl + sz.zl - step // sz.chips_y) % sz.zl
        y = (self.y + sz.chips_y - step % sz.chips_y) % sz.chips_y
        return zl, y

    def index(self, chip):
        return chip[0] * self.sz.chips_y + chip[1]

    def device(self, chip):
        return (self.f, self.zh * self.sz.zl + chip[0], 2 * chip[1] + self.k)

    @property
    def twin(self):
        return (self.f, self.c, self.t + 1 - 2 * self.k)


    def ctx_ahead(self, step):
        sz = self.sz
        return (self.zh + step // sz.zl) % sz.images * sz.zl + (self.zl + step % sz.zl) % sz.zl

    def ctx_back(self, step):
        sz = self.sz
        zh = (self.zh + sz.images - step // sz.zl) % sz.images
        return zh * sz.zl + (self.zl + sz.zl - step % sz.zl) % sz.zl


def split_refs(refs, *counts):
    out, at = [], 0
    for count in counts:
        out.append(refs[at:at + count])
        at += count
    assert at == len(refs)
    return out


class Greeting:
    def __init__(self, others):
        self.count = len(others)
        self.barrier = pltpu.get_barrier_semaphore()
        for other in others:
            pl.semaphore_signal(self.barrier, inc=1, device_id=other, device_id_type=MESH)

    def wait(self):
        pl.semaphore_wait(self.barrier, self.count)


def send(src, dst, send_sem, recv_sem, device):
    return pltpu.make_async_remote_copy(
        src_ref=src, dst_ref=dst, send_sem=send_sem, recv_sem=recv_sem, device_id=device, device_id_type=MESH
    )


def team_peers(pc):
    return [pc.device(pc.chip_at(step)) for step in range(1, pc.sz.chips)] + [pc.twin]


def line_peers(pc):
    sz = pc.sz
    return [(pc.f, pc.c, 2 * ((pc.y + dy) % sz.chips_y) + 1 - pc.k) for dy in range(1, sz.chips_y)]


def weight_peers(pc, team=False):
    sz = pc.sz
    first = sz.zl if team else 1
    return [(pc.f, pc.ctx_ahead(step), pc.t) for step in range(first, sz.ctx)] + [
        ((pc.f + jump) % sz.fsdp, pc.c, pc.t) for jump in range(1, sz.fsdp)
    ]


def pick(step, values):
    if isinstance(step, int):
        return values[step]
    out = jnp.int32(values[0])
    for i in range(1, len(values)):
        out = jnp.where(step == i, jnp.int32(values[i]), out)
    return out


def when(condition, run):
    if isinstance(condition, (bool, int)):
        if condition:
            run()
    else:
        pl.when(condition)(run)


class Routes:
    def __init__(self, sz):
        self.sz = sz
        pieces = range(sz.images)
        z = [dz * sz.chips_y for dz in range(1, sz.zl)]
        y = list(range(1, sz.chips_y))
        self.straight = z + y
        self.turned = [dz + dy for dz in z for dy in y]
        own = [(0, p) for p in pieces]
        near = [(b, p) for p in pieces for b in self.straight]
        far = [(b, p) for p in pieces for b in self.turned]
        self.arriving = own + near + far
        self.leaving = far + [(b, p) for b in z for p in pieces] + [(b, p) for b in y for p in pieces] + own


def backs(order):
    return [b for b, _ in order]


def pieces_of(order):
    return [p for _, p in order]


class Gather:
    def __init__(self, pc, buf, sems, turn_z=()):
        self.pc, self.buf, self.sems = pc, buf, sems
        self.routes = Routes(pc.sz)
        self.order = self.routes.arriving
        self.turn_z = turn_z

    def put(self, low):
        sz = self.pc.sz
        self.buf[self.pc.slot] = low.reshape(sz.images, sz.part, sz.d)

    def move(self, kind, back, piece, slot, device):
        return send(self.buf.at[slot, piece], self.buf.at[slot, piece], self.sems.at[kind, back, piece],
                    self.sems.at[kind + 1, back, piece], device)

    def near(self, back, piece, slot):
        return self.move(2, back, piece, slot, self.pc.twin)

    def start(self):
        pc = self.pc
        for piece in range(pc.sz.images):
            for step in self.routes.straight:
                self.move(0, step, piece, pc.slot, pc.device(pc.chip_at(step))).start()
            self.near(0, piece, pc.slot).start()

    def relays(self, back, piece):
        sz = self.pc.sz
        if back == 0 or back in self.routes.turned:
            return []
        if back % sz.chips_y == 0:
            return [] if piece in self.turn_z else [(back + dy, dy) for dy in range(1, sz.chips_y)]
        return [(back + dz * sz.chips_y, dz * sz.chips_y) for dz in range(1, sz.zl)] if piece in self.turn_z else []

    def forward(self, step):
        pc, order = self.pc, self.order
        back, piece = pick(step, backs(order)), pick(step, pieces_of(order))
        slot = 2 * pc.index(pc.chip_back(back)) + pc.k

        def other():
            self.move(0, back, piece, slot, pc.twin).wait_recv()
            self.near(back, piece, slot).start()

        when(back > 0, other)
        for at, (b, p) in enumerate(order):
            for seen, ahead in self.relays(b, p):
                when(step == at, self.move(0, seen, p, slot, pc.device(pc.chip_at(ahead))).start)

    def ready(self, step):
        pc = self.pc
        back, piece = pick(step, backs(self.order)), pick(step, pieces_of(self.order))
        at = pc.index(pc.chip_back(back))
        self.near(back, piece, 2 * at + 1 - pc.k).wait_recv()
        return at * pc.sz.images + piece, at, piece

    def ahead(self, step):
        if isinstance(step, int):
            if step + 1 < len(self.order):
                self.forward(step + 1)
        else:
            pl.when(step + 1 < len(self.order))(lambda: self.forward(step + 1))

    def tokens(self, at, piece):
        sz = self.pc.sz
        return self.buf[pl.ds(2 * at, 2), piece].reshape(sz.tile, sz.d)

    def finish(self):
        pc = self.pc
        for b, p in self.order:
            if b:
                self.move(0, b, p, pc.slot, pc.twin).wait_send()
            self.near(b, p, pc.slot).wait_send()


class Scatter:
    def __init__(self, pc, bufs, sems, turn):
        self.pc, self.sems, self.turn = pc, sems, turn
        self.both, self.keep, self.tsend, self.trecv, self.rsend, self.rrecv = bufs
        self.routes = Routes(pc.sz)
        self.order = self.routes.leaving if turn else self.routes.arriving

    def near(self, back, piece):
        return send(self.tsend.at[back, piece], self.trecv.at[back, piece], self.sems.at[0, back, piece],
                    self.sems.at[1, back, piece], self.pc.twin)

    def far(self, back, piece):
        pc, sz = self.pc, self.pc.sz
        to = back
        if self.turn:
            if isinstance(back, int):
                to = back % sz.chips_y or back
            else:
                dy = lax.rem(back, jnp.int32(sz.chips_y))
                to = jnp.where(dy > 0, dy, back)
        return send(self.rsend.at[back, piece], self.rrecv.at[back, piece], self.sems.at[2, back, piece],
                    self.sems.at[3, back, piece], pc.device(pc.chip_back(to)))

    def at(self, step):
        return pick(step, backs(self.order)), pick(step, pieces_of(self.order))

    def unit(self, step):
        back, piece = self.at(step)
        return self.pc.index(self.pc.chip_back(back)) * self.pc.sz.images + piece

    def push(self, step, partial):
        pc = self.pc
        back, piece = self.at(step)
        self.both[...] = partial.reshape(2, pc.sz.part, partial.shape[-1])
        self.tsend[back, piece] = self.both[1 - pc.k].astype(bf16)
        self.near(back, piece).start()
        self.keep[back, piece] = self.both[pc.k]
        pl.when(step > 0)(lambda: self.relay(step - 1))

    def relay(self, step):
        sz = self.pc.sz
        back, piece = self.at(step)
        self.near(back, piece).wait_recv()
        self.keep[back, piece] += self.trecv[back, piece].astype(f32)
        if self.turn:
            for at, (b, p) in enumerate(self.order):
                if b and b % sz.chips_y == 0:

                    def extra(b=b, p=p):
                        for dy in range(1, sz.chips_y):
                            self.far(b + dy, p).wait_recv()
                            self.keep[b, p] += self.rrecv[b + dy, p].astype(f32)

                    when(step == at, extra)

        def leave():
            self.rsend[back, piece] = self.keep[back, piece].astype(bf16)
            self.far(back, piece).start()

        when(back > 0, leave)

    def flush(self):
        self.relay(self.pc.sz.units - 1)

    def finish(self):
        sz = self.pc.sz
        total = self.keep[0]
        for back in range(1, sz.chips):
            if self.turn and back in self.routes.turned:
                continue
            for piece in range(sz.images):
                self.far(back, piece).wait_recv()
            total = total + self.rrecv[back].astype(f32)
        for back, piece in self.order:
            self.near(back, piece).wait_send()
            if back:
                self.far(back, piece).wait_send()
        return total.reshape(sz.block, sz.d)


def team_scratch(sz, phases):
    n = (sz.chips, sz.images)
    return [
        VMEM((2, sz.part, sz.d), f32),
        VMEM(n + (sz.part, sz.d), f32),
        VMEM(n + (sz.part, sz.d), bf16),
        VMEM(n + (sz.part, sz.d), bf16),
        VMEM(n + (sz.part, sz.d), bf16),
        VMEM(n + (sz.part, sz.d), bf16),
        DMA((phases, 4) + n),
        DMA((phases, 4) + n),
    ]


def normalised(values):
    centre = jnp.mean(values, axis=-1, keepdims=True)
    centred = values - centre
    spread = jnp.mean(centred * centred, axis=-1, keepdims=True)
    inverse = lax.rsqrt(spread + norm_eps)
    return centred * inverse, inverse


def norm_back(values, gain, grad):
    high, inverse = normalised(values)
    scaled = grad * gain
    term = inverse * (
        scaled
        - jnp.mean(scaled, axis=-1, keepdims=True)
        - high * jnp.mean(scaled * high, axis=-1, keepdims=True)
    )
    return term, jnp.sum(grad * high, axis=0, keepdims=True), jnp.sum(grad, axis=0, keepdims=True)


def lanes_of(shape):
    return lax.broadcasted_iota(jnp.int32, shape, len(shape) - 1)


def unpack_out(sz, w_ref, o_ref):
    at = 3 * sz.wide // 128 * 128
    shift = 3 * sz.wide - at

    def step(i, carry):
        rows = pl.ds(pl.multiple_of(i * 128, 128), 128)
        piece = pltpu.roll(w_ref[rows, at:at + sz.headp].astype(f32), sz.headp - shift, 1)
        o_ref[rows, :] = jnp.where(lanes_of(piece.shape) < sz.wide, piece, 0.0).astype(bf16)
        return carry

    lax.fori_loop(0, sz.d // 128, step, 0)


def take(sz, values, kind):
    at = kind * sz.wide // 128 * 128
    shift = kind * sz.wide - at
    piece = values[:, at:at + sz.headp]
    if shift:
        piece = pltpu.roll(piece, sz.headp - shift, 1)
    return jnp.where(lanes_of(piece.shape) < sz.wide, piece, 0.0)


def head_of(values, head):
    lanes = lanes_of(values.shape)
    mine = (lanes >= head * HEAD_DIM) & (lanes < (head + 1) * HEAD_DIM)
    return jnp.where(mine, values, jnp.zeros_like(values))


def probabilities(q_head, keys, valid):
    scores = dot(q_head, keys, (1, 1)) * HEAD_DIM ** (-0.5)
    scores = jnp.where(valid > 0.0, scores, masked_score)
    weights = jnp.exp(scores - jnp.max(scores, axis=-1, keepdims=True))
    return weights / jnp.sum(weights, axis=-1, keepdims=True)


FF_TURN = (1,)


class Jobs:
    def __init__(self, **places):
        self.places = places

    def run(self, place):
        for job in self.places.get(place, ()):
            job()

    def at(self, place, step):
        for when_step, jobs in self.places.get(place, {}).items():

            def run(jobs=jobs):
                for job in jobs:
                    job()

            when(step == when_step, run)


class Copies:
    def __init__(self, sems):
        self.sems, self.made = sems, []

    def start(self, src, dst):
        copy = pltpu.make_async_copy(src, dst, self.sems.at[len(self.made)])
        self.made.append(copy)
        copy.start()
        return copy

    def wait(self):
        for copy in self.made:
            copy.wait()


class Fetch:
    def __init__(self, pc, own, everything, sems):
        self.pc, self.own, self.all, self.sems = pc, own, everything, sems

    def rows(self, group):
        rows = self.pc.sz.wrowsp
        return self.all.at[pl.ds(pl.multiple_of(group * rows, 16), rows)]

    def along_ctx(self, step):
        pc = self.pc
        c = pc.ctx_ahead(step)
        return send(self.own.at[c % pc.sz.zl], self.rows(pc.f * pc.sz.ctx + pc.c), self.sems.at[0, 0, step],
                    self.sems.at[0, 1, step], (pc.f, c, pc.t))

    def own_copy(self):
        pc = self.pc
        return pltpu.make_async_copy(self.own.at[pc.zl], self.rows(pc.f * pc.sz.ctx + pc.c), self.sems.at[0, 0, 0])

    def along_fsdp(self, jump, step):
        pc, sz = self.pc, self.pc.sz
        rows = self.rows(pc.f * sz.ctx + pc.ctx_back(step))
        return send(rows, rows, self.sems.at[jump, 0, step], self.sems.at[jump, 1, step],
                    ((pc.f + jump) % sz.fsdp, pc.c, pc.t))

    def start(self):
        self.own_copy().start()
        for step in range(1, min(3, self.pc.sz.ctx)):
            self.along_ctx(step).start()

    def pass_own(self):
        self.own_copy().wait()
        for jump in range(1, self.pc.sz.fsdp):
            self.along_fsdp(jump, 0).start()

    def pass_on(self, step):
        if step >= self.pc.sz.ctx:
            return
        self.along_ctx(step).wait_recv()
        if step + 2 < self.pc.sz.ctx:
            self.along_ctx(step + 2).start()
        for jump in range(1, self.pc.sz.fsdp):
            self.along_fsdp(jump, step).start()

    def pass_rest(self):
        for step in range(3, self.pc.sz.ctx):
            self.pass_on(step)

    def part(self, step):
        return functools.partial(self.pass_on, step)

    def finish(self):
        sz = self.pc.sz
        for step in range(sz.ctx):
            if step:
                self.along_ctx(step).wait_send()
            for jump in range(1, sz.fsdp):
                self.along_fsdp(jump, step).wait()


class Give:
    def __init__(self, pc, dw, recv, got, sems):
        self.pc, self.dw, self.recv, self.got, self.sems = pc, dw, recv, got, sems
        self.order = list(range(pc.sz.ctx - 1, -1, -1))

    def rows(self, group):
        rows = self.pc.sz.wrowsp
        return pl.ds(pl.multiple_of(group * rows, 16), rows)

    def along_fsdp(self, jump, step):
        pc, sz = self.pc, self.pc.sz
        f = (pc.f + jump) % sz.fsdp
        return send(self.dw.at[self.rows(f * sz.ctx + pc.ctx_ahead(step))], self.got.at[jump - 1, step],
                    self.sems.at[jump, 0, step], self.sems.at[jump, 1, step], (f, pc.c, pc.t))

    def along_ctx(self, step):
        pc = self.pc
        return send(self.got.at[0, step], self.recv.at[pc.c], self.sems.at[0, 0, step], self.sems.at[0, 1, step],
                    (pc.f, pc.ctx_ahead(step), pc.t))

    def from_ctx(self, step):
        pc = self.pc
        return send(self.got.at[0, step], self.recv.at[pc.ctx_back(step)], self.sems.at[0, 0, step],
                    self.sems.at[0, 1, step], (pc.f, pc.ctx_back(step), pc.t))

    def own_copy(self):
        return pltpu.make_async_copy(self.got.at[0, 0], self.recv.at[self.pc.c], self.sems.at[0, 0, 0])

    def start(self):
        for step in self.order[:2]:
            for jump in range(1, self.pc.sz.fsdp):
                self.along_fsdp(jump, step).start()

    def pass_on(self, step):
        pc, sz = self.pc, self.pc.sz
        for jump in range(1, sz.fsdp):
            self.along_fsdp(jump, step).wait_recv()
            if step >= 2:
                self.along_fsdp(jump, step - 2).start()
        total = self.dw[self.rows(pc.f * sz.ctx + pc.ctx_ahead(step))].astype(f32)
        for jump in range(1, sz.fsdp):
            total = total + self.got[jump - 1, step].astype(f32)
        self.got[0, step] = total.astype(bf16)
        if step:
            self.along_ctx(step).start()
        else:
            self.own_copy().start()

    def pass_early(self):
        for step in self.order[:-3]:
            self.pass_on(step)

    def part(self, step):
        return functools.partial(self.pass_on, step)

    def finish(self):
        sz = self.pc.sz
        self.own_copy().wait()
        for step in range(sz.ctx):
            if step:
                self.from_ctx(step).wait_recv()
                self.along_ctx(step).wait_send()
            for jump in range(1, sz.fsdp):
                self.along_fsdp(jump, step).wait_send()


def mover_sems(sz):
    return DMA((sz.fsdp, 2, sz.ctx))


def chosen(sz, group, lanes_shape):
    row = lax.broadcasted_iota(jnp.int32, lanes_shape, 0)
    col = lax.broadcasted_iota(jnp.int32, lanes_shape, 1)
    return jnp.where((row - group * sz.wrows == col) & (col < sz.wrows), 1.0, 0.0).astype(bf16)


def drop_padding(sz, src, dst):
    for at in range(0, dst.shape[-1], 128):
        lanes = slice(at, at + 128)

        def step(group, total):
            rows = pl.ds(pl.multiple_of(group * sz.wrowsp, 16), sz.wrowsp)
            return total + dot(chosen(sz, group, (sz.d, sz.wrowsp)), src[rows, lanes], (1, 0))

        dst[:, lanes] = lax.fori_loop(0, sz.groups, step, jnp.zeros((sz.d, 128), f32)).astype(bf16)


def add_padding(sz, src, dst):
    def step(group, carry):
        rows = pl.ds(pl.multiple_of(group * sz.wrowsp, 16), sz.wrowsp)
        for at in range(0, dst.shape[-1], 128):
            lanes = slice(at, at + 128)
            dst[rows, lanes] = dot(chosen(sz, group, (sz.d, sz.wrowsp)), src[:, lanes], (0, 0)).astype(bf16)
        return carry

    lax.fori_loop(0, sz.groups, step, 0)


def by_unit(sz, values):
    values = values.reshape(sz.chips, 2, sz.images, sz.part, values.shape[-1])
    return jnp.swapaxes(values, 1, 2).reshape(sz.keys, values.shape[-1])


def shift_lanes(values, start, count, at, width):
    have = values.shape[-1]
    first, last = start // 128 * 128, up_to(start + count, 128)
    to = at // 128 * 128
    span = max(last - first, up_to(at + count, 128) - to)
    piece = values[:, first:min(last, have)].astype(f32)
    if piece.shape[-1] < span:
        piece = jnp.pad(piece, ((0, 0), (0, span - piece.shape[-1])))
    turn = ((at - to) - (start - first)) % span
    if turn:
        piece = pltpu.roll(piece, turn, 1)
    lanes = lanes_of(piece.shape)
    piece = jnp.where((lanes >= at - to) & (lanes < at - to + count), piece, 0.0)
    piece = piece[:, 0:min(span, width - to)]
    return jnp.pad(piece, ((0, 0), (to, width - to - piece.shape[-1])))


def half_of(pc, values, count, width):
    out = shift_lanes(values, 0, count, 0, width)
    for j in range(1, pc.sz.zl):
        out = jnp.where(pc.zl == j, shift_lanes(values, j * count, count, 0, width), out)
    return out


def piece_of(pc, values):
    sz = pc.sz
    values = values.astype(f32)
    over = sz.tp * sz.part - sz.rows
    if over:
        values = jnp.concatenate([values, jnp.zeros((over, sz.d), f32)], axis=0)
    out = values[0:sz.part]
    for t in range(1, sz.tp):
        out = jnp.where(pc.t == t, values[t * sz.part:(t + 1) * sz.part], out)
    return out


def steps_below(values, unit, count):
    out = jnp.zeros_like(values)
    for m in range(1, count):
        out = out + jnp.where(values >= m * unit, 1, 0)
    return out


def key_valid(pc, count):
    sz = pc.sz
    row = lax.broadcasted_iota(jnp.int32, (1, sz.keys), 1)
    unit = steps_below(row, sz.tile, sz.units)
    within = row - unit * sz.tile
    core = steps_below(within, sz.part, 2)
    chip = steps_below(unit, sz.images, sz.chips)
    zl = steps_below(chip, sz.chips_y, sz.zl)
    t = 2 * (chip - zl * sz.chips_y) + core
    token = t * sz.part + within - core * sz.part
    position = ((unit - chip * sz.images) * sz.zl + zl) * sz.rows + token
    return jnp.where((token < sz.rows) & (position < count), 1.0, 0.0)


def own_valid(pc, count):
    sz = pc.sz
    row = lax.broadcasted_iota(jnp.int32, (sz.block, 1), 0)
    piece = steps_below(row, sz.part, sz.images)
    token = pc.t * sz.part + row - piece * sz.part
    position = (piece * sz.zl + pc.zl) * sz.rows + token
    return jnp.where((token < sz.rows) & (position < count), 1.0, 0.0)


def attn_forward(pc, jobs, gather, w_ref, stream, qv, resid, valid_ref, q_ref, k_ref, v_ref, mixed_ref, o_ref,
                 scatter):
    sz = pc.sz
    unpack_out(sz, w_ref, o_ref)

    def project(step, carry):
        unit, at, piece = gather.ready(step)
        both3 = dot(gather.tokens(at, piece), w_ref[:, 0:sz.qkvp], (1, 0))
        gather.ahead(step)
        q_ref[unit] = (take(sz, both3, 0) + qv[0:1, :]).astype(bf16)
        k_ref[unit] = take(sz, both3, 1).astype(bf16)
        v_ref[unit] = (take(sz, both3, 2) + qv[1:2, :]).astype(bf16)
        jobs.at("project", step)
        return carry

    lax.fori_loop(0, sz.units, project, 0)
    gather.finish()

    def attend(step, carry):
        unit = scatter.unit(step)
        keys = k_ref[...].reshape(sz.keys, sz.headp)
        values = v_ref[...].reshape(sz.keys, sz.headp)
        queries = q_ref[unit]
        total = jnp.zeros((sz.tile, sz.headp), f32)
        for head in range(sz.heads):
            probs = probabilities(head_of(queries, head), keys, valid_ref[...])
            total = total + dot(probs.astype(bf16), head_of(values, head), (1, 0))
        mixed = total.astype(bf16)
        mixed_ref[unit] = mixed
        scatter.push(step, dot(mixed, o_ref[...], (1, 1)))
        jobs.at("attend", step)
        return carry

    lax.fori_loop(0, sz.units, attend, 0)
    scatter.flush()
    jobs.run("flush")
    return stream + (scatter.finish() + resid)


def ff_forward(pc, jobs, gather, w_ref, middle_ref, upb, resid, pre_ref, hidden_ref, scatter):
    sz = pc.sz

    def feed(step, carry):
        unit, at, piece = gather.ready(step)
        pre = dot(gather.tokens(at, piece), w_ref[:, 0:sz.ffp], (1, 0)) + upb
        gather.ahead(step)
        pre_ref[unit] = pre
        hidden = 0.5 * pre * (1.0 + jnp.tanh(gelu_root * (pre + gelu_cubic * pre * pre * pre)))
        hidden = jnp.where(lanes_of(hidden.shape) < sz.ff, hidden, 0.0)
        if sz.down_shift:
            hidden = pltpu.roll(hidden, sz.down_shift, 1)
        hidden = hidden.astype(bf16)
        hidden_ref[unit] = hidden
        scatter.push(step, dot(hidden, w_ref[:, sz.down_at:], (1, 1)))
        jobs.at("feed", step)
        return carry

    lax.fori_loop(0, sz.units, feed, 0)
    scatter.flush()
    jobs.run("flush")
    gather.finish()
    return middle_ref[...] + (scatter.finish() + resid)


def norm_low(values, gain, shift):
    high, _ = normalised(values)
    return (high * gain + shift).astype(bf16)


def forward_kernel(sz, *refs):
    n = sz.layers
    aligned = sz.wrowsp == sz.wrows
    ins, outs, scratch = refs[:12], refs[12:12 + 13 * n + 1], refs[12 + 13 * n + 1:]
    (count_ref, in_ref, cot_ref, wqkv_ref, wout_ref, wup_ref, wdown_ref, gain_ref, shift_ref, qv_ref, upb_ref,
     resid_ref) = ins
    saved, (wattn_outs, wff_outs, ends_ref) = outs[:11 * n], split_refs(outs[11 * n:], n, n, 1)
    saved = [saved[l * 11:(l + 1) * 11] for l in range(n)]
    ends_ref = ends_ref[0]
    (own_attn, own_ff, all_attn, all_ff, swap_ref, mine_ref, n_ref, q_ref, k_ref, v_ref, mixed_ref, pre_ref,
     hidden_ref, stream_ref, middle_ref, valid_ref, o_ref, tsems, csems, wsems), team, joined = split_refs(
        scratch, 20, 8, 0 if aligned else 2)
    bufs, (gsems, ssems) = team[:6], team[6:]
    pc = Place(sz)
    greeting = Greeting(team_peers(pc) + weight_peers(pc, True))

    def pack(ref, pieces):
        total = None
        for values, start, count, at in pieces:
            piece = shift_lanes(values, start, count, at, ref.shape[-1])
            total = piece if total is None else total + piece
        ref[0:sz.wrows, :] = total.astype(bf16)
        if not aligned:
            ref[sz.wrows:, :] = jnp.zeros((sz.wrowsp - sz.wrows, ref.shape[-1]), bf16)

    def pack_attn(layer):
        full = sz.wide * sz.zl
        for half in range(sz.zl):
            pieces = [(wqkv_ref[layer], kind * full + half * sz.wide, sz.wide, kind * sz.wide) for kind in range(3)]
            pack(own_attn.at[layer, half], pieces + [(wout_ref[layer], half * sz.wide, sz.wide, 3 * sz.wide)])

    def pack_ff(layer):
        for half in range(sz.zl):
            pack(own_ff.at[layer, half], [(wup_ref[layer], half * sz.ff, sz.ff, 0),
                                          (wdown_ref[layer], half * sz.ff, sz.ff, sz.ff)])

    for image in range(sz.images):
        swap_ref[image, 0] = piece_of(pc, in_ref[image]).astype(bf16)
        swap_ref[image, 1] = piece_of(pc, cot_ref[image]).astype(bf16)
    pack_attn(0)
    attn = [Fetch(pc, own_attn.at[l], all_attn.at[l], wsems.at[2 * l]) for l in range(n)]
    ff = [Fetch(pc, own_ff.at[l], all_ff.at[l], wsems.at[2 * l + 1]) for l in range(n)]
    copies = Copies(csems)

    def swap(step):
        zh = (pc.zh + step) % sz.images
        return send(swap_ref.at[zh], mine_ref.at[pc.zh], tsems.at[0, step], tsems.at[1, step],
                    (pc.f, zh * sz.zl + pc.zl, pc.t))

    greeting.wait()
    for step in range(1, sz.images):
        swap(step).start()
    attn[0].start()
    mine_ref[pc.zh] = swap_ref[pc.zh]
    count = count_ref[pc.zh]
    valid_ref[...] = key_valid(pc, count)
    for step in range(1, sz.images):
        swap(step).wait()
    stream_ref[0] = mine_ref[:, 0].reshape(sz.block, sz.d).astype(f32)
    gathers = [Gather(pc, n_ref.at[i], gsems.at[i], FF_TURN if i % 2 or i == 0 else ()) for i in range(2 * n)]
    scatters = [Scatter(pc, bufs, ssems.at[i], i % 2 == 0) for i in range(2 * n)]
    gathers[0].put(norm_low(stream_ref[0], gain_ref[0, 0:1, :], shift_ref[0, 0:1, :]))
    gathers[0].start()
    attn[0].pass_own()
    pack_ff(0)
    attn[0].pass_on(1)
    for layer in range(1, n):
        pack_attn(layer)
    attn[0].pass_on(2)
    ff[0].start()
    ends_ref[...] = mine_ref[:, 1].reshape(sz.block, sz.d).astype(f32) * own_valid(pc, count)
    attn[0].pass_rest()
    ff[0].pass_own()
    for layer in range(1, n):
        pack_ff(layer)
    attn[0].finish()

    def ready(fetch, refs, kind, layer, out):
        ref = refs.at[layer]
        if not aligned:
            drop_padding(sz, ref, joined[kind])
            ref = joined[kind]
            pltpu.sync_copy(ref, out)
        else:
            copies.start(ref, out)
        return ref

    for l in range(n):
        more = l + 1 < n
        w = ready(attn[l], all_attn, 0, l, wattn_outs[l])
        qv = half_of(pc, qv_ref[l], sz.wide, sz.headp)
        jobs = Jobs(
            project={sz.units - 2: [ff[l].part(1)]},
            attend={2: [ff[l].part(2)], sz.units - 1: ([attn[l + 1].start] if more else [])},
            flush=[ff[l].pass_rest] + ([attn[l + 1].pass_own] if more else []),
        )
        middle_ref[l] = attn_forward(
            pc, jobs, gathers[2 * l], w, stream_ref[l], qv, resid_ref[l, 0:1, :], valid_ref,
            q_ref.at[l], k_ref.at[l], v_ref.at[l], mixed_ref.at[l], o_ref, scatters[2 * l],
        )
        gathers[2 * l + 1].put(norm_low(middle_ref[l], gain_ref[l, 1:2, :], shift_ref[l, 1:2, :]))
        gathers[2 * l + 1].start()
        for ref, to in ((stream_ref.at[l], 0), (middle_ref.at[l], 1), (n_ref.at[2 * l], 2), (q_ref.at[l], 4),
                        (k_ref.at[l], 5), (v_ref.at[l], 6), (mixed_ref.at[l], 7)):
            copies.start(ref, saved[l][to])
        ff[l].finish()
        w = ready(ff[l], all_ff, 1, l, wff_outs[l])
        upb = half_of(pc, upb_ref[l:l + 1, :], sz.ff, sz.ffp)
        if more:
            jobs = Jobs(
                feed={1: [attn[l + 1].part(1)], 3: [attn[l + 1].part(2)], 5: [ff[l + 1].start],
                      6: [attn[l + 1].pass_rest], 7: [ff[l + 1].pass_own]},
            )
        else:
            jobs = Jobs()
        out = ff_forward(pc, jobs, gathers[2 * l + 1], w, middle_ref.at[l], upb, resid_ref[l, 1:2, :],
                         pre_ref.at[l], hidden_ref.at[l], scatters[2 * l + 1])
        stream_ref[l + 1] = out
        if more:
            gathers[2 * l + 2].put(norm_low(out, gain_ref[l + 1, 0:1, :], shift_ref[l + 1, 0:1, :]))
            gathers[2 * l + 2].start()
            attn[l + 1].finish()
        for ref, to in ((n_ref.at[2 * l + 1], 3), (pre_ref.at[l], 8), (hidden_ref.at[l], 9)):
            copies.start(ref, saved[l][to])
    copies.start(stream_ref.at[n], saved[0][10])
    copies.start(valid_ref, saved[n - 1][10])
    copies.wait()


def forward_call(sz, *operands):
    n = sz.layers
    own, team = ((sz.block, sz.d), f32), ((sz.team, sz.images, sz.part, sz.d), bf16)
    head, hidden = ((sz.units, sz.tile, sz.headp), bf16), (sz.units, sz.tile, sz.ffp)
    shapes = []
    for l in range(n):
        last = ((1, sz.keys), f32) if l == n - 1 else own
        shapes += [own, own, team, team, head, head, head, head, (hidden, f32), (hidden, bf16), last]
    shapes += [((sz.d, sz.attnp), bf16)] * n + [((sz.d, sz.ffw), bf16)] * n + [own]
    vmem, hbm = pl.BlockSpec(memory_space=pltpu.VMEM), pl.BlockSpec(memory_space=pl.ANY)
    padded = sz.groups * sz.wrowsp
    scratch = [
        VMEM((n, sz.zl, sz.wrowsp, sz.attnp), bf16), VMEM((n, sz.zl, sz.wrowsp, sz.ffw), bf16),
        VMEM((n, padded, sz.attnp), bf16), VMEM((n, padded, sz.ffw), bf16),
        VMEM((sz.images, 2, sz.part, sz.d), bf16), VMEM((sz.images, 2, sz.part, sz.d), bf16),
        VMEM((2 * n,) + team[0], bf16),
        *[VMEM((n,) + head[0], bf16) for _ in range(4)],
        VMEM((n,) + hidden, f32), VMEM((n,) + hidden, bf16),
        VMEM((n + 1, sz.block, sz.d), f32), VMEM((n, sz.block, sz.d), f32), VMEM((1, sz.keys), f32),
        VMEM((sz.d, sz.headp), bf16),
        DMA((2, sz.images)), DMA((12 * n + 2,)), DMA((2 * n, sz.fsdp, 2, sz.ctx)),
    ] + team_scratch(sz, 2 * n)
    if sz.wrowsp != sz.wrows:
        scratch += [VMEM((sz.d, sz.attnp), bf16), VMEM((sz.d, sz.ffw), bf16)]
    return pl.pallas_call(
        functools.partial(forward_kernel, sz),
        out_shape=[jax.ShapeDtypeStruct(*s) for s in shapes],
        in_specs=[pl.BlockSpec(memory_space=pltpu.SMEM)] + [vmem] * (len(operands) - 1),
        out_specs=[hbm] * (len(shapes) - 1) + [vmem],
        scratch_shapes=scratch,
        compiler_params=params(1),
        name="forward",
    )(*operands)


def params(collective_id):
    return pltpu.CompilerParams(
        collective_id=collective_id, has_side_effects=True, vmem_limit_bytes=63 * 1024 * 1024
    )


def ff_backward(pc, jobs, gather, w_ref, n2_ref, pre_ref, hidden_ref, dup_ref, pg_ref, dw_ref, scatter):
    sz = pc.sz
    span = 384 if sz.d % 384 == 0 else 128
    dup_ref[...] = jnp.zeros_like(dup_ref)

    def feed(step, carry):
        unit, at, piece = gather.ready(step)
        back = dot(gather.tokens(at, piece), w_ref[:, sz.down_at:], (1, 0))
        gather.ahead(step)
        if sz.down_shift:
            back = pltpu.roll(back, sz.ffp - sz.down_shift, 1)
        pre = pre_ref[unit]
        bent = jnp.tanh(gelu_root * (pre + gelu_cubic * pre * pre * pre))
        slope = 0.5 * (1.0 + bent) + 0.5 * pre * (1.0 - bent * bent) * (
            gelu_root * (1.0 + 3.0 * gelu_cubic * pre * pre)
        )
        pre_grad = jnp.where(lanes_of(back.shape) < sz.ff, back * slope, 0.0).astype(bf16)
        pg_ref[unit] = pre_grad
        dup_ref[...] += jnp.sum(pre_grad.astype(f32), axis=0, keepdims=True)
        scatter.push(step, dot(pre_grad, w_ref[:, 0:sz.ffp], (1, 1)))
        jobs.at("feed", step)
        return carry

    lax.fori_loop(0, sz.units, feed, 0)
    scatter.flush()
    jobs.run("flush")

    def grads(i, carry):
        lanes = pl.ds(pl.multiple_of(i * span, 128), span)
        hidden = hidden_ref[...].reshape(sz.keys, sz.ffp)
        down = dot(by_unit(sz, gather.buf[:, :, :, lanes]), hidden, (0, 0))
        pre_grad = pg_ref[...].reshape(sz.keys, sz.ffp)
        up = dot(by_unit(sz, n2_ref[:, :, :, lanes]), pre_grad, (0, 0))
        dw_ref[lanes, 0:sz.down_at] = up[:, 0:sz.down_at].astype(bf16)
        over = sz.ffp - sz.down_at
        if over:
            dw_ref[lanes, sz.down_at:sz.ffp] = (up[:, sz.down_at:] + down[:, 0:over]).astype(bf16)
        dw_ref[lanes, sz.ffp:] = down[:, over:].astype(bf16)
        return carry

    lax.fori_loop(0, sz.d // span, grads, 0)
    jobs.run("grads")
    gather.finish()
    return scatter.finish()


def attn_backward(pc, jobs, gather, w_ref, n1_ref, q_ref, k_ref, v_ref, mixed_ref, valid_ref, dqv_ref,
                  o_ref, dk_ref, dv_ref, stack_ref, dw_ref, scatter):
    sz = pc.sz
    span = 384 if sz.d % 384 == 0 else 128
    unpack_out(sz, w_ref, o_ref)
    dk_ref[...] = jnp.zeros_like(dk_ref)
    dv_ref[...] = jnp.zeros_like(dv_ref)
    dqv_ref[...] = jnp.zeros_like(dqv_ref)
    scale = HEAD_DIM ** (-0.5)

    def attend(step, carry):
        unit, at, piece = gather.ready(step)
        mixed_grad = dot(gather.tokens(at, piece), o_ref[...], (1, 0)).astype(bf16)
        gather.ahead(step)
        keys = k_ref[...].reshape(sz.keys, sz.headp)
        values = v_ref[...].reshape(sz.keys, sz.headp)
        total = jnp.zeros((sz.tile, sz.headp), f32)
        for head in range(sz.heads):
            q_head = head_of(q_ref[unit], head)
            g_head = head_of(mixed_grad, head)
            probs = probabilities(q_head, keys, valid_ref[...])
            dprobs = dot(g_head, values, (1, 1))
            inner = jnp.sum(probs * dprobs, axis=-1, keepdims=True)
            dscores = (probs * (dprobs - inner)).astype(bf16)
            total = total + dot(dscores, head_of(keys, head), (1, 0))
            dk_ref[...] += dot(dscores, q_head, (0, 0))
            dv_ref[...] += dot(probs.astype(bf16), g_head, (0, 0))
        dq = (scale * total).astype(bf16).astype(f32)
        dqv_ref[0:1, :] += jnp.sum(dq, axis=0, keepdims=True)
        stack_ref[unit, :, 0:sz.headp] = dq.astype(bf16)
        jobs.at("attend", step)
        return carry

    lax.fori_loop(0, sz.units, attend, 0)
    gather.finish()
    jobs.run("middle")

    def back_project(step, carry):
        unit = scatter.unit(step)
        rows = pl.ds(pl.multiple_of(unit * sz.tile, sz.tile), sz.tile)
        dk = (scale * dk_ref[rows, :]).astype(bf16).astype(f32)
        dv = dv_ref[rows, :].astype(bf16).astype(f32)
        dqv_ref[1:2, :] += jnp.sum(dv, axis=0, keepdims=True)
        dq = stack_ref[unit, :, 0:sz.headp].astype(f32)
        total = jnp.pad(dq, ((0, 0), (0, sz.qkvp - sz.headp)))
        for kind, piece in ((1, dk), (2, dv)):
            start = kind * sz.wide // 128 * 128
            shift = kind * sz.wide - start
            moved = pltpu.roll(piece, shift, 1) if shift else piece
            total = total + jnp.pad(moved, ((0, 0), (start, sz.qkvp - start - sz.headp)))
        stacked = total.astype(bf16)
        stack_ref[unit] = stacked
        scatter.push(step, dot(stacked, w_ref[:, 0:sz.qkvp], (1, 1)))
        return carry

    lax.fori_loop(0, sz.units, back_project, 0)
    scatter.flush()
    jobs.run("flush")
    o_at = 3 * sz.wide // 128 * 128
    o_shift = 3 * sz.wide - o_at

    def grads(i, carry):
        lanes = pl.ds(pl.multiple_of(i * span, 128), span)
        stacked = stack_ref[...].reshape(sz.keys, sz.qkvp)
        dqkv = dot(by_unit(sz, n1_ref[:, :, :, lanes]), stacked, (0, 0))
        mixed = mixed_ref[...].reshape(sz.keys, sz.headp)
        dout = dot(by_unit(sz, gather.buf[:, :, :, lanes]), mixed, (0, 0))
        if o_shift:
            dout = pltpu.roll(dout, o_shift, 1)
        total = jnp.pad(dqkv, ((0, 0), (0, sz.attnp - sz.qkvp))) + jnp.pad(
            dout, ((0, 0), (o_at, sz.attnp - o_at - sz.headp))
        )
        dw_ref[lanes, 0:sz.attnp] = total.astype(bf16)
        return carry

    lax.fori_loop(0, sz.d // span, grads, 0)
    jobs.run("grads")
    return scatter.finish()


def backward_kernel(sz, *refs):
    n = sz.layers
    aligned = sz.wrowsp == sz.wrows
    saved = [refs[l * 11:(l + 1) * 11] for l in range(n)]
    wattn_ins, wff_ins, (cot_ref, gain_ref), outs, scratch = split_refs(
        refs[11 * n:], n, n, 2, 2 * n + 2, len(refs) - 11 * n - 2 * n - 2 - 2 * n - 2)
    attn_outs, ff_outs, (whole_ref, small_ref) = split_refs(outs, n, n, 2)
    (stream_ref, middle_ref, n1_ref, n2_ref, q_ref, k_ref, v_ref, mixed_ref, pre_ref, hidden_ref, valid_ref, out_ref,
     wattn_ref, wff_ref, gl_ref, ml_ref, pg_ref, o_ref, dk_ref, dv_ref, stack_ref, dwattn_ref, dwff_ref, got_attn,
     got_ff, dqv_ref, dup_ref, grad_ref, ends_ref, first, from_tp, from_ctx, from_fsdp, sum_tp, sum_ctx,
     lsems, wsems, esems, ysems, tsems), team, padded = split_refs(scratch, 40, 8, 0 if aligned else 2)
    bufs, (gsems, ssems) = team[:6], team[6:]
    pc = Place(sz)
    greeting = Greeting(team_peers(pc) + weight_peers(pc, True) + line_peers(pc))
    copies = Copies(lsems)
    into = [stream_ref, middle_ref, n1_ref, n2_ref, q_ref, k_ref, v_ref, mixed_ref, pre_ref, hidden_ref]
    loads = [None] * n

    def load(l, kinds):
        return [copies.start(saved[l][kind], into[kind].at[l]) for kind in kinds]

    ff_loads, attn_loads = [None] * n, [None] * n
    out_load = copies.start(saved[0][10], out_ref)
    for l in reversed(range(n)):
        ff_loads[l] = [copies.start(wff_ins[l], wff_ref.at[l])] + load(l, (8, 3, 9, 1))
        attn_loads[l] = [copies.start(wattn_ins[l], wattn_ref.at[l])] + load(l, (4, 5, 6, 7, 2, 0))
        if l == n - 1:
            attn_loads[l].append(copies.start(saved[l][10], valid_ref))
    give_attn = [Give(pc, dwattn_ref if aligned else padded[0], attn_outs[l], got_attn.at[l], wsems.at[2 * l])
                 for l in range(n)]
    give_ff = [Give(pc, dwff_ref if aligned else padded[1], ff_outs[l], got_ff.at[l], wsems.at[2 * l + 1])
               for l in range(n)]

    def begin(give, dw, kind):
        def run():
            if not aligned:
                add_padding(sz, dw, padded[kind])
            give.start()

        return run

    def swap(kind, step):
        zh = (pc.zh + step) % sz.images
        return send(ends_ref.at[kind, zh], whole_ref.at[kind, pc.t, pc.zh], esems.at[kind, 0, step],
                    esems.at[kind, 1, step], (pc.f, zh * sz.zl + pc.zl, pc.t))

    def own_end(kind):
        return pltpu.make_async_copy(ends_ref.at[kind, pc.zh], whole_ref.at[kind, pc.t, pc.zh], esems.at[kind, 0, 0])

    def spread(kind, step):
        return send(whole_ref.at[kind, pc.t], whole_ref.at[kind, pc.t], ysems.at[kind, 0, step],
                    ysems.at[kind, 1, step], (pc.f, pc.c, (pc.t + step) % sz.tp))

    def spread_from(kind, step):
        back = (pc.t + sz.tp - step) % sz.tp
        return send(whole_ref.at[kind, back], whole_ref.at[kind, back], ysems.at[kind, 0, step],
                    ysems.at[kind, 1, step], (pc.f, pc.c, back))

    def swap_start(kind):
        own_end(kind).start()
        for step in range(1, sz.images):
            swap(kind, step).start()

    def spread_start(kind):
        own_end(kind).wait()
        for step in range(1, sz.images):
            swap(kind, step).wait()
        for step in range(1, sz.tp):
            spread(kind, step).start()

    def spread_wait(kind):
        for step in range(1, sz.tp):
            spread_from(kind, step).wait_recv()
            spread(kind, step).wait_send()

    def over_tp(step):
        return send(first, from_tp.at[step - 1], tsems.at[0, 0, step], tsems.at[0, 1, step],
                    (pc.f, pc.c, (pc.t + step) % sz.tp))

    def over_ctx(step):
        return send(sum_tp, from_ctx.at[step - 1], tsems.at[1, 0, step], tsems.at[1, 1, step],
                    (pc.f, pc.ctx_ahead(step), pc.t))

    def over_fsdp(step):
        return send(sum_ctx, from_fsdp.at[step - 1], tsems.at[2, 0, step], tsems.at[2, 1, step],
                    ((pc.f + step) % sz.fsdp, pc.c, pc.t))

    sum_tp[...] = jnp.zeros_like(sum_tp)
    first[...] = jnp.zeros_like(first)
    out_load.wait()
    ends_ref[0] = out_ref[...].reshape(sz.images, sz.part, sz.d).astype(bf16)
    grad_ref[...] = cot_ref[...]
    gathers = [Gather(pc, (gl_ref, ml_ref)[i % 2], gsems.at[i], FF_TURN if i % 2 == 0 else ()) for i in range(2 * n)]
    scatters = [Scatter(pc, bufs, ssems.at[i], i % 2 == 1) for i in range(2 * n)]
    greeting.wait()
    for turn in range(n):
        l = n - 1 - turn
        start = turn == 0
        low = grad_ref[...].astype(bf16)
        gathers[2 * turn].put(low)
        gathers[2 * turn].start()
        if start:
            swap_start(0)
        first[l, 5:6, :] = jnp.sum(low.astype(f32), axis=0, keepdims=True)
        for copy in ff_loads[l]:
            copy.wait()
        if start:
            jobs = Jobs(feed={4: [lambda: spread_start(0)]}, grads=[begin(give_ff[l], dwff_ref, 1)])
        else:
            after = give_attn[l + 1]
            jobs = Jobs(
                feed={1: [after.pass_early], 3: [after.part(2)], 5: [after.part(1)], 6: [after.part(0)]},
                flush=[give_ff[l + 1].finish],
                grads=[begin(give_ff[l], dwff_ref, 1)],
            )
        second = ff_backward(pc, jobs, gathers[2 * turn], wff_ref.at[l], n2_ref.at[l], pre_ref.at[l],
                             hidden_ref.at[l], dup_ref, pg_ref, dwff_ref, scatters[2 * turn])
        sum_tp[n + pc.zl, 3 * l + 2:3 * l + 3, 0:sz.ffp] = dup_ref[...]
        term, dgain, dshift = norm_back(middle_ref[l], gain_ref[l, 1:2, :], second)
        first[l, 1:2, :] = dgain
        first[l, 3:4, :] = dshift
        grad_ref[...] += term
        low = grad_ref[...].astype(bf16)
        gathers[2 * turn + 1].put(low)
        gathers[2 * turn + 1].start()
        first[l, 4:5, :] = jnp.sum(low.astype(f32), axis=0, keepdims=True)
        for copy in attn_loads[l]:
            copy.wait()
        if start:
            spread_wait(0)
        now = give_ff[l]
        jobs = Jobs(
            attend={2: [now.pass_early], 3: [now.part(2)], 5: [now.part(1)], 6: [now.part(0)]},
            flush=([] if start else [give_attn[l + 1].finish]),
            grads=[begin(give_attn[l], dwattn_ref, 0)],
        )
        below = attn_backward(pc, jobs, gathers[2 * turn + 1], wattn_ref.at[l], n1_ref.at[l], q_ref.at[l],
                              k_ref.at[l], v_ref.at[l], mixed_ref.at[l], valid_ref, dqv_ref, o_ref, dk_ref, dv_ref,
                              stack_ref, dwattn_ref, scatters[2 * turn + 1])
        sum_tp[n + pc.zl, 3 * l:3 * l + 2, 0:sz.headp] = dqv_ref[...]
        term, dgain, dshift = norm_back(stream_ref[l], gain_ref[l, 0:1, :], below)
        first[l, 0:1, :] = dgain
        first[l, 2:3, :] = dshift
        grad_ref[...] += term
    last = give_attn[0]
    ends_ref[1] = grad_ref[...].reshape(sz.images, sz.part, sz.d).astype(bf16)
    swap_start(1)
    for step in range(1, sz.tp):
        over_tp(step).start()
    last.pass_early()
    spread_start(1)
    last.pass_on(2)
    value = first[...]
    for step in range(1, sz.tp):
        over_tp(step).wait()
        value = value + from_tp[step - 1]
    sum_tp[0:n] = value
    for step in range(1, sz.ctx):
        over_ctx(step).start()
    last.pass_on(1)
    value = sum_tp[...]
    for step in range(1, sz.ctx):
        over_ctx(step).wait()
        value = value + from_ctx[step - 1]
    sum_ctx[...] = value
    for step in range(1, sz.fsdp):
        over_fsdp(step).start()
    last.pass_on(0)
    value = sum_ctx[...]
    for step in range(1, sz.fsdp):
        over_fsdp(step).wait()
        value = value + from_fsdp[step - 1]
    small_ref[...] = value
    give_ff[0].finish()
    spread_wait(1)
    last.finish()


def backward_call(sz, saved, wattn, wff, cot, gains):
    n = sz.layers
    own, team = (sz.block, sz.d), (sz.team, sz.images, sz.part, sz.d)
    head, hidden = (sz.units, sz.tile, sz.headp), (sz.units, sz.tile, sz.ffp)
    deep = up_to(max(6, 3 * n), 8)
    small = (n + sz.zl, deep, sz.d)
    ends = (sz.images, sz.part, sz.d)
    attn_sum, ff_sum = (sz.ctx, sz.wrowsp, sz.attnp), (sz.ctx, sz.wrowsp, sz.ffw)
    shapes = [(attn_sum, bf16)] * n + [(ff_sum, bf16)] * n + [((2, sz.tp) + ends, bf16), (small, f32)]
    vmem, hbm = pl.BlockSpec(memory_space=pltpu.VMEM), pl.BlockSpec(memory_space=pl.ANY)
    far, jumps = max(sz.tp, sz.ctx, sz.fsdp), max(sz.fsdp - 1, 1)
    scratch = [
        VMEM((n,) + own, f32), VMEM((n,) + own, f32), VMEM((n,) + team, bf16), VMEM((n,) + team, bf16),
        *[VMEM((n,) + head, bf16) for _ in range(4)], VMEM((n,) + hidden, f32), VMEM((n,) + hidden, bf16),
        VMEM((1, sz.keys), f32), VMEM(own, f32),
        VMEM((n, sz.d, sz.attnp), bf16), VMEM((n, sz.d, sz.ffw), bf16),
        VMEM(team, bf16), VMEM(team, bf16), VMEM(hidden, bf16), VMEM((sz.d, sz.headp), bf16),
        VMEM((sz.keys, sz.headp), f32), VMEM((sz.keys, sz.headp), f32), VMEM((sz.units, sz.tile, sz.qkvp), bf16),
        VMEM((sz.d, sz.attnp), bf16), VMEM((sz.d, sz.ffw), bf16),
        VMEM((n, jumps) + attn_sum, bf16), VMEM((n, jumps) + ff_sum, bf16),
        VMEM((2, sz.headp), f32), VMEM((1, sz.ffp), f32), VMEM(own, f32), VMEM((2,) + ends, bf16),
        VMEM((n, deep, sz.d), f32), VMEM((sz.tp - 1, n, deep, sz.d), f32),
        VMEM((max(sz.ctx - 1, 1),) + small, f32), VMEM((jumps,) + small, f32), VMEM(small, f32), VMEM(small, f32),
        DMA((12 * n + 2,)), DMA((2 * n, sz.fsdp, 2, sz.ctx)), DMA((2, 2, sz.images)), DMA((2, 2, sz.tp)),
        DMA((3, 2, far)),
    ] + team_scratch(sz, 2 * n)
    if sz.wrowsp != sz.wrows:
        padded = sz.groups * sz.wrowsp
        scratch += [VMEM((padded, sz.attnp), bf16), VMEM((padded, sz.ffw), bf16)]
    operands = (*saved, *wattn, *wff, cot, gains)
    return pl.pallas_call(
        functools.partial(backward_kernel, sz),
        out_shape=[jax.ShapeDtypeStruct(*s) for s in shapes],
        in_specs=[hbm] * (len(operands) - 2) + [vmem] * 2,
        out_specs=[hbm] * (2 * n + 1) + [vmem],
        scratch_shapes=scratch,
        compiler_params=params(2),
        name="backward",
    )(*operands)


def close_kernel(sz, *refs):
    n = sz.layers
    attn_refs, ff_refs, (whole_ref, small_ref), outs = split_refs(refs, n, n, 2, 11)
    out_ref, gin_ref, gain_ref, bias_ref, qkv_ref, qv_ref, wout_ref, up_ref, upb_ref, down_ref, resid_ref = outs
    full, ff = sz.wide * sz.zl, sz.ff * sz.zl

    def summed(ref):
        return [sum(ref[zh * sz.zl + j].astype(f32) for zh in range(sz.images)) for j in range(sz.zl)]

    def join(halves, start, count, width):
        total = None
        for j, values in enumerate(halves):
            piece = shift_lanes(values, start, count, j * count, up_to(width, 128))
            total = piece if total is None else total + piece
        return total[0:sz.wrows, 0:width]

    for layer in range(n):
        halves = summed(attn_refs[layer])
        for kind in range(3):
            at = kind * full
            qkv_ref[layer, :, at:at + full] = join(halves, kind * sz.wide, sz.wide, full)
        wout_ref[layer] = join(halves, 3 * sz.wide, sz.wide, full)
        halves = summed(ff_refs[layer])
        up_ref[layer] = join(halves, 0, sz.ff, ff)
        down_ref[layer] = join(halves, sz.ff, sz.ff, ff)
        values = small_ref[layer]
        gain_ref[layer] = values[0:2]
        bias_ref[layer] = values[2:4]
        resid_ref[layer] = values[4:6]
        total_qv, total_up = None, None
        for half in range(sz.zl):
            values = small_ref[n + half]
            qv = shift_lanes(values, 0, sz.wide, half * sz.wide, up_to(full, 128))
            up = shift_lanes(values, 0, sz.ff, half * sz.ff, up_to(ff, 128))
            total_qv = qv if total_qv is None else total_qv + qv
            total_up = up if total_up is None else total_up + up
        qv_ref[layer] = total_qv[3 * layer:3 * layer + 2, 0:full]
        upb_ref[layer:layer + 1, :] = total_up[3 * layer + 2:3 * layer + 3, 0:ff]
    for image in range(sz.images):
        rows = whole_ref[0, :, image].reshape(sz.tp * sz.part, sz.d)
        out_ref[image] = rows[0:sz.rows]
        rows = whole_ref[1, :, image].reshape(sz.tp * sz.part, sz.d)
        gin_ref[image] = rows.astype(f32)[0:sz.rows]


def close_call(sz, attn_sums, ff_sums, ends, small):
    n, full, ff = sz.layers, sz.wide * sz.zl, sz.ff * sz.zl
    tokens = (sz.images, sz.rows, sz.d)
    vec, up = ((n, 2, sz.d), f32), ((n, sz.wrows, ff), f32)
    shapes = [
        (tokens, bf16), (tokens, f32), vec, vec, ((n, sz.wrows, 3 * full), f32), ((n, 2, full), f32),
        ((n, sz.wrows, full), f32), up, ((n, ff), f32), up, vec,
    ]
    vmem = pl.BlockSpec(memory_space=pltpu.VMEM)
    results = pl.pallas_call(
        functools.partial(close_kernel, sz),
        out_shape=[jax.ShapeDtypeStruct(*s) for s in shapes],
        in_specs=[vmem] * (2 * n + 2),
        out_specs=[vmem] * len(shapes),
        compiler_params=pltpu.CompilerParams(vmem_limit_bytes=60 * 1024 * 1024),
        name="close",
    )(*attn_sums, *ff_sums, ends, small)
    results = list(results)
    results[4] = results[4].reshape(n, sz.wrows, 3, full)
    return tuple(results)


def per_device(mesh, inputs, cotangent, valid_count, norm_gain, norm_bias, w_qkv, bias_qv, w_out, w_up, bias_up,
               w_down, bias_resid):
    sz = Sizes(mesh, inputs, w_qkv, w_up)
    n = sz.layers
    *made, cot = forward_call(sz, valid_count, inputs, cotangent, w_qkv.reshape(n, sz.wrows, -1), w_out, w_up,
                              w_down, norm_gain, norm_bias, bias_qv, bias_up, bias_resid)
    saved, wattn, wff = split_refs(made, 11 * n, n, n)
    *sums, ends, small = backward_call(sz, saved, wattn, wff, cot, norm_gain)
    return close_call(sz, sums[:n], sums[n:], ends, small)


def solution(mesh):
    tokens, rows = P("fsdp", "ctx", None), P(None, ("fsdp", "ctx"), "tp")
    qkv = P(None, ("fsdp", "ctx"), None, "tp")
    qv, up = P(None, None, "tp"), P(None, "tp")
    return jax.shard_map(
        functools.partial(per_device, mesh),
        mesh=mesh,
        in_specs=(tokens, tokens, P("fsdp"), P(), P(), qkv, qv, rows, rows, up, rows, P()),
        out_specs=(tokens, tokens, P(), P(), qkv, qv, rows, rows, up, rows, P()),
        check_vma=False,
    )
```

```python
import functools

import jax
import jax.numpy as jnp
from jax import lax
from jax.experimental import pallas as pl
from jax.experimental.pallas import tpu as pltpu
from jax.sharding import PartitionSpec as P

HEAD_DIM = 72
norm_eps = 1e-06
gelu_root = 0.7978845608028654
gelu_cubic = 0.044715
masked_score = -1e30
LOG2_E = 1.4426950408889634

MESH = pl.DeviceIdType.MESH
f32 = jnp.float32
bf16 = jnp.bfloat16
VMEM = pltpu.VMEM
DMA = pltpu.SemaphoreType.DMA


def up_to(value, unit):
    return (value + unit - 1) // unit * unit


def dot(a, b, over):
    return lax.dot_general(a, b, (((over[0],), (over[1],)), ((), ())), preferred_element_type=f32)


class Sizes:
    def __init__(self, mesh, inputs, w_qkv, w_up):
        self.fsdp, self.ctx, self.tp = mesh.shape["fsdp"], mesh.shape["ctx"], mesh.shape["tp"]
        self.images, self.rows, self.d = inputs.shape
        self.layers, self.wrows = w_qkv.shape[0], w_qkv.shape[1]
        self.zl = self.ctx // self.images
        self.chips_y = self.tp // 2
        self.chips = self.zl * self.chips_y
        self.team = self.chips * 2
        self.part = up_to(-(-self.rows // self.tp), 16)
        self.block = self.images * self.part
        self.units = self.chips * self.images
        self.half = self.units * self.part
        self.tile = 2 * self.part
        self.steps = self.units // 2
        self.keys = 2 * self.half
        self.wide = w_qkv.shape[3] // self.zl
        self.heads = self.wide // HEAD_DIM
        self.ff = w_up.shape[2] // self.zl
        self.headp = up_to(self.wide, 128)
        self.qkvp = up_to(3 * self.wide, 128)
        self.attnp = up_to(4 * self.wide, 128)
        self.spare = self.attnp - 4 * self.wide
        self.ff_at = 4 * self.wide % 128
        self.ff_sent = 128 if self.spare else 0
        end = self.ff_at + self.ff
        self.ffw = up_to(end + self.ff, 128)
        self.ffs = self.ffw - self.ff_sent
        self.down_at = end // 128 * 128
        self.down_shift = end - self.down_at
        self.ffp = self.ffw - self.down_at
        assert up_to(end, 128) <= self.ffp and self.spare < self.ff
        self.wrowsp = up_to(self.wrows, 16)
        self.chunk = 48 if self.wrowsp % 48 == 0 else self.wrowsp
        self.chunks = self.wrowsp // self.chunk
        self.groups = self.fsdp * self.ctx


class Place:
    def __init__(self, sz):
        self.sz = sz
        self.f, self.c, self.t = lax.axis_index("fsdp"), lax.axis_index("ctx"), lax.axis_index("tp")
        self.zh, self.zl = self.c // sz.zl, self.c % sz.zl
        self.y, self.k = self.t // 2, self.t % 2
        self.chip = self.zl * sz.chips_y + self.y
        self.slot = 2 * self.chip + self.k

    def chip_at(self, step):
        sz = self.sz
        zl = (self.zl + step // sz.chips_y) % sz.zl
        y = (self.y + step % sz.chips_y) % sz.chips_y
        return zl, y

    def chip_back(self, step):
        sz = self.sz
        zl = (self.zl + sz.zl - step // sz.chips_y) % sz.zl
        y = (self.y + sz.chips_y - step % sz.chips_y) % sz.chips_y
        return zl, y

    def index(self, chip):
        return chip[0] * self.sz.chips_y + chip[1]

    def device(self, chip):
        return (self.f, self.zh * self.sz.zl + chip[0], 2 * chip[1] + self.k)

    @property
    def twin(self):
        return (self.f, self.c, self.t + 1 - 2 * self.k)


    def ctx_ahead(self, step):
        sz = self.sz
        return (self.zh + step // sz.zl) % sz.images * sz.zl + (self.zl + step % sz.zl) % sz.zl

    def ctx_back(self, step):
        sz = self.sz
        zh = (self.zh + sz.images - step // sz.zl) % sz.images
        return zh * sz.zl + (self.zl + sz.zl - step % sz.zl) % sz.zl


def split_refs(refs, *counts):
    out, at = [], 0
    for count in counts:
        out.append(refs[at:at + count])
        at += count
    assert at == len(refs)
    return out


class Greeting:
    def __init__(self, others):
        self.count = len(others)
        self.barrier = pltpu.get_barrier_semaphore()
        for other in others:
            pl.semaphore_signal(self.barrier, inc=1, device_id=other, device_id_type=MESH)

    def wait(self):
        pl.semaphore_wait(self.barrier, self.count)


def send(src, dst, send_sem, recv_sem, device):
    return pltpu.make_async_remote_copy(
        src_ref=src, dst_ref=dst, send_sem=send_sem, recv_sem=recv_sem, device_id=device, device_id_type=MESH
    )


def team_peers(pc):
    return [pc.device(pc.chip_at(step)) for step in range(1, pc.sz.chips)] + [pc.twin]


def line_peers(pc):
    sz = pc.sz
    return [(pc.f, pc.c, 2 * ((pc.y + dy) % sz.chips_y) + 1 - pc.k) for dy in range(1, sz.chips_y)]


def weight_peers(pc, team=False):
    sz = pc.sz
    first = sz.zl if team else 1
    return [(pc.f, pc.ctx_ahead(step), pc.t) for step in range(first, sz.ctx)] + [
        ((pc.f + jump) % sz.fsdp, pc.c, pc.t) for jump in range(1, sz.fsdp)
    ]


def pick(step, values):
    if isinstance(step, int):
        return values[step]
    out = jnp.int32(values[0])
    for i in range(1, len(values)):
        out = jnp.where(step == i, jnp.int32(values[i]), out)
    return out


def when(condition, run):
    if isinstance(condition, (bool, int)):
        if condition:
            run()
    else:
        pl.when(condition)(run)


FF_OVER = 3

FORWARD_TURN = (False, True)
BACKWARD_TURN = (True, False)
SUM_TURN = (True, True)


class Routes:
    def __init__(self, sz):
        self.sz = sz
        self.z = [dz * sz.chips_y for dz in range(1, sz.zl)]
        self.y = list(range(1, sz.chips_y))
        self.turned = [dz + dy for dz in self.z for dy in self.y]
        self.arriving = [0] + self.z + self.y + self.turned
        self.leaving = self.turned + self.y + self.z + [0]

    def at(self, order, step):
        per = len(order) // 2
        firsts, seconds = order[0::2] * self.sz.images, order[1::2] * self.sz.images
        pieces = [p for p in range(self.sz.images) for _ in range(per)]
        return pick(step, firsts), pick(step, seconds), pick(step, pieces)


class Gather:
    def __init__(self, pc, buf, sems, turn):
        self.pc, self.buf, self.sems, self.turn = pc, buf, sems, turn
        self.routes = Routes(pc.sz)

    def move(self, back, piece, at, device):
        return send(self.buf.at[at, piece], self.buf.at[at, piece], self.sems.at[0, back, piece],
                    self.sems.at[1, back, piece], device)

    def start(self, piece, low):
        pc, routes = self.pc, self.routes
        self.buf[pc.chip, piece] = low
        for step in routes.z + routes.y + ([] if self.turn else routes.turned):
            self.move(step, piece, pc.chip, pc.device(pc.chip_at(step))).start()

    def ready(self, step):
        pc, sz = self.pc, self.pc.sz
        *chips, piece = self.routes.at(self.routes.arriving, step)
        places = []
        for back in chips:
            at = pc.index(pc.chip_back(back))
            when(back > 0, self.move(back, piece, at, pc.twin).wait_recv)
            if self.turn:
                for dz in self.routes.z:

                    def pass_on(dz=dz, at=at):
                        for dy in self.routes.y:
                            self.move(dz + dy, piece, at, pc.device(pc.chip_at(dy))).start()

                    when(back == dz, pass_on)
            places.append(at)
        tokens = jnp.concatenate([self.buf[at, piece] for at in places], axis=0)
        return [piece * sz.chips + at for at in places], tokens

    def finish(self):
        for piece in range(self.pc.sz.images):
            for back in self.routes.arriving[1:]:
                self.move(back, piece, self.pc.chip, self.pc.twin).wait_send()


class Scatter:
    def __init__(self, pc, bufs, sems, own_last, turn):
        self.pc, self.sems, self.turn = pc, sems, turn
        self.keep, self.hold, self.sent, self.got = bufs
        self.routes = Routes(pc.sz)
        self.order = self.routes.leaving if own_last else self.routes.arriving

    def far(self, back, piece):
        pc, sz = self.pc, self.pc.sz
        to = back
        if self.turn:
            if isinstance(back, int):
                to = back % sz.chips_y or back
            else:
                dy = lax.rem(back, jnp.int32(sz.chips_y))
                to = jnp.where(dy > 0, dy, back)
        return send(self.sent.at[back, piece], self.got.at[back, piece], self.sems.at[0, back, piece],
                    self.sems.at[1, back, piece], pc.device(pc.chip_back(to)))

    def units(self, step):
        pc = self.pc
        *chips, piece = self.routes.at(self.order, step)
        return [piece * pc.sz.chips + pc.index(pc.chip_back(back)) for back in chips]

    def push(self, step, partial):
        sz, part = self.pc.sz, self.pc.sz.part
        *chips, piece = self.routes.at(self.order, step)
        for i, back in enumerate(chips):
            terms = partial[i * part:(i + 1) * part]

            def own(terms=terms):
                self.keep[piece] = terms

            def leave(terms=terms, back=back):
                self.sent[back, piece] = terms.astype(bf16)
                self.far(back, piece).start()

            def hold(terms=terms, dz=None):
                self.hold[dz // sz.chips_y - 1] = terms

            when(back == 0, own)
            held = back < 0
            if self.turn:
                for dz in self.routes.z:
                    when(back == dz, functools.partial(hold, dz=dz))
                    held = held | (back == dz)
            when((back > 0) & jnp.logical_not(held), leave)
        if self.turn:
            per = sz.chips // 2
            for p in range(1, sz.images):
                when(step == p * per, functools.partial(self.merge, p - 1))

    def merge(self, piece):
        sz = self.pc.sz
        for dz in self.routes.z:
            total = self.hold[dz // sz.chips_y - 1]
            for dy in self.routes.y:
                self.far(dz + dy, piece).wait_recv()
                total = total + self.got[dz + dy, piece].astype(f32)
            self.sent[dz, piece] = total.astype(bf16)
            self.far(dz, piece).start()

    def flush(self):
        if self.turn:
            self.merge(self.pc.sz.images - 1)

    def finish(self, piece):
        total = self.keep[piece]
        for back in self.routes.z + self.routes.y + ([] if self.turn else self.routes.turned):
            self.far(back, piece).wait_recv()
            total = total + self.got[back, piece].astype(f32)
        for back in self.routes.arriving[1:]:
            self.far(back, piece).wait_send()
        return total


class Swap:
    def __init__(self, pc, src, dst, send_sem, recv_sem):
        self.copy = send(src, dst, send_sem, recv_sem, pc.twin)

    def start(self):
        self.copy.start()

    def wait(self):
        self.copy.wait()


def team_scratch(sz, phases):
    n = (sz.chips, sz.images)
    return [
        VMEM((sz.images, sz.part, sz.d), f32),
        VMEM((max(sz.zl - 1, 1), sz.part, sz.d), f32),
        VMEM(n + (sz.part, sz.d), bf16),
        VMEM(n + (sz.part, sz.d), bf16),
        DMA((phases, 2) + n),
        DMA((phases, 2) + n),
    ]


def normalised(values):
    centre = jnp.mean(values, axis=-1, keepdims=True)
    centred = values - centre
    spread = jnp.mean(centred * centred, axis=-1, keepdims=True)
    inverse = lax.rsqrt(spread + norm_eps)
    return centred * inverse, inverse


def norm_back(values, gain, grad):
    high, inverse = normalised(values)
    scaled = grad * gain
    term = inverse * (
        scaled
        - jnp.mean(scaled, axis=-1, keepdims=True)
        - high * jnp.mean(scaled * high, axis=-1, keepdims=True)
    )
    return term, jnp.sum(grad * high, axis=0, keepdims=True), jnp.sum(grad, axis=0, keepdims=True)


def lanes_of(shape):
    return lax.broadcasted_iota(jnp.int32, shape, len(shape) - 1)


def unpack_out(sz, w_ref, o_ref):
    at = 3 * sz.wide // 128 * 128
    shift = 3 * sz.wide - at

    def step(i, carry):
        rows = pl.ds(pl.multiple_of(i * 128, 128), 128)
        piece = pltpu.roll(w_ref[rows, at:at + sz.headp].astype(f32), sz.headp - shift, 1)
        o_ref[rows, :] = jnp.where(lanes_of(piece.shape) < sz.wide, piece, 0.0).astype(bf16)
        return carry

    lax.fori_loop(0, sz.d // 128, step, 0)


def take(sz, values, kind):
    at = kind * sz.wide // 128 * 128
    shift = kind * sz.wide - at
    piece = values[:, at:at + sz.headp]
    if shift:
        piece = pltpu.roll(piece, sz.headp - shift, 1)
    return jnp.where(lanes_of(piece.shape) < sz.wide, piece, 0.0)


def head_of(values, head):
    lanes = lanes_of(values.shape)
    mine = (lanes >= head * HEAD_DIM) & (lanes < (head + 1) * HEAD_DIM)
    return jnp.where(mine, values, jnp.zeros_like(values))


def probabilities(q_head, keys, valid):
    scores = jnp.where(valid > 0.0, dot(q_head, keys, (1, 1)), masked_score)
    high = jnp.max(scores, axis=-1, keepdims=True)
    weights = jnp.exp2((scores - high) * (HEAD_DIM ** (-0.5) * LOG2_E))
    return weights * (1.0 / jnp.sum(weights, axis=-1, keepdims=True))


class Jobs:
    def __init__(self, **places):
        self.places = places

    def run(self, place):
        for job in self.places.get(place, ()):
            job()

    def at(self, place, step):
        for when_step, jobs in self.places.get(place, {}).items():

            def run(jobs=jobs):
                for job in jobs:
                    job()

            when(step == when_step, run)


class Copies:
    def __init__(self, sems):
        self.sems, self.made = sems, []

    def start(self, src, dst):
        ident = len(self.made)
        self.made.append((src, dst))
        pltpu.make_async_copy(src, dst, self.sems.at[ident]).start()
        return ident

    def wait(self, idents=None):
        for ident in range(len(self.made)) if idents is None else idents:
            src, dst = self.made[ident]
            pltpu.make_async_copy(src, dst, self.sems.at[ident]).wait()


class Fetch:
    def __init__(self, pc, own, everything, sems, twin_sems, first=0):
        self.lanes = pl.ds(first, own.shape[-1])
        self.pc, self.own, self.all, self.sems, self.twin_sems = pc, own, everything, sems, twin_sems

    def rows(self, group, chunk):
        sz = self.pc.sz
        at = group * sz.wrowsp + chunk * sz.chunk
        return self.all.at[self.pc.k, pl.ds(pl.multiple_of(at, 16), sz.chunk), self.lanes]

    def own_rows(self, half, chunk):
        return self.own.at[half, pl.ds(chunk * self.pc.sz.chunk, self.pc.sz.chunk)]

    def along_ctx(self, step, chunk):
        pc = self.pc
        c = pc.ctx_ahead(step)
        return send(self.own_rows(c % pc.sz.zl, chunk), self.rows(pc.f * pc.sz.ctx + pc.c, chunk),
                    self.sems.at[chunk, 0, 0, step], self.sems.at[chunk, 0, 1, step], (pc.f, c, pc.t))

    def own_copy(self, chunk):
        pc = self.pc
        return pltpu.make_async_copy(self.own_rows(pc.zl, chunk), self.rows(pc.f * pc.sz.ctx + pc.c, chunk),
                                     self.sems.at[chunk, 0, 0, 0])

    def along_fsdp(self, jump, step, chunk):
        pc, sz = self.pc, self.pc.sz
        rows = self.rows(pc.f * sz.ctx + pc.ctx_back(step), chunk)
        return send(rows, rows, self.sems.at[chunk, jump, 0, step], self.sems.at[chunk, jump, 1, step],
                    ((pc.f + jump) % sz.fsdp, pc.c, pc.t))

    def to_twin(self, jump, step, chunk):
        pc, sz = self.pc, self.pc.sz
        rows = self.rows((pc.f + sz.fsdp - jump) % sz.fsdp * sz.ctx + pc.ctx_back(step), chunk)
        return send(rows, rows, self.twin_sems.at[chunk, jump, 0, step], self.twin_sems.at[chunk, jump, 1, step],
                    pc.twin)

    def depart(self, chunk):
        if chunk < self.pc.sz.chunks:
            self.own_copy(chunk).start()
            for step in range(self.pc.sz.ctx - 1, 0, -1):
                self.along_ctx(step, chunk).start()

    def turn(self, chunk):
        if chunk < self.pc.sz.chunks:
            for step in range(self.pc.sz.ctx):
                self.along_ctx(step, chunk).wait_recv() if step else self.own_copy(chunk).wait()
                for jump in range(1, self.pc.sz.fsdp):
                    self.along_fsdp(jump, step, chunk).start()
                self.to_twin(0, step, chunk).start()

    def land(self, chunk):
        if chunk < self.pc.sz.chunks:
            for step in range(self.pc.sz.ctx):
                for jump in range(1, self.pc.sz.fsdp):
                    self.along_fsdp(jump, step, chunk).wait_recv()
                    self.to_twin(jump, step, chunk).start()

    def jobs(self, parts):
        calls = {"d": self.depart, "t": self.turn, "l": self.land}
        return [functools.partial(calls[part[0]], int(part[1])) for part in parts.split()]

    def run(self, parts):
        for job in self.jobs(parts):
            job()

    def finish(self):
        sz = self.pc.sz
        for chunk in range(sz.chunks):
            for step in range(sz.ctx):
                if step:
                    self.along_ctx(step, chunk).wait_send()
                for jump in range(sz.fsdp):
                    if jump:
                        self.along_fsdp(jump, step, chunk).wait_send()
                    self.to_twin(jump, step, chunk).wait()


class Give:
    def __init__(self, pc, dw, recv, got, sems, first=0):
        self.lanes = pl.ds(first, recv.shape[-1])
        self.pc, self.dw, self.recv, self.got, self.sems = pc, dw, recv, got, sems
        self.order = list(range(pc.sz.ctx - 1, -1, -1))

    def rows(self, group, chunk):
        sz = self.pc.sz
        return pl.ds(pl.multiple_of(group * sz.wrowsp + chunk * sz.chunk, 16), sz.chunk)

    def part(self, chunk):
        return pl.ds(chunk * self.pc.sz.chunk, self.pc.sz.chunk)

    def along_fsdp(self, jump, step, chunk):
        pc, sz = self.pc, self.pc.sz
        f = (pc.f + jump) % sz.fsdp
        return send(self.dw.at[self.rows(f * sz.ctx + pc.ctx_ahead(step), chunk), self.lanes],
                    self.got.at[jump - 1, step, self.part(chunk)],
                    self.sems.at[chunk, jump, 0, step], self.sems.at[chunk, jump, 1, step], (f, pc.c, pc.t))

    def along_ctx(self, step, chunk, back=False):
        pc = self.pc
        there = pc.ctx_back(step) if back else pc.ctx_ahead(step)
        return send(self.got.at[0, step, self.part(chunk)],
                    self.recv.at[pc.ctx_back(step) if back else pc.c, self.part(chunk)],
                    self.sems.at[chunk, 0, 0, step], self.sems.at[chunk, 0, 1, step], (pc.f, there, pc.t))

    def own_copy(self, chunk):
        return pltpu.make_async_copy(self.got.at[0, 0, self.part(chunk)], self.recv.at[self.pc.c, self.part(chunk)],
                                     self.sems.at[chunk, 0, 0, 0])

    def depart(self, chunk):
        if chunk < self.pc.sz.chunks:
            for step in self.order:
                for jump in range(1, self.pc.sz.fsdp):
                    self.along_fsdp(jump, step, chunk).start()

    def turn(self, chunk):
        pc, sz = self.pc, self.pc.sz
        if chunk >= sz.chunks:
            return
        for step in self.order:
            for jump in range(1, sz.fsdp):
                self.along_fsdp(jump, step, chunk).wait_recv()
            total = self.dw[self.rows(pc.f * sz.ctx + pc.ctx_ahead(step), chunk), self.lanes].astype(f32)
            for jump in range(1, sz.fsdp):
                total = total + self.got[jump - 1, step, self.part(chunk)].astype(f32)
            self.got[0, step, self.part(chunk)] = total.astype(bf16)
            self.along_ctx(step, chunk).start() if step else self.own_copy(chunk).start()

    def jobs(self, parts):
        calls = {"d": self.depart, "t": self.turn}
        return [functools.partial(calls[part[0]], int(part[1])) for part in parts.split()]

    def run(self, parts):
        for job in self.jobs(parts):
            job()

    def finish(self):
        sz = self.pc.sz
        for chunk in range(sz.chunks):
            self.own_copy(chunk).wait()
            for step in range(sz.ctx):
                if step:
                    self.along_ctx(step, chunk, True).wait_recv()
                    self.along_ctx(step, chunk).wait_send()
                for jump in range(1, sz.fsdp):
                    self.along_fsdp(jump, step, chunk).wait_send()


def chosen(sz, group, lanes_shape):
    row = lax.broadcasted_iota(jnp.int32, lanes_shape, 0)
    col = lax.broadcasted_iota(jnp.int32, lanes_shape, 1)
    return jnp.where((row - group * sz.wrows == col) & (col < sz.wrows), 1.0, 0.0).astype(bf16)


def drop_padding(sz, src, dst):
    for at in range(0, dst.shape[-1], 128):
        lanes = slice(at, at + 128)

        def step(group, total):
            rows = pl.ds(pl.multiple_of(group * sz.wrowsp, 16), sz.wrowsp)
            return total + dot(chosen(sz, group, (sz.d, sz.wrowsp)), src[rows, lanes], (1, 0))

        dst[:, lanes] = lax.fori_loop(0, sz.groups, step, jnp.zeros((sz.d, 128), f32)).astype(bf16)


def add_padding(sz, src, dst):
    def step(group, carry):
        rows = pl.ds(pl.multiple_of(group * sz.wrowsp, 16), sz.wrowsp)
        for at in range(0, dst.shape[-1], 128):
            lanes = slice(at, at + 128)
            dst[rows, lanes] = dot(chosen(sz, group, (sz.d, sz.wrowsp)), src[:, lanes], (0, 0)).astype(bf16)
        return carry

    lax.fori_loop(0, sz.groups, step, 0)


def by_unit(sz, values):
    return jnp.swapaxes(values, 0, 1).reshape(sz.half, values.shape[-1])


def shift_lanes(values, start, count, at, width):
    have = values.shape[-1]
    first, last = start // 128 * 128, up_to(start + count, 128)
    to = at // 128 * 128
    span = max(last - first, up_to(at + count, 128) - to)
    piece = values[:, first:min(last, have)].astype(f32)
    if piece.shape[-1] < span:
        piece = jnp.pad(piece, ((0, 0), (0, span - piece.shape[-1])))
    turn = ((at - to) - (start - first)) % span
    if turn:
        piece = pltpu.roll(piece, turn, 1)
    lanes = lanes_of(piece.shape)
    piece = jnp.where((lanes >= at - to) & (lanes < at - to + count), piece, 0.0)
    piece = piece[:, 0:min(span, width - to)]
    return jnp.pad(piece, ((0, 0), (to, width - to - piece.shape[-1])))


def half_of(pc, values, count, width, at=0):
    out = shift_lanes(values, 0, count, at, width)
    for j in range(1, pc.sz.zl):
        out = jnp.where(pc.zl == j, shift_lanes(values, j * count, count, at, width), out)
    return out


def piece_of(pc, values):
    sz = pc.sz
    values = values.astype(f32)
    over = sz.tp * sz.part - sz.rows
    if over:
        values = jnp.concatenate([values, jnp.zeros((over, sz.d), f32)], axis=0)
    out = values[0:sz.part]
    for t in range(1, sz.tp):
        out = jnp.where(pc.t == t, values[t * sz.part:(t + 1) * sz.part], out)
    return out


def steps_below(values, unit, count):
    out = jnp.zeros_like(values)
    for m in range(1, count):
        out = out + jnp.where(values >= m * unit, 1, 0)
    return out


def key_valid(pc, count):
    sz = pc.sz
    row = lax.broadcasted_iota(jnp.int32, (1, sz.keys), 1)
    core = steps_below(row, sz.half, 2)
    within = row - core * sz.half
    unit = steps_below(within, sz.part, sz.units)
    piece = steps_below(unit, sz.chips, sz.images)
    chip = unit - piece * sz.chips
    zl = steps_below(chip, sz.chips_y, sz.zl)
    t = 2 * (chip - zl * sz.chips_y) + core
    token = t * sz.part + within - unit * sz.part
    position = (piece * sz.zl + zl) * sz.rows + token
    return jnp.where((token < sz.rows) & (position < count), 1.0, 0.0)


def own_valid(pc, count):
    sz = pc.sz
    shape = (sz.images, sz.part, 1)
    piece = lax.broadcasted_iota(jnp.int32, shape, 0)
    token = pc.t * sz.part + lax.broadcasted_iota(jnp.int32, shape, 1)
    position = (piece * sz.zl + pc.zl) * sz.rows + token
    return jnp.where((token < sz.rows) & (position < count), 1.0, 0.0)


def ff_lanes(sz, values):
    lanes = lanes_of(values.shape)
    return jnp.where((lanes >= sz.ff_at) & (lanes < sz.ff_at + sz.ff), values, 0.0)


def ride(sz, src, dst, src_at, dst_at):
    def step(i, carry):
        rows = pl.ds(pl.multiple_of(i * 128, 128), 128)
        there = src[rows, src_at:src_at + 128].astype(f32)
        here = dst[rows, dst_at:dst_at + 128].astype(f32) if dst_at else jnp.zeros_like(there)
        dst[rows, dst_at:dst_at + 128] = jnp.where(lanes_of(there.shape) >= sz.ff_at, there, here).astype(bf16)
        return carry

    if sz.spare:
        lax.fori_loop(0, src.shape[0] // 128, step, 0)


def rows_of(ref, units):
    return jnp.concatenate([ref[unit] for unit in units], axis=0)


def put_rows(sz, ref, units, values):
    for i, unit in enumerate(units):
        ref[unit] = values[i * sz.part:(i + 1) * sz.part]


def attn_forward(pc, jobs, gather, w_ref, qv_ref, valid_ref, q_ref, k_ref, v_ref, mixed_ref, o_ref, kv_sems,
                 scatter):
    sz = pc.sz
    for s in range(2):
        unpack_out(sz, w_ref.at[s], o_ref.at[s])

    def project(step, carry):
        units, tokens = gather.ready(step)
        for s in range(2):
            both3 = dot(tokens, w_ref[s, :, 0:sz.qkvp], (1, 0))
            put_rows(sz, q_ref.at[s], units, (take(sz, both3, 0) + qv_ref[s, 0:1, 0:sz.headp]).astype(bf16))
            put_rows(sz, k_ref.at[s, pc.k], units, take(sz, both3, 1).astype(bf16))
            put_rows(sz, v_ref.at[s, pc.k], units, (take(sz, both3, 2) + qv_ref[s, 1:2, 0:sz.headp]).astype(bf16))
        jobs.at("project", step)
        return carry

    def swaps(piece):
        units = pl.ds(piece * sz.chips, sz.chips)
        return [Swap(pc, ref.at[s, pc.k, units], ref.at[s, pc.k, units], kv_sems.at[0, i, s, piece],
                     kv_sems.at[1, i, s, piece]) for s in range(2) for i, ref in enumerate((k_ref, v_ref))]

    per = sz.steps // sz.images
    for piece in range(sz.images):
        lax.fori_loop(piece * per, (piece + 1) * per, project, 0)
        for swap in swaps(piece):
            swap.start()
    gather.finish()
    for piece in range(sz.images):
        for swap in swaps(piece):
            swap.wait()

    def attend(step, carry):
        units = scatter.units(step)
        partial = None
        for s in range(2):
            keys = k_ref[s].reshape(sz.keys, sz.headp)
            values = v_ref[s].reshape(sz.keys, sz.headp)
            queries = rows_of(q_ref.at[s], units)
            total = jnp.zeros((sz.tile, sz.headp), f32)
            for head in range(sz.heads):
                probs = probabilities(head_of(queries, head), keys, valid_ref[...])
                total = total + dot(probs.astype(bf16), head_of(values, head), (1, 0))
            mixed = total.astype(bf16)
            put_rows(sz, mixed_ref.at[s], units, mixed)
            terms = dot(mixed, o_ref[s], (1, 1))
            partial = terms if partial is None else partial + terms
        scatter.push(step, partial)
        jobs.at("attend", step)
        return carry

    lax.fori_loop(0, sz.steps, attend, 0)
    jobs.run("turnover")
    scatter.flush()
    jobs.run("flush")


def ff_forward(pc, jobs, gather, w_ref, upb_ref, pre_ref, hidden_ref, scatter):
    sz = pc.sz

    def feed(step, carry):
        units, tokens = gather.ready(step)
        partial = None
        for s in range(2):
            pre = dot(tokens, w_ref[s, :, 0:sz.ffp], (1, 0)) + upb_ref[s, 2:3, 0:sz.ffp]
            put_rows(sz, pre_ref.at[s], units, pre)
            hidden = 0.5 * pre * (1.0 + jnp.tanh(gelu_root * (pre + gelu_cubic * pre * pre * pre)))
            hidden = ff_lanes(sz, hidden)
            if sz.down_shift != sz.ff_at:
                hidden = pltpu.roll(hidden, (sz.down_shift - sz.ff_at) % sz.ffp, 1)
            hidden = hidden.astype(bf16)
            put_rows(sz, hidden_ref.at[s], units, hidden)
            terms = dot(hidden, w_ref[s, :, sz.down_at:], (1, 1))
            partial = terms if partial is None else partial + terms
        scatter.push(step, partial)
        jobs.at("feed", step)
        return carry

    lax.fori_loop(0, sz.steps, feed, 0)
    jobs.run("flush")
    gather.finish()


def plan(steps, more_steps, flush, what, ff, attn):
    for place, ff_parts, attn_parts in what:
        jobs = (ff.jobs(ff_parts) if ff else []) + (attn.jobs(attn_parts) if attn else [])
        if place == "f":
            flush.extend(jobs)
        else:
            table = steps if place[0] == "s" else more_steps
            table[int(place[1])] = table.get(int(place[1]), []) + jobs


def planned(what, give):
    steps = {}
    plan(steps, None, None, what, give, None)
    return steps


GIVE_FF = (("s0", "", "t0"), ("s1", "", "d2 t1"), ("s3", "", "t2"))
GIVE_ATTN = (("s0", "t0", ""), ("s1", "d2", ""), ("s2", "t1", ""), ("s3", "t2", ""))
PLAN_ATTN_FIRST = (("s0", "d2", ""), ("s3", "t1", ""), ("m0", "l0", ""), ("m1", "", "d0"), ("m2", "t2 l1", ""),
                   ("m3", "", "d1"), ("f", "l2", "d2 t0"))
PLAN_ATTN = (("s1", "t1", "d0"), ("s2", "d2", ""), ("s3", "l0", ""), ("m0", "", "d1"), ("m1", "t2 l1", ""),
             ("m3", "", "d2"), ("f", "l2", "t0"))
PLAN_FF = (("s0", "d0", "t1 l0"), ("s1", "d1", "t2"), ("s2", "t0", "l1"), ("s3", "", "l2"))


def norm_low(values, gain, shift):
    high, _ = normalised(values)
    return (high * gain + shift).astype(bf16)


def forward_kernel(sz, *refs):
    n = sz.layers
    aligned = sz.wrowsp == sz.wrows
    ins, outs, scratch = refs[:12], refs[12:12 + 13 * n + 1], refs[12 + 13 * n + 1:]
    (count_ref, in_ref, cot_ref, wqkv_ref, wout_ref, wup_ref, wdown_ref, gain_ref, shift_ref, qv_ref, upb_ref,
     resid_ref) = ins
    saved, (wattn_outs, wff_outs, ends_ref) = outs[:11 * n], split_refs(outs[11 * n:], n, n, 1)
    saved = [saved[l * 11:(l + 1) * 11] for l in range(n)]
    ends_ref = ends_ref[0]
    (own_attn, own_ff, all_attn, all_ff, swap_ref, mine_ref, n_ref, q_ref, k_ref, v_ref, mixed_ref, pre_ref,
     hidden_ref, stream_ref, middle_ref, valid_ref, o_ref, bias_ref, tsems, csems, wsems, vsems, kv_sems,
     bsems), team, joined = split_refs(scratch, 24, 6, 0 if aligned else 2)
    bufs, (gsems, ssems) = team[:4], team[4:]
    pc = Place(sz)
    greeting = Greeting(team_peers(pc) + weight_peers(pc, True))

    def pack(ref, pieces):
        total = None
        for values, start, count, at in pieces:
            piece = shift_lanes(values, start, count, at, ref.shape[-1])
            total = piece if total is None else total + piece
        ref[0:sz.wrows, :] = total.astype(bf16)
        if not aligned:
            ref[sz.wrows:, :] = jnp.zeros((sz.wrowsp - sz.wrows, ref.shape[-1]), bf16)

    def pack_attn(layer):
        full = sz.wide * sz.zl
        for half in range(sz.zl):
            pieces = [(wqkv_ref[layer], kind * full + half * sz.wide, sz.wide, kind * sz.wide) for kind in range(3)]
            pieces += [(wout_ref[layer], half * sz.wide, sz.wide, 3 * sz.wide)]
            if sz.spare:
                pieces += [(wup_ref[layer], half * sz.ff, sz.spare, 4 * sz.wide)]
            pack(own_attn.at[layer, half], pieces)

    def pack_ff(layer):
        for half in range(sz.zl):
            rest = sz.ff - sz.spare
            pack(own_ff.at[layer, half], [(wup_ref[layer], half * sz.ff + sz.spare, rest, 0),
                                          (wdown_ref[layer], half * sz.ff, sz.ff, rest)])

    for image in range(sz.images):
        swap_ref[image, 0] = piece_of(pc, in_ref[image]).astype(bf16)
        swap_ref[image, 1] = piece_of(pc, cot_ref[image]).astype(bf16)
    pack_attn(0)
    attn = [Fetch(pc, own_attn.at[l], all_attn.at[l], wsems.at[2 * l], vsems.at[2 * l]) for l in range(n)]
    ff = [Fetch(pc, own_ff.at[l], all_ff.at[l], wsems.at[2 * l + 1], vsems.at[2 * l + 1], sz.ff_sent)
          for l in range(n)]
    bias_ref[:, pc.k] = jnp.zeros((n, 8, bias_ref.shape[-1]), f32)
    for l in range(n):
        bias_ref[l, pc.k, 0:2, 0:sz.headp] = half_of(pc, qv_ref[l], sz.wide, sz.headp)
        bias_ref[l, pc.k, 2:3, 0:sz.ffp] = half_of(pc, upb_ref[l:l + 1, :], sz.ff, sz.ffp, sz.ff_at)
    bias_swaps = [Swap(pc, bias_ref.at[l, pc.k], bias_ref.at[l, pc.k], bsems.at[0, l], bsems.at[1, l])
                  for l in range(n)]
    copies = Copies(csems)

    def swap(step):
        zh = (pc.zh + step) % sz.images
        return send(swap_ref.at[zh], mine_ref.at[pc.zh], tsems.at[0, step], tsems.at[1, step],
                    (pc.f, zh * sz.zl + pc.zl, pc.t))

    greeting.wait()
    for step in range(1, sz.images):
        swap(step).start()
    attn[0].run("d0 d1 d2")
    for move in bias_swaps:
        move.start()
    mine_ref[pc.zh] = swap_ref[pc.zh]
    count = count_ref[pc.zh]
    valid_ref[...] = key_valid(pc, count)
    for step in range(1, sz.images):
        swap(step).wait()
    stream_ref[0] = mine_ref[:, 0].astype(f32)
    gathers = [Gather(pc, n_ref.at[i], gsems.at[i], FORWARD_TURN[i % 2]) for i in range(2 * n)]
    scatters = [Scatter(pc, bufs, ssems.at[i], i % 2 == 0, i % 2 == 0 and SUM_TURN[0]) for i in range(2 * n)]
    for p in range(sz.images):
        gathers[0].start(p, norm_low(stream_ref[0, p], gain_ref[0, 0:1, :], shift_ref[0, 0:1, :]))
    pack_ff(0)
    attn[0].run("t0")
    ff[0].run("d0")
    for layer in range(1, n):
        pack_attn(layer)
    attn[0].run("t1")
    ff[0].run("d1")
    ends_ref[...] = mine_ref[:, 1].astype(f32) * own_valid(pc, count)
    attn[0].run("l0 t2")
    for layer in range(1, n):
        pack_ff(layer)
    attn[0].run("l1")
    ff[0].run("t0")
    attn[0].run("l2")
    for move in bias_swaps:
        move.wait()
    attn[0].finish()

    def ready(fetch, refs, kind, layer, out):
        ref = refs.at[layer]
        if not aligned:
            for s in range(2):
                drop_padding(sz, ref.at[s], joined[kind].at[s])
            ref = joined[kind]
            pltpu.sync_copy(ref, out)
        else:
            copies.start(ref, out)
        return ref

    def after_attn(l, p):
        def run():
            middle = stream_ref[l, p] + (scatters[2 * l].finish(p) + resid_ref[l, 0:1, :])
            middle_ref[l, p] = middle
            gathers[2 * l + 1].start(p, norm_low(middle, gain_ref[l, 1:2, :], shift_ref[l, 1:2, :]))

        return run

    def after_ff(l, p):
        def run():
            out = middle_ref[l, p] + (scatters[2 * l + 1].finish(p) + resid_ref[l, 1:2, :])
            stream_ref[l + 1, p] = out
            if l + 1 < n:
                gathers[2 * l + 2].start(p, norm_low(out, gain_ref[l + 1, 0:1, :], shift_ref[l + 1, 0:1, :]))

        return run

    per = sz.steps // sz.images
    rest = range(1, sz.images)
    for l in range(n):
        more = l + 1 < n
        w = ready(attn[l], all_attn, 0, l, wattn_outs[l])
        project = {p * per - 1: [after_ff(l - 1, p)] for p in rest} if l else {}
        attend, flush = {}, []
        plan(project, attend, flush, PLAN_ATTN_FIRST if l == 0 else PLAN_ATTN, ff[l], attn[l + 1] if more else None)
        jobs = Jobs(project=project, attend=attend, flush=flush, turnover=[after_attn(l, 0)])
        attn_forward(pc, jobs, gathers[2 * l], w, bias_ref.at[l], valid_ref, q_ref.at[l], k_ref.at[l], v_ref.at[l],
                     mixed_ref.at[l], o_ref, kv_sems.at[l], scatters[2 * l])
        for ref, to in ((stream_ref.at[l], 0), (n_ref.at[2 * l], 2), (q_ref.at[l], 4), (k_ref.at[l], 5),
                        (v_ref.at[l], 6), (mixed_ref.at[l], 7)):
            copies.start(ref, saved[l][to])
        ff[l].finish()
        for core in range(2):
            ride(sz, all_attn.at[l, core], all_ff.at[l, core], 4 * sz.wide - sz.ff_at, 0)
        w = ready(ff[l], all_ff, 1, l, wff_outs[l])
        feed = {(p - 1) * per: [after_attn(l, p)] for p in rest}
        if more:
            plan(feed, None, None, PLAN_FF, ff[l + 1], attn[l + 1])
        feed[FF_OVER] = [after_ff(l, 0)] + feed.get(FF_OVER, [])
        ff_forward(pc, Jobs(feed=feed), gathers[2 * l + 1], w, bias_ref.at[l], pre_ref.at[l],
                   hidden_ref.at[l], scatters[2 * l + 1])
        if more:
            attn[l + 1].finish()
        else:
            for p in rest:
                after_ff(l, p)()
        for ref, to in ((middle_ref.at[l], 1), (n_ref.at[2 * l + 1], 3), (pre_ref.at[l], 8), (hidden_ref.at[l], 9)):
            copies.start(ref, saved[l][to])
    copies.start(stream_ref.at[n], saved[0][10])
    copies.start(valid_ref, saved[n - 1][10])
    copies.wait()


def forward_call(sz, *operands):
    n = sz.layers
    own, team = ((sz.images, sz.part, sz.d), f32), ((sz.chips, sz.images, sz.part, sz.d), bf16)
    head, pair = (2, sz.units, sz.part, sz.headp), (2, 2, sz.units, sz.part, sz.headp)
    hidden = (2, sz.units, sz.part, sz.ffp)
    shapes = []
    for l in range(n):
        last = ((1, sz.keys), f32) if l == n - 1 else own
        shapes += [own, own, team, team, (head, bf16), (pair, bf16), (pair, bf16), (head, bf16), (hidden, f32),
                   (hidden, bf16), last]
    shapes += [((2, sz.d, sz.attnp), bf16)] * n + [((2, sz.d, sz.ffw), bf16)] * n + [own]
    vmem, hbm = pl.BlockSpec(memory_space=pltpu.VMEM), pl.BlockSpec(memory_space=pl.ANY)
    padded = sz.groups * sz.wrowsp
    scratch = [
        VMEM((n, sz.zl, sz.wrowsp, sz.attnp), bf16), VMEM((n, sz.zl, sz.wrowsp, sz.ffs), bf16),
        VMEM((n, 2, padded, sz.attnp), bf16), VMEM((n, 2, padded, sz.ffw), bf16),
        VMEM((sz.images, 2, sz.part, sz.d), bf16), VMEM((sz.images, 2, sz.part, sz.d), bf16),
        VMEM((2 * n,) + team[0], bf16),
        VMEM((n,) + head, bf16), VMEM((n,) + pair, bf16), VMEM((n,) + pair, bf16), VMEM((n,) + head, bf16),
        VMEM((n,) + hidden, f32), VMEM((n,) + hidden, bf16),
        VMEM((n + 1,) + own[0], f32), VMEM((n,) + own[0], f32), VMEM((1, sz.keys), f32),
        VMEM((2, sz.d, sz.headp), bf16), VMEM((n, 2, 8, max(sz.headp, sz.ffp)), f32),
        DMA((2, sz.images)), DMA((12 * n + 2,)), DMA((2 * n, sz.chunks, sz.fsdp, 2, sz.ctx)),
        DMA((2 * n, sz.chunks, sz.fsdp, 2, sz.ctx)), DMA((n, 2, 2, 2, sz.images)), DMA((2, n)),
    ] + team_scratch(sz, 2 * n)
    if sz.wrowsp != sz.wrows:
        scratch += [VMEM((2, sz.d, sz.attnp), bf16), VMEM((2, sz.d, sz.ffw), bf16)]
    return pl.pallas_call(
        functools.partial(forward_kernel, sz),
        out_shape=[jax.ShapeDtypeStruct(*s) for s in shapes],
        in_specs=[pl.BlockSpec(memory_space=pltpu.SMEM)] + [vmem] * (len(operands) - 1),
        out_specs=[hbm] * (len(shapes) - 1) + [vmem],
        scratch_shapes=scratch,
        compiler_params=params(1),
        name="forward",
    )(*operands)


def params(collective_id):
    return pltpu.CompilerParams(
        collective_id=collective_id, has_side_effects=True, vmem_limit_bytes=63 * 1024 * 1024
    )


class Twins:
    def __init__(self, pc, dw, got, sems, span):
        self.pc, self.dw, self.got, self.sems, self.span = pc, dw, got, sems, span
        self.count = pc.sz.d // span

    def copy(self, i):
        rows = pl.ds(pl.multiple_of(i * self.span, 128), self.span)
        return send(self.dw.at[1 - self.pc.k, rows], self.got.at[rows], self.sems.at[0, i], self.sems.at[1, i],
                    self.pc.twin)

    def put(self, core, i, pieces):
        rows = pl.ds(pl.multiple_of(i * self.span, 128), self.span)
        for at, values in pieces:
            self.dw[core, rows, at:at + values.shape[-1]] = values.astype(bf16)

    def run(self, make, jobs, between=None):
        def other(i, carry):
            self.put(1 - self.pc.k, i, make(1 - self.pc.k, i))
            self.copy(i).start()
            return carry

        def own(i, carry):
            self.put(self.pc.k, i, make(self.pc.k, i))
            jobs.at("step_grads", i)
            return carry

        def add(i, carry):
            self.copy(i).wait_recv()
            rows = pl.ds(pl.multiple_of(i * self.span, 128), self.span)
            self.dw[self.pc.k, rows, :] = (
                self.dw[self.pc.k, rows, :].astype(f32) + self.got[rows, :].astype(f32)
            ).astype(bf16)
            self.copy(i).wait_send()
            return carry

        lax.fori_loop(0, self.count, other, 0)
        if between:
            between()
        lax.fori_loop(0, self.count, own, 0)
        lax.fori_loop(0, self.count, add, 0)


def ff_backward(pc, jobs, gather, w_ref, n2_ref, pre_ref, hidden_ref, dup_ref, pg_ref, twins, scatter):
    sz = pc.sz
    dup_ref[...] = jnp.zeros_like(dup_ref)

    def feed(step, carry):
        units, tokens = gather.ready(step)
        partial = None
        for s in range(2):
            back = dot(tokens, w_ref[s, :, sz.down_at:], (1, 0))
            if sz.down_shift != sz.ff_at:
                back = pltpu.roll(back, (sz.ff_at - sz.down_shift) % sz.ffp, 1)
            pre = rows_of(pre_ref.at[s], units)
            bent = jnp.tanh(gelu_root * (pre + gelu_cubic * pre * pre * pre))
            slope = 0.5 * (1.0 + bent) + 0.5 * pre * (1.0 - bent * bent) * (
                gelu_root * (1.0 + 3.0 * gelu_cubic * pre * pre)
            )
            pre_grad = ff_lanes(sz, back * slope).astype(bf16)
            put_rows(sz, pg_ref.at[s], units, pre_grad)
            dup_ref[s] += jnp.sum(pre_grad.astype(f32), axis=0, keepdims=True)
            terms = dot(pre_grad, w_ref[s, :, 0:sz.ffp], (1, 1))
            partial = terms if partial is None else partial + terms
        scatter.push(step, partial)
        jobs.at("feed", step)
        return carry

    lax.fori_loop(0, sz.steps, feed, 0)
    jobs.run("flush")

    def make(core, i):
        lanes = pl.ds(pl.multiple_of(i * twins.span, 128), twins.span)
        hidden = hidden_ref[core].reshape(sz.half, sz.ffp)
        down = dot(by_unit(sz, gather.buf[:, :, :, lanes]), hidden, (0, 0))
        pre_grad = pg_ref[core].reshape(sz.half, sz.ffp)
        up = dot(by_unit(sz, n2_ref[:, :, :, lanes]), pre_grad, (0, 0))
        over = sz.ffp - sz.down_at
        both = [(sz.down_at, up[:, sz.down_at:] + down[:, 0:over])] if over else []
        return [(0, up[:, 0:sz.down_at])] + both + [(sz.ffp, down[:, over:])]

    twins.run(make, jobs)
    jobs.run("grads")
    gather.finish()


def attn_backward(pc, jobs, gather, w_ref, n1_ref, q_ref, k_ref, v_ref, mixed_ref, valid_ref, dqv_ref,
                  o_ref, dkv_ref, kvsend_ref, kvgot_ref, stack_ref, kv_sems, twins, scatter):
    sz = pc.sz
    for s in range(2):
        unpack_out(sz, w_ref.at[s], o_ref.at[s])
    dkv_ref[...] = jnp.zeros_like(dkv_ref)
    dqv_ref[...] = jnp.zeros_like(dqv_ref)
    scale = HEAD_DIM ** (-0.5)

    def attend(step, carry):
        units, tokens = gather.ready(step)
        for s in range(2):
            mixed_grad = dot(tokens, o_ref[s], (1, 0)).astype(bf16)
            keys = k_ref[s].reshape(sz.keys, sz.headp)
            values = v_ref[s].reshape(sz.keys, sz.headp)
            queries = rows_of(q_ref.at[s], units)
            total = jnp.zeros((sz.tile, sz.headp), f32)
            dkey, dvalue = None, None
            for head in range(sz.heads):
                q_head = head_of(queries, head)
                g_head = head_of(mixed_grad, head)
                probs = probabilities(q_head, keys, valid_ref[...])
                dprobs = dot(g_head, values, (1, 1))
                inner = jnp.sum(probs * dprobs, axis=-1, keepdims=True)
                dscores = (probs * (dprobs - inner)).astype(bf16)
                total = total + dot(dscores, head_of(keys, head), (1, 0))
                dk, dv = dot(dscores, q_head, (0, 0)), dot(probs.astype(bf16), g_head, (0, 0))
                dkey = dk if dkey is None else dkey + dk
                dvalue = dv if dvalue is None else dvalue + dv
            dkv_ref[s, 0] += dkey.reshape(2, sz.half, sz.headp)
            dkv_ref[s, 1] += dvalue.reshape(2, sz.half, sz.headp)
            dq = (scale * total).astype(bf16).astype(f32)
            dqv_ref[s, 0:1, :] += jnp.sum(dq, axis=0, keepdims=True)
            dq = dq.astype(bf16)
            for i, unit in enumerate(units):
                stack_ref[s, unit, :, 0:sz.headp] = dq[i * sz.part:(i + 1) * sz.part]
        jobs.at("attend", step)
        return carry

    lax.fori_loop(0, sz.steps, attend, 0)
    for s in range(2):
        kvsend_ref[s] = dkv_ref[s, :, 1 - pc.k].astype(bf16)
    moves = [Swap(pc, kvsend_ref.at[s], kvgot_ref.at[s], kv_sems.at[0, s], kv_sems.at[1, s]) for s in range(2)]
    for move in moves:
        move.start()
    gather.finish()
    jobs.run("middle")
    for move in moves:
        move.wait()

    def back_project(step, carry):
        units = scatter.units(step)
        partial = None
        for s in range(2):

            def both(kind):
                rows = [pl.ds(pl.multiple_of(unit * sz.part, sz.part), sz.part) for unit in units]
                return jnp.concatenate(
                    [dkv_ref[s, kind, pc.k, r, :] + kvgot_ref[s, kind, r, :].astype(f32) for r in rows], axis=0
                )

            dk = (scale * both(0)).astype(bf16).astype(f32)
            dv = both(1).astype(bf16).astype(f32)
            dqv_ref[s, 1:2, :] += jnp.sum(dv, axis=0, keepdims=True)
            dq = rows_of(stack_ref.at[s], units)[:, 0:sz.headp].astype(f32)
            total = jnp.pad(dq, ((0, 0), (0, sz.qkvp - sz.headp)))
            for kind, piece in ((1, dk), (2, dv)):
                start = kind * sz.wide // 128 * 128
                shift = kind * sz.wide - start
                moved = pltpu.roll(piece, shift, 1) if shift else piece
                total = total + jnp.pad(moved, ((0, 0), (start, sz.qkvp - start - sz.headp)))
            stacked = total.astype(bf16)
            put_rows(sz, stack_ref.at[s], units, stacked)
            terms = dot(stacked, w_ref[s, :, 0:sz.qkvp], (1, 1))
            partial = terms if partial is None else partial + terms
        scatter.push(step, partial)
        return carry

    lax.fori_loop(0, sz.steps, back_project, 0)
    jobs.run("flush")
    o_at = 3 * sz.wide // 128 * 128
    o_shift = 3 * sz.wide - o_at

    def make(core, i):
        lanes = pl.ds(pl.multiple_of(i * twins.span, 128), twins.span)
        stacked = stack_ref[core].reshape(sz.half, sz.qkvp)
        dqkv = dot(by_unit(sz, n1_ref[:, :, :, lanes]), stacked, (0, 0))
        mixed = mixed_ref[core].reshape(sz.half, sz.headp)
        dout = dot(by_unit(sz, gather.buf[:, :, :, lanes]), mixed, (0, 0))
        if o_shift:
            dout = pltpu.roll(dout, o_shift, 1)
        total = jnp.pad(dqkv, ((0, 0), (0, sz.attnp - sz.qkvp))) + jnp.pad(
            dout, ((0, 0), (o_at, sz.attnp - o_at - sz.headp))
        )
        return [(0, total)]

    twins.run(make, jobs, scatter.flush)
    jobs.run("grads")


def backward_kernel(sz, *refs):
    n = sz.layers
    aligned = sz.wrowsp == sz.wrows
    saved = [refs[l * 11:(l + 1) * 11] for l in range(n)]
    wattn_ins, wff_ins, (cot_ref, gain_ref), outs, scratch = split_refs(
        refs[11 * n:], n, n, 2, 2 * n + 2, len(refs) - 11 * n - 2 * n - 2 - 2 * n - 2)
    attn_outs, ff_outs, (whole_ref, small_ref) = split_refs(outs, n, n, 2)
    (stream_ref, middle_ref, n1_ref, n2_ref, q_ref, k_ref, v_ref, mixed_ref, pre_ref, hidden_ref, valid_ref, out_ref,
     wattn_ref, wff_ref, gl_ref, ml_ref, pg_ref, o_ref, dkv_ref, kvsend_ref, kvgot_ref, stack_ref, dwattn_ref,
     dwff_ref, twattn_ref, twff_ref, got_attn, got_ff, dqv_ref, dup_ref, grad_ref, ends_ref, first, from_tp, from_ctx,
     from_fsdp, sum_tp, sum_ctx, share_ref, shgot_ref, lsems, wsems, esems, ysems, tsems, kv_sems, twsems,
     shsems), team, padded = split_refs(scratch, 48, 6, 0 if aligned else 2)
    bufs, (gsems, ssems) = team[:4], team[4:]
    pc = Place(sz)
    greeting = Greeting(team_peers(pc) + weight_peers(pc, True) + line_peers(pc))
    copies = Copies(lsems)
    into = [stream_ref, middle_ref, n1_ref, n2_ref, q_ref, k_ref, v_ref, mixed_ref, pre_ref, hidden_ref]

    def load(l, weights, ref, kinds):
        return [copies.start(weights[l], ref)] + [copies.start(saved[l][kind], into[kind]) for kind in kinds]

    def load_ff(l):
        return load(l, wff_ins, wff_ref, (8, 3, 9, 1))

    def load_attn(l):
        return load(l, wattn_ins, wattn_ref, (4, 5, 6, 7, 2, 0))

    out_load = copies.start(saved[0][10], out_ref)
    ff_loads, attn_loads = load_ff(n - 1), load_attn(n - 1)
    attn_loads.append(copies.start(saved[n - 1][10], valid_ref))
    own_attn, own_ff = dwattn_ref.at[pc.k], dwff_ref.at[pc.k]
    give_attn = [Give(pc, own_attn if aligned else padded[0], attn_outs[l], got_attn.at[l], wsems.at[2 * l])
                 for l in range(n)]
    give_ff = [Give(pc, own_ff if aligned else padded[1], ff_outs[l], got_ff.at[l], wsems.at[2 * l + 1], sz.ff_sent)
               for l in range(n)]

    def begin(give, dw, kind):
        def run():
            if kind == 0:
                ride(sz, own_ff, dw, 0, 4 * sz.wide - sz.ff_at)
            if not aligned:
                add_padding(sz, dw, padded[kind])
            give.run("d0 d1")

        return run

    def swap(kind, step):
        zh = (pc.zh + step) % sz.images
        return send(ends_ref.at[kind, zh], whole_ref.at[kind, pc.t, pc.zh], esems.at[kind, 0, step],
                    esems.at[kind, 1, step], (pc.f, zh * sz.zl + pc.zl, pc.t))

    def own_end(kind):
        return pltpu.make_async_copy(ends_ref.at[kind, pc.zh], whole_ref.at[kind, pc.t, pc.zh], esems.at[kind, 0, 0])

    def spread(kind, step):
        return send(whole_ref.at[kind, pc.t], whole_ref.at[kind, pc.t], ysems.at[kind, 0, step],
                    ysems.at[kind, 1, step], (pc.f, pc.c, (pc.t + step) % sz.tp))

    def spread_from(kind, step):
        back = (pc.t + sz.tp - step) % sz.tp
        return send(whole_ref.at[kind, back], whole_ref.at[kind, back], ysems.at[kind, 0, step],
                    ysems.at[kind, 1, step], (pc.f, pc.c, back))

    def swap_start(kind):
        own_end(kind).start()
        for step in range(1, sz.images):
            swap(kind, step).start()

    def spread_start(kind):
        own_end(kind).wait()
        for step in range(1, sz.images):
            swap(kind, step).wait()
        for step in range(1, sz.tp):
            spread(kind, step).start()

    def spread_wait(kind):
        for step in range(1, sz.tp):
            spread_from(kind, step).wait_recv()
            spread(kind, step).wait_send()

    def over_tp(step):
        return send(first, from_tp.at[step - 1], tsems.at[0, 0, step], tsems.at[0, 1, step],
                    (pc.f, pc.c, (pc.t + step) % sz.tp))

    def over_ctx(step):
        return send(sum_tp, from_ctx.at[step - 1], tsems.at[1, 0, step], tsems.at[1, 1, step],
                    (pc.f, pc.ctx_ahead(step), pc.t))

    def over_fsdp(step):
        return send(sum_ctx, from_fsdp.at[step - 1], tsems.at[2, 0, step], tsems.at[2, 1, step],
                    ((pc.f + step) % sz.fsdp, pc.c, pc.t))

    sum_tp[...] = jnp.zeros_like(sum_tp)
    share_ref[...] = jnp.zeros_like(share_ref)
    first[...] = jnp.zeros_like(first)
    copies.wait([out_load])
    ends_ref[0] = out_ref[...].astype(bf16)
    grad_ref[...] = cot_ref[...]
    gathers = [Gather(pc, (gl_ref, ml_ref)[i % 2], gsems.at[i], BACKWARD_TURN[1 - i % 2]) for i in range(2 * n)]
    scatters = [Scatter(pc, bufs, ssems.at[i], i % 2 == 1, i % 2 == 1 and SUM_TURN[1]) for i in range(2 * n)]
    def low_of(l, p, row):
        low = grad_ref[p].astype(bf16)
        first[l, row:row + 1, :] += jnp.sum(low.astype(f32), axis=0, keepdims=True)
        return low

    def after_ff(l, p):
        def run():
            turn = n - 1 - l
            term, dgain, dshift = norm_back(middle_ref[p], gain_ref[l, 1:2, :], scatters[2 * turn].finish(p))
            grad_ref[p] += term
            gathers[2 * turn + 1].start(p, low_of(l, p, 4))
            first[l, 1:2, :] += dgain
            first[l, 3:4, :] += dshift

        return run

    def after_attn(l, p):
        def run():
            turn = n - 1 - l
            term, dgain, dshift = norm_back(stream_ref[p], gain_ref[l, 0:1, :], scatters[2 * turn + 1].finish(p))
            grad_ref[p] += term
            if l:
                gathers[2 * turn + 2].start(p, low_of(l - 1, p, 5))
            else:
                ends_ref[1, p] = grad_ref[p].astype(bf16)
            first[l, 0:1, :] += dgain
            first[l, 2:3, :] += dshift

        return run

    greeting.wait()
    per, rest = sz.steps // sz.images, range(1, sz.images)
    span = 384 if sz.d % 384 == 0 else 128
    for p in range(sz.images):
        gathers[0].start(p, low_of(n - 1, p, 5))
    swap_start(0)
    for turn in range(n):
        l = n - 1 - turn
        start = turn == 0
        copies.wait(ff_loads)
        feed = {}
        if start:
            feed[1] = [lambda: spread_start(0)]
        else:
            after = give_attn[l + 1]
            feed.update({(p - 1) * per: [after_attn(l + 1, p)] for p in rest})
            feed[(sz.images - 2) * per] = feed[(sz.images - 2) * per] + [lambda: attn_loads.extend(load_attn(l))]
            plan(feed, None, None, GIVE_FF, None, after)
        feed[FF_OVER] = [after_ff(l, 0)] + feed.get(FF_OVER, [])
        jobs = Jobs(feed=feed, flush=([] if start else [give_ff[l + 1].finish]),
                    grads=[begin(give_ff[l], own_ff, 1)] + [after_ff(l, p) for p in rest])
        twins = Twins(pc, dwff_ref, twff_ref, twsems.at[2 * l + 1], span)
        ff_backward(pc, jobs, gathers[2 * turn], wff_ref, n2_ref, pre_ref, hidden_ref, dup_ref, pg_ref, twins,
                    scatters[2 * turn])
        for core in range(2):
            share_ref[core, 3 * l + 2:3 * l + 3, 0:sz.ffp] = dup_ref[core]
        copies.wait(attn_loads)
        del attn_loads[:]
        if l:
            ff_loads = load_ff(l - 1)
        if start:
            spread_wait(0)
        now = give_ff[l]
        jobs = Jobs(
            attend=planned(GIVE_ATTN, now),
            flush=([] if start else [give_attn[l + 1].finish]),
            step_grads={0: [after_attn(l, 0)]}, grads=[begin(give_attn[l], own_attn, 0)],
        )
        twins = Twins(pc, dwattn_ref, twattn_ref, twsems.at[2 * l], span)
        attn_backward(pc, jobs, gathers[2 * turn + 1], wattn_ref, n1_ref, q_ref, k_ref, v_ref, mixed_ref, valid_ref,
                      dqv_ref, o_ref, dkv_ref, kvsend_ref, kvgot_ref, stack_ref, kv_sems.at[l], twins,
                      scatters[2 * turn + 1])
        for core in range(2):
            share_ref[core, 3 * l:3 * l + 2, 0:sz.headp] = dqv_ref[core]
    share = Swap(pc, share_ref.at[1 - pc.k], shgot_ref, shsems.at[0], shsems.at[1])
    share.start()
    for p in rest:
        after_attn(0, p)()
    last = give_attn[0]
    swap_start(1)
    for step in range(1, sz.tp):
        over_tp(step).start()
    last.run("d2 t0")
    spread_start(1)
    last.run("t1")
    value = first[...]
    for step in range(1, sz.tp):
        over_tp(step).wait()
        value = value + from_tp[step - 1]
    sum_tp[0:n] = value
    share.wait()
    sum_tp[n + pc.zl] = share_ref[pc.k] + shgot_ref[...]
    for step in range(1, sz.ctx):
        over_ctx(step).start()
    last.run("t2")
    value = sum_tp[...]
    for step in range(1, sz.ctx):
        over_ctx(step).wait()
        value = value + from_ctx[step - 1]
    sum_ctx[...] = value
    for step in range(1, sz.fsdp):
        over_fsdp(step).start()
    value = sum_ctx[...]
    for step in range(1, sz.fsdp):
        over_fsdp(step).wait()
        value = value + from_fsdp[step - 1]
    small_ref[...] = value
    give_ff[0].finish()
    spread_wait(1)
    last.finish()


def backward_call(sz, saved, wattn, wff, cot, gains):
    n = sz.layers
    own, team = (sz.images, sz.part, sz.d), (sz.chips, sz.images, sz.part, sz.d)
    head, pair = (2, sz.units, sz.part, sz.headp), (2, 2, sz.units, sz.part, sz.headp)
    hidden = (2, sz.units, sz.part, sz.ffp)
    deep = up_to(max(6, 3 * n), 8)
    small = (n + sz.zl, deep, sz.d)
    ends = (sz.images, sz.part, sz.d)
    attn_sum, ff_sum = (sz.ctx, sz.wrowsp, sz.attnp), (sz.ctx, sz.wrowsp, sz.ffs)
    shapes = [(attn_sum, bf16)] * n + [(ff_sum, bf16)] * n + [((2, sz.tp) + ends, bf16), (small, f32)]
    vmem, hbm = pl.BlockSpec(memory_space=pltpu.VMEM), pl.BlockSpec(memory_space=pl.ANY)
    far, jumps = max(sz.tp, sz.ctx, sz.fsdp), max(sz.fsdp - 1, 1)
    scratch = [
        VMEM(own, f32), VMEM(own, f32), VMEM(team, bf16), VMEM(team, bf16),
        VMEM(head, bf16), VMEM(pair, bf16), VMEM(pair, bf16), VMEM(head, bf16), VMEM(hidden, f32), VMEM(hidden, bf16),
        VMEM((1, sz.keys), f32), VMEM(own, f32),
        VMEM((2, sz.d, sz.attnp), bf16), VMEM((2, sz.d, sz.ffw), bf16),
        VMEM(team, bf16), VMEM(team, bf16), VMEM(hidden, bf16), VMEM((2, sz.d, sz.headp), bf16),
        VMEM((2, 2, 2, sz.half, sz.headp), f32), VMEM((2, 2, sz.half, sz.headp), bf16),
        VMEM((2, 2, sz.half, sz.headp), bf16), VMEM((2, sz.units, sz.part, sz.qkvp), bf16),
        VMEM((2, sz.d, sz.attnp), bf16), VMEM((2, sz.d, sz.ffw), bf16),
        VMEM((sz.d, sz.attnp), bf16), VMEM((sz.d, sz.ffw), bf16),
        VMEM((n, jumps) + attn_sum, bf16), VMEM((n, jumps) + ff_sum, bf16),
        VMEM((2, 2, sz.headp), f32), VMEM((2, 1, sz.ffp), f32), VMEM(own, f32), VMEM((2,) + ends, bf16),
        VMEM((n, deep, sz.d), f32), VMEM((sz.tp - 1, n, deep, sz.d), f32),
        VMEM((max(sz.ctx - 1, 1),) + small, f32), VMEM((jumps,) + small, f32), VMEM(small, f32), VMEM(small, f32),
        VMEM((2, deep, sz.d), f32), VMEM((deep, sz.d), f32),
        DMA((12 * n + 2,)), DMA((2 * n, sz.chunks, sz.fsdp, 2, sz.ctx)), DMA((2, 2, sz.images)), DMA((2, 2, sz.tp)),
        DMA((3, 2, far)), DMA((n, 2, 2)), DMA((2 * n, 2, sz.d // 128)), DMA((2,)),
    ] + team_scratch(sz, 2 * n)
    if sz.wrowsp != sz.wrows:
        padded = sz.groups * sz.wrowsp
        scratch += [VMEM((padded, sz.attnp), bf16), VMEM((padded, sz.ffw), bf16)]
    operands = (*saved, *wattn, *wff, cot, gains)
    return pl.pallas_call(
        functools.partial(backward_kernel, sz),
        out_shape=[jax.ShapeDtypeStruct(*s) for s in shapes],
        in_specs=[hbm] * (len(operands) - 2) + [vmem] * 2,
        out_specs=[hbm] * (2 * n + 1) + [vmem],
        scratch_shapes=scratch,
        compiler_params=params(2),
        name="backward",
    )(*operands)


def close_kernel(sz, *refs):
    n = sz.layers
    attn_refs, ff_refs, (whole_ref, small_ref), outs = split_refs(refs, n, n, 2, 11)
    out_ref, gin_ref, gain_ref, bias_ref, qkv_ref, qv_ref, wout_ref, up_ref, upb_ref, down_ref, resid_ref = outs
    full, ff = sz.wide * sz.zl, sz.ff * sz.zl

    def summed(ref):
        return [sum(ref[zh * sz.zl + j].astype(f32) for zh in range(sz.images)) for j in range(sz.zl)]

    def join(width, count, *runs):
        total = None
        for j, halves, start, lanes, place in [(j, *run) for run in runs for j in range(sz.zl)]:
            piece = shift_lanes(halves[j], start, lanes, j * count + place, up_to(width, 128))
            total = piece if total is None else total + piece
        return total[0:sz.wrows, 0:width]

    for layer in range(n):
        attn, hidden = summed(attn_refs[layer]), summed(ff_refs[layer])
        for kind in range(3):
            at = kind * full
            qkv_ref[layer, :, at:at + full] = join(full, sz.wide, (attn, kind * sz.wide, sz.wide, 0))
        wout_ref[layer] = join(full, sz.wide, (attn, 3 * sz.wide, sz.wide, 0))
        rest = sz.ff - sz.spare
        first = [(attn, 4 * sz.wide, sz.spare, 0)] if sz.spare else []
        up_ref[layer] = join(ff, sz.ff, *first, (hidden, 0, rest, sz.spare))
        down_ref[layer] = join(ff, sz.ff, (hidden, rest, sz.ff, 0))
        values = small_ref[layer]
        gain_ref[layer] = values[0:2]
        bias_ref[layer] = values[2:4]
        resid_ref[layer] = values[4:6]
        total_qv, total_up = None, None
        for half in range(sz.zl):
            values = small_ref[n + half]
            qv = shift_lanes(values, 0, sz.wide, half * sz.wide, up_to(full, 128))
            up = shift_lanes(values, sz.ff_at, sz.ff, half * sz.ff, up_to(ff, 128))
            total_qv = qv if total_qv is None else total_qv + qv
            total_up = up if total_up is None else total_up + up
        qv_ref[layer] = total_qv[3 * layer:3 * layer + 2, 0:full]
        upb_ref[layer:layer + 1, :] = total_up[3 * layer + 2:3 * layer + 3, 0:ff]
    for image in range(sz.images):
        rows = whole_ref[0, :, image].reshape(sz.tp * sz.part, sz.d)
        out_ref[image] = rows[0:sz.rows]
        rows = whole_ref[1, :, image].reshape(sz.tp * sz.part, sz.d)
        gin_ref[image] = rows.astype(f32)[0:sz.rows]


def close_call(sz, attn_sums, ff_sums, ends, small):
    n, full, ff = sz.layers, sz.wide * sz.zl, sz.ff * sz.zl
    tokens = (sz.images, sz.rows, sz.d)
    vec, up = ((n, 2, sz.d), f32), ((n, sz.wrows, ff), f32)
    shapes = [
        (tokens, bf16), (tokens, f32), vec, vec, ((n, sz.wrows, 3 * full), f32), ((n, 2, full), f32),
        ((n, sz.wrows, full), f32), up, ((n, ff), f32), up, vec,
    ]
    vmem = pl.BlockSpec(memory_space=pltpu.VMEM)
    results = pl.pallas_call(
        functools.partial(close_kernel, sz),
        out_shape=[jax.ShapeDtypeStruct(*s) for s in shapes],
        in_specs=[vmem] * (2 * n + 2),
        out_specs=[vmem] * len(shapes),
        compiler_params=pltpu.CompilerParams(vmem_limit_bytes=60 * 1024 * 1024),
        name="close",
    )(*attn_sums, *ff_sums, ends, small)
    results = list(results)
    results[4] = results[4].reshape(n, sz.wrows, 3, full)
    return tuple(results)


def per_device(mesh, inputs, cotangent, valid_count, norm_gain, norm_bias, w_qkv, bias_qv, w_out, w_up, bias_up,
               w_down, bias_resid):
    sz = Sizes(mesh, inputs, w_qkv, w_up)
    n = sz.layers
    *made, cot = forward_call(sz, valid_count, inputs, cotangent, w_qkv.reshape(n, sz.wrows, -1), w_out, w_up,
                              w_down, norm_gain, norm_bias, bias_qv, bias_up, bias_resid)
    saved, wattn, wff = split_refs(made, 11 * n, n, n)
    *sums, ends, small = backward_call(sz, saved, wattn, wff, cot, norm_gain)
    return close_call(sz, sums[:n], sums[n:], ends, small)


def solution(mesh):
    tokens, rows = P("fsdp", "ctx", None), P(None, ("fsdp", "ctx"), "tp")
    qkv = P(None, ("fsdp", "ctx"), None, "tp")
    qv, up = P(None, None, "tp"), P(None, "tp")
    return jax.shard_map(
        functools.partial(per_device, mesh),
        mesh=mesh,
        in_specs=(tokens, tokens, P("fsdp"), P(), P(), qkv, qv, rows, rows, up, rows, P()),
        out_specs=(tokens, tokens, P(), P(), qkv, qv, rows, rows, up, rows, P()),
        check_vma=False,
    )
```

```python
import functools

import jax
import jax.numpy as jnp
from jax import lax
from jax.experimental import pallas as pl
from jax.experimental.pallas import tpu as pltpu
from jax.sharding import PartitionSpec as P

HEAD_DIM = 72
norm_eps = 1e-06
gelu_root = 0.7978845608028654
gelu_cubic = 0.044715
masked_score = -1e30
LOG2_E = 1.4426950408889634

MESH = pl.DeviceIdType.MESH
f32 = jnp.float32
bf16 = jnp.bfloat16
VMEM = pltpu.VMEM
DMA = pltpu.SemaphoreType.DMA


def up_to(value, unit):
    return (value + unit - 1) // unit * unit


def dot(a, b, over):
    return lax.dot_general(a, b, (((over[0],), (over[1],)), ((), ())), preferred_element_type=f32)


class Sizes:
    def __init__(self, mesh, inputs, w_qkv, w_up):
        self.fsdp, self.ctx, self.tp = mesh.shape["fsdp"], mesh.shape["ctx"], mesh.shape["tp"]
        self.images, self.rows, self.d = inputs.shape
        self.layers, self.wrows = w_qkv.shape[0], w_qkv.shape[1]
        self.zl = self.ctx // self.images
        self.chips_y = self.tp // 2
        self.chips = self.zl * self.chips_y
        self.team = self.chips * 2
        self.part = up_to(-(-self.rows // self.tp), 16)
        self.block = self.images * self.part
        self.units = self.chips * self.images
        self.half = self.units * self.part
        self.tile = 2 * self.part
        self.steps = self.units // 2
        self.keys = 2 * self.half
        self.wide = w_qkv.shape[3] // self.zl
        self.heads = self.wide // HEAD_DIM
        self.ff = w_up.shape[2] // self.zl
        self.headp = up_to(self.wide, 128)
        self.qkvp = up_to(3 * self.wide, 128)
        self.attnp = up_to(4 * self.wide, 128)
        self.spare = self.attnp - 4 * self.wide
        self.ff_at = 4 * self.wide % 128
        self.ff_sent = 128 if self.spare else 0
        end = self.ff_at + self.ff
        self.ffw = up_to(end + self.ff, 128)
        self.ffs = self.ffw - self.ff_sent
        self.down_at = end // 128 * 128
        self.down_shift = end - self.down_at
        self.ffp = self.ffw - self.down_at
        assert up_to(end, 128) <= self.ffp and self.spare < self.ff
        self.wrowsp = up_to(self.wrows, 16)
        self.chunk = 48 if self.wrowsp % 48 == 0 else self.wrowsp
        self.chunks = self.wrowsp // self.chunk
        self.groups = self.fsdp * self.ctx


class Place:
    def __init__(self, sz):
        self.sz = sz
        self.f, self.c, self.t = lax.axis_index("fsdp"), lax.axis_index("ctx"), lax.axis_index("tp")
        self.zh, self.zl = self.c // sz.zl, self.c % sz.zl
        self.y, self.k = self.t // 2, self.t % 2
        self.chip = self.zl * sz.chips_y + self.y
        self.slot = 2 * self.chip + self.k

    def chip_at(self, step):
        sz = self.sz
        zl = (self.zl + step // sz.chips_y) % sz.zl
        y = (self.y + step % sz.chips_y) % sz.chips_y
        return zl, y

    def chip_back(self, step):
        sz = self.sz
        zl = (self.zl + sz.zl - step // sz.chips_y) % sz.zl
        y = (self.y + sz.chips_y - step % sz.chips_y) % sz.chips_y
        return zl, y

    def index(self, chip):
        return chip[0] * self.sz.chips_y + chip[1]

    def device(self, chip):
        return (self.f, self.zh * self.sz.zl + chip[0], 2 * chip[1] + self.k)

    @property
    def twin(self):
        return (self.f, self.c, self.t + 1 - 2 * self.k)


    def ctx_ahead(self, step):
        sz = self.sz
        return (self.zh + step // sz.zl) % sz.images * sz.zl + (self.zl + step % sz.zl) % sz.zl

    def ctx_back(self, step):
        sz = self.sz
        zh = (self.zh + sz.images - step // sz.zl) % sz.images
        return zh * sz.zl + (self.zl + sz.zl - step % sz.zl) % sz.zl


def split_refs(refs, *counts):
    out, at = [], 0
    for count in counts:
        out.append(refs[at:at + count])
        at += count
    assert at == len(refs)
    return out


class Greeting:
    def __init__(self, others):
        self.count = len(others)
        self.barrier = pltpu.get_barrier_semaphore()
        for other in others:
            pl.semaphore_signal(self.barrier, inc=1, device_id=other, device_id_type=MESH)

    def wait(self):
        pl.semaphore_wait(self.barrier, self.count)


def send(src, dst, send_sem, recv_sem, device):
    return pltpu.make_async_remote_copy(
        src_ref=src, dst_ref=dst, send_sem=send_sem, recv_sem=recv_sem, device_id=device, device_id_type=MESH
    )


def team_peers(pc):
    return [pc.device(pc.chip_at(step)) for step in range(1, pc.sz.chips)] + [pc.twin]


def line_peers(pc):
    sz = pc.sz
    return [(pc.f, pc.c, 2 * ((pc.y + dy) % sz.chips_y) + 1 - pc.k) for dy in range(1, sz.chips_y)]


def weight_peers(pc, team=False):
    sz = pc.sz
    first = sz.zl if team else 1
    return [(pc.f, pc.ctx_ahead(step), pc.t) for step in range(first, sz.ctx)] + [
        ((pc.f + jump) % sz.fsdp, pc.c, pc.t) for jump in range(1, sz.fsdp)
    ]


def pick(step, values):
    if isinstance(step, int):
        return values[step]
    out = jnp.int32(values[0])
    for i in range(1, len(values)):
        out = jnp.where(step == i, jnp.int32(values[i]), out)
    return out


def when(condition, run):
    if isinstance(condition, (bool, int)):
        if condition:
            run()
    else:
        pl.when(condition)(run)


FF_OVER = 3

FORWARD_TURN = (False, True)
BACKWARD_TURN = (True, False)
SUM_TURN = (True, True)


class Routes:
    def __init__(self, sz):
        self.sz = sz
        self.z = [dz * sz.chips_y for dz in range(1, sz.zl)]
        self.y = list(range(1, sz.chips_y))
        self.turned = [dz + dy for dz in self.z for dy in self.y]
        self.arriving = [0] + self.z + self.y + self.turned
        self.leaving = self.turned + self.y + self.z + [0]

    def at(self, order, step):
        per = len(order) // 2
        firsts, seconds = order[0::2] * self.sz.images, order[1::2] * self.sz.images
        pieces = [p for p in range(self.sz.images) for _ in range(per)]
        return pick(step, firsts), pick(step, seconds), pick(step, pieces)


class Gather:
    def __init__(self, pc, buf, sems, turn):
        self.pc, self.buf, self.sems, self.turn = pc, buf, sems, turn
        self.routes = Routes(pc.sz)

    def move(self, back, piece, at, device):
        return send(self.buf.at[at, piece], self.buf.at[at, piece], self.sems.at[0, back, piece],
                    self.sems.at[1, back, piece], device)

    def start(self, piece, low):
        pc, routes = self.pc, self.routes
        self.buf[pc.chip, piece] = low
        for step in routes.z + routes.y + ([] if self.turn else routes.turned):
            self.move(step, piece, pc.chip, pc.device(pc.chip_at(step))).start()

    def ready(self, step):
        pc, sz = self.pc, self.pc.sz
        *chips, piece = self.routes.at(self.routes.arriving, step)
        places = []
        for back in chips:
            at = pc.index(pc.chip_back(back))
            when(back > 0, self.move(back, piece, at, pc.twin).wait_recv)
            if self.turn:
                for dz in self.routes.z:

                    def pass_on(dz=dz, at=at):
                        for dy in self.routes.y:
                            self.move(dz + dy, piece, at, pc.device(pc.chip_at(dy))).start()

                    when(back == dz, pass_on)
            places.append(at)
        tokens = jnp.concatenate([self.buf[at, piece] for at in places], axis=0)
        return [piece * sz.chips + at for at in places], tokens

    def finish(self):
        for piece in range(self.pc.sz.images):
            for back in self.routes.arriving[1:]:
                self.move(back, piece, self.pc.chip, self.pc.twin).wait_send()


class Scatter:
    def __init__(self, pc, bufs, sems, own_last, turn):
        self.pc, self.sems, self.turn = pc, sems, turn
        self.keep, self.hold, self.sent, self.got = bufs
        self.routes = Routes(pc.sz)
        self.order = self.routes.leaving if own_last else self.routes.arriving

    def far(self, back, piece):
        pc, sz = self.pc, self.pc.sz
        to = back
        if self.turn:
            if isinstance(back, int):
                to = back % sz.chips_y or back
            else:
                dy = lax.rem(back, jnp.int32(sz.chips_y))
                to = jnp.where(dy > 0, dy, back)
        return send(self.sent.at[back, piece], self.got.at[back, piece], self.sems.at[0, back, piece],
                    self.sems.at[1, back, piece], pc.device(pc.chip_back(to)))

    def units(self, step):
        pc = self.pc
        *chips, piece = self.routes.at(self.order, step)
        return [piece * pc.sz.chips + pc.index(pc.chip_back(back)) for back in chips]

    def push(self, step, partial):
        sz, part = self.pc.sz, self.pc.sz.part
        *chips, piece = self.routes.at(self.order, step)
        for i, back in enumerate(chips):
            terms = partial[i * part:(i + 1) * part]

            def own(terms=terms):
                self.keep[piece] = terms

            def leave(terms=terms, back=back):
                self.sent[back, piece] = terms.astype(bf16)
                self.far(back, piece).start()

            def hold(terms=terms, dz=None):
                self.hold[dz // sz.chips_y - 1] = terms

            when(back == 0, own)
            held = back < 0
            if self.turn:
                for dz in self.routes.z:
                    when(back == dz, functools.partial(hold, dz=dz))
                    held = held | (back == dz)
            when((back > 0) & jnp.logical_not(held), leave)
        if self.turn:
            per = sz.chips // 2
            for p in range(1, sz.images):
                when(step == p * per, functools.partial(self.merge, p - 1))

    def merge(self, piece):
        sz = self.pc.sz
        for dz in self.routes.z:
            total = self.hold[dz // sz.chips_y - 1]
            for dy in self.routes.y:
                self.far(dz + dy, piece).wait_recv()
                total = total + self.got[dz + dy, piece].astype(f32)
            self.sent[dz, piece] = total.astype(bf16)
            self.far(dz, piece).start()

    def flush(self):
        if self.turn:
            self.merge(self.pc.sz.images - 1)

    def finish(self, piece):
        total = self.keep[piece]
        for back in self.routes.z + self.routes.y + ([] if self.turn else self.routes.turned):
            self.far(back, piece).wait_recv()
            total = total + self.got[back, piece].astype(f32)
        for back in self.routes.arriving[1:]:
            self.far(back, piece).wait_send()
        return total


class Swap:
    def __init__(self, pc, src, dst, send_sem, recv_sem):
        self.copy = send(src, dst, send_sem, recv_sem, pc.twin)

    def start(self):
        self.copy.start()

    def wait(self):
        self.copy.wait()


def team_scratch(sz, phases):
    n = (sz.chips, sz.images)
    return [
        VMEM((sz.images, sz.part, sz.d), f32),
        VMEM((max(sz.zl - 1, 1), sz.part, sz.d), f32),
        VMEM(n + (sz.part, sz.d), bf16),
        VMEM(n + (sz.part, sz.d), bf16),
        DMA((phases, 2) + n),
        DMA((phases, 2) + n),
    ]


def normalised(values):
    centre = jnp.mean(values, axis=-1, keepdims=True)
    centred = values - centre
    spread = jnp.mean(centred * centred, axis=-1, keepdims=True)
    inverse = lax.rsqrt(spread + norm_eps)
    return centred * inverse, inverse


def norm_back(values, gain, grad):
    high, inverse = normalised(values)
    scaled = grad * gain
    term = inverse * (
        scaled
        - jnp.mean(scaled, axis=-1, keepdims=True)
        - high * jnp.mean(scaled * high, axis=-1, keepdims=True)
    )
    return term, jnp.sum(grad * high, axis=0, keepdims=True), jnp.sum(grad, axis=0, keepdims=True)


def lanes_of(shape):
    return lax.broadcasted_iota(jnp.int32, shape, len(shape) - 1)


def unpack_out(sz, w_ref, o_ref):
    at = 3 * sz.wide // 128 * 128
    shift = 3 * sz.wide - at

    def step(i, carry):
        rows = pl.ds(pl.multiple_of(i * 128, 128), 128)
        piece = pltpu.roll(w_ref[rows, at:at + sz.headp].astype(f32), sz.headp - shift, 1)
        o_ref[rows, :] = jnp.where(lanes_of(piece.shape) < sz.wide, piece, 0.0).astype(bf16)
        return carry

    lax.fori_loop(0, sz.d // 128, step, 0)


def take(sz, values, kind):
    at = kind * sz.wide // 128 * 128
    shift = kind * sz.wide - at
    piece = values[:, at:at + sz.headp]
    if shift:
        piece = pltpu.roll(piece, sz.headp - shift, 1)
    return jnp.where(lanes_of(piece.shape) < sz.wide, piece, 0.0)


def head_of(values, head):
    lanes = lanes_of(values.shape)
    mine = (lanes >= head * HEAD_DIM) & (lanes < (head + 1) * HEAD_DIM)
    return jnp.where(mine, values, jnp.zeros_like(values))


def probabilities(q_head, keys, valid):
    scores = jnp.where(valid > 0.0, dot(q_head, keys, (1, 1)), masked_score)
    high = jnp.max(scores, axis=-1, keepdims=True)
    weights = jnp.exp2((scores - high) * (HEAD_DIM ** (-0.5) * LOG2_E))
    return weights * (1.0 / jnp.sum(weights, axis=-1, keepdims=True))


class Jobs:
    def __init__(self, **places):
        self.places = places

    def run(self, place):
        for job in self.places.get(place, ()):
            job()

    def at(self, place, step):
        for when_step, jobs in self.places.get(place, {}).items():

            def run(jobs=jobs):
                for job in jobs:
                    job()

            when(step == when_step, run)


class Copies:
    def __init__(self, sems):
        self.sems, self.made = sems, []

    def start(self, src, dst):
        ident = len(self.made)
        self.made.append((src, dst))
        pltpu.make_async_copy(src, dst, self.sems.at[ident]).start()
        return ident

    def wait(self, idents=None):
        for ident in range(len(self.made)) if idents is None else idents:
            src, dst = self.made[ident]
            pltpu.make_async_copy(src, dst, self.sems.at[ident]).wait()


class Fetch:
    def __init__(self, pc, own, everything, sems, twin_sems, first=0):
        self.lanes = pl.ds(first, own.shape[-1])
        self.pc, self.own, self.all, self.sems, self.twin_sems = pc, own, everything, sems, twin_sems

    def rows(self, group, chunk):
        sz = self.pc.sz
        at = group * sz.wrowsp + chunk * sz.chunk
        return self.all.at[self.pc.k, pl.ds(pl.multiple_of(at, 16), sz.chunk), self.lanes]

    def own_rows(self, half, chunk):
        return self.own.at[half, pl.ds(chunk * self.pc.sz.chunk, self.pc.sz.chunk)]

    def along_ctx(self, step, chunk):
        pc = self.pc
        c = pc.ctx_ahead(step)
        return send(self.own_rows(c % pc.sz.zl, chunk), self.rows(pc.f * pc.sz.ctx + pc.c, chunk),
                    self.sems.at[chunk, 0, 0, step], self.sems.at[chunk, 0, 1, step], (pc.f, c, pc.t))

    def own_copy(self, chunk):
        pc = self.pc
        return pltpu.make_async_copy(self.own_rows(pc.zl, chunk), self.rows(pc.f * pc.sz.ctx + pc.c, chunk),
                                     self.sems.at[chunk, 0, 0, 0])

    def along_fsdp(self, jump, step, chunk):
        pc, sz = self.pc, self.pc.sz
        rows = self.rows(pc.f * sz.ctx + pc.ctx_back(step), chunk)
        return send(rows, rows, self.sems.at[chunk, jump, 0, step], self.sems.at[chunk, jump, 1, step],
                    ((pc.f + jump) % sz.fsdp, pc.c, pc.t))

    def to_twin(self, jump, step, chunk):
        pc, sz = self.pc, self.pc.sz
        rows = self.rows((pc.f + sz.fsdp - jump) % sz.fsdp * sz.ctx + pc.ctx_back(step), chunk)
        return send(rows, rows, self.twin_sems.at[chunk, jump, 0, step], self.twin_sems.at[chunk, jump, 1, step],
                    pc.twin)

    def depart(self, chunk):
        if chunk < self.pc.sz.chunks:
            self.own_copy(chunk).start()
            for step in range(self.pc.sz.ctx - 1, 0, -1):
                self.along_ctx(step, chunk).start()

    def turn(self, chunk):
        if chunk < self.pc.sz.chunks:
            for step in range(self.pc.sz.ctx):
                self.along_ctx(step, chunk).wait_recv() if step else self.own_copy(chunk).wait()
                for jump in range(1, self.pc.sz.fsdp):
                    self.along_fsdp(jump, step, chunk).start()
                self.to_twin(0, step, chunk).start()

    def land(self, chunk):
        if chunk < self.pc.sz.chunks:
            for step in range(self.pc.sz.ctx):
                for jump in range(1, self.pc.sz.fsdp):
                    self.along_fsdp(jump, step, chunk).wait_recv()
                    self.to_twin(jump, step, chunk).start()

    def jobs(self, parts):
        calls = {"d": self.depart, "t": self.turn, "l": self.land}
        return [functools.partial(calls[part[0]], int(part[1])) for part in parts.split()]

    def run(self, parts):
        for job in self.jobs(parts):
            job()

    def finish(self):
        sz = self.pc.sz
        for chunk in range(sz.chunks):
            for step in range(sz.ctx):
                if step:
                    self.along_ctx(step, chunk).wait_send()
                for jump in range(sz.fsdp):
                    if jump:
                        self.along_fsdp(jump, step, chunk).wait_send()
                    self.to_twin(jump, step, chunk).wait()


class Give:
    def __init__(self, pc, dw, recv, got, sems, first=0):
        self.lanes = pl.ds(first, recv.shape[-1])
        self.pc, self.dw, self.recv, self.got, self.sems = pc, dw, recv, got, sems
        self.order = list(range(pc.sz.ctx - 1, -1, -1))

    def rows(self, group, chunk):
        sz = self.pc.sz
        return pl.ds(pl.multiple_of(group * sz.wrowsp + chunk * sz.chunk, 16), sz.chunk)

    def part(self, chunk):
        return pl.ds(chunk * self.pc.sz.chunk, self.pc.sz.chunk)

    def along_fsdp(self, jump, step, chunk):
        pc, sz = self.pc, self.pc.sz
        f = (pc.f + jump) % sz.fsdp
        return send(self.dw.at[self.rows(f * sz.ctx + pc.ctx_ahead(step), chunk), self.lanes],
                    self.got.at[jump - 1, step, self.part(chunk)],
                    self.sems.at[chunk, jump, 0, step], self.sems.at[chunk, jump, 1, step], (f, pc.c, pc.t))

    def along_ctx(self, step, chunk, back=False):
        pc = self.pc
        there = pc.ctx_back(step) if back else pc.ctx_ahead(step)
        return send(self.got.at[0, step, self.part(chunk)],
                    self.recv.at[pc.ctx_back(step) if back else pc.c, self.part(chunk)],
                    self.sems.at[chunk, 0, 0, step], self.sems.at[chunk, 0, 1, step], (pc.f, there, pc.t))

    def own_copy(self, chunk):
        return pltpu.make_async_copy(self.got.at[0, 0, self.part(chunk)], self.recv.at[self.pc.c, self.part(chunk)],
                                     self.sems.at[chunk, 0, 0, 0])

    def depart(self, chunk):
        if chunk < self.pc.sz.chunks:
            for step in self.order:
                for jump in range(1, self.pc.sz.fsdp):
                    self.along_fsdp(jump, step, chunk).start()

    def turn(self, chunk):
        pc, sz = self.pc, self.pc.sz
        if chunk >= sz.chunks:
            return
        for step in self.order:
            for jump in range(1, sz.fsdp):
                self.along_fsdp(jump, step, chunk).wait_recv()
            total = self.dw[self.rows(pc.f * sz.ctx + pc.ctx_ahead(step), chunk), self.lanes].astype(f32)
            for jump in range(1, sz.fsdp):
                total = total + self.got[jump - 1, step, self.part(chunk)].astype(f32)
            self.got[0, step, self.part(chunk)] = total.astype(bf16)
            self.along_ctx(step, chunk).start() if step else self.own_copy(chunk).start()

    def jobs(self, parts):
        calls = {"d": self.depart, "t": self.turn}
        return [functools.partial(calls[part[0]], int(part[1])) for part in parts.split()]

    def run(self, parts):
        for job in self.jobs(parts):
            job()

    def finish(self):
        sz = self.pc.sz
        for chunk in range(sz.chunks):
            self.own_copy(chunk).wait()
            for step in range(sz.ctx):
                if step:
                    self.along_ctx(step, chunk, True).wait_recv()
                    self.along_ctx(step, chunk).wait_send()
                for jump in range(1, sz.fsdp):
                    self.along_fsdp(jump, step, chunk).wait_send()


def chosen(sz, group, lanes_shape):
    row = lax.broadcasted_iota(jnp.int32, lanes_shape, 0)
    col = lax.broadcasted_iota(jnp.int32, lanes_shape, 1)
    return jnp.where((row - group * sz.wrows == col) & (col < sz.wrows), 1.0, 0.0).astype(bf16)


def drop_padding(sz, src, dst):
    for at in range(0, dst.shape[-1], 128):
        lanes = slice(at, at + 128)

        def step(group, total):
            rows = pl.ds(pl.multiple_of(group * sz.wrowsp, 16), sz.wrowsp)
            return total + dot(chosen(sz, group, (sz.d, sz.wrowsp)), src[rows, lanes], (1, 0))

        dst[:, lanes] = lax.fori_loop(0, sz.groups, step, jnp.zeros((sz.d, 128), f32)).astype(bf16)


def add_padding(sz, src, dst):
    def step(group, carry):
        rows = pl.ds(pl.multiple_of(group * sz.wrowsp, 16), sz.wrowsp)
        for at in range(0, dst.shape[-1], 128):
            lanes = slice(at, at + 128)
            dst[rows, lanes] = dot(chosen(sz, group, (sz.d, sz.wrowsp)), src[:, lanes], (0, 0)).astype(bf16)
        return carry

    lax.fori_loop(0, sz.groups, step, 0)


def by_unit(sz, values):
    return jnp.swapaxes(values, 0, 1).reshape(sz.half, values.shape[-1])


def shift_lanes(values, start, count, at, width):
    have = values.shape[-1]
    first, last = start // 128 * 128, up_to(start + count, 128)
    to = at // 128 * 128
    span = max(last - first, up_to(at + count, 128) - to)
    piece = values[:, first:min(last, have)].astype(f32)
    if piece.shape[-1] < span:
        piece = jnp.pad(piece, ((0, 0), (0, span - piece.shape[-1])))
    turn = ((at - to) - (start - first)) % span
    if turn:
        piece = pltpu.roll(piece, turn, 1)
    lanes = lanes_of(piece.shape)
    piece = jnp.where((lanes >= at - to) & (lanes < at - to + count), piece, 0.0)
    piece = piece[:, 0:min(span, width - to)]
    return jnp.pad(piece, ((0, 0), (to, width - to - piece.shape[-1])))


def by_rows(sz, step):
    if sz.wrows % 16:
        step(slice(0, sz.wrows))
    else:

        def one(i, carry):
            step(pl.ds(pl.multiple_of(i * 16, 16), 16))
            return carry

        lax.fori_loop(0, sz.wrows // 16, one, 0)


def half_of(pc, values, count, width, at=0):
    out = shift_lanes(values, 0, count, at, width)
    for j in range(1, pc.sz.zl):
        out = jnp.where(pc.zl == j, shift_lanes(values, j * count, count, at, width), out)
    return out


def piece_of(pc, values):
    sz = pc.sz
    values = values.astype(f32)
    over = sz.tp * sz.part - sz.rows
    if over:
        values = jnp.concatenate([values, jnp.zeros((over, sz.d), f32)], axis=0)
    out = values[0:sz.part]
    for t in range(1, sz.tp):
        out = jnp.where(pc.t == t, values[t * sz.part:(t + 1) * sz.part], out)
    return out


def steps_below(values, unit, count):
    out = jnp.zeros_like(values)
    for m in range(1, count):
        out = out + jnp.where(values >= m * unit, 1, 0)
    return out


def key_valid(pc, count):
    sz = pc.sz
    row = lax.broadcasted_iota(jnp.int32, (1, sz.keys), 1)
    core = steps_below(row, sz.half, 2)
    within = row - core * sz.half
    unit = steps_below(within, sz.part, sz.units)
    piece = steps_below(unit, sz.chips, sz.images)
    chip = unit - piece * sz.chips
    zl = steps_below(chip, sz.chips_y, sz.zl)
    t = 2 * (chip - zl * sz.chips_y) + core
    token = t * sz.part + within - unit * sz.part
    position = (piece * sz.zl + zl) * sz.rows + token
    return jnp.where((token < sz.rows) & (position < count), 1.0, 0.0)


def own_valid(pc, count):
    sz = pc.sz
    shape = (sz.images, sz.part, 1)
    piece = lax.broadcasted_iota(jnp.int32, shape, 0)
    token = pc.t * sz.part + lax.broadcasted_iota(jnp.int32, shape, 1)
    position = (piece * sz.zl + pc.zl) * sz.rows + token
    return jnp.where((token < sz.rows) & (position < count), 1.0, 0.0)


def ff_lanes(sz, values):
    lanes = lanes_of(values.shape)
    return jnp.where((lanes >= sz.ff_at) & (lanes < sz.ff_at + sz.ff), values, 0.0)


def ride(sz, src, dst, src_at, dst_at):
    def step(i, carry):
        rows = pl.ds(pl.multiple_of(i * 128, 128), 128)
        there = src[rows, src_at:src_at + 128].astype(f32)
        here = dst[rows, dst_at:dst_at + 128].astype(f32) if dst_at else jnp.zeros_like(there)
        dst[rows, dst_at:dst_at + 128] = jnp.where(lanes_of(there.shape) >= sz.ff_at, there, here).astype(bf16)
        return carry

    if sz.spare:
        lax.fori_loop(0, src.shape[0] // 128, step, 0)


def rows_of(ref, units):
    return jnp.concatenate([ref[unit] for unit in units], axis=0)


def put_rows(sz, ref, units, values):
    for i, unit in enumerate(units):
        ref[unit] = values[i * sz.part:(i + 1) * sz.part]


def attn_forward(pc, jobs, gather, w_ref, qv_ref, valid_ref, q_ref, k_ref, v_ref, mixed_ref, o_ref, kv_sems,
                 scatter):
    sz = pc.sz
    for s in range(2):
        unpack_out(sz, w_ref.at[s], o_ref.at[s])

    def project(step, carry):
        units, tokens = gather.ready(step)

        def shard(s, none):
            both3 = dot(tokens, w_ref[s, :, 0:sz.qkvp], (1, 0))
            put_rows(sz, q_ref.at[s], units, (take(sz, both3, 0) + qv_ref[s, 0:1, 0:sz.headp]).astype(bf16))
            put_rows(sz, k_ref.at[s, pc.k], units, take(sz, both3, 1).astype(bf16))
            put_rows(sz, v_ref.at[s, pc.k], units, (take(sz, both3, 2) + qv_ref[s, 1:2, 0:sz.headp]).astype(bf16))
            return none

        lax.fori_loop(0, 2, shard, 0)
        jobs.at("project", step)
        return carry

    def swaps(piece):
        units = pl.ds(piece * sz.chips, sz.chips)
        return [Swap(pc, ref.at[s, pc.k, units], ref.at[s, pc.k, units], kv_sems.at[0, i, s, piece],
                     kv_sems.at[1, i, s, piece]) for s in range(2) for i, ref in enumerate((k_ref, v_ref))]

    per = sz.steps // sz.images
    for piece in range(sz.images):
        lax.fori_loop(piece * per, (piece + 1) * per, project, 0)
        for swap in swaps(piece):
            swap.start()
    gather.finish()
    for piece in range(sz.images):
        for swap in swaps(piece):
            swap.wait()

    def attend(step, carry):
        units = scatter.units(step)

        def shard(s, partial):
            keys = k_ref[s].reshape(sz.keys, sz.headp)
            values = v_ref[s].reshape(sz.keys, sz.headp)
            queries = rows_of(q_ref.at[s], units)
            total = jnp.zeros((sz.tile, sz.headp), f32)
            for head in range(sz.heads):
                probs = probabilities(head_of(queries, head), keys, valid_ref[...])
                total = total + dot(probs.astype(bf16), head_of(values, head), (1, 0))
            mixed = total.astype(bf16)
            put_rows(sz, mixed_ref.at[s], units, mixed)
            return partial + dot(mixed, o_ref[s], (1, 1))

        partial = lax.fori_loop(0, 2, shard, jnp.zeros((sz.tile, sz.d), f32))
        scatter.push(step, partial)
        jobs.at("attend", step)
        return carry

    lax.fori_loop(0, sz.steps, attend, 0)
    jobs.run("turnover")
    scatter.flush()
    jobs.run("flush")


def ff_forward(pc, jobs, gather, w_ref, upb_ref, pre_ref, hidden_ref, scatter):
    sz = pc.sz

    def feed(step, carry):
        units, tokens = gather.ready(step)

        def shard(s, partial):
            pre = dot(tokens, w_ref[s, :, 0:sz.ffp], (1, 0)) + upb_ref[s, 2:3, 0:sz.ffp]
            put_rows(sz, pre_ref.at[s], units, pre)
            hidden = 0.5 * pre * (1.0 + jnp.tanh(gelu_root * (pre + gelu_cubic * pre * pre * pre)))
            hidden = ff_lanes(sz, hidden)
            if sz.down_shift != sz.ff_at:
                hidden = pltpu.roll(hidden, (sz.down_shift - sz.ff_at) % sz.ffp, 1)
            hidden = hidden.astype(bf16)
            put_rows(sz, hidden_ref.at[s], units, hidden)
            return partial + dot(hidden, w_ref[s, :, sz.down_at:], (1, 1))

        partial = lax.fori_loop(0, 2, shard, jnp.zeros((sz.tile, sz.d), f32))
        scatter.push(step, partial)
        jobs.at("feed", step)
        return carry

    lax.fori_loop(0, sz.steps, feed, 0)
    jobs.run("flush")
    gather.finish()


def plan(steps, more_steps, flush, what, ff, attn):
    for place, ff_parts, attn_parts in what:
        jobs = (ff.jobs(ff_parts) if ff else []) + (attn.jobs(attn_parts) if attn else [])
        if place == "f":
            flush.extend(jobs)
        else:
            table = steps if place[0] == "s" else more_steps
            table[int(place[1])] = table.get(int(place[1]), []) + jobs


def planned(what, give):
    steps = {}
    plan(steps, None, None, what, give, None)
    return steps


GIVE_FF = (("s0", "", "t0"), ("s1", "", "d2 t1"), ("s3", "", "t2"))
GIVE_ATTN = (("s0", "t0", ""), ("s1", "d2", ""), ("s2", "t1", ""), ("s3", "t2", ""))
PLAN_ATTN_FIRST = (("s0", "d2", ""), ("s3", "t1", ""), ("m0", "l0", ""), ("m1", "", "d0"), ("m2", "t2 l1", ""),
                   ("m3", "", "d1"), ("f", "l2", "d2 t0"))
PLAN_ATTN = (("s1", "t1", "d0"), ("s2", "d2", ""), ("s3", "l0", ""), ("m0", "", "d1"), ("m1", "t2 l1", ""),
             ("m3", "", "d2"), ("f", "l2", "t0"))
PLAN_FF = (("s0", "d0", "t1 l0"), ("s1", "d1", "t2"), ("s2", "t0", "l1"), ("s3", "", "l2"))


def norm_low(values, gain, shift):
    high, _ = normalised(values)
    return (high * gain + shift).astype(bf16)


def forward_kernel(sz, *refs):
    n = sz.layers
    aligned = sz.wrowsp == sz.wrows
    ins, outs, scratch = refs[:12], refs[12:12 + 13 * n + 1], refs[12 + 13 * n + 1:]
    (count_ref, in_ref, cot_ref, wqkv_ref, wout_ref, wup_ref, wdown_ref, gain_ref, shift_ref, qv_ref, upb_ref,
     resid_ref) = ins
    saved, (wattn_outs, wff_outs, ends_ref) = outs[:11 * n], split_refs(outs[11 * n:], n, n, 1)
    saved = [saved[l * 11:(l + 1) * 11] for l in range(n)]
    ends_ref = ends_ref[0]
    (own_attn, own_ff, all_attn, all_ff, swap_ref, mine_ref, n_ref, q_ref, k_ref, v_ref, mixed_ref, pre_ref,
     hidden_ref, stream_ref, middle_ref, valid_ref, o_ref, bias_ref, tsems, csems, wsems, vsems, kv_sems,
     bsems), team, joined = split_refs(scratch, 24, 6, 0 if aligned else 2)
    bufs, (gsems, ssems) = team[:4], team[4:]
    pc = Place(sz)
    greeting = Greeting(team_peers(pc) + weight_peers(pc, True))

    def pack(ref, pieces):
        def step(rows):
            total = None
            for values, start, count, at in pieces:
                piece = shift_lanes(values[rows, :], start, count, at, ref.shape[-1])
                total = piece if total is None else total + piece
            ref[rows, :] = total.astype(bf16)

        by_rows(sz, step)
        if not aligned:
            ref[sz.wrows:, :] = jnp.zeros((sz.wrowsp - sz.wrows, ref.shape[-1]), bf16)

    def pack_attn(layer):
        for half in range(sz.zl):
            pieces = [(wqkv_ref.at[layer, kind], half * sz.wide, sz.wide, kind * sz.wide) for kind in range(3)]
            pieces += [(wout_ref.at[layer], half * sz.wide, sz.wide, 3 * sz.wide)]
            if sz.spare:
                pieces += [(wup_ref.at[layer], half * sz.ff, sz.spare, 4 * sz.wide)]
            pack(own_attn.at[layer, half], pieces)

    def pack_ff(layer):
        for half in range(sz.zl):
            rest = sz.ff - sz.spare
            pack(own_ff.at[layer, half], [(wup_ref.at[layer], half * sz.ff + sz.spare, rest, 0),
                                          (wdown_ref.at[layer], half * sz.ff, sz.ff, rest)])

    for image in range(sz.images):
        swap_ref[image, 0] = piece_of(pc, in_ref[image]).astype(bf16)
        swap_ref[image, 1] = piece_of(pc, cot_ref[image]).astype(bf16)
    pack_attn(0)
    attn = [Fetch(pc, own_attn.at[l], all_attn.at[l], wsems.at[2 * l], vsems.at[2 * l]) for l in range(n)]
    ff = [Fetch(pc, own_ff.at[l], all_ff.at[l], wsems.at[2 * l + 1], vsems.at[2 * l + 1], sz.ff_sent)
          for l in range(n)]
    bias_ref[:, pc.k] = jnp.zeros((n, 8, bias_ref.shape[-1]), f32)
    for l in range(n):
        bias_ref[l, pc.k, 0:2, 0:sz.headp] = half_of(pc, qv_ref[l], sz.wide, sz.headp)
        bias_ref[l, pc.k, 2:3, 0:sz.ffp] = half_of(pc, upb_ref[l:l + 1, :], sz.ff, sz.ffp, sz.ff_at)
    bias_swaps = [Swap(pc, bias_ref.at[l, pc.k], bias_ref.at[l, pc.k], bsems.at[0, l], bsems.at[1, l])
                  for l in range(n)]
    copies = Copies(csems)

    def swap(step):
        zh = (pc.zh + step) % sz.images
        return send(swap_ref.at[zh], mine_ref.at[pc.zh], tsems.at[0, step], tsems.at[1, step],
                    (pc.f, zh * sz.zl + pc.zl, pc.t))

    greeting.wait()
    for step in range(1, sz.images):
        swap(step).start()
    attn[0].run("d0 d1 d2")
    for move in bias_swaps:
        move.start()
    mine_ref[pc.zh] = swap_ref[pc.zh]
    count = count_ref[pc.zh]
    valid_ref[...] = key_valid(pc, count)
    for step in range(1, sz.images):
        swap(step).wait()
    stream_ref[0] = mine_ref[:, 0].astype(f32)
    gathers = [Gather(pc, n_ref.at[i], gsems.at[i], FORWARD_TURN[i % 2]) for i in range(2 * n)]
    scatters = [Scatter(pc, bufs, ssems.at[i], i % 2 == 0, i % 2 == 0 and SUM_TURN[0]) for i in range(2 * n)]
    for p in range(sz.images):
        gathers[0].start(p, norm_low(stream_ref[0, p], gain_ref[0, 0:1, :], shift_ref[0, 0:1, :]))
    pack_ff(0)
    attn[0].run("t0")
    ff[0].run("d0")
    for layer in range(1, n):
        pack_attn(layer)
    attn[0].run("t1")
    ff[0].run("d1")
    ends_ref[...] = mine_ref[:, 1].astype(f32) * own_valid(pc, count)
    attn[0].run("l0 t2")
    for layer in range(1, n):
        pack_ff(layer)
    attn[0].run("l1")
    ff[0].run("t0")
    attn[0].run("l2")
    for move in bias_swaps:
        move.wait()
    attn[0].finish()

    def ready(fetch, refs, kind, layer, out):
        ref = refs.at[layer]
        if not aligned:
            for s in range(2):
                drop_padding(sz, ref.at[s], joined[kind].at[s])
            ref = joined[kind]
            pltpu.sync_copy(ref, out)
        else:
            copies.start(ref, out)
        return ref

    def after_attn(l, p):
        def run():
            middle = stream_ref[l, p] + (scatters[2 * l].finish(p) + resid_ref[l, 0:1, :])
            middle_ref[l, p] = middle
            gathers[2 * l + 1].start(p, norm_low(middle, gain_ref[l, 1:2, :], shift_ref[l, 1:2, :]))

        return run

    def after_ff(l, p):
        def run():
            out = middle_ref[l, p] + (scatters[2 * l + 1].finish(p) + resid_ref[l, 1:2, :])
            stream_ref[l + 1, p] = out
            if l + 1 < n:
                gathers[2 * l + 2].start(p, norm_low(out, gain_ref[l + 1, 0:1, :], shift_ref[l + 1, 0:1, :]))

        return run

    per = sz.steps // sz.images
    rest = range(1, sz.images)
    for l in range(n):
        more = l + 1 < n
        w = ready(attn[l], all_attn, 0, l, wattn_outs[l])
        project = {p * per - 1: [after_ff(l - 1, p)] for p in rest} if l else {}
        attend, flush = {}, []
        plan(project, attend, flush, PLAN_ATTN_FIRST if l == 0 else PLAN_ATTN, ff[l], attn[l + 1] if more else None)
        jobs = Jobs(project=project, attend=attend, flush=flush, turnover=[after_attn(l, 0)])
        attn_forward(pc, jobs, gathers[2 * l], w, bias_ref.at[l], valid_ref, q_ref.at[l], k_ref.at[l], v_ref.at[l],
                     mixed_ref.at[l], o_ref, kv_sems.at[l], scatters[2 * l])
        for ref, to in ((stream_ref.at[l], 0), (n_ref.at[2 * l], 2), (q_ref.at[l], 4), (k_ref.at[l], 5),
                        (v_ref.at[l], 6), (mixed_ref.at[l], 7)):
            copies.start(ref, saved[l][to])
        ff[l].finish()
        for core in range(2):
            ride(sz, all_attn.at[l, core], all_ff.at[l, core], 4 * sz.wide - sz.ff_at, 0)
        w = ready(ff[l], all_ff, 1, l, wff_outs[l])
        feed = {(p - 1) * per: [after_attn(l, p)] for p in rest}
        if more:
            plan(feed, None, None, PLAN_FF, ff[l + 1], attn[l + 1])
        feed[FF_OVER] = [after_ff(l, 0)] + feed.get(FF_OVER, [])
        ff_forward(pc, Jobs(feed=feed), gathers[2 * l + 1], w, bias_ref.at[l], pre_ref.at[l],
                   hidden_ref.at[l], scatters[2 * l + 1])
        if more:
            attn[l + 1].finish()
        else:
            for p in rest:
                after_ff(l, p)()
        for ref, to in ((middle_ref.at[l], 1), (n_ref.at[2 * l + 1], 3), (pre_ref.at[l], 8), (hidden_ref.at[l], 9)):
            copies.start(ref, saved[l][to])
    copies.start(stream_ref.at[n], saved[0][10])
    copies.start(valid_ref, saved[n - 1][10])
    copies.wait()


def forward_call(sz, *operands):
    n = sz.layers
    own, team = ((sz.images, sz.part, sz.d), f32), ((sz.chips, sz.images, sz.part, sz.d), bf16)
    head, pair = (2, sz.units, sz.part, sz.headp), (2, 2, sz.units, sz.part, sz.headp)
    hidden = (2, sz.units, sz.part, sz.ffp)
    shapes = []
    for l in range(n):
        last = ((1, sz.keys), f32) if l == n - 1 else own
        shapes += [own, own, team, team, (head, bf16), (pair, bf16), (pair, bf16), (head, bf16), (hidden, f32),
                   (hidden, bf16), last]
    shapes += [((2, sz.d, sz.attnp), bf16)] * n + [((2, sz.d, sz.ffw), bf16)] * n + [own]
    vmem, hbm = pl.BlockSpec(memory_space=pltpu.VMEM), pl.BlockSpec(memory_space=pl.ANY)
    padded = sz.groups * sz.wrowsp
    scratch = [
        VMEM((n, sz.zl, sz.wrowsp, sz.attnp), bf16), VMEM((n, sz.zl, sz.wrowsp, sz.ffs), bf16),
        VMEM((n, 2, padded, sz.attnp), bf16), VMEM((n, 2, padded, sz.ffw), bf16),
        VMEM((sz.images, 2, sz.part, sz.d), bf16), VMEM((sz.images, 2, sz.part, sz.d), bf16),
        VMEM((2 * n,) + team[0], bf16),
        VMEM((n,) + head, bf16), VMEM((n,) + pair, bf16), VMEM((n,) + pair, bf16), VMEM((n,) + head, bf16),
        VMEM((n,) + hidden, f32), VMEM((n,) + hidden, bf16),
        VMEM((n + 1,) + own[0], f32), VMEM((n,) + own[0], f32), VMEM((1, sz.keys), f32),
        VMEM((2, sz.d, sz.headp), bf16), VMEM((n, 2, 8, max(sz.headp, sz.ffp)), f32),
        DMA((2, sz.images)), DMA((12 * n + 2,)), DMA((2 * n, sz.chunks, sz.fsdp, 2, sz.ctx)),
        DMA((2 * n, sz.chunks, sz.fsdp, 2, sz.ctx)), DMA((n, 2, 2, 2, sz.images)), DMA((2, n)),
    ] + team_scratch(sz, 2 * n)
    if sz.wrowsp != sz.wrows:
        scratch += [VMEM((2, sz.d, sz.attnp), bf16), VMEM((2, sz.d, sz.ffw), bf16)]
    return pl.pallas_call(
        functools.partial(forward_kernel, sz),
        out_shape=[jax.ShapeDtypeStruct(*s) for s in shapes],
        in_specs=[pl.BlockSpec(memory_space=pltpu.SMEM)] + [vmem] * (len(operands) - 1),
        out_specs=[hbm] * (len(shapes) - 1) + [vmem],
        scratch_shapes=scratch,
        compiler_params=params(1),
        name="forward",
    )(*operands)


def params(collective_id):
    return pltpu.CompilerParams(
        collective_id=collective_id, has_side_effects=True, vmem_limit_bytes=63 * 1024 * 1024
    )


class Twins:
    def __init__(self, pc, dw, got, sems, span):
        self.pc, self.dw, self.got, self.sems, self.span = pc, dw, got, sems, span
        self.count = pc.sz.d // span

    def copy(self, i):
        rows = pl.ds(pl.multiple_of(i * self.span, 128), self.span)
        return send(self.dw.at[1 - self.pc.k, rows], self.got.at[rows], self.sems.at[0, i], self.sems.at[1, i],
                    self.pc.twin)

    def put(self, core, i, pieces):
        rows = pl.ds(pl.multiple_of(i * self.span, 128), self.span)
        for at, values in pieces:
            self.dw[core, rows, at:at + values.shape[-1]] = values.astype(bf16)

    def run(self, make, jobs, between=None):
        def other(i, carry):
            self.put(1 - self.pc.k, i, make(1 - self.pc.k, i))
            self.copy(i).start()
            return carry

        def own(i, carry):
            self.put(self.pc.k, i, make(self.pc.k, i))
            jobs.at("step_grads", i)
            return carry

        def add(i, carry):
            self.copy(i).wait_recv()
            rows = pl.ds(pl.multiple_of(i * self.span, 128), self.span)
            self.dw[self.pc.k, rows, :] = (
                self.dw[self.pc.k, rows, :].astype(f32) + self.got[rows, :].astype(f32)
            ).astype(bf16)
            self.copy(i).wait_send()
            return carry

        lax.fori_loop(0, self.count, other, 0)
        if between:
            between()
        lax.fori_loop(0, self.count, own, 0)
        lax.fori_loop(0, self.count, add, 0)


def ff_backward(pc, jobs, gather, w_ref, n2_ref, pre_ref, hidden_ref, dup_ref, pg_ref, twins, scatter):
    sz = pc.sz
    dup_ref[...] = jnp.zeros_like(dup_ref)

    def feed(step, carry):
        units, tokens = gather.ready(step)

        def shard(s, partial):
            back = dot(tokens, w_ref[s, :, sz.down_at:], (1, 0))
            if sz.down_shift != sz.ff_at:
                back = pltpu.roll(back, (sz.ff_at - sz.down_shift) % sz.ffp, 1)
            pre = rows_of(pre_ref.at[s], units)
            bent = jnp.tanh(gelu_root * (pre + gelu_cubic * pre * pre * pre))
            slope = 0.5 * (1.0 + bent) + 0.5 * pre * (1.0 - bent * bent) * (
                gelu_root * (1.0 + 3.0 * gelu_cubic * pre * pre)
            )
            pre_grad = ff_lanes(sz, back * slope).astype(bf16)
            put_rows(sz, pg_ref.at[s], units, pre_grad)
            dup_ref[s] += jnp.sum(pre_grad.astype(f32), axis=0, keepdims=True)
            return partial + dot(pre_grad, w_ref[s, :, 0:sz.ffp], (1, 1))

        partial = lax.fori_loop(0, 2, shard, jnp.zeros((sz.tile, sz.d), f32))
        scatter.push(step, partial)
        jobs.at("feed", step)
        return carry

    lax.fori_loop(0, sz.steps, feed, 0)
    jobs.run("flush")

    def make(core, i):
        lanes = pl.ds(pl.multiple_of(i * twins.span, 128), twins.span)
        hidden = hidden_ref[core].reshape(sz.half, sz.ffp)
        down = dot(by_unit(sz, gather.buf[:, :, :, lanes]), hidden, (0, 0))
        pre_grad = pg_ref[core].reshape(sz.half, sz.ffp)
        up = dot(by_unit(sz, n2_ref[:, :, :, lanes]), pre_grad, (0, 0))
        over = sz.ffp - sz.down_at
        both = [(sz.down_at, up[:, sz.down_at:] + down[:, 0:over])] if over else []
        return [(0, up[:, 0:sz.down_at])] + both + [(sz.ffp, down[:, over:])]

    twins.run(make, jobs)
    jobs.run("grads")
    gather.finish()


def attn_backward(pc, jobs, gather, w_ref, n1_ref, q_ref, k_ref, v_ref, mixed_ref, valid_ref, dqv_ref,
                  o_ref, dkv_ref, kvsend_ref, kvgot_ref, stack_ref, kv_sems, twins, scatter):
    sz = pc.sz
    for s in range(2):
        unpack_out(sz, w_ref.at[s], o_ref.at[s])
    dkv_ref[...] = jnp.zeros_like(dkv_ref)
    dqv_ref[...] = jnp.zeros_like(dqv_ref)
    scale = HEAD_DIM ** (-0.5)

    def attend(step, carry):
        units, tokens = gather.ready(step)

        def shard(s, none):
            mixed_grad = dot(tokens, o_ref[s], (1, 0)).astype(bf16)
            keys = k_ref[s].reshape(sz.keys, sz.headp)
            values = v_ref[s].reshape(sz.keys, sz.headp)
            queries = rows_of(q_ref.at[s], units)
            total = jnp.zeros((sz.tile, sz.headp), f32)
            dkey, dvalue = None, None
            for head in range(sz.heads):
                q_head = head_of(queries, head)
                g_head = head_of(mixed_grad, head)
                probs = probabilities(q_head, keys, valid_ref[...])
                dprobs = dot(g_head, values, (1, 1))
                inner = jnp.sum(probs * dprobs, axis=-1, keepdims=True)
                dscores = (probs * (dprobs - inner)).astype(bf16)
                total = total + dot(dscores, head_of(keys, head), (1, 0))
                dk, dv = dot(dscores, q_head, (0, 0)), dot(probs.astype(bf16), g_head, (0, 0))
                dkey = dk if dkey is None else dkey + dk
                dvalue = dv if dvalue is None else dvalue + dv
            dkv_ref[s, 0] += dkey.reshape(2, sz.half, sz.headp)
            dkv_ref[s, 1] += dvalue.reshape(2, sz.half, sz.headp)
            dq = (scale * total).astype(bf16).astype(f32)
            dqv_ref[s, 0:1, :] += jnp.sum(dq, axis=0, keepdims=True)
            dq = dq.astype(bf16)
            for i, unit in enumerate(units):
                stack_ref[s, unit, :, 0:sz.headp] = dq[i * sz.part:(i + 1) * sz.part]
            return none

        lax.fori_loop(0, 2, shard, 0)
        jobs.at("attend", step)
        return carry

    lax.fori_loop(0, sz.steps, attend, 0)
    for s in range(2):
        kvsend_ref[s] = dkv_ref[s, :, 1 - pc.k].astype(bf16)
    moves = [Swap(pc, kvsend_ref.at[s], kvgot_ref.at[s], kv_sems.at[0, s], kv_sems.at[1, s]) for s in range(2)]
    for move in moves:
        move.start()
    gather.finish()
    jobs.run("middle")
    for move in moves:
        move.wait()

    def back_project(step, carry):
        units = scatter.units(step)

        def shard(s, partial):

            def both(kind):
                rows = [pl.ds(pl.multiple_of(unit * sz.part, sz.part), sz.part) for unit in units]
                return jnp.concatenate(
                    [dkv_ref[s, kind, pc.k, r, :] + kvgot_ref[s, kind, r, :].astype(f32) for r in rows], axis=0
                )

            dk = (scale * both(0)).astype(bf16).astype(f32)
            dv = both(1).astype(bf16).astype(f32)
            dqv_ref[s, 1:2, :] += jnp.sum(dv, axis=0, keepdims=True)
            dq = rows_of(stack_ref.at[s], units)[:, 0:sz.headp].astype(f32)
            total = jnp.pad(dq, ((0, 0), (0, sz.qkvp - sz.headp)))
            for kind, piece in ((1, dk), (2, dv)):
                start = kind * sz.wide // 128 * 128
                shift = kind * sz.wide - start
                moved = pltpu.roll(piece, shift, 1) if shift else piece
                total = total + jnp.pad(moved, ((0, 0), (start, sz.qkvp - start - sz.headp)))
            stacked = total.astype(bf16)
            put_rows(sz, stack_ref.at[s], units, stacked)
            return partial + dot(stacked, w_ref[s, :, 0:sz.qkvp], (1, 1))

        partial = lax.fori_loop(0, 2, shard, jnp.zeros((sz.tile, sz.d), f32))
        scatter.push(step, partial)
        return carry

    lax.fori_loop(0, sz.steps, back_project, 0)
    jobs.run("flush")
    o_at = 3 * sz.wide // 128 * 128
    o_shift = 3 * sz.wide - o_at

    def make(core, i):
        lanes = pl.ds(pl.multiple_of(i * twins.span, 128), twins.span)
        stacked = stack_ref[core].reshape(sz.half, sz.qkvp)
        dqkv = dot(by_unit(sz, n1_ref[:, :, :, lanes]), stacked, (0, 0))
        mixed = mixed_ref[core].reshape(sz.half, sz.headp)
        dout = dot(by_unit(sz, gather.buf[:, :, :, lanes]), mixed, (0, 0))
        if o_shift:
            dout = pltpu.roll(dout, o_shift, 1)
        total = jnp.pad(dqkv, ((0, 0), (0, sz.attnp - sz.qkvp))) + jnp.pad(
            dout, ((0, 0), (o_at, sz.attnp - o_at - sz.headp))
        )
        return [(0, total)]

    twins.run(make, jobs, scatter.flush)
    jobs.run("grads")


def backward_kernel(sz, *refs):
    n = sz.layers
    aligned = sz.wrowsp == sz.wrows
    saved = [refs[l * 11:(l + 1) * 11] for l in range(n)]
    wattn_ins, wff_ins, (cot_ref, gain_ref), outs, scratch = split_refs(
        refs[11 * n:], n, n, 2, 2 * n + 2, len(refs) - 11 * n - 2 * n - 2 - 2 * n - 2)
    attn_outs, ff_outs, (whole_ref, small_ref) = split_refs(outs, n, n, 2)
    (stream_ref, middle_ref, n1_ref, n2_ref, q_ref, k_ref, v_ref, mixed_ref, pre_ref, hidden_ref, valid_ref, out_ref,
     wattn_ref, wff_ref, gl_ref, ml_ref, pg_ref, o_ref, dkv_ref, kvsend_ref, kvgot_ref, stack_ref, dwattn_ref,
     dwff_ref, twattn_ref, twff_ref, got_attn, got_ff, dqv_ref, dup_ref, grad_ref, ends_ref, first, from_tp, from_ctx,
     from_fsdp, sum_tp, sum_ctx, share_ref, shgot_ref, lsems, wsems, esems, ysems, tsems, kv_sems, twsems,
     shsems), team, padded = split_refs(scratch, 48, 6, 0 if aligned else 2)
    bufs, (gsems, ssems) = team[:4], team[4:]
    pc = Place(sz)
    greeting = Greeting(team_peers(pc) + weight_peers(pc, True) + line_peers(pc))
    copies = Copies(lsems)
    into = [stream_ref, middle_ref, n1_ref, n2_ref, q_ref, k_ref, v_ref, mixed_ref, pre_ref, hidden_ref]

    def load(l, weights, ref, kinds):
        return [copies.start(weights[l], ref)] + [copies.start(saved[l][kind], into[kind]) for kind in kinds]

    def load_ff(l):
        return load(l, wff_ins, wff_ref, (8, 3, 9, 1))

    def load_attn(l):
        return load(l, wattn_ins, wattn_ref, (4, 5, 6, 7, 2, 0))

    out_load = copies.start(saved[0][10], out_ref)
    ff_loads, attn_loads = load_ff(n - 1), load_attn(n - 1)
    attn_loads.append(copies.start(saved[n - 1][10], valid_ref))
    own_attn, own_ff = dwattn_ref.at[pc.k], dwff_ref.at[pc.k]
    give_attn = [Give(pc, own_attn if aligned else padded[0], attn_outs[l], got_attn.at[l], wsems.at[2 * l])
                 for l in range(n)]
    give_ff = [Give(pc, own_ff if aligned else padded[1], ff_outs[l], got_ff.at[l], wsems.at[2 * l + 1], sz.ff_sent)
               for l in range(n)]

    def begin(give, dw, kind):
        def run():
            if kind == 0:
                ride(sz, own_ff, dw, 0, 4 * sz.wide - sz.ff_at)
            if not aligned:
                add_padding(sz, dw, padded[kind])
            give.run("d0 d1")

        return run

    def swap(kind, step):
        zh = (pc.zh + step) % sz.images
        return send(ends_ref.at[kind, zh], whole_ref.at[kind, pc.t, pc.zh], esems.at[kind, 0, step],
                    esems.at[kind, 1, step], (pc.f, zh * sz.zl + pc.zl, pc.t))

    def own_end(kind):
        return pltpu.make_async_copy(ends_ref.at[kind, pc.zh], whole_ref.at[kind, pc.t, pc.zh], esems.at[kind, 0, 0])

    def spread(kind, step):
        return send(whole_ref.at[kind, pc.t], whole_ref.at[kind, pc.t], ysems.at[kind, 0, step],
                    ysems.at[kind, 1, step], (pc.f, pc.c, (pc.t + step) % sz.tp))

    def spread_from(kind, step):
        back = (pc.t + sz.tp - step) % sz.tp
        return send(whole_ref.at[kind, back], whole_ref.at[kind, back], ysems.at[kind, 0, step],
                    ysems.at[kind, 1, step], (pc.f, pc.c, back))

    def swap_start(kind):
        own_end(kind).start()
        for step in range(1, sz.images):
            swap(kind, step).start()

    def spread_start(kind):
        own_end(kind).wait()
        for step in range(1, sz.images):
            swap(kind, step).wait()
        for step in range(1, sz.tp):
            spread(kind, step).start()

    def spread_wait(kind):
        for step in range(1, sz.tp):
            spread_from(kind, step).wait_recv()
            spread(kind, step).wait_send()

    def over_tp(step):
        return send(first, from_tp.at[step - 1], tsems.at[0, 0, step], tsems.at[0, 1, step],
                    (pc.f, pc.c, (pc.t + step) % sz.tp))

    def over_ctx(step):
        return send(sum_tp, from_ctx.at[step - 1], tsems.at[1, 0, step], tsems.at[1, 1, step],
                    (pc.f, pc.ctx_ahead(step), pc.t))

    def over_fsdp(step):
        return send(sum_ctx, from_fsdp.at[step - 1], tsems.at[2, 0, step], tsems.at[2, 1, step],
                    ((pc.f + step) % sz.fsdp, pc.c, pc.t))

    sum_tp[...] = jnp.zeros_like(sum_tp)
    share_ref[...] = jnp.zeros_like(share_ref)
    first[...] = jnp.zeros_like(first)
    copies.wait([out_load])
    ends_ref[0] = out_ref[...].astype(bf16)
    grad_ref[...] = cot_ref[...]
    gathers = [Gather(pc, (gl_ref, ml_ref)[i % 2], gsems.at[i], BACKWARD_TURN[1 - i % 2]) for i in range(2 * n)]
    scatters = [Scatter(pc, bufs, ssems.at[i], i % 2 == 1, i % 2 == 1 and SUM_TURN[1]) for i in range(2 * n)]
    def low_of(l, p, row):
        low = grad_ref[p].astype(bf16)
        first[l, row:row + 1, :] += jnp.sum(low.astype(f32), axis=0, keepdims=True)
        return low

    def after_ff(l, p):
        def run():
            turn = n - 1 - l
            term, dgain, dshift = norm_back(middle_ref[p], gain_ref[l, 1:2, :], scatters[2 * turn].finish(p))
            grad_ref[p] += term
            gathers[2 * turn + 1].start(p, low_of(l, p, 4))
            first[l, 1:2, :] += dgain
            first[l, 3:4, :] += dshift

        return run

    def after_attn(l, p):
        def run():
            turn = n - 1 - l
            term, dgain, dshift = norm_back(stream_ref[p], gain_ref[l, 0:1, :], scatters[2 * turn + 1].finish(p))
            grad_ref[p] += term
            if l:
                gathers[2 * turn + 2].start(p, low_of(l - 1, p, 5))
            else:
                ends_ref[1, p] = grad_ref[p].astype(bf16)
            first[l, 0:1, :] += dgain
            first[l, 2:3, :] += dshift

        return run

    greeting.wait()
    per, rest = sz.steps // sz.images, range(1, sz.images)
    span = 384 if sz.d % 384 == 0 else 128
    for p in range(sz.images):
        gathers[0].start(p, low_of(n - 1, p, 5))
    swap_start(0)
    for turn in range(n):
        l = n - 1 - turn
        start = turn == 0
        copies.wait(ff_loads)
        feed = {}
        if start:
            feed[1] = [lambda: spread_start(0)]
        else:
            after = give_attn[l + 1]
            feed.update({(p - 1) * per: [after_attn(l + 1, p)] for p in rest})
            feed[(sz.images - 2) * per] = feed[(sz.images - 2) * per] + [lambda: attn_loads.extend(load_attn(l))]
            plan(feed, None, None, GIVE_FF, None, after)
        feed[FF_OVER] = [after_ff(l, 0)] + feed.get(FF_OVER, [])
        jobs = Jobs(feed=feed, flush=([] if start else [give_ff[l + 1].finish]),
                    grads=[begin(give_ff[l], own_ff, 1)] + [after_ff(l, p) for p in rest])
        twins = Twins(pc, dwff_ref, twff_ref, twsems.at[2 * l + 1], span)
        ff_backward(pc, jobs, gathers[2 * turn], wff_ref, n2_ref, pre_ref, hidden_ref, dup_ref, pg_ref, twins,
                    scatters[2 * turn])
        for core in range(2):
            share_ref[core, 3 * l + 2:3 * l + 3, 0:sz.ffp] = dup_ref[core]
        copies.wait(attn_loads)
        del attn_loads[:]
        if l:
            ff_loads = load_ff(l - 1)
        if start:
            spread_wait(0)
        now = give_ff[l]
        jobs = Jobs(
            attend=planned(GIVE_ATTN, now),
            flush=([] if start else [give_attn[l + 1].finish]),
            step_grads={0: [after_attn(l, 0)]}, grads=[begin(give_attn[l], own_attn, 0)],
        )
        twins = Twins(pc, dwattn_ref, twattn_ref, twsems.at[2 * l], span)
        attn_backward(pc, jobs, gathers[2 * turn + 1], wattn_ref, n1_ref, q_ref, k_ref, v_ref, mixed_ref, valid_ref,
                      dqv_ref, o_ref, dkv_ref, kvsend_ref, kvgot_ref, stack_ref, kv_sems.at[l], twins,
                      scatters[2 * turn + 1])
        for core in range(2):
            share_ref[core, 3 * l:3 * l + 2, 0:sz.headp] = dqv_ref[core]
    share = Swap(pc, share_ref.at[1 - pc.k], shgot_ref, shsems.at[0], shsems.at[1])
    share.start()
    for p in rest:
        after_attn(0, p)()
    last = give_attn[0]
    swap_start(1)
    for step in range(1, sz.tp):
        over_tp(step).start()
    last.run("d2 t0")
    spread_start(1)
    last.run("t1")
    value = first[...]
    for step in range(1, sz.tp):
        over_tp(step).wait()
        value = value + from_tp[step - 1]
    sum_tp[0:n] = value
    share.wait()
    sum_tp[n + pc.zl] = share_ref[pc.k] + shgot_ref[...]
    for step in range(1, sz.ctx):
        over_ctx(step).start()
    last.run("t2")
    value = sum_tp[...]
    for step in range(1, sz.ctx):
        over_ctx(step).wait()
        value = value + from_ctx[step - 1]
    sum_ctx[...] = value
    for step in range(1, sz.fsdp):
        over_fsdp(step).start()
    value = sum_ctx[...]
    for step in range(1, sz.fsdp):
        over_fsdp(step).wait()
        value = value + from_fsdp[step - 1]
    small_ref[...] = value
    give_ff[0].finish()
    spread_wait(1)
    last.finish()


def backward_call(sz, saved, wattn, wff, cot, gains):
    n = sz.layers
    own, team = (sz.images, sz.part, sz.d), (sz.chips, sz.images, sz.part, sz.d)
    head, pair = (2, sz.units, sz.part, sz.headp), (2, 2, sz.units, sz.part, sz.headp)
    hidden = (2, sz.units, sz.part, sz.ffp)
    deep = up_to(max(6, 3 * n), 8)
    small = (n + sz.zl, deep, sz.d)
    ends = (sz.images, sz.part, sz.d)
    attn_sum, ff_sum = (sz.ctx, sz.wrowsp, sz.attnp), (sz.ctx, sz.wrowsp, sz.ffs)
    shapes = [(attn_sum, bf16)] * n + [(ff_sum, bf16)] * n + [((2, sz.tp) + ends, bf16), (small, f32)]
    vmem, hbm = pl.BlockSpec(memory_space=pltpu.VMEM), pl.BlockSpec(memory_space=pl.ANY)
    far, jumps = max(sz.tp, sz.ctx, sz.fsdp), max(sz.fsdp - 1, 1)
    scratch = [
        VMEM(own, f32), VMEM(own, f32), VMEM(team, bf16), VMEM(team, bf16),
        VMEM(head, bf16), VMEM(pair, bf16), VMEM(pair, bf16), VMEM(head, bf16), VMEM(hidden, f32), VMEM(hidden, bf16),
        VMEM((1, sz.keys), f32), VMEM(own, f32),
        VMEM((2, sz.d, sz.attnp), bf16), VMEM((2, sz.d, sz.ffw), bf16),
        VMEM(team, bf16), VMEM(team, bf16), VMEM(hidden, bf16), VMEM((2, sz.d, sz.headp), bf16),
        VMEM((2, 2, 2, sz.half, sz.headp), f32), VMEM((2, 2, sz.half, sz.headp), bf16),
        VMEM((2, 2, sz.half, sz.headp), bf16), VMEM((2, sz.units, sz.part, sz.qkvp), bf16),
        VMEM((2, sz.d, sz.attnp), bf16), VMEM((2, sz.d, sz.ffw), bf16),
        VMEM((sz.d, sz.attnp), bf16), VMEM((sz.d, sz.ffw), bf16),
        VMEM((n, jumps) + attn_sum, bf16), VMEM((n, jumps) + ff_sum, bf16),
        VMEM((2, 2, sz.headp), f32), VMEM((2, 1, sz.ffp), f32), VMEM(own, f32), VMEM((2,) + ends, bf16),
        VMEM((n, deep, sz.d), f32), VMEM((sz.tp - 1, n, deep, sz.d), f32),
        VMEM((max(sz.ctx - 1, 1),) + small, f32), VMEM((jumps,) + small, f32), VMEM(small, f32), VMEM(small, f32),
        VMEM((2, deep, sz.d), f32), VMEM((deep, sz.d), f32),
        DMA((12 * n + 2,)), DMA((2 * n, sz.chunks, sz.fsdp, 2, sz.ctx)), DMA((2, 2, sz.images)), DMA((2, 2, sz.tp)),
        DMA((3, 2, far)), DMA((n, 2, 2)), DMA((2 * n, 2, sz.d // 128)), DMA((2,)),
    ] + team_scratch(sz, 2 * n)
    if sz.wrowsp != sz.wrows:
        padded = sz.groups * sz.wrowsp
        scratch += [VMEM((padded, sz.attnp), bf16), VMEM((padded, sz.ffw), bf16)]
    operands = (*saved, *wattn, *wff, cot, gains)
    return pl.pallas_call(
        functools.partial(backward_kernel, sz),
        out_shape=[jax.ShapeDtypeStruct(*s) for s in shapes],
        in_specs=[hbm] * (len(operands) - 2) + [vmem] * 2,
        out_specs=[hbm] * (2 * n + 1) + [vmem],
        scratch_shapes=scratch,
        compiler_params=params(2),
        name="backward",
    )(*operands)


def close_kernel(sz, *refs):
    n = sz.layers
    attn_refs, ff_refs, (whole_ref, small_ref), outs = split_refs(refs, n, n, 2, 11)
    out_ref, gin_ref, gain_ref, bias_ref, qkv_ref, qv_ref, wout_ref, up_ref, upb_ref, down_ref, resid_ref = outs
    full, ff = sz.wide * sz.zl, sz.ff * sz.zl

    def summed(ref):
        return [sum(ref[zh * sz.zl + j].astype(f32) for zh in range(sz.images)) for j in range(sz.zl)]

    def join(width, count, *runs):
        total = None
        for j, halves, start, lanes, place in [(j, *run) for run in runs for j in range(sz.zl)]:
            piece = shift_lanes(halves[j], start, lanes, j * count + place, up_to(width, 128))
            total = piece if total is None else total + piece
        return total[0:sz.wrows, 0:width]

    for layer in range(n):
        attn, hidden = summed(attn_refs[layer]), summed(ff_refs[layer])
        for kind in range(3):
            qkv_ref[layer, kind] = join(full, sz.wide, (attn, kind * sz.wide, sz.wide, 0))
        wout_ref[layer] = join(full, sz.wide, (attn, 3 * sz.wide, sz.wide, 0))
        rest = sz.ff - sz.spare
        first = [(attn, 4 * sz.wide, sz.spare, 0)] if sz.spare else []
        up_ref[layer] = join(ff, sz.ff, *first, (hidden, 0, rest, sz.spare))
        down_ref[layer] = join(ff, sz.ff, (hidden, rest, sz.ff, 0))
        values = small_ref[layer]
        gain_ref[layer] = values[0:2]
        bias_ref[layer] = values[2:4]
        resid_ref[layer] = values[4:6]
        total_qv, total_up = None, None
        for half in range(sz.zl):
            values = small_ref[n + half]
            qv = shift_lanes(values, 0, sz.wide, half * sz.wide, up_to(full, 128))
            up = shift_lanes(values, sz.ff_at, sz.ff, half * sz.ff, up_to(ff, 128))
            total_qv = qv if total_qv is None else total_qv + qv
            total_up = up if total_up is None else total_up + up
        qv_ref[layer] = total_qv[3 * layer:3 * layer + 2, 0:full]
        upb_ref[layer:layer + 1, :] = total_up[3 * layer + 2:3 * layer + 3, 0:ff]
    for image in range(sz.images):
        rows = whole_ref[0, :, image].reshape(sz.tp * sz.part, sz.d)
        out_ref[image] = rows[0:sz.rows]
        rows = whole_ref[1, :, image].reshape(sz.tp * sz.part, sz.d)
        gin_ref[image] = rows.astype(f32)[0:sz.rows]


def close_call(sz, attn_sums, ff_sums, ends, small):
    n, full, ff = sz.layers, sz.wide * sz.zl, sz.ff * sz.zl
    tokens = (sz.images, sz.rows, sz.d)
    vec, up = ((n, 2, sz.d), f32), ((n, sz.wrows, ff), f32)
    shapes = [
        (tokens, bf16), (tokens, f32), vec, vec, ((n, 3, sz.wrows, full), f32), ((n, 2, full), f32),
        ((n, sz.wrows, full), f32), up, ((n, ff), f32), up, vec,
    ]
    vmem = pl.BlockSpec(memory_space=pltpu.VMEM)
    results = pl.pallas_call(
        functools.partial(close_kernel, sz),
        out_shape=[jax.ShapeDtypeStruct(*s) for s in shapes],
        in_specs=[vmem] * (2 * n + 2),
        out_specs=[vmem] * len(shapes),
        compiler_params=pltpu.CompilerParams(vmem_limit_bytes=60 * 1024 * 1024),
        name="close",
    )(*attn_sums, *ff_sums, ends, small)
    results = list(results)
    results[4] = jnp.swapaxes(results[4], 1, 2)
    return tuple(results)


def per_device(mesh, inputs, cotangent, valid_count, norm_gain, norm_bias, w_qkv, bias_qv, w_out, w_up, bias_up,
               w_down, bias_resid):
    sz = Sizes(mesh, inputs, w_qkv, w_up)
    n = sz.layers
    *made, cot = forward_call(sz, valid_count, inputs, cotangent, jnp.swapaxes(w_qkv, 1, 2), w_out, w_up,
                              w_down, norm_gain, norm_bias, bias_qv, bias_up, bias_resid)
    saved, wattn, wff = split_refs(made, 11 * n, n, n)
    *sums, ends, small = backward_call(sz, saved, wattn, wff, cot, norm_gain)
    return close_call(sz, sums[:n], sums[n:], ends, small)


def solution(mesh):
    tokens, rows = P("fsdp", "ctx", None), P(None, ("fsdp", "ctx"), "tp")
    qkv = P(None, ("fsdp", "ctx"), None, "tp")
    qv, up = P(None, None, "tp"), P(None, "tp")
    return jax.shard_map(
        functools.partial(per_device, mesh),
        mesh=mesh,
        in_specs=(tokens, tokens, P("fsdp"), P(), P(), qkv, qv, rows, rows, up, rows, P()),
        out_specs=(tokens, tokens, P(), P(), qkv, qv, rows, rows, up, rows, P()),
        check_vma=False,
    )
```

```python
import functools

import jax
import jax.numpy as jnp
from jax import lax
from jax.experimental import pallas as pl
from jax.experimental.pallas import tpu as pltpu
from jax.sharding import PartitionSpec as P

HEAD_DIM = 72
norm_eps = 1e-06
gelu_root = 0.7978845608028654
gelu_cubic = 0.044715
masked_score = -1e30
LOG2_E = 1.4426950408889634

MESH = pl.DeviceIdType.MESH
f32 = jnp.float32
bf16 = jnp.bfloat16
VMEM = pltpu.VMEM
DMA = pltpu.SemaphoreType.DMA


def up_to(value, unit):
    return (value + unit - 1) // unit * unit


def dot(a, b, over):
    return lax.dot_general(a, b, (((over[0],), (over[1],)), ((), ())), preferred_element_type=f32)


class Sizes:
    def __init__(self, mesh, inputs, w_qkv, w_up):
        self.fsdp, self.ctx, self.tp = mesh.shape["fsdp"], mesh.shape["ctx"], mesh.shape["tp"]
        self.images, self.rows, self.d = inputs.shape
        self.layers, self.wrows = w_qkv.shape[0], w_qkv.shape[1]
        self.zl = self.ctx // self.images
        self.chips_y = self.tp // 2
        self.chips = self.zl * self.chips_y
        self.team = self.chips * 2
        self.part = up_to(-(-self.rows // self.tp), 16)
        self.block = self.images * self.part
        self.units = self.chips * self.images
        self.half = self.units * self.part
        self.tile = 2 * self.part
        self.steps = self.units // 2
        self.keys = 2 * self.half
        self.wide = w_qkv.shape[3] // self.zl
        self.heads = self.wide // HEAD_DIM
        self.ff = w_up.shape[2] // self.zl
        self.headp = up_to(self.wide, 128)
        self.qkvp = up_to(3 * self.wide, 128)
        self.attnp = up_to(4 * self.wide, 128)
        self.spare = self.attnp - 4 * self.wide
        self.ff_at = 4 * self.wide % 128
        self.ff_sent = 128 if self.spare else 0
        end = self.ff_at + self.ff
        self.ffw = up_to(end + self.ff, 128)
        self.ffs = self.ffw - self.ff_sent
        self.down_at = end // 128 * 128
        self.down_shift = end - self.down_at
        self.ffp = self.ffw - self.down_at
        assert up_to(end, 128) <= self.ffp and self.spare < self.ff
        self.wrowsp = up_to(self.wrows, 16)
        self.chunk = 48 if self.wrowsp % 48 == 0 else self.wrowsp
        self.chunks = self.wrowsp // self.chunk
        self.groups = self.fsdp * self.ctx


class Place:
    def __init__(self, sz):
        self.sz = sz
        self.f, self.c, self.t = lax.axis_index("fsdp"), lax.axis_index("ctx"), lax.axis_index("tp")
        self.zh, self.zl = self.c // sz.zl, self.c % sz.zl
        self.y, self.k = self.t // 2, self.t % 2
        self.chip = self.zl * sz.chips_y + self.y
        self.slot = 2 * self.chip + self.k

    def chip_at(self, step):
        sz = self.sz
        zl = (self.zl + step // sz.chips_y) % sz.zl
        y = (self.y + step % sz.chips_y) % sz.chips_y
        return zl, y

    def chip_back(self, step):
        sz = self.sz
        zl = (self.zl + sz.zl - step // sz.chips_y) % sz.zl
        y = (self.y + sz.chips_y - step % sz.chips_y) % sz.chips_y
        return zl, y

    def index(self, chip):
        return chip[0] * self.sz.chips_y + chip[1]

    def device(self, chip):
        return (self.f, self.zh * self.sz.zl + chip[0], 2 * chip[1] + self.k)

    @property
    def twin(self):
        return (self.f, self.c, self.t + 1 - 2 * self.k)


    def ctx_ahead(self, step):
        sz = self.sz
        return (self.zh + step // sz.zl) % sz.images * sz.zl + (self.zl + step % sz.zl) % sz.zl

    def ctx_back(self, step):
        sz = self.sz
        zh = (self.zh + sz.images - step // sz.zl) % sz.images
        return zh * sz.zl + (self.zl + sz.zl - step % sz.zl) % sz.zl


def split_refs(refs, *counts):
    out, at = [], 0
    for count in counts:
        out.append(refs[at:at + count])
        at += count
    assert at == len(refs)
    return out


class Greeting:
    def __init__(self, others):
        self.count = len(others)
        self.barrier = pltpu.get_barrier_semaphore()
        for other in others:
            pl.semaphore_signal(self.barrier, inc=1, device_id=other, device_id_type=MESH)

    def wait(self):
        pl.semaphore_wait(self.barrier, self.count)


def send(src, dst, send_sem, recv_sem, device):
    return pltpu.make_async_remote_copy(
        src_ref=src, dst_ref=dst, send_sem=send_sem, recv_sem=recv_sem, device_id=device, device_id_type=MESH
    )


def team_peers(pc):
    return [pc.device(pc.chip_at(step)) for step in range(1, pc.sz.chips)] + [pc.twin]


def line_peers(pc):
    sz = pc.sz
    return [(pc.f, pc.c, 2 * ((pc.y + dy) % sz.chips_y) + 1 - pc.k) for dy in range(1, sz.chips_y)]


def weight_peers(pc, team=False):
    sz = pc.sz
    first = sz.zl if team else 1
    return [(pc.f, pc.ctx_ahead(step), pc.t) for step in range(first, sz.ctx)] + [
        ((pc.f + jump) % sz.fsdp, pc.c, pc.t) for jump in range(1, sz.fsdp)
    ]


def pick(step, values):
    if isinstance(step, int):
        return values[step]
    out = jnp.int32(values[0])
    for i in range(1, len(values)):
        out = jnp.where(step == i, jnp.int32(values[i]), out)
    return out


def when(condition, run):
    if isinstance(condition, (bool, int)):
        if condition:
            run()
    else:
        pl.when(condition)(run)


FF_OVER = 3

FORWARD_TURN = (False, True)
BACKWARD_TURN = (True, False)
SUM_TURN = (True, True)


class Routes:
    def __init__(self, sz):
        self.sz = sz
        self.z = [dz * sz.chips_y for dz in range(1, sz.zl)]
        self.y = list(range(1, sz.chips_y))
        self.turned = [dz + dy for dz in self.z for dy in self.y]
        self.arriving = [0] + self.z + self.y + self.turned
        self.leaving = self.turned + self.y + self.z + [0]

    def at(self, order, step):
        per = len(order) // 2
        firsts, seconds = order[0::2] * self.sz.images, order[1::2] * self.sz.images
        pieces = [p for p in range(self.sz.images) for _ in range(per)]
        return pick(step, firsts), pick(step, seconds), pick(step, pieces)


class Gather:
    def __init__(self, pc, buf, sems, turn):
        self.pc, self.buf, self.sems, self.turn = pc, buf, sems, turn
        self.routes = Routes(pc.sz)

    def move(self, back, piece, at, device):
        return send(self.buf.at[at, piece], self.buf.at[at, piece], self.sems.at[0, back, piece],
                    self.sems.at[1, back, piece], device)

    def start(self, piece, low):
        pc, routes = self.pc, self.routes
        self.buf[pc.chip, piece] = low
        for step in routes.z + routes.y + ([] if self.turn else routes.turned):
            self.move(step, piece, pc.chip, pc.device(pc.chip_at(step))).start()

    def ready(self, step):
        pc, sz = self.pc, self.pc.sz
        *chips, piece = self.routes.at(self.routes.arriving, step)
        places = []
        for back in chips:
            at = pc.index(pc.chip_back(back))
            when(back > 0, self.move(back, piece, at, pc.twin).wait_recv)
            if self.turn:
                for dz in self.routes.z:

                    def pass_on(dz=dz, at=at):
                        for dy in self.routes.y:
                            self.move(dz + dy, piece, at, pc.device(pc.chip_at(dy))).start()

                    when(back == dz, pass_on)
            places.append(at)
        tokens = jnp.concatenate([self.buf[at, piece] for at in places], axis=0)
        return [piece * sz.chips + at for at in places], tokens

    def finish(self):
        for piece in range(self.pc.sz.images):
            for back in self.routes.arriving[1:]:
                self.move(back, piece, self.pc.chip, self.pc.twin).wait_send()


class Scatter:
    def __init__(self, pc, bufs, sems, own_last, turn):
        self.pc, self.sems, self.turn = pc, sems, turn
        self.keep, self.hold, self.sent, self.got = bufs
        self.routes = Routes(pc.sz)
        self.order = self.routes.leaving if own_last else self.routes.arriving

    def far(self, back, piece):
        pc, sz = self.pc, self.pc.sz
        to = back
        if self.turn:
            if isinstance(back, int):
                to = back % sz.chips_y or back
            else:
                dy = lax.rem(back, jnp.int32(sz.chips_y))
                to = jnp.where(dy > 0, dy, back)
        return send(self.sent.at[back, piece], self.got.at[back, piece], self.sems.at[0, back, piece],
                    self.sems.at[1, back, piece], pc.device(pc.chip_back(to)))

    def units(self, step):
        pc = self.pc
        *chips, piece = self.routes.at(self.order, step)
        return [piece * pc.sz.chips + pc.index(pc.chip_back(back)) for back in chips]

    def push(self, step, partial):
        sz, part = self.pc.sz, self.pc.sz.part
        *chips, piece = self.routes.at(self.order, step)
        for i, back in enumerate(chips):
            terms = partial[i * part:(i + 1) * part]

            def own(terms=terms):
                self.keep[piece] = terms

            def leave(terms=terms, back=back):
                self.sent[back, piece] = terms.astype(bf16)
                self.far(back, piece).start()

            def hold(terms=terms, dz=None):
                self.hold[dz // sz.chips_y - 1] = terms

            when(back == 0, own)
            held = back < 0
            if self.turn:
                for dz in self.routes.z:
                    when(back == dz, functools.partial(hold, dz=dz))
                    held = held | (back == dz)
            when((back > 0) & jnp.logical_not(held), leave)
        if self.turn:
            per = sz.chips // 2
            for p in range(1, sz.images):
                when(step == p * per, functools.partial(self.merge, p - 1))

    def merge(self, piece):
        sz = self.pc.sz
        for dz in self.routes.z:
            total = self.hold[dz // sz.chips_y - 1]
            for dy in self.routes.y:
                self.far(dz + dy, piece).wait_recv()
                total = total + self.got[dz + dy, piece].astype(f32)
            self.sent[dz, piece] = total.astype(bf16)
            self.far(dz, piece).start()

    def flush(self):
        if self.turn:
            self.merge(self.pc.sz.images - 1)

    def finish(self, piece):
        total = self.keep[piece]
        for back in self.routes.z + self.routes.y + ([] if self.turn else self.routes.turned):
            self.far(back, piece).wait_recv()
            total = total + self.got[back, piece].astype(f32)
        for back in self.routes.arriving[1:]:
            self.far(back, piece).wait_send()
        return total


class Swap:
    def __init__(self, pc, src, dst, send_sem, recv_sem):
        self.copy = send(src, dst, send_sem, recv_sem, pc.twin)

    def start(self):
        self.copy.start()

    def wait(self):
        self.copy.wait()


def team_scratch(sz, phases):
    n = (sz.chips, sz.images)
    return [
        VMEM((sz.images, sz.part, sz.d), f32),
        VMEM((max(sz.zl - 1, 1), sz.part, sz.d), f32),
        VMEM(n + (sz.part, sz.d), bf16),
        VMEM(n + (sz.part, sz.d), bf16),
        DMA((phases, 2) + n),
        DMA((phases, 2) + n),
    ]


def normalised(values):
    centre = jnp.mean(values, axis=-1, keepdims=True)
    centred = values - centre
    spread = jnp.mean(centred * centred, axis=-1, keepdims=True)
    inverse = lax.rsqrt(spread + norm_eps)
    return centred * inverse, inverse


def norm_back(values, gain, grad):
    high, inverse = normalised(values)
    scaled = grad * gain
    term = inverse * (
        scaled
        - jnp.mean(scaled, axis=-1, keepdims=True)
        - high * jnp.mean(scaled * high, axis=-1, keepdims=True)
    )
    return term, jnp.sum(grad * high, axis=0, keepdims=True), jnp.sum(grad, axis=0, keepdims=True)


def lanes_of(shape):
    return lax.broadcasted_iota(jnp.int32, shape, len(shape) - 1)


def unpack_out(sz, w_ref, o_ref):
    at = 3 * sz.wide // 128 * 128
    shift = 3 * sz.wide - at

    def step(i, carry):
        rows = pl.ds(pl.multiple_of(i * 128, 128), 128)
        piece = pltpu.roll(w_ref[rows, at:at + sz.headp].astype(f32), sz.headp - shift, 1)
        o_ref[rows, :] = jnp.where(lanes_of(piece.shape) < sz.wide, piece, 0.0).astype(bf16)
        return carry

    lax.fori_loop(0, sz.d // 128, step, 0)


def take(sz, values, kind):
    at = kind * sz.wide // 128 * 128
    shift = kind * sz.wide - at
    piece = values[:, at:at + sz.headp]
    if shift:
        piece = pltpu.roll(piece, sz.headp - shift, 1)
    return jnp.where(lanes_of(piece.shape) < sz.wide, piece, 0.0)


def head_of(values, head):
    lanes = lanes_of(values.shape)
    mine = (lanes >= head * HEAD_DIM) & (lanes < (head + 1) * HEAD_DIM)
    return jnp.where(mine, values, jnp.zeros_like(values))


def probabilities(q_head, keys, valid):
    scores = jnp.where(valid > 0.0, dot(q_head, keys, (1, 1)), masked_score)
    high = jnp.max(scores, axis=-1, keepdims=True)
    weights = jnp.exp2((scores - high) * (HEAD_DIM ** (-0.5) * LOG2_E))
    return weights * (1.0 / jnp.sum(weights, axis=-1, keepdims=True))


class Jobs:
    def __init__(self, **places):
        self.places = places

    def run(self, place):
        for job in self.places.get(place, ()):
            job()

    def at(self, place, step):
        for when_step, jobs in self.places.get(place, {}).items():

            def run(jobs=jobs):
                for job in jobs:
                    job()

            when(step == when_step, run)


class Copies:
    def __init__(self, sems):
        self.sems, self.made = sems, []

    def start(self, src, dst):
        ident = len(self.made)
        self.made.append((src, dst))
        pltpu.make_async_copy(src, dst, self.sems.at[ident]).start()
        return ident

    def wait(self, idents=None):
        for ident in range(len(self.made)) if idents is None else idents:
            src, dst = self.made[ident]
            pltpu.make_async_copy(src, dst, self.sems.at[ident]).wait()


class Fetch:
    def __init__(self, pc, own, everything, sems, twin_sems, first=0):
        self.lanes = pl.ds(first, own.shape[-1])
        self.pc, self.own, self.all, self.sems, self.twin_sems = pc, own, everything, sems, twin_sems

    def rows(self, group, chunk):
        sz = self.pc.sz
        at = group * sz.wrowsp + chunk * sz.chunk
        return self.all.at[self.pc.k, pl.ds(pl.multiple_of(at, 16), sz.chunk), self.lanes]

    def own_rows(self, half, chunk):
        return self.own.at[half, pl.ds(chunk * self.pc.sz.chunk, self.pc.sz.chunk)]

    def along_ctx(self, step, chunk):
        pc = self.pc
        c = pc.ctx_ahead(step)
        return send(self.own_rows(c % pc.sz.zl, chunk), self.rows(pc.f * pc.sz.ctx + pc.c, chunk),
                    self.sems.at[chunk, 0, 0, step], self.sems.at[chunk, 0, 1, step], (pc.f, c, pc.t))

    def own_copy(self, chunk):
        pc = self.pc
        return pltpu.make_async_copy(self.own_rows(pc.zl, chunk), self.rows(pc.f * pc.sz.ctx + pc.c, chunk),
                                     self.sems.at[chunk, 0, 0, 0])

    def along_fsdp(self, jump, step, chunk):
        pc, sz = self.pc, self.pc.sz
        rows = self.rows(pc.f * sz.ctx + pc.ctx_back(step), chunk)
        return send(rows, rows, self.sems.at[chunk, jump, 0, step], self.sems.at[chunk, jump, 1, step],
                    ((pc.f + jump) % sz.fsdp, pc.c, pc.t))

    def to_twin(self, jump, step, chunk):
        pc, sz = self.pc, self.pc.sz
        rows = self.rows((pc.f + sz.fsdp - jump) % sz.fsdp * sz.ctx + pc.ctx_back(step), chunk)
        return send(rows, rows, self.twin_sems.at[chunk, jump, 0, step], self.twin_sems.at[chunk, jump, 1, step],
                    pc.twin)

    def depart(self, chunk):
        if chunk < self.pc.sz.chunks:
            self.own_copy(chunk).start()
            for step in range(self.pc.sz.ctx - 1, 0, -1):
                self.along_ctx(step, chunk).start()

    def turn(self, chunk):
        if chunk < self.pc.sz.chunks:
            for step in range(self.pc.sz.ctx):
                self.along_ctx(step, chunk).wait_recv() if step else self.own_copy(chunk).wait()
                for jump in range(1, self.pc.sz.fsdp):
                    self.along_fsdp(jump, step, chunk).start()
                self.to_twin(0, step, chunk).start()

    def land(self, chunk):
        if chunk < self.pc.sz.chunks:
            for step in range(self.pc.sz.ctx):
                for jump in range(1, self.pc.sz.fsdp):
                    self.along_fsdp(jump, step, chunk).wait_recv()
                    self.to_twin(jump, step, chunk).start()

    def jobs(self, parts):
        calls = {"d": self.depart, "t": self.turn, "l": self.land}
        return [functools.partial(calls[part[0]], int(part[1])) for part in parts.split()]

    def run(self, parts):
        for job in self.jobs(parts):
            job()

    def finish(self):
        sz = self.pc.sz
        for chunk in range(sz.chunks):
            for step in range(sz.ctx):
                if step:
                    self.along_ctx(step, chunk).wait_send()
                for jump in range(sz.fsdp):
                    if jump:
                        self.along_fsdp(jump, step, chunk).wait_send()
                    self.to_twin(jump, step, chunk).wait()


class Give:
    def __init__(self, pc, dw, recv, got, sems, first=0):
        self.lanes = pl.ds(first, recv.shape[-1])
        self.pc, self.dw, self.recv, self.got, self.sems = pc, dw, recv, got, sems
        self.order = list(range(pc.sz.ctx - 1, -1, -1))

    def rows(self, group, chunk):
        sz = self.pc.sz
        return pl.ds(pl.multiple_of(group * sz.wrowsp + chunk * sz.chunk, 16), sz.chunk)

    def part(self, chunk):
        return pl.ds(chunk * self.pc.sz.chunk, self.pc.sz.chunk)

    def along_fsdp(self, jump, step, chunk):
        pc, sz = self.pc, self.pc.sz
        f = (pc.f + jump) % sz.fsdp
        return send(self.dw.at[self.rows(f * sz.ctx + pc.ctx_ahead(step), chunk), self.lanes],
                    self.got.at[jump - 1, step, self.part(chunk)],
                    self.sems.at[chunk, jump, 0, step], self.sems.at[chunk, jump, 1, step], (f, pc.c, pc.t))

    def along_ctx(self, step, chunk, back=False):
        pc = self.pc
        there = pc.ctx_back(step) if back else pc.ctx_ahead(step)
        return send(self.got.at[0, step, self.part(chunk)],
                    self.recv.at[pc.ctx_back(step) if back else pc.c, self.part(chunk)],
                    self.sems.at[chunk, 0, 0, step], self.sems.at[chunk, 0, 1, step], (pc.f, there, pc.t))

    def own_copy(self, chunk):
        return pltpu.make_async_copy(self.got.at[0, 0, self.part(chunk)], self.recv.at[self.pc.c, self.part(chunk)],
                                     self.sems.at[chunk, 0, 0, 0])

    def depart(self, chunk):
        if chunk < self.pc.sz.chunks:
            for step in self.order:
                for jump in range(1, self.pc.sz.fsdp):
                    self.along_fsdp(jump, step, chunk).start()

    def turn(self, chunk):
        pc, sz = self.pc, self.pc.sz
        if chunk >= sz.chunks:
            return
        for step in self.order:
            for jump in range(1, sz.fsdp):
                self.along_fsdp(jump, step, chunk).wait_recv()
            total = self.dw[self.rows(pc.f * sz.ctx + pc.ctx_ahead(step), chunk), self.lanes].astype(f32)
            for jump in range(1, sz.fsdp):
                total = total + self.got[jump - 1, step, self.part(chunk)].astype(f32)
            self.got[0, step, self.part(chunk)] = total.astype(bf16)
            self.along_ctx(step, chunk).start() if step else self.own_copy(chunk).start()

    def jobs(self, parts):
        calls = {"d": self.depart, "t": self.turn}
        return [functools.partial(calls[part[0]], int(part[1])) for part in parts.split()]

    def run(self, parts):
        for job in self.jobs(parts):
            job()

    def finish(self):
        sz = self.pc.sz
        for chunk in range(sz.chunks):
            self.own_copy(chunk).wait()
            for step in range(sz.ctx):
                if step:
                    self.along_ctx(step, chunk, True).wait_recv()
                    self.along_ctx(step, chunk).wait_send()
                for jump in range(1, sz.fsdp):
                    self.along_fsdp(jump, step, chunk).wait_send()


def chosen(sz, group, lanes_shape):
    row = lax.broadcasted_iota(jnp.int32, lanes_shape, 0)
    col = lax.broadcasted_iota(jnp.int32, lanes_shape, 1)
    return jnp.where((row - group * sz.wrows == col) & (col < sz.wrows), 1.0, 0.0).astype(bf16)


def drop_padding(sz, src, dst):
    for at in range(0, dst.shape[-1], 128):
        lanes = slice(at, at + 128)

        def step(group, total):
            rows = pl.ds(pl.multiple_of(group * sz.wrowsp, 16), sz.wrowsp)
            return total + dot(chosen(sz, group, (sz.d, sz.wrowsp)), src[rows, lanes], (1, 0))

        dst[:, lanes] = lax.fori_loop(0, sz.groups, step, jnp.zeros((sz.d, 128), f32)).astype(bf16)


def add_padding(sz, src, dst):
    def step(group, carry):
        rows = pl.ds(pl.multiple_of(group * sz.wrowsp, 16), sz.wrowsp)
        for at in range(0, dst.shape[-1], 128):
            lanes = slice(at, at + 128)
            dst[rows, lanes] = dot(chosen(sz, group, (sz.d, sz.wrowsp)), src[:, lanes], (0, 0)).astype(bf16)
        return carry

    lax.fori_loop(0, sz.groups, step, 0)


def by_unit(sz, values):
    return jnp.swapaxes(values, 0, 1).reshape(sz.half, values.shape[-1])


def shift_lanes(values, start, count, at, width):
    have = values.shape[-1]
    first, last = start // 128 * 128, up_to(start + count, 128)
    to = at // 128 * 128
    span = max(last - first, up_to(at + count, 128) - to)
    piece = values[:, first:min(last, have)].astype(f32)
    if piece.shape[-1] < span:
        piece = jnp.pad(piece, ((0, 0), (0, span - piece.shape[-1])))
    turn = ((at - to) - (start - first)) % span
    if turn:
        piece = pltpu.roll(piece, turn, 1)
    lanes = lanes_of(piece.shape)
    piece = jnp.where((lanes >= at - to) & (lanes < at - to + count), piece, 0.0)
    piece = piece[:, 0:min(span, width - to)]
    return jnp.pad(piece, ((0, 0), (to, width - to - piece.shape[-1])))


def by_rows(sz, step):
    if sz.wrows % 16:
        step(slice(0, sz.wrows))
    else:

        def one(i, carry):
            step(pl.ds(pl.multiple_of(i * 16, 16), 16))
            return carry

        lax.fori_loop(0, sz.wrows // 16, one, 0)


def half_of(pc, values, count, width, at=0):
    out = shift_lanes(values, 0, count, at, width)
    for j in range(1, pc.sz.zl):
        out = jnp.where(pc.zl == j, shift_lanes(values, j * count, count, at, width), out)
    return out


def piece_of(pc, values):
    sz = pc.sz
    values = values.astype(f32)
    over = sz.tp * sz.part - sz.rows
    if over:
        values = jnp.concatenate([values, jnp.zeros((over, sz.d), f32)], axis=0)
    out = values[0:sz.part]
    for t in range(1, sz.tp):
        out = jnp.where(pc.t == t, values[t * sz.part:(t + 1) * sz.part], out)
    return out


def steps_below(values, unit, count):
    out = jnp.zeros_like(values)
    for m in range(1, count):
        out = out + jnp.where(values >= m * unit, 1, 0)
    return out


def key_valid(pc, count):
    sz = pc.sz
    row = lax.broadcasted_iota(jnp.int32, (1, sz.keys), 1)
    core = steps_below(row, sz.half, 2)
    within = row - core * sz.half
    unit = steps_below(within, sz.part, sz.units)
    piece = steps_below(unit, sz.chips, sz.images)
    chip = unit - piece * sz.chips
    zl = steps_below(chip, sz.chips_y, sz.zl)
    t = 2 * (chip - zl * sz.chips_y) + core
    token = t * sz.part + within - unit * sz.part
    position = (piece * sz.zl + zl) * sz.rows + token
    return jnp.where((token < sz.rows) & (position < count), 1.0, 0.0)


def own_valid(pc, count):
    sz = pc.sz
    shape = (sz.images, sz.part, 1)
    piece = lax.broadcasted_iota(jnp.int32, shape, 0)
    token = pc.t * sz.part + lax.broadcasted_iota(jnp.int32, shape, 1)
    position = (piece * sz.zl + pc.zl) * sz.rows + token
    return jnp.where((token < sz.rows) & (position < count), 1.0, 0.0)


def ff_lanes(sz, values):
    lanes = lanes_of(values.shape)
    return jnp.where((lanes >= sz.ff_at) & (lanes < sz.ff_at + sz.ff), values, 0.0)


def ride(sz, src, dst, src_at, dst_at):
    def step(i, carry):
        rows = pl.ds(pl.multiple_of(i * 128, 128), 128)
        there = src[rows, src_at:src_at + 128].astype(f32)
        here = dst[rows, dst_at:dst_at + 128].astype(f32) if dst_at else jnp.zeros_like(there)
        dst[rows, dst_at:dst_at + 128] = jnp.where(lanes_of(there.shape) >= sz.ff_at, there, here).astype(bf16)
        return carry

    if sz.spare:
        lax.fori_loop(0, src.shape[0] // 128, step, 0)


def rows_of(ref, units):
    return jnp.concatenate([ref[unit] for unit in units], axis=0)


def put_rows(sz, ref, units, values):
    for i, unit in enumerate(units):
        ref[unit] = values[i * sz.part:(i + 1) * sz.part]


def attn_forward(pc, jobs, gather, w_ref, qv_ref, valid_ref, q_ref, k_ref, v_ref, mixed_ref, o_ref, kv_sems,
                 scatter):
    sz = pc.sz
    for s in range(2):
        unpack_out(sz, w_ref.at[s], o_ref.at[s])

    def project(step, carry):
        units, tokens = gather.ready(step)
        for s in range(2):
            both3 = dot(tokens, w_ref[s, :, 0:sz.qkvp], (1, 0))
            put_rows(sz, q_ref.at[s], units, (take(sz, both3, 0) + qv_ref[s, 0:1, 0:sz.headp]).astype(bf16))
            put_rows(sz, k_ref.at[s, pc.k], units, take(sz, both3, 1).astype(bf16))
            put_rows(sz, v_ref.at[s, pc.k], units, (take(sz, both3, 2) + qv_ref[s, 1:2, 0:sz.headp]).astype(bf16))
        jobs.at("project", step)
        return carry

    def swaps(piece):
        units = pl.ds(piece * sz.chips, sz.chips)
        return [Swap(pc, ref.at[s, pc.k, units], ref.at[s, pc.k, units], kv_sems.at[0, i, s, piece],
                     kv_sems.at[1, i, s, piece]) for s in range(2) for i, ref in enumerate((k_ref, v_ref))]

    per = sz.steps // sz.images
    for piece in range(sz.images):
        lax.fori_loop(piece * per, (piece + 1) * per, project, 0)
        for swap in swaps(piece):
            swap.start()
    gather.finish()
    for piece in range(sz.images):
        for swap in swaps(piece):
            swap.wait()

    def attend(step, carry):
        units = scatter.units(step)
        partial = None
        for s in range(2):
            keys = k_ref[s].reshape(sz.keys, sz.headp)
            values = v_ref[s].reshape(sz.keys, sz.headp)
            queries = rows_of(q_ref.at[s], units)
            total = jnp.zeros((sz.tile, sz.headp), f32)
            for head in range(sz.heads):
                probs = probabilities(head_of(queries, head), keys, valid_ref[...])
                total = total + dot(probs.astype(bf16), head_of(values, head), (1, 0))
            mixed = total.astype(bf16)
            put_rows(sz, mixed_ref.at[s], units, mixed)
            terms = dot(mixed, o_ref[s], (1, 1))
            partial = terms if partial is None else partial + terms
        scatter.push(step, partial)
        jobs.at("attend", step)
        return carry

    lax.fori_loop(0, sz.steps, attend, 0)
    jobs.run("turnover")
    scatter.flush()
    jobs.run("flush")


def ff_forward(pc, jobs, gather, w_ref, upb_ref, pre_ref, hidden_ref, scatter):
    sz = pc.sz

    def feed(step, carry):
        units, tokens = gather.ready(step)
        partial = None
        for s in range(2):
            pre = dot(tokens, w_ref[s, :, 0:sz.ffp], (1, 0)) + upb_ref[s, 2:3, 0:sz.ffp]
            put_rows(sz, pre_ref.at[s], units, pre)
            hidden = 0.5 * pre * (1.0 + jnp.tanh(gelu_root * (pre + gelu_cubic * pre * pre * pre)))
            hidden = ff_lanes(sz, hidden)
            if sz.down_shift != sz.ff_at:
                hidden = pltpu.roll(hidden, (sz.down_shift - sz.ff_at) % sz.ffp, 1)
            hidden = hidden.astype(bf16)
            put_rows(sz, hidden_ref.at[s], units, hidden)
            terms = dot(hidden, w_ref[s, :, sz.down_at:], (1, 1))
            partial = terms if partial is None else partial + terms
        scatter.push(step, partial)
        jobs.at("feed", step)
        return carry

    lax.fori_loop(0, sz.steps, feed, 0)
    jobs.run("flush")
    gather.finish()


def plan(steps, more_steps, flush, what, ff, attn):
    for place, ff_parts, attn_parts in what:
        jobs = (ff.jobs(ff_parts) if ff else []) + (attn.jobs(attn_parts) if attn else [])
        if place == "f":
            flush.extend(jobs)
        else:
            table = steps if place[0] == "s" else more_steps
            table[int(place[1])] = table.get(int(place[1]), []) + jobs


def planned(what, give):
    steps = {}
    plan(steps, None, None, what, give, None)
    return steps


GIVE_FF = (("s1", "", "d2 t0"), ("s2", "", "t1"), ("s3", "", "t2"))
GIVE_ATTN = (("s0", "t0", ""), ("s1", "d2", ""), ("s2", "t1", ""), ("s3", "t2", ""))
PLAN_ATTN_FIRST = (("s0", "d2", ""), ("s3", "t1", ""), ("m0", "l0", ""), ("m1", "", "d0"), ("m2", "t2 l1", ""),
                   ("m3", "", "d1"), ("f", "l2", "d2 t0"))
PLAN_ATTN = (("s1", "t1", "d0"), ("s2", "d2", ""), ("s3", "l0", ""), ("m0", "", "d1"), ("m1", "t2 l1", ""),
             ("m3", "", "d2"), ("f", "l2", "t0"))
PLAN_FF = (("s0", "d0", "t1 l0"), ("s1", "d1", "t2"), ("s2", "t0", "l1"), ("s3", "", "l2"))


def norm_low(values, gain, shift):
    high, _ = normalised(values)
    return (high * gain + shift).astype(bf16)


def forward_kernel(sz, *refs):
    n = sz.layers
    aligned = sz.wrowsp == sz.wrows
    ins, outs, scratch = refs[:12], refs[12:12 + 13 * n + 1], refs[12 + 13 * n + 1:]
    (count_ref, in_ref, cot_ref, wqkv_ref, wout_ref, wup_ref, wdown_ref, gain_ref, shift_ref, qv_ref, upb_ref,
     resid_ref) = ins
    saved, (wattn_outs, wff_outs, ends_ref) = outs[:11 * n], split_refs(outs[11 * n:], n, n, 1)
    saved = [saved[l * 11:(l + 1) * 11] for l in range(n)]
    ends_ref = ends_ref[0]
    (own_attn, own_ff, all_attn, all_ff, swap_ref, mine_ref, n_ref, q_ref, k_ref, v_ref, mixed_ref, pre_ref,
     hidden_ref, stream_ref, middle_ref, valid_ref, o_ref, bias_ref, tsems, csems, wsems, vsems, kv_sems,
     bsems), team, joined = split_refs(scratch, 24, 6, 0 if aligned else 2)
    bufs, (gsems, ssems) = team[:4], team[4:]
    pc = Place(sz)
    greeting = Greeting(team_peers(pc) + weight_peers(pc, True))

    def pack(ref, pieces):
        def step(rows):
            total = None
            for values, start, count, at in pieces:
                piece = shift_lanes(values[rows, :], start, count, at, ref.shape[-1])
                total = piece if total is None else total + piece
            ref[rows, :] = total.astype(bf16)

        by_rows(sz, step)
        if not aligned:
            ref[sz.wrows:, :] = jnp.zeros((sz.wrowsp - sz.wrows, ref.shape[-1]), bf16)

    def pack_attn(layer):
        for half in range(sz.zl):
            pieces = [(wqkv_ref.at[layer, kind], half * sz.wide, sz.wide, kind * sz.wide) for kind in range(3)]
            pieces += [(wout_ref.at[layer], half * sz.wide, sz.wide, 3 * sz.wide)]
            if sz.spare:
                pieces += [(wup_ref.at[layer], half * sz.ff, sz.spare, 4 * sz.wide)]
            pack(own_attn.at[layer, half], pieces)

    def pack_ff(layer):
        for half in range(sz.zl):
            rest = sz.ff - sz.spare
            pack(own_ff.at[layer, half], [(wup_ref.at[layer], half * sz.ff + sz.spare, rest, 0),
                                          (wdown_ref.at[layer], half * sz.ff, sz.ff, rest)])

    for image in range(sz.images):
        swap_ref[image, 0] = piece_of(pc, in_ref[image]).astype(bf16)
        swap_ref[image, 1] = piece_of(pc, cot_ref[image]).astype(bf16)
    pack_attn(0)
    attn = [Fetch(pc, own_attn.at[l], all_attn.at[l], wsems.at[2 * l], vsems.at[2 * l]) for l in range(n)]
    ff = [Fetch(pc, own_ff.at[l], all_ff.at[l], wsems.at[2 * l + 1], vsems.at[2 * l + 1], sz.ff_sent)
          for l in range(n)]
    bias_ref[:, pc.k] = jnp.zeros((n, 8, bias_ref.shape[-1]), f32)
    for l in range(n):
        bias_ref[l, pc.k, 0:2, 0:sz.headp] = half_of(pc, qv_ref[l], sz.wide, sz.headp)
        bias_ref[l, pc.k, 2:3, 0:sz.ffp] = half_of(pc, upb_ref[l:l + 1, :], sz.ff, sz.ffp, sz.ff_at)
    bias_swaps = [Swap(pc, bias_ref.at[l, pc.k], bias_ref.at[l, pc.k], bsems.at[0, l], bsems.at[1, l])
                  for l in range(n)]
    copies = Copies(csems)

    def swap(step):
        zh = (pc.zh + step) % sz.images
        return send(swap_ref.at[zh], mine_ref.at[pc.zh], tsems.at[0, step], tsems.at[1, step],
                    (pc.f, zh * sz.zl + pc.zl, pc.t))

    greeting.wait()
    for step in range(1, sz.images):
        swap(step).start()
    attn[0].run("d0 d1 d2")
    for move in bias_swaps:
        move.start()
    mine_ref[pc.zh] = swap_ref[pc.zh]
    count = count_ref[pc.zh]
    valid_ref[...] = key_valid(pc, count)
    for step in range(1, sz.images):
        swap(step).wait()
    stream_ref[0] = mine_ref[:, 0].astype(f32)
    gathers = [Gather(pc, n_ref.at[i], gsems.at[i], FORWARD_TURN[i % 2]) for i in range(2 * n)]
    scatters = [Scatter(pc, bufs, ssems.at[i], i % 2 == 0, i % 2 == 0 and SUM_TURN[0]) for i in range(2 * n)]
    for p in range(sz.images):
        gathers[0].start(p, norm_low(stream_ref[0, p], gain_ref[0, 0:1, :], shift_ref[0, 0:1, :]))
    pack_ff(0)
    attn[0].run("t0")
    ff[0].run("d0")
    for layer in range(1, n):
        pack_attn(layer)
    attn[0].run("t1")
    ff[0].run("d1")
    ends_ref[...] = mine_ref[:, 1].astype(f32) * own_valid(pc, count)
    attn[0].run("l0 t2")
    for layer in range(1, n):
        pack_ff(layer)
    attn[0].run("l1")
    ff[0].run("t0")
    attn[0].run("l2")
    for move in bias_swaps:
        move.wait()
    attn[0].finish()

    def ready(fetch, refs, kind, layer, out):
        ref = refs.at[layer]
        if not aligned:
            for s in range(2):
                drop_padding(sz, ref.at[s], joined[kind].at[s])
            ref = joined[kind]
            pltpu.sync_copy(ref, out)
        else:
            copies.start(ref, out)
        return ref

    def after_attn(l, p):
        def run():
            middle = stream_ref[l, p] + (scatters[2 * l].finish(p) + resid_ref[l, 0:1, :])
            middle_ref[l, p] = middle
            gathers[2 * l + 1].start(p, norm_low(middle, gain_ref[l, 1:2, :], shift_ref[l, 1:2, :]))

        return run

    def after_ff(l, p):
        def run():
            out = middle_ref[l, p] + (scatters[2 * l + 1].finish(p) + resid_ref[l, 1:2, :])
            stream_ref[l + 1, p] = out
            if l + 1 < n:
                gathers[2 * l + 2].start(p, norm_low(out, gain_ref[l + 1, 0:1, :], shift_ref[l + 1, 0:1, :]))

        return run

    per = sz.steps // sz.images
    rest = range(1, sz.images)
    for l in range(n):
        more = l + 1 < n
        w = ready(attn[l], all_attn, 0, l, wattn_outs[l])
        project = {p * per - 1: [after_ff(l - 1, p)] for p in rest} if l else {}
        attend, flush = {}, []
        plan(project, attend, flush, PLAN_ATTN_FIRST if l == 0 else PLAN_ATTN, ff[l], attn[l + 1] if more else None)
        jobs = Jobs(project=project, attend=attend, flush=flush, turnover=[after_attn(l, 0)])
        attn_forward(pc, jobs, gathers[2 * l], w, bias_ref.at[l], valid_ref, q_ref.at[l], k_ref.at[l], v_ref.at[l],
                     mixed_ref.at[l], o_ref, kv_sems.at[l], scatters[2 * l])
        for ref, to in ((stream_ref.at[l], 0), (n_ref.at[2 * l], 2), (q_ref.at[l], 4), (k_ref.at[l], 5),
                        (v_ref.at[l], 6), (mixed_ref.at[l], 7)):
            copies.start(ref, saved[l][to])
        ff[l].finish()
        for core in range(2):
            ride(sz, all_attn.at[l, core], all_ff.at[l, core], 4 * sz.wide - sz.ff_at, 0)
        w = ready(ff[l], all_ff, 1, l, wff_outs[l])
        feed = {(p - 1) * per: [after_attn(l, p)] for p in rest}
        if more:
            plan(feed, None, None, PLAN_FF, ff[l + 1], attn[l + 1])
        feed[FF_OVER] = [after_ff(l, 0)] + feed.get(FF_OVER, [])
        ff_forward(pc, Jobs(feed=feed), gathers[2 * l + 1], w, bias_ref.at[l], pre_ref.at[l],
                   hidden_ref.at[l], scatters[2 * l + 1])
        if more:
            attn[l + 1].finish()
        else:
            for p in rest:
                after_ff(l, p)()
        for ref, to in ((middle_ref.at[l], 1), (n_ref.at[2 * l + 1], 3), (pre_ref.at[l], 8), (hidden_ref.at[l], 9)):
            copies.start(ref, saved[l][to])
    copies.start(stream_ref.at[n], saved[0][10])
    copies.start(valid_ref, saved[n - 1][10])
    copies.wait()


def forward_call(sz, *operands):
    n = sz.layers
    own, team = ((sz.images, sz.part, sz.d), f32), ((sz.chips, sz.images, sz.part, sz.d), bf16)
    head, pair = (2, sz.units, sz.part, sz.headp), (2, 2, sz.units, sz.part, sz.headp)
    hidden = (2, sz.units, sz.part, sz.ffp)
    shapes = []
    for l in range(n):
        last = ((1, sz.keys), f32) if l == n - 1 else own
        shapes += [own, own, team, team, (head, bf16), (pair, bf16), (pair, bf16), (head, bf16), (hidden, f32),
                   (hidden, bf16), last]
    shapes += [((2, sz.d, sz.attnp), bf16)] * n + [((2, sz.d, sz.ffw), bf16)] * n + [own]
    vmem, hbm = pl.BlockSpec(memory_space=pltpu.VMEM), pl.BlockSpec(memory_space=pl.ANY)
    padded = sz.groups * sz.wrowsp
    scratch = [
        VMEM((n, sz.zl, sz.wrowsp, sz.attnp), bf16), VMEM((n, sz.zl, sz.wrowsp, sz.ffs), bf16),
        VMEM((n, 2, padded, sz.attnp), bf16), VMEM((n, 2, padded, sz.ffw), bf16),
        VMEM((sz.images, 2, sz.part, sz.d), bf16), VMEM((sz.images, 2, sz.part, sz.d), bf16),
        VMEM((2 * n,) + team[0], bf16),
        VMEM((n,) + head, bf16), VMEM((n,) + pair, bf16), VMEM((n,) + pair, bf16), VMEM((n,) + head, bf16),
        VMEM((n,) + hidden, f32), VMEM((n,) + hidden, bf16),
        VMEM((n + 1,) + own[0], f32), VMEM((n,) + own[0], f32), VMEM((1, sz.keys), f32),
        VMEM((2, sz.d, sz.headp), bf16), VMEM((n, 2, 8, max(sz.headp, sz.ffp)), f32),
        DMA((2, sz.images)), DMA((12 * n + 2,)), DMA((2 * n, sz.chunks, sz.fsdp, 2, sz.ctx)),
        DMA((2 * n, sz.chunks, sz.fsdp, 2, sz.ctx)), DMA((n, 2, 2, 2, sz.images)), DMA((2, n)),
    ] + team_scratch(sz, 2 * n)
    if sz.wrowsp != sz.wrows:
        scratch += [VMEM((2, sz.d, sz.attnp), bf16), VMEM((2, sz.d, sz.ffw), bf16)]
    return pl.pallas_call(
        functools.partial(forward_kernel, sz),
        out_shape=[jax.ShapeDtypeStruct(*s) for s in shapes],
        in_specs=[pl.BlockSpec(memory_space=pltpu.SMEM)] + [vmem] * (len(operands) - 1),
        out_specs=[hbm] * (len(shapes) - 1) + [vmem],
        scratch_shapes=scratch,
        compiler_params=params(1),
        name="forward",
    )(*operands)


def params(collective_id):
    return pltpu.CompilerParams(
        collective_id=collective_id, has_side_effects=True, vmem_limit_bytes=63 * 1024 * 1024
    )


class Twins:
    def __init__(self, pc, dw, got, sems, span):
        self.pc, self.dw, self.got, self.sems, self.span = pc, dw, got, sems, span
        self.count = pc.sz.d // span

    def copy(self, i):
        rows = pl.ds(pl.multiple_of(i * self.span, 128), self.span)
        return send(self.dw.at[1 - self.pc.k, rows], self.got.at[rows], self.sems.at[0, i], self.sems.at[1, i],
                    self.pc.twin)

    def put(self, core, i, pieces):
        rows = pl.ds(pl.multiple_of(i * self.span, 128), self.span)
        for at, values in pieces:
            self.dw[core, rows, at:at + values.shape[-1]] = values.astype(bf16)

    def run(self, make, jobs, between=None):
        def other(i, carry):
            self.put(1 - self.pc.k, i, make(1 - self.pc.k, i))
            self.copy(i).start()
            return carry

        def own(i, carry):
            self.put(self.pc.k, i, make(self.pc.k, i))
            jobs.at("step_grads", i)
            return carry

        def add(i, carry):
            self.copy(i).wait_recv()
            rows = pl.ds(pl.multiple_of(i * self.span, 128), self.span)
            self.dw[self.pc.k, rows, :] = (
                self.dw[self.pc.k, rows, :].astype(f32) + self.got[rows, :].astype(f32)
            ).astype(bf16)
            self.copy(i).wait_send()
            return carry

        lax.fori_loop(0, self.count, other, 0)
        if between:
            between()
        lax.fori_loop(0, self.count, own, 0)
        lax.fori_loop(0, self.count, add, 0)


def ff_backward(pc, jobs, gather, w_ref, n2_ref, pre_ref, hidden_ref, dup_ref, pg_ref, twins, scatter):
    sz = pc.sz
    dup_ref[...] = jnp.zeros_like(dup_ref)

    def feed(step, carry):
        units, tokens = gather.ready(step)

        def shard(s, partial):
            back = dot(tokens, w_ref[s, :, sz.down_at:], (1, 0))
            if sz.down_shift != sz.ff_at:
                back = pltpu.roll(back, (sz.ff_at - sz.down_shift) % sz.ffp, 1)
            pre = rows_of(pre_ref.at[s], units)
            bent = jnp.tanh(gelu_root * (pre + gelu_cubic * pre * pre * pre))
            slope = 0.5 * (1.0 + bent) + 0.5 * pre * (1.0 - bent * bent) * (
                gelu_root * (1.0 + 3.0 * gelu_cubic * pre * pre)
            )
            pre_grad = ff_lanes(sz, back * slope).astype(bf16)
            put_rows(sz, pg_ref.at[s], units, pre_grad)
            dup_ref[s] += jnp.sum(pre_grad.astype(f32), axis=0, keepdims=True)
            return partial + dot(pre_grad, w_ref[s, :, 0:sz.ffp], (1, 1))

        partial = lax.fori_loop(0, 2, shard, jnp.zeros((sz.tile, sz.d), f32))
        scatter.push(step, partial)
        jobs.at("feed", step)
        return carry

    lax.fori_loop(0, sz.steps, feed, 0)
    jobs.run("flush")

    def make(core, i):
        lanes = pl.ds(pl.multiple_of(i * twins.span, 128), twins.span)
        hidden = hidden_ref[core].reshape(sz.half, sz.ffp)
        down = dot(by_unit(sz, gather.buf[:, :, :, lanes]), hidden, (0, 0))
        pre_grad = pg_ref[core].reshape(sz.half, sz.ffp)
        up = dot(by_unit(sz, n2_ref[:, :, :, lanes]), pre_grad, (0, 0))
        over = sz.ffp - sz.down_at
        both = [(sz.down_at, up[:, sz.down_at:] + down[:, 0:over])] if over else []
        return [(0, up[:, 0:sz.down_at])] + both + [(sz.ffp, down[:, over:])]

    twins.run(make, jobs)
    jobs.run("grads")
    gather.finish()


def attn_backward(pc, jobs, gather, w_ref, n1_ref, q_ref, k_ref, v_ref, mixed_ref, valid_ref, dqv_ref,
                  o_ref, dkv_ref, kvsend_ref, kvgot_ref, stack_ref, kv_sems, twins, scatter):
    sz = pc.sz
    for s in range(2):
        unpack_out(sz, w_ref.at[s], o_ref.at[s])
    dkv_ref[...] = jnp.zeros_like(dkv_ref)
    dqv_ref[...] = jnp.zeros_like(dqv_ref)
    scale = HEAD_DIM ** (-0.5)

    def attend(step, carry):
        units, tokens = gather.ready(step)

        def shard(s, none):
            mixed_grad = dot(tokens, o_ref[s], (1, 0)).astype(bf16)
            keys = k_ref[s].reshape(sz.keys, sz.headp)
            values = v_ref[s].reshape(sz.keys, sz.headp)
            queries = rows_of(q_ref.at[s], units)
            total = jnp.zeros((sz.tile, sz.headp), f32)
            dkey, dvalue = None, None
            for head in range(sz.heads):
                q_head = head_of(queries, head)
                g_head = head_of(mixed_grad, head)
                probs = probabilities(q_head, keys, valid_ref[...])
                dprobs = dot(g_head, values, (1, 1))
                inner = jnp.sum(probs * dprobs, axis=-1, keepdims=True)
                dscores = (probs * (dprobs - inner)).astype(bf16)
                total = total + dot(dscores, head_of(keys, head), (1, 0))
                dk, dv = dot(dscores, q_head, (0, 0)), dot(probs.astype(bf16), g_head, (0, 0))
                dkey = dk if dkey is None else dkey + dk
                dvalue = dv if dvalue is None else dvalue + dv
            dkv_ref[s, 0] += dkey.reshape(2, sz.half, sz.headp)
            dkv_ref[s, 1] += dvalue.reshape(2, sz.half, sz.headp)
            dq = (scale * total).astype(bf16).astype(f32)
            dqv_ref[s, 0:1, :] += jnp.sum(dq, axis=0, keepdims=True)
            dq = dq.astype(bf16)
            for i, unit in enumerate(units):
                stack_ref[s, unit, :, 0:sz.headp] = dq[i * sz.part:(i + 1) * sz.part]
            return none

        lax.fori_loop(0, 2, shard, 0)
        jobs.at("attend", step)
        return carry

    lax.fori_loop(0, sz.steps, attend, 0)
    for s in range(2):
        kvsend_ref[s] = dkv_ref[s, :, 1 - pc.k].astype(bf16)
    moves = [Swap(pc, kvsend_ref.at[s], kvgot_ref.at[s], kv_sems.at[0, s], kv_sems.at[1, s]) for s in range(2)]
    for move in moves:
        move.start()
    gather.finish()
    jobs.run("middle")
    for move in moves:
        move.wait()

    def back_project(step, carry):
        units = scatter.units(step)

        def shard(s, partial):

            def both(kind):
                rows = [pl.ds(pl.multiple_of(unit * sz.part, sz.part), sz.part) for unit in units]
                return jnp.concatenate(
                    [dkv_ref[s, kind, pc.k, r, :] + kvgot_ref[s, kind, r, :].astype(f32) for r in rows], axis=0
                )

            dk = (scale * both(0)).astype(bf16).astype(f32)
            dv = both(1).astype(bf16).astype(f32)
            dqv_ref[s, 1:2, :] += jnp.sum(dv, axis=0, keepdims=True)
            dq = rows_of(stack_ref.at[s], units)[:, 0:sz.headp].astype(f32)
            total = jnp.pad(dq, ((0, 0), (0, sz.qkvp - sz.headp)))
            for kind, piece in ((1, dk), (2, dv)):
                start = kind * sz.wide // 128 * 128
                shift = kind * sz.wide - start
                moved = pltpu.roll(piece, shift, 1) if shift else piece
                total = total + jnp.pad(moved, ((0, 0), (start, sz.qkvp - start - sz.headp)))
            stacked = total.astype(bf16)
            put_rows(sz, stack_ref.at[s], units, stacked)
            return partial + dot(stacked, w_ref[s, :, 0:sz.qkvp], (1, 1))

        partial = lax.fori_loop(0, 2, shard, jnp.zeros((sz.tile, sz.d), f32))
        scatter.push(step, partial)
        return carry

    lax.fori_loop(0, sz.steps, back_project, 0)
    jobs.run("flush")
    o_at = 3 * sz.wide // 128 * 128
    o_shift = 3 * sz.wide - o_at

    def make(core, i):
        lanes = pl.ds(pl.multiple_of(i * twins.span, 128), twins.span)
        stacked = stack_ref[core].reshape(sz.half, sz.qkvp)
        dqkv = dot(by_unit(sz, n1_ref[:, :, :, lanes]), stacked, (0, 0))
        mixed = mixed_ref[core].reshape(sz.half, sz.headp)
        dout = dot(by_unit(sz, gather.buf[:, :, :, lanes]), mixed, (0, 0))
        if o_shift:
            dout = pltpu.roll(dout, o_shift, 1)
        total = jnp.pad(dqkv, ((0, 0), (0, sz.attnp - sz.qkvp))) + jnp.pad(
            dout, ((0, 0), (o_at, sz.attnp - o_at - sz.headp))
        )
        return [(0, total)]

    twins.run(make, jobs, scatter.flush)
    jobs.run("grads")


def backward_kernel(sz, *refs):
    n = sz.layers
    aligned = sz.wrowsp == sz.wrows
    saved = [refs[l * 11:(l + 1) * 11] for l in range(n)]
    wattn_ins, wff_ins, (cot_ref, gain_ref), outs, scratch = split_refs(
        refs[11 * n:], n, n, 2, 2 * n + 2, len(refs) - 11 * n - 2 * n - 2 - 2 * n - 2)
    attn_outs, ff_outs, (whole_ref, small_ref) = split_refs(outs, n, n, 2)
    (stream_ref, middle_ref, n1_ref, n2_ref, q_ref, k_ref, v_ref, mixed_ref, pre_ref, hidden_ref, valid_ref, out_ref,
     wattn_ref, wff_ref, gl_ref, ml_ref, pg_ref, o_ref, dkv_ref, kvsend_ref, kvgot_ref, stack_ref, dwattn_ref,
     dwff_ref, twattn_ref, twff_ref, got_attn, got_ff, dqv_ref, dup_ref, grad_ref, ends_ref, first, from_tp, from_ctx,
     from_fsdp, sum_tp, sum_ctx, share_ref, shgot_ref, lsems, wsems, esems, ysems, tsems, kv_sems, twsems,
     shsems), team, padded = split_refs(scratch, 48, 6, 0 if aligned else 2)
    bufs, (gsems, ssems) = team[:4], team[4:]
    pc = Place(sz)
    greeting = Greeting(team_peers(pc) + weight_peers(pc, True) + line_peers(pc))
    copies = Copies(lsems)
    into = [stream_ref, middle_ref, n1_ref, n2_ref, q_ref, k_ref, v_ref, mixed_ref, pre_ref, hidden_ref]

    def load(l, weights, ref, kinds):
        return [copies.start(weights[l], ref)] + [copies.start(saved[l][kind], into[kind]) for kind in kinds]

    def load_ff(l):
        return load(l, wff_ins, wff_ref, (8, 3, 9, 1))

    def load_attn(l):
        return load(l, wattn_ins, wattn_ref, (4, 5, 6, 7, 2, 0))

    out_load = copies.start(saved[0][10], out_ref)
    ff_loads, attn_loads = load_ff(n - 1), load_attn(n - 1)
    attn_loads.append(copies.start(saved[n - 1][10], valid_ref))
    own_attn, own_ff = dwattn_ref.at[pc.k], dwff_ref.at[pc.k]
    give_attn = [Give(pc, own_attn if aligned else padded[0], attn_outs[l], got_attn.at[l], wsems.at[2 * l])
                 for l in range(n)]
    give_ff = [Give(pc, own_ff if aligned else padded[1], ff_outs[l], got_ff.at[l], wsems.at[2 * l + 1], sz.ff_sent)
               for l in range(n)]

    def begin(give, dw, kind):
        def run():
            if kind == 0:
                ride(sz, own_ff, dw, 0, 4 * sz.wide - sz.ff_at)
            if not aligned:
                add_padding(sz, dw, padded[kind])
            give.run("d0 d1")

        return run

    def swap(kind, step):
        zh = (pc.zh + step) % sz.images
        return send(ends_ref.at[kind, zh], whole_ref.at[kind, pc.t, pc.zh], esems.at[kind, 0, step],
                    esems.at[kind, 1, step], (pc.f, zh * sz.zl + pc.zl, pc.t))

    def own_end(kind):
        return pltpu.make_async_copy(ends_ref.at[kind, pc.zh], whole_ref.at[kind, pc.t, pc.zh], esems.at[kind, 0, 0])

    def spread(kind, step):
        return send(whole_ref.at[kind, pc.t], whole_ref.at[kind, pc.t], ysems.at[kind, 0, step],
                    ysems.at[kind, 1, step], (pc.f, pc.c, (pc.t + step) % sz.tp))

    def spread_from(kind, step):
        back = (pc.t + sz.tp - step) % sz.tp
        return send(whole_ref.at[kind, back], whole_ref.at[kind, back], ysems.at[kind, 0, step],
                    ysems.at[kind, 1, step], (pc.f, pc.c, back))

    def swap_start(kind):
        own_end(kind).start()
        for step in range(1, sz.images):
            swap(kind, step).start()

    def spread_start(kind):
        own_end(kind).wait()
        for step in range(1, sz.images):
            swap(kind, step).wait()
        for step in range(1, sz.tp):
            spread(kind, step).start()

    def spread_wait(kind):
        for step in range(1, sz.tp):
            spread_from(kind, step).wait_recv()
            spread(kind, step).wait_send()

    def over_tp(step):
        return send(first, from_tp.at[step - 1], tsems.at[0, 0, step], tsems.at[0, 1, step],
                    (pc.f, pc.c, (pc.t + step) % sz.tp))

    def over_ctx(step):
        return send(sum_tp, from_ctx.at[step - 1], tsems.at[1, 0, step], tsems.at[1, 1, step],
                    (pc.f, pc.ctx_ahead(step), pc.t))

    def over_fsdp(step):
        return send(sum_ctx, from_fsdp.at[step - 1], tsems.at[2, 0, step], tsems.at[2, 1, step],
                    ((pc.f + step) % sz.fsdp, pc.c, pc.t))

    sum_tp[...] = jnp.zeros_like(sum_tp)
    share_ref[...] = jnp.zeros_like(share_ref)
    first[...] = jnp.zeros_like(first)
    copies.wait([out_load])
    ends_ref[0] = out_ref[...].astype(bf16)
    grad_ref[...] = cot_ref[...]
    gathers = [Gather(pc, (gl_ref, ml_ref)[i % 2], gsems.at[i], BACKWARD_TURN[1 - i % 2]) for i in range(2 * n)]
    scatters = [Scatter(pc, bufs, ssems.at[i], i % 2 == 1, i % 2 == 1 and SUM_TURN[1]) for i in range(2 * n)]
    def low_of(l, p, row):
        low = grad_ref[p].astype(bf16)
        first[l, row:row + 1, :] += jnp.sum(low.astype(f32), axis=0, keepdims=True)
        return low

    def after_ff(l, p):
        def run():
            turn = n - 1 - l
            term, dgain, dshift = norm_back(middle_ref[p], gain_ref[l, 1:2, :], scatters[2 * turn].finish(p))
            grad_ref[p] += term
            gathers[2 * turn + 1].start(p, low_of(l, p, 4))
            first[l, 1:2, :] += dgain
            first[l, 3:4, :] += dshift

        return run

    def after_attn(l, p):
        def run():
            turn = n - 1 - l
            term, dgain, dshift = norm_back(stream_ref[p], gain_ref[l, 0:1, :], scatters[2 * turn + 1].finish(p))
            grad_ref[p] += term
            if l:
                gathers[2 * turn + 2].start(p, low_of(l - 1, p, 5))
            else:
                ends_ref[1, p] = grad_ref[p].astype(bf16)
            first[l, 0:1, :] += dgain
            first[l, 2:3, :] += dshift

        return run

    greeting.wait()
    per, rest = sz.steps // sz.images, range(1, sz.images)
    span = 384 if sz.d % 384 == 0 else 128
    for p in range(sz.images):
        gathers[0].start(p, low_of(n - 1, p, 5))
    swap_start(0)
    for turn in range(n):
        l = n - 1 - turn
        start = turn == 0
        copies.wait(ff_loads)
        feed = {}
        if start:
            feed[1] = [lambda: spread_start(0)]
        else:
            after = give_attn[l + 1]
            feed.update({(p - 1) * per: [after_attn(l + 1, p)] for p in rest})
            feed[(sz.images - 2) * per] = feed[(sz.images - 2) * per] + [lambda: attn_loads.extend(load_attn(l))]
            plan(feed, None, None, GIVE_FF, None, after)
        feed[FF_OVER] = [after_ff(l, 0)] + feed.get(FF_OVER, [])
        jobs = Jobs(feed=feed, flush=([] if start else [give_ff[l + 1].finish]),
                    grads=[begin(give_ff[l], own_ff, 1)] + [after_ff(l, p) for p in rest])
        twins = Twins(pc, dwff_ref, twff_ref, twsems.at[2 * l + 1], span)
        ff_backward(pc, jobs, gathers[2 * turn], wff_ref, n2_ref, pre_ref, hidden_ref, dup_ref, pg_ref, twins,
                    scatters[2 * turn])
        for core in range(2):
            share_ref[core, 3 * l + 2:3 * l + 3, 0:sz.ffp] = dup_ref[core]
        copies.wait(attn_loads)
        del attn_loads[:]
        if l:
            ff_loads = load_ff(l - 1)
        if start:
            spread_wait(0)
        now = give_ff[l]
        jobs = Jobs(
            attend=planned(GIVE_ATTN, now),
            flush=([] if start else [give_attn[l + 1].finish]),
            step_grads={0: [after_attn(l, 0)]}, grads=[begin(give_attn[l], own_attn, 0)],
        )
        twins = Twins(pc, dwattn_ref, twattn_ref, twsems.at[2 * l], span)
        attn_backward(pc, jobs, gathers[2 * turn + 1], wattn_ref, n1_ref, q_ref, k_ref, v_ref, mixed_ref, valid_ref,
                      dqv_ref, o_ref, dkv_ref, kvsend_ref, kvgot_ref, stack_ref, kv_sems.at[l], twins,
                      scatters[2 * turn + 1])
        for core in range(2):
            share_ref[core, 3 * l:3 * l + 2, 0:sz.headp] = dqv_ref[core]
    share = Swap(pc, share_ref.at[1 - pc.k], shgot_ref, shsems.at[0], shsems.at[1])
    share.start()
    for p in rest:
        after_attn(0, p)()
    last = give_attn[0]
    swap_start(1)
    for step in range(1, sz.tp):
        over_tp(step).start()
    last.run("d2 t0")
    spread_start(1)
    last.run("t1")
    value = first[...]
    for step in range(1, sz.tp):
        over_tp(step).wait()
        value = value + from_tp[step - 1]
    sum_tp[0:n] = value
    share.wait()
    sum_tp[n + pc.zl] = share_ref[pc.k] + shgot_ref[...]
    for step in range(1, sz.ctx):
        over_ctx(step).start()
    last.run("t2")
    value = sum_tp[...]
    for step in range(1, sz.ctx):
        over_ctx(step).wait()
        value = value + from_ctx[step - 1]
    sum_ctx[...] = value
    for step in range(1, sz.fsdp):
        over_fsdp(step).start()
    value = sum_ctx[...]
    for step in range(1, sz.fsdp):
        over_fsdp(step).wait()
        value = value + from_fsdp[step - 1]
    small_ref[...] = value
    give_ff[0].finish()
    spread_wait(1)
    last.finish()


def backward_call(sz, saved, wattn, wff, cot, gains):
    n = sz.layers
    own, team = (sz.images, sz.part, sz.d), (sz.chips, sz.images, sz.part, sz.d)
    head, pair = (2, sz.units, sz.part, sz.headp), (2, 2, sz.units, sz.part, sz.headp)
    hidden = (2, sz.units, sz.part, sz.ffp)
    deep = up_to(max(6, 3 * n), 8)
    small = (n + sz.zl, deep, sz.d)
    ends = (sz.images, sz.part, sz.d)
    attn_sum, ff_sum = (sz.ctx, sz.wrowsp, sz.attnp), (sz.ctx, sz.wrowsp, sz.ffs)
    shapes = [(attn_sum, bf16)] * n + [(ff_sum, bf16)] * n + [((2, sz.tp) + ends, bf16), (small, f32)]
    vmem, hbm = pl.BlockSpec(memory_space=pltpu.VMEM), pl.BlockSpec(memory_space=pl.ANY)
    far, jumps = max(sz.tp, sz.ctx, sz.fsdp), max(sz.fsdp - 1, 1)
    scratch = [
        VMEM(own, f32), VMEM(own, f32), VMEM(team, bf16), VMEM(team, bf16),
        VMEM(head, bf16), VMEM(pair, bf16), VMEM(pair, bf16), VMEM(head, bf16), VMEM(hidden, f32), VMEM(hidden, bf16),
        VMEM((1, sz.keys), f32), VMEM(own, f32),
        VMEM((2, sz.d, sz.attnp), bf16), VMEM((2, sz.d, sz.ffw), bf16),
        VMEM(team, bf16), VMEM(team, bf16), VMEM(hidden, bf16), VMEM((2, sz.d, sz.headp), bf16),
        VMEM((2, 2, 2, sz.half, sz.headp), f32), VMEM((2, 2, sz.half, sz.headp), bf16),
        VMEM((2, 2, sz.half, sz.headp), bf16), VMEM((2, sz.units, sz.part, sz.qkvp), bf16),
        VMEM((2, sz.d, sz.attnp), bf16), VMEM((2, sz.d, sz.ffw), bf16),
        VMEM((sz.d, sz.attnp), bf16), VMEM((sz.d, sz.ffw), bf16),
        VMEM((n, jumps) + attn_sum, bf16), VMEM((n, jumps) + ff_sum, bf16),
        VMEM((2, 2, sz.headp), f32), VMEM((2, 1, sz.ffp), f32), VMEM(own, f32), VMEM((2,) + ends, bf16),
        VMEM((n, deep, sz.d), f32), VMEM((sz.tp - 1, n, deep, sz.d), f32),
        VMEM((max(sz.ctx - 1, 1),) + small, f32), VMEM((jumps,) + small, f32), VMEM(small, f32), VMEM(small, f32),
        VMEM((2, deep, sz.d), f32), VMEM((deep, sz.d), f32),
        DMA((12 * n + 2,)), DMA((2 * n, sz.chunks, sz.fsdp, 2, sz.ctx)), DMA((2, 2, sz.images)), DMA((2, 2, sz.tp)),
        DMA((3, 2, far)), DMA((n, 2, 2)), DMA((2 * n, 2, sz.d // 128)), DMA((2,)),
    ] + team_scratch(sz, 2 * n)
    if sz.wrowsp != sz.wrows:
        padded = sz.groups * sz.wrowsp
        scratch += [VMEM((padded, sz.attnp), bf16), VMEM((padded, sz.ffw), bf16)]
    operands = (*saved, *wattn, *wff, cot, gains)
    return pl.pallas_call(
        functools.partial(backward_kernel, sz),
        out_shape=[jax.ShapeDtypeStruct(*s) for s in shapes],
        in_specs=[hbm] * (len(operands) - 2) + [vmem] * 2,
        out_specs=[hbm] * (2 * n + 1) + [vmem],
        scratch_shapes=scratch,
        compiler_params=params(2),
        name="backward",
    )(*operands)


def close_kernel(sz, *refs):
    n = sz.layers
    attn_refs, ff_refs, (whole_ref, small_ref), outs = split_refs(refs, n, n, 2, 11)
    out_ref, gin_ref, gain_ref, bias_ref, qkv_ref, qv_ref, wout_ref, up_ref, upb_ref, down_ref, resid_ref = outs
    full, ff = sz.wide * sz.zl, sz.ff * sz.zl

    def summed(ref):
        return [sum(ref[zh * sz.zl + j].astype(f32) for zh in range(sz.images)) for j in range(sz.zl)]

    def join(width, count, *runs):
        total = None
        for j, halves, start, lanes, place in [(j, *run) for run in runs for j in range(sz.zl)]:
            piece = shift_lanes(halves[j], start, lanes, j * count + place, up_to(width, 128))
            total = piece if total is None else total + piece
        return total[0:sz.wrows, 0:width]

    for layer in range(n):
        attn, hidden = summed(attn_refs[layer]), summed(ff_refs[layer])
        for kind in range(3):
            qkv_ref[layer, kind] = join(full, sz.wide, (attn, kind * sz.wide, sz.wide, 0))
        wout_ref[layer] = join(full, sz.wide, (attn, 3 * sz.wide, sz.wide, 0))
        rest = sz.ff - sz.spare
        first = [(attn, 4 * sz.wide, sz.spare, 0)] if sz.spare else []
        up_ref[layer] = join(ff, sz.ff, *first, (hidden, 0, rest, sz.spare))
        down_ref[layer] = join(ff, sz.ff, (hidden, rest, sz.ff, 0))
        values = small_ref[layer]
        gain_ref[layer] = values[0:2]
        bias_ref[layer] = values[2:4]
        resid_ref[layer] = values[4:6]
        total_qv, total_up = None, None
        for half in range(sz.zl):
            values = small_ref[n + half]
            qv = shift_lanes(values, 0, sz.wide, half * sz.wide, up_to(full, 128))
            up = shift_lanes(values, sz.ff_at, sz.ff, half * sz.ff, up_to(ff, 128))
            total_qv = qv if total_qv is None else total_qv + qv
            total_up = up if total_up is None else total_up + up
        qv_ref[layer] = total_qv[3 * layer:3 * layer + 2, 0:full]
        upb_ref[layer:layer + 1, :] = total_up[3 * layer + 2:3 * layer + 3, 0:ff]
    for image in range(sz.images):
        rows = whole_ref[0, :, image].reshape(sz.tp * sz.part, sz.d)
        out_ref[image] = rows[0:sz.rows]
        rows = whole_ref[1, :, image].reshape(sz.tp * sz.part, sz.d)
        gin_ref[image] = rows.astype(f32)[0:sz.rows]


def close_call(sz, attn_sums, ff_sums, ends, small):
    n, full, ff = sz.layers, sz.wide * sz.zl, sz.ff * sz.zl
    tokens = (sz.images, sz.rows, sz.d)
    vec, up = ((n, 2, sz.d), f32), ((n, sz.wrows, ff), f32)
    shapes = [
        (tokens, bf16), (tokens, f32), vec, vec, ((n, 3, sz.wrows, full), f32), ((n, 2, full), f32),
        ((n, sz.wrows, full), f32), up, ((n, ff), f32), up, vec,
    ]
    vmem = pl.BlockSpec(memory_space=pltpu.VMEM)
    results = pl.pallas_call(
        functools.partial(close_kernel, sz),
        out_shape=[jax.ShapeDtypeStruct(*s) for s in shapes],
        in_specs=[vmem] * (2 * n + 2),
        out_specs=[vmem] * len(shapes),
        compiler_params=pltpu.CompilerParams(vmem_limit_bytes=60 * 1024 * 1024),
        name="close",
    )(*attn_sums, *ff_sums, ends, small)
    results = list(results)
    results[4] = jnp.swapaxes(results[4], 1, 2)
    return tuple(results)


def per_device(mesh, inputs, cotangent, valid_count, norm_gain, norm_bias, w_qkv, bias_qv, w_out, w_up, bias_up,
               w_down, bias_resid):
    sz = Sizes(mesh, inputs, w_qkv, w_up)
    n = sz.layers
    *made, cot = forward_call(sz, valid_count, inputs, cotangent, jnp.swapaxes(w_qkv, 1, 2), w_out, w_up,
                              w_down, norm_gain, norm_bias, bias_qv, bias_up, bias_resid)
    saved, wattn, wff = split_refs(made, 11 * n, n, n)
    *sums, ends, small = backward_call(sz, saved, wattn, wff, cot, norm_gain)
    return close_call(sz, sums[:n], sums[n:], ends, small)


def solution(mesh):
    tokens, rows = P("fsdp", "ctx", None), P(None, ("fsdp", "ctx"), "tp")
    qkv = P(None, ("fsdp", "ctx"), None, "tp")
    qv, up = P(None, None, "tp"), P(None, "tp")
    return jax.shard_map(
        functools.partial(per_device, mesh),
        mesh=mesh,
        in_specs=(tokens, tokens, P("fsdp"), P(), P(), qkv, qv, rows, rows, up, rows, P()),
        out_specs=(tokens, tokens, P(), P(), qkv, qv, rows, rows, up, rows, P()),
        check_vma=False,
    )
```

```python
import functools

import jax
import jax.numpy as jnp
from jax import lax
from jax.experimental import pallas as pl
from jax.experimental.pallas import tpu as pltpu
from jax.sharding import PartitionSpec as P

HEAD_DIM = 72
norm_eps = 1e-06
gelu_root = 0.7978845608028654
gelu_cubic = 0.044715
masked_score = -1e30
LOG2_E = 1.4426950408889634

MESH = pl.DeviceIdType.MESH
f32 = jnp.float32
bf16 = jnp.bfloat16
VMEM = pltpu.VMEM
DMA = pltpu.SemaphoreType.DMA


def up_to(value, unit):
    return (value + unit - 1) // unit * unit


def dot(a, b, over):
    return lax.dot_general(a, b, (((over[0],), (over[1],)), ((), ())), preferred_element_type=f32)


class Sizes:
    def __init__(self, mesh, inputs, w_qkv, w_up):
        self.fsdp, self.ctx, self.tp = mesh.shape["fsdp"], mesh.shape["ctx"], mesh.shape["tp"]
        self.images, self.rows, self.d = inputs.shape
        self.layers, self.wrows = w_qkv.shape[0], w_qkv.shape[1]
        self.zl = self.ctx // self.images
        self.chips_y = self.tp // 2
        self.chips = self.zl * self.chips_y
        self.team = self.chips * 2
        self.part = up_to(-(-self.rows // self.tp), 16)
        self.block = self.images * self.part
        self.units = self.chips * self.images
        self.half = self.units * self.part
        self.tile = 2 * self.part
        self.steps = self.units // 2
        self.keys = 2 * self.half
        self.wide = w_qkv.shape[3] // self.zl
        self.heads = self.wide // HEAD_DIM
        self.ff = w_up.shape[2] // self.zl
        self.headp = up_to(self.wide, 128)
        self.qkvp = up_to(3 * self.wide, 128)
        self.attnp = up_to(4 * self.wide, 128)
        self.spare = self.attnp - 4 * self.wide
        self.ff_at = 4 * self.wide % 128
        self.ff_sent = 128 if self.spare else 0
        end = self.ff_at + self.ff
        self.ffw = up_to(end + self.ff, 128)
        self.ffs = self.ffw - self.ff_sent
        self.down_at = end // 128 * 128
        self.down_shift = end - self.down_at
        self.ffp = self.ffw - self.down_at
        assert up_to(end, 128) <= self.ffp and self.spare < self.ff
        self.wrowsp = up_to(self.wrows, 16)
        self.chunk = 48 if self.wrowsp % 48 == 0 else self.wrowsp
        self.chunks = self.wrowsp // self.chunk
        self.groups = self.fsdp * self.ctx


class Place:
    def __init__(self, sz):
        self.sz = sz
        self.f, self.c, self.t = lax.axis_index("fsdp"), lax.axis_index("ctx"), lax.axis_index("tp")
        self.zh, self.zl = self.c // sz.zl, self.c % sz.zl
        self.y, self.k = self.t // 2, self.t % 2
        self.chip = self.zl * sz.chips_y + self.y
        self.slot = 2 * self.chip + self.k

    def chip_at(self, step):
        sz = self.sz
        zl = (self.zl + step // sz.chips_y) % sz.zl
        y = (self.y + step % sz.chips_y) % sz.chips_y
        return zl, y

    def chip_back(self, step):
        sz = self.sz
        zl = (self.zl + sz.zl - step // sz.chips_y) % sz.zl
        y = (self.y + sz.chips_y - step % sz.chips_y) % sz.chips_y
        return zl, y

    def index(self, chip):
        return chip[0] * self.sz.chips_y + chip[1]

    def device(self, chip):
        return (self.f, self.zh * self.sz.zl + chip[0], 2 * chip[1] + self.k)

    @property
    def twin(self):
        return (self.f, self.c, self.t + 1 - 2 * self.k)


    def ctx_ahead(self, step):
        sz = self.sz
        return (self.zh + step // sz.zl) % sz.images * sz.zl + (self.zl + step % sz.zl) % sz.zl

    def ctx_back(self, step):
        sz = self.sz
        zh = (self.zh + sz.images - step // sz.zl) % sz.images
        return zh * sz.zl + (self.zl + sz.zl - step % sz.zl) % sz.zl


def split_refs(refs, *counts):
    out, at = [], 0
    for count in counts:
        out.append(refs[at:at + count])
        at += count
    assert at == len(refs)
    return out


class Greeting:
    def __init__(self, others):
        self.count = len(others)
        self.barrier = pltpu.get_barrier_semaphore()
        for other in others:
            pl.semaphore_signal(self.barrier, inc=1, device_id=other, device_id_type=MESH)

    def wait(self):
        pl.semaphore_wait(self.barrier, self.count)


def send(src, dst, send_sem, recv_sem, device):
    return pltpu.make_async_remote_copy(
        src_ref=src, dst_ref=dst, send_sem=send_sem, recv_sem=recv_sem, device_id=device, device_id_type=MESH
    )


def team_peers(pc):
    return [pc.device(pc.chip_at(step)) for step in range(1, pc.sz.chips)] + [pc.twin]


def line_peers(pc):
    sz = pc.sz
    return [(pc.f, pc.c, 2 * ((pc.y + dy) % sz.chips_y) + 1 - pc.k) for dy in range(1, sz.chips_y)]


def weight_peers(pc, team=False):
    sz = pc.sz
    first = sz.zl if team else 1
    return [(pc.f, pc.ctx_ahead(step), pc.t) for step in range(first, sz.ctx)] + [
        ((pc.f + jump) % sz.fsdp, pc.c, pc.t) for jump in range(1, sz.fsdp)
    ]


def pick(step, values):
    if isinstance(step, int):
        return values[step]
    out = jnp.int32(values[0])
    for i in range(1, len(values)):
        out = jnp.where(step == i, jnp.int32(values[i]), out)
    return out


def when(condition, run):
    if isinstance(condition, (bool, int)):
        if condition:
            run()
    else:
        pl.when(condition)(run)


FF_OVER = 3

FORWARD_TURN = (False, True)
BACKWARD_TURN = (True, False)
SUM_TURN = (True, False)


class Routes:
    def __init__(self, sz):
        self.sz = sz
        self.z = [dz * sz.chips_y for dz in range(1, sz.zl)]
        self.y = list(range(1, sz.chips_y))
        self.turned = [dz + dy for dz in self.z for dy in self.y]
        self.arriving = [0] + self.z + self.y + self.turned
        self.leaving = self.turned + self.y + self.z + [0]

    def at(self, order, step):
        per = len(order) // 2
        firsts, seconds = order[0::2] * self.sz.images, order[1::2] * self.sz.images
        pieces = [p for p in range(self.sz.images) for _ in range(per)]
        return pick(step, firsts), pick(step, seconds), pick(step, pieces)


class Gather:
    def __init__(self, pc, buf, sems, turn):
        self.pc, self.buf, self.sems, self.turn = pc, buf, sems, turn
        self.routes = Routes(pc.sz)

    def move(self, back, piece, at, device):
        return send(self.buf.at[at, piece], self.buf.at[at, piece], self.sems.at[0, back, piece],
                    self.sems.at[1, back, piece], device)

    def start(self, piece, low):
        pc, routes = self.pc, self.routes
        self.buf[pc.chip, piece] = low
        for step in routes.z + routes.y + ([] if self.turn else routes.turned):
            self.move(step, piece, pc.chip, pc.device(pc.chip_at(step))).start()

    def ready(self, step):
        pc, sz = self.pc, self.pc.sz
        *chips, piece = self.routes.at(self.routes.arriving, step)
        places = []
        for back in chips:
            at = pc.index(pc.chip_back(back))
            when(back > 0, self.move(back, piece, at, pc.twin).wait_recv)
            if self.turn:
                for dz in self.routes.z:

                    def pass_on(dz=dz, at=at):
                        for dy in self.routes.y:
                            self.move(dz + dy, piece, at, pc.device(pc.chip_at(dy))).start()

                    when(back == dz, pass_on)
            places.append(at)
        tokens = jnp.concatenate([self.buf[at, piece] for at in places], axis=0)
        return [piece * sz.chips + at for at in places], tokens

    def finish(self):
        for piece in range(self.pc.sz.images):
            for back in self.routes.arriving[1:]:
                self.move(back, piece, self.pc.chip, self.pc.twin).wait_send()


class Scatter:
    def __init__(self, pc, bufs, sems, own_last, turn):
        self.pc, self.sems, self.turn = pc, sems, turn
        self.keep, self.hold, self.sent, self.got = bufs
        self.routes = Routes(pc.sz)
        self.order = self.routes.leaving if own_last else self.routes.arriving

    def far(self, back, piece):
        pc, sz = self.pc, self.pc.sz
        to = back
        if self.turn:
            if isinstance(back, int):
                to = back % sz.chips_y or back
            else:
                dy = lax.rem(back, jnp.int32(sz.chips_y))
                to = jnp.where(dy > 0, dy, back)
        return send(self.sent.at[back, piece], self.got.at[back, piece], self.sems.at[0, back, piece],
                    self.sems.at[1, back, piece], pc.device(pc.chip_back(to)))

    def units(self, step):
        pc = self.pc
        *chips, piece = self.routes.at(self.order, step)
        return [piece * pc.sz.chips + pc.index(pc.chip_back(back)) for back in chips]

    def push(self, step, partial):
        sz, part = self.pc.sz, self.pc.sz.part
        *chips, piece = self.routes.at(self.order, step)
        for i, back in enumerate(chips):
            terms = partial[i * part:(i + 1) * part]

            def own(terms=terms):
                self.keep[piece] = terms

            def leave(terms=terms, back=back):
                self.sent[back, piece] = terms.astype(bf16)
                self.far(back, piece).start()

            def hold(terms=terms, dz=None):
                self.hold[dz // sz.chips_y - 1] = terms

            when(back == 0, own)
            held = back < 0
            if self.turn:
                for dz in self.routes.z:
                    when(back == dz, functools.partial(hold, dz=dz))
                    held = held | (back == dz)
            when((back > 0) & jnp.logical_not(held), leave)
        if self.turn:
            per = sz.chips // 2
            for p in range(1, sz.images):
                when(step == p * per, functools.partial(self.merge, p - 1))

    def merge(self, piece):
        sz = self.pc.sz
        for dz in self.routes.z:
            total = self.hold[dz // sz.chips_y - 1]
            for dy in self.routes.y:
                self.far(dz + dy, piece).wait_recv()
                total = total + self.got[dz + dy, piece].astype(f32)
            self.sent[dz, piece] = total.astype(bf16)
            self.far(dz, piece).start()

    def flush(self):
        if self.turn:
            self.merge(self.pc.sz.images - 1)

    def finish(self, piece):
        total = self.keep[piece]
        for back in self.routes.z + self.routes.y + ([] if self.turn else self.routes.turned):
            self.far(back, piece).wait_recv()
            total = total + self.got[back, piece].astype(f32)
        for back in self.routes.arriving[1:]:
            self.far(back, piece).wait_send()
        return total


class Swap:
    def __init__(self, pc, src, dst, send_sem, recv_sem):
        self.copy = send(src, dst, send_sem, recv_sem, pc.twin)

    def start(self):
        self.copy.start()

    def wait(self):
        self.copy.wait()


def team_scratch(sz, phases):
    n = (sz.chips, sz.images)
    return [
        VMEM((sz.images, sz.part, sz.d), f32),
        VMEM((max(sz.zl - 1, 1), sz.part, sz.d), f32),
        VMEM(n + (sz.part, sz.d), bf16),
        VMEM(n + (sz.part, sz.d), bf16),
        DMA((phases, 2) + n),
        DMA((phases, 2) + n),
    ]


def normalised(values):
    centre = jnp.mean(values, axis=-1, keepdims=True)
    centred = values - centre
    spread = jnp.mean(centred * centred, axis=-1, keepdims=True)
    inverse = lax.rsqrt(spread + norm_eps)
    return centred * inverse, inverse


def norm_back(values, gain, grad):
    high, inverse = normalised(values)
    scaled = grad * gain
    term = inverse * (
        scaled
        - jnp.mean(scaled, axis=-1, keepdims=True)
        - high * jnp.mean(scaled * high, axis=-1, keepdims=True)
    )
    return term, jnp.sum(grad * high, axis=0, keepdims=True), jnp.sum(grad, axis=0, keepdims=True)


def lanes_of(shape):
    return lax.broadcasted_iota(jnp.int32, shape, len(shape) - 1)


def unpack_out(sz, w_ref, o_ref):
    at = 3 * sz.wide // 128 * 128
    shift = 3 * sz.wide - at

    def step(i, carry):
        rows = pl.ds(pl.multiple_of(i * 128, 128), 128)
        piece = pltpu.roll(w_ref[rows, at:at + sz.headp].astype(f32), sz.headp - shift, 1)
        o_ref[rows, :] = jnp.where(lanes_of(piece.shape) < sz.wide, piece, 0.0).astype(bf16)
        return carry

    lax.fori_loop(0, sz.d // 128, step, 0)


def take(sz, values, kind):
    at = kind * sz.wide // 128 * 128
    shift = kind * sz.wide - at
    piece = values[:, at:at + sz.headp]
    if shift:
        piece = pltpu.roll(piece, sz.headp - shift, 1)
    return jnp.where(lanes_of(piece.shape) < sz.wide, piece, 0.0)


def head_of(values, head):
    lanes = lanes_of(values.shape)
    mine = (lanes >= head * HEAD_DIM) & (lanes < (head + 1) * HEAD_DIM)
    return jnp.where(mine, values, jnp.zeros_like(values))


def probabilities(q_head, keys, valid):
    scores = jnp.where(valid > 0.0, dot(q_head, keys, (1, 1)), masked_score)
    high = jnp.max(scores, axis=-1, keepdims=True)
    weights = jnp.exp2((scores - high) * (HEAD_DIM ** (-0.5) * LOG2_E))
    return weights * (1.0 / jnp.sum(weights, axis=-1, keepdims=True))


class Jobs:
    def __init__(self, **places):
        self.places = places

    def run(self, place):
        for job in self.places.get(place, ()):
            job()

    def at(self, place, step):
        for when_step, jobs in self.places.get(place, {}).items():

            def run(jobs=jobs):
                for job in jobs:
                    job()

            when(step == when_step, run)


class Copies:
    def __init__(self, sems):
        self.sems, self.made = sems, []

    def start(self, src, dst):
        ident = len(self.made)
        self.made.append((src, dst))
        pltpu.make_async_copy(src, dst, self.sems.at[ident]).start()
        return ident

    def wait(self, idents=None):
        for ident in range(len(self.made)) if idents is None else idents:
            src, dst = self.made[ident]
            pltpu.make_async_copy(src, dst, self.sems.at[ident]).wait()


class Fetch:
    def __init__(self, pc, own, everything, sems, twin_sems, first=0):
        self.lanes = pl.ds(first, own.shape[-1])
        self.pc, self.own, self.all, self.sems, self.twin_sems = pc, own, everything, sems, twin_sems

    def rows(self, group, chunk):
        sz = self.pc.sz
        at = group * sz.wrowsp + chunk * sz.chunk
        return self.all.at[self.pc.k, pl.ds(pl.multiple_of(at, 16), sz.chunk), self.lanes]

    def own_rows(self, half, chunk):
        return self.own.at[half, pl.ds(chunk * self.pc.sz.chunk, self.pc.sz.chunk)]

    def along_ctx(self, step, chunk):
        pc = self.pc
        c = pc.ctx_ahead(step)
        return send(self.own_rows(c % pc.sz.zl, chunk), self.rows(pc.f * pc.sz.ctx + pc.c, chunk),
                    self.sems.at[chunk, 0, 0, step], self.sems.at[chunk, 0, 1, step], (pc.f, c, pc.t))

    def own_copy(self, chunk):
        pc = self.pc
        return pltpu.make_async_copy(self.own_rows(pc.zl, chunk), self.rows(pc.f * pc.sz.ctx + pc.c, chunk),
                                     self.sems.at[chunk, 0, 0, 0])

    def along_fsdp(self, jump, step, chunk):
        pc, sz = self.pc, self.pc.sz
        rows = self.rows(pc.f * sz.ctx + pc.ctx_back(step), chunk)
        return send(rows, rows, self.sems.at[chunk, jump, 0, step], self.sems.at[chunk, jump, 1, step],
                    ((pc.f + jump) % sz.fsdp, pc.c, pc.t))

    def to_twin(self, jump, step, chunk):
        pc, sz = self.pc, self.pc.sz
        rows = self.rows((pc.f + sz.fsdp - jump) % sz.fsdp * sz.ctx + pc.ctx_back(step), chunk)
        return send(rows, rows, self.twin_sems.at[chunk, jump, 0, step], self.twin_sems.at[chunk, jump, 1, step],
                    pc.twin)

    def depart(self, chunk):
        if chunk < self.pc.sz.chunks:
            self.own_copy(chunk).start()
            for step in range(self.pc.sz.ctx - 1, 0, -1):
                self.along_ctx(step, chunk).start()

    def turn(self, chunk):
        if chunk < self.pc.sz.chunks:
            for step in range(self.pc.sz.ctx):
                self.along_ctx(step, chunk).wait_recv() if step else self.own_copy(chunk).wait()
                for jump in range(1, self.pc.sz.fsdp):
                    self.along_fsdp(jump, step, chunk).start()
                self.to_twin(0, step, chunk).start()

    def land(self, chunk):
        if chunk < self.pc.sz.chunks:
            for step in range(self.pc.sz.ctx):
                for jump in range(1, self.pc.sz.fsdp):
                    self.along_fsdp(jump, step, chunk).wait_recv()
                    self.to_twin(jump, step, chunk).start()

    def jobs(self, parts):
        calls = {"d": self.depart, "t": self.turn, "l": self.land}
        return [functools.partial(calls[part[0]], int(part[1])) for part in parts.split()]

    def run(self, parts):
        for job in self.jobs(parts):
            job()

    def finish(self):
        sz = self.pc.sz
        for chunk in range(sz.chunks):
            for step in range(sz.ctx):
                if step:
                    self.along_ctx(step, chunk).wait_send()
                for jump in range(sz.fsdp):
                    if jump:
                        self.along_fsdp(jump, step, chunk).wait_send()
                    self.to_twin(jump, step, chunk).wait()


class Give:
    def __init__(self, pc, dw, recv, got, sems, first=0):
        self.lanes = pl.ds(first, recv.shape[-1])
        self.pc, self.dw, self.recv, self.got, self.sems = pc, dw, recv, got, sems
        self.order = list(range(pc.sz.ctx - 1, -1, -1))

    def rows(self, group, chunk):
        sz = self.pc.sz
        return pl.ds(pl.multiple_of(group * sz.wrowsp + chunk * sz.chunk, 16), sz.chunk)

    def part(self, chunk):
        return pl.ds(chunk * self.pc.sz.chunk, self.pc.sz.chunk)

    def along_fsdp(self, jump, step, chunk):
        pc, sz = self.pc, self.pc.sz
        f = (pc.f + jump) % sz.fsdp
        return send(self.dw.at[self.rows(f * sz.ctx + pc.ctx_ahead(step), chunk), self.lanes],
                    self.got.at[jump - 1, step, self.part(chunk)],
                    self.sems.at[chunk, jump, 0, step], self.sems.at[chunk, jump, 1, step], (f, pc.c, pc.t))

    def along_ctx(self, step, chunk, back=False):
        pc = self.pc
        there = pc.ctx_back(step) if back else pc.ctx_ahead(step)
        return send(self.got.at[0, step, self.part(chunk)],
                    self.recv.at[pc.ctx_back(step) if back else pc.c, self.part(chunk)],
                    self.sems.at[chunk, 0, 0, step], self.sems.at[chunk, 0, 1, step], (pc.f, there, pc.t))

    def own_copy(self, chunk):
        return pltpu.make_async_copy(self.got.at[0, 0, self.part(chunk)], self.recv.at[self.pc.c, self.part(chunk)],
                                     self.sems.at[chunk, 0, 0, 0])

    def depart(self, chunk):
        if chunk < self.pc.sz.chunks:
            for step in self.order:
                for jump in range(1, self.pc.sz.fsdp):
                    self.along_fsdp(jump, step, chunk).start()

    def turn(self, chunk):
        pc, sz = self.pc, self.pc.sz
        if chunk >= sz.chunks:
            return
        for step in self.order:
            for jump in range(1, sz.fsdp):
                self.along_fsdp(jump, step, chunk).wait_recv()
            total = self.dw[self.rows(pc.f * sz.ctx + pc.ctx_ahead(step), chunk), self.lanes].astype(f32)
            for jump in range(1, sz.fsdp):
                total = total + self.got[jump - 1, step, self.part(chunk)].astype(f32)
            self.got[0, step, self.part(chunk)] = total.astype(bf16)
            self.along_ctx(step, chunk).start() if step else self.own_copy(chunk).start()

    def jobs(self, parts):
        calls = {"d": self.depart, "t": self.turn}
        return [functools.partial(calls[part[0]], int(part[1])) for part in parts.split()]

    def run(self, parts):
        for job in self.jobs(parts):
            job()

    def finish(self):
        sz = self.pc.sz
        for chunk in range(sz.chunks):
            self.own_copy(chunk).wait()
            for step in range(sz.ctx):
                if step:
                    self.along_ctx(step, chunk, True).wait_recv()
                    self.along_ctx(step, chunk).wait_send()
                for jump in range(1, sz.fsdp):
                    self.along_fsdp(jump, step, chunk).wait_send()


def chosen(sz, group, lanes_shape):
    row = lax.broadcasted_iota(jnp.int32, lanes_shape, 0)
    col = lax.broadcasted_iota(jnp.int32, lanes_shape, 1)
    return jnp.where((row - group * sz.wrows == col) & (col < sz.wrows), 1.0, 0.0).astype(bf16)


def drop_padding(sz, src, dst):
    for at in range(0, dst.shape[-1], 128):
        lanes = slice(at, at + 128)

        def step(group, total):
            rows = pl.ds(pl.multiple_of(group * sz.wrowsp, 16), sz.wrowsp)
            return total + dot(chosen(sz, group, (sz.d, sz.wrowsp)), src[rows, lanes], (1, 0))

        dst[:, lanes] = lax.fori_loop(0, sz.groups, step, jnp.zeros((sz.d, 128), f32)).astype(bf16)


def add_padding(sz, src, dst):
    def step(group, carry):
        rows = pl.ds(pl.multiple_of(group * sz.wrowsp, 16), sz.wrowsp)
        for at in range(0, dst.shape[-1], 128):
            lanes = slice(at, at + 128)
            dst[rows, lanes] = dot(chosen(sz, group, (sz.d, sz.wrowsp)), src[:, lanes], (0, 0)).astype(bf16)
        return carry

    lax.fori_loop(0, sz.groups, step, 0)


def by_unit(sz, values):
    return jnp.swapaxes(values, 0, 1).reshape(sz.half, values.shape[-1])


def shift_lanes(values, start, count, at, width):
    have = values.shape[-1]
    first, last = start // 128 * 128, up_to(start + count, 128)
    to = at // 128 * 128
    span = max(last - first, up_to(at + count, 128) - to)
    piece = values[:, first:min(last, have)].astype(f32)
    if piece.shape[-1] < span:
        piece = jnp.pad(piece, ((0, 0), (0, span - piece.shape[-1])))
    turn = ((at - to) - (start - first)) % span
    if turn:
        piece = pltpu.roll(piece, turn, 1)
    lanes = lanes_of(piece.shape)
    piece = jnp.where((lanes >= at - to) & (lanes < at - to + count), piece, 0.0)
    piece = piece[:, 0:min(span, width - to)]
    return jnp.pad(piece, ((0, 0), (to, width - to - piece.shape[-1])))


def by_rows(sz, step):
    if sz.wrows % 16:
        step(slice(0, sz.wrows))
    else:

        def one(i, carry):
            step(pl.ds(pl.multiple_of(i * 16, 16), 16))
            return carry

        lax.fori_loop(0, sz.wrows // 16, one, 0)


def half_of(pc, values, count, width, at=0):
    out = shift_lanes(values, 0, count, at, width)
    for j in range(1, pc.sz.zl):
        out = jnp.where(pc.zl == j, shift_lanes(values, j * count, count, at, width), out)
    return out


def piece_of(pc, values):
    sz = pc.sz
    values = values.astype(f32)
    over = sz.tp * sz.part - sz.rows
    if over:
        values = jnp.concatenate([values, jnp.zeros((over, sz.d), f32)], axis=0)
    out = values[0:sz.part]
    for t in range(1, sz.tp):
        out = jnp.where(pc.t == t, values[t * sz.part:(t + 1) * sz.part], out)
    return out


def steps_below(values, unit, count):
    out = jnp.zeros_like(values)
    for m in range(1, count):
        out = out + jnp.where(values >= m * unit, 1, 0)
    return out


def key_valid(pc, count):
    sz = pc.sz
    row = lax.broadcasted_iota(jnp.int32, (1, sz.keys), 1)
    core = steps_below(row, sz.half, 2)
    within = row - core * sz.half
    unit = steps_below(within, sz.part, sz.units)
    piece = steps_below(unit, sz.chips, sz.images)
    chip = unit - piece * sz.chips
    zl = steps_below(chip, sz.chips_y, sz.zl)
    t = 2 * (chip - zl * sz.chips_y) + core
    token = t * sz.part + within - unit * sz.part
    position = (piece * sz.zl + zl) * sz.rows + token
    return jnp.where((token < sz.rows) & (position < count), 1.0, 0.0)


def own_valid(pc, count):
    sz = pc.sz
    shape = (sz.images, sz.part, 1)
    piece = lax.broadcasted_iota(jnp.int32, shape, 0)
    token = pc.t * sz.part + lax.broadcasted_iota(jnp.int32, shape, 1)
    position = (piece * sz.zl + pc.zl) * sz.rows + token
    return jnp.where((token < sz.rows) & (position < count), 1.0, 0.0)


def ff_lanes(sz, values):
    lanes = lanes_of(values.shape)
    return jnp.where((lanes >= sz.ff_at) & (lanes < sz.ff_at + sz.ff), values, 0.0)


def ride(sz, src, dst, src_at, dst_at):
    def step(i, carry):
        rows = pl.ds(pl.multiple_of(i * 128, 128), 128)
        there = src[rows, src_at:src_at + 128].astype(f32)
        here = dst[rows, dst_at:dst_at + 128].astype(f32) if dst_at else jnp.zeros_like(there)
        dst[rows, dst_at:dst_at + 128] = jnp.where(lanes_of(there.shape) >= sz.ff_at, there, here).astype(bf16)
        return carry

    if sz.spare:
        lax.fori_loop(0, src.shape[0] // 128, step, 0)


def rows_of(ref, units):
    return jnp.concatenate([ref[unit] for unit in units], axis=0)


def put_rows(sz, ref, units, values):
    for i, unit in enumerate(units):
        ref[unit] = values[i * sz.part:(i + 1) * sz.part]


def attn_forward(pc, jobs, gather, w_ref, qv_ref, valid_ref, q_ref, k_ref, v_ref, mixed_ref, o_ref, kv_sems,
                 scatter):
    sz = pc.sz
    for s in range(2):
        unpack_out(sz, w_ref.at[s], o_ref.at[s])

    def project(step, carry):
        units, tokens = gather.ready(step)
        for s in range(2):
            both3 = dot(tokens, w_ref[s, :, 0:sz.qkvp], (1, 0))
            put_rows(sz, q_ref.at[s], units, (take(sz, both3, 0) + qv_ref[s, 0:1, 0:sz.headp]).astype(bf16))
            put_rows(sz, k_ref.at[s, pc.k], units, take(sz, both3, 1).astype(bf16))
            put_rows(sz, v_ref.at[s, pc.k], units, (take(sz, both3, 2) + qv_ref[s, 1:2, 0:sz.headp]).astype(bf16))
        jobs.at("project", step)
        return carry

    def swaps(piece):
        units = pl.ds(piece * sz.chips, sz.chips)
        return [Swap(pc, ref.at[s, pc.k, units], ref.at[s, pc.k, units], kv_sems.at[0, i, s, piece],
                     kv_sems.at[1, i, s, piece]) for s in range(2) for i, ref in enumerate((k_ref, v_ref))]

    per = sz.steps // sz.images
    for piece in range(sz.images):
        lax.fori_loop(piece * per, (piece + 1) * per, project, 0)
        for swap in swaps(piece):
            swap.start()
    gather.finish()
    for piece in range(sz.images):
        for swap in swaps(piece):
            swap.wait()

    def attend(step, carry):
        units = scatter.units(step)
        partial = None
        for s in range(2):
            keys = k_ref[s].reshape(sz.keys, sz.headp)
            values = v_ref[s].reshape(sz.keys, sz.headp)
            queries = rows_of(q_ref.at[s], units)
            total = jnp.zeros((sz.tile, sz.headp), f32)
            for head in range(sz.heads):
                probs = probabilities(head_of(queries, head), keys, valid_ref[...])
                total = total + dot(probs.astype(bf16), head_of(values, head), (1, 0))
            mixed = total.astype(bf16)
            put_rows(sz, mixed_ref.at[s], units, mixed)
            terms = dot(mixed, o_ref[s], (1, 1))
            partial = terms if partial is None else partial + terms
        scatter.push(step, partial)
        jobs.at("attend", step)
        return carry

    lax.fori_loop(0, sz.steps, attend, 0)
    jobs.run("turnover")
    scatter.flush()
    jobs.run("flush")


def ff_forward(pc, jobs, gather, w_ref, upb_ref, pre_ref, hidden_ref, scatter):
    sz = pc.sz

    def feed(step, carry):
        units, tokens = gather.ready(step)
        partial = None
        for s in range(2):
            pre = dot(tokens, w_ref[s, :, 0:sz.ffp], (1, 0)) + upb_ref[s, 2:3, 0:sz.ffp]
            put_rows(sz, pre_ref.at[s], units, pre)
            hidden = 0.5 * pre * (1.0 + jnp.tanh(gelu_root * (pre + gelu_cubic * pre * pre * pre)))
            hidden = ff_lanes(sz, hidden)
            if sz.down_shift != sz.ff_at:
                hidden = pltpu.roll(hidden, (sz.down_shift - sz.ff_at) % sz.ffp, 1)
            hidden = hidden.astype(bf16)
            put_rows(sz, hidden_ref.at[s], units, hidden)
            terms = dot(hidden, w_ref[s, :, sz.down_at:], (1, 1))
            partial = terms if partial is None else partial + terms
        scatter.push(step, partial)
        jobs.at("feed", step)
        return carry

    lax.fori_loop(0, sz.steps, feed, 0)
    jobs.run("flush")
    gather.finish()


def plan(steps, more_steps, flush, what, ff, attn):
    for place, ff_parts, attn_parts in what:
        jobs = (ff.jobs(ff_parts) if ff else []) + (attn.jobs(attn_parts) if attn else [])
        if place == "f":
            flush.extend(jobs)
        else:
            table = steps if place[0] == "s" else more_steps
            table[int(place[1])] = table.get(int(place[1]), []) + jobs


def planned(what, give):
    steps = {}
    plan(steps, None, None, what, give, None)
    return steps


GIVE_FF = (("s1", "", "d2 t0"), ("s2", "", "t1"), ("s3", "", "t2"))
GIVE_ATTN = (("s0", "t0", ""), ("s1", "d2", ""), ("s2", "t1", ""), ("s3", "t2", ""))
PLAN_ATTN_FIRST = (("s2", "t1", ""), ("m0", "l0", ""), ("m1", "", "d0"), ("m2", "t2 l1", ""),
                   ("m3", "", "d1"), ("f", "l2", "d2 t0"))
PLAN_ATTN = (("s1", "t1", "d0"), ("s2", "d2", ""), ("s3", "l0", ""), ("m0", "", "d1"), ("m1", "t2 l1", ""),
             ("m3", "", "d2"), ("f", "l2", "t0"))
PLAN_FF = (("s0", "d0", "t1 l0"), ("s1", "d1", "t2"), ("s2", "t0", "l1"), ("s3", "", "l2"))


def norm_low(values, gain, shift):
    high, _ = normalised(values)
    return (high * gain + shift).astype(bf16)


def forward_kernel(sz, *refs):
    n = sz.layers
    aligned = sz.wrowsp == sz.wrows
    ins, outs, scratch = refs[:12], refs[12:12 + 13 * n + 1], refs[12 + 13 * n + 1:]
    (count_ref, in_ref, cot_ref, wqkv_ref, wout_ref, wup_ref, wdown_ref, gain_ref, shift_ref, qv_ref, upb_ref,
     resid_ref) = ins
    saved, (wattn_outs, wff_outs, ends_ref) = outs[:11 * n], split_refs(outs[11 * n:], n, n, 1)
    saved = [saved[l * 11:(l + 1) * 11] for l in range(n)]
    ends_ref = ends_ref[0]
    (own_attn, own_ff, all_attn, all_ff, swap_ref, mine_ref, n_ref, q_ref, k_ref, v_ref, mixed_ref, pre_ref,
     hidden_ref, stream_ref, middle_ref, valid_ref, o_ref, bias_ref, tsems, csems, wsems, vsems, kv_sems,
     bsems), team, joined = split_refs(scratch, 24, 6, 0 if aligned else 2)
    bufs, (gsems, ssems) = team[:4], team[4:]
    pc = Place(sz)
    greeting = Greeting(team_peers(pc) + weight_peers(pc, True))

    def pack(ref, pieces):
        def step(rows):
            total = None
            for values, start, count, at in pieces:
                piece = shift_lanes(values[rows, :], start, count, at, ref.shape[-1])
                total = piece if total is None else total + piece
            ref[rows, :] = total.astype(bf16)

        by_rows(sz, step)
        if not aligned:
            ref[sz.wrows:, :] = jnp.zeros((sz.wrowsp - sz.wrows, ref.shape[-1]), bf16)

    def pack_attn(layer):
        for half in range(sz.zl):
            pieces = [(wqkv_ref.at[layer, kind], half * sz.wide, sz.wide, kind * sz.wide) for kind in range(3)]
            pieces += [(wout_ref.at[layer], half * sz.wide, sz.wide, 3 * sz.wide)]
            if sz.spare:
                pieces += [(wup_ref.at[layer], half * sz.ff, sz.spare, 4 * sz.wide)]
            pack(own_attn.at[layer, half], pieces)

    def pack_ff(layer):
        for half in range(sz.zl):
            rest = sz.ff - sz.spare
            pack(own_ff.at[layer, half], [(wup_ref.at[layer], half * sz.ff + sz.spare, rest, 0),
                                          (wdown_ref.at[layer], half * sz.ff, sz.ff, rest)])

    for image in range(sz.images):
        swap_ref[image, 0] = piece_of(pc, in_ref[image]).astype(bf16)
        swap_ref[image, 1] = piece_of(pc, cot_ref[image]).astype(bf16)
    pack_attn(0)
    attn = [Fetch(pc, own_attn.at[l], all_attn.at[l], wsems.at[2 * l], vsems.at[2 * l]) for l in range(n)]
    ff = [Fetch(pc, own_ff.at[l], all_ff.at[l], wsems.at[2 * l + 1], vsems.at[2 * l + 1], sz.ff_sent)
          for l in range(n)]
    bias_ref[:, pc.k] = jnp.zeros((n, 8, bias_ref.shape[-1]), f32)
    for l in range(n):
        bias_ref[l, pc.k, 0:2, 0:sz.headp] = half_of(pc, qv_ref[l], sz.wide, sz.headp)
        bias_ref[l, pc.k, 2:3, 0:sz.ffp] = half_of(pc, upb_ref[l:l + 1, :], sz.ff, sz.ffp, sz.ff_at)
    bias_swaps = [Swap(pc, bias_ref.at[l, pc.k], bias_ref.at[l, pc.k], bsems.at[0, l], bsems.at[1, l])
                  for l in range(n)]
    copies = Copies(csems)

    def swap(step):
        zh = (pc.zh + step) % sz.images
        return send(swap_ref.at[zh], mine_ref.at[pc.zh], tsems.at[0, step], tsems.at[1, step],
                    (pc.f, zh * sz.zl + pc.zl, pc.t))

    greeting.wait()
    for step in range(1, sz.images):
        swap(step).start()
    attn[0].run("d0 d1 d2")
    for move in bias_swaps:
        move.start()
    mine_ref[pc.zh] = swap_ref[pc.zh]
    count = count_ref[pc.zh]
    valid_ref[...] = key_valid(pc, count)
    for step in range(1, sz.images):
        swap(step).wait()
    stream_ref[0] = mine_ref[:, 0].astype(f32)
    gathers = [Gather(pc, n_ref.at[i], gsems.at[i], FORWARD_TURN[i % 2]) for i in range(2 * n)]
    scatters = [Scatter(pc, bufs, ssems.at[i], i % 2 == 0, i % 2 == 0 and SUM_TURN[0]) for i in range(2 * n)]
    for p in range(sz.images):
        gathers[0].start(p, norm_low(stream_ref[0, p], gain_ref[0, 0:1, :], shift_ref[0, 0:1, :]))
    pack_ff(0)
    attn[0].run("t0")
    ff[0].run("d0")
    for layer in range(1, n):
        pack_attn(layer)
    attn[0].run("t1")
    ff[0].run("d1")
    ends_ref[...] = mine_ref[:, 1].astype(f32) * own_valid(pc, count)
    attn[0].run("l0 t2")
    for layer in range(1, n):
        pack_ff(layer)
    attn[0].run("l1")
    ff[0].run("t0 d2")
    attn[0].run("l2")
    for move in bias_swaps:
        move.wait()
    attn[0].finish()

    def ready(fetch, refs, kind, layer, out):
        ref = refs.at[layer]
        if not aligned:
            for s in range(2):
                drop_padding(sz, ref.at[s], joined[kind].at[s])
            ref = joined[kind]
            pltpu.sync_copy(ref, out)
        else:
            copies.start(ref, out)
        return ref

    def after_attn(l, p):
        def run():
            middle = stream_ref[l, p] + (scatters[2 * l].finish(p) + resid_ref[l, 0:1, :])
            middle_ref[l, p] = middle
            gathers[2 * l + 1].start(p, norm_low(middle, gain_ref[l, 1:2, :], shift_ref[l, 1:2, :]))

        return run

    def after_ff(l, p):
        def run():
            out = middle_ref[l, p] + (scatters[2 * l + 1].finish(p) + resid_ref[l, 1:2, :])
            stream_ref[l + 1, p] = out
            if l + 1 < n:
                gathers[2 * l + 2].start(p, norm_low(out, gain_ref[l + 1, 0:1, :], shift_ref[l + 1, 0:1, :]))

        return run

    per = sz.steps // sz.images
    rest = range(1, sz.images)
    for l in range(n):
        more = l + 1 < n
        w = ready(attn[l], all_attn, 0, l, wattn_outs[l])
        project = {p * per - 1: [after_ff(l - 1, p)] for p in rest} if l else {}
        attend, flush = {}, []
        plan(project, attend, flush, PLAN_ATTN_FIRST if l == 0 else PLAN_ATTN, ff[l], attn[l + 1] if more else None)
        jobs = Jobs(project=project, attend=attend, flush=flush, turnover=[after_attn(l, 0)])
        attn_forward(pc, jobs, gathers[2 * l], w, bias_ref.at[l], valid_ref, q_ref.at[l], k_ref.at[l], v_ref.at[l],
                     mixed_ref.at[l], o_ref, kv_sems.at[l], scatters[2 * l])
        for ref, to in ((stream_ref.at[l], 0), (n_ref.at[2 * l], 2), (q_ref.at[l], 4), (k_ref.at[l], 5),
                        (v_ref.at[l], 6), (mixed_ref.at[l], 7)):
            copies.start(ref, saved[l][to])
        ff[l].finish()
        for core in range(2):
            ride(sz, all_attn.at[l, core], all_ff.at[l, core], 4 * sz.wide - sz.ff_at, 0)
        w = ready(ff[l], all_ff, 1, l, wff_outs[l])
        feed = {(p - 1) * per: [after_attn(l, p)] for p in rest}
        if more:
            plan(feed, None, None, PLAN_FF, ff[l + 1], attn[l + 1])
        feed[FF_OVER] = [after_ff(l, 0)] + feed.get(FF_OVER, [])
        ff_forward(pc, Jobs(feed=feed), gathers[2 * l + 1], w, bias_ref.at[l], pre_ref.at[l],
                   hidden_ref.at[l], scatters[2 * l + 1])
        if more:
            attn[l + 1].finish()
        else:
            for p in rest:
                after_ff(l, p)()
        for ref, to in ((middle_ref.at[l], 1), (n_ref.at[2 * l + 1], 3), (pre_ref.at[l], 8), (hidden_ref.at[l], 9)):
            copies.start(ref, saved[l][to])
    copies.start(stream_ref.at[n], saved[0][10])
    copies.start(valid_ref, saved[n - 1][10])
    copies.wait()


def forward_call(sz, *operands):
    n = sz.layers
    own, team = ((sz.images, sz.part, sz.d), f32), ((sz.chips, sz.images, sz.part, sz.d), bf16)
    head, pair = (2, sz.units, sz.part, sz.headp), (2, 2, sz.units, sz.part, sz.headp)
    hidden = (2, sz.units, sz.part, sz.ffp)
    shapes = []
    for l in range(n):
        last = ((1, sz.keys), f32) if l == n - 1 else own
        shapes += [own, own, team, team, (head, bf16), (pair, bf16), (pair, bf16), (head, bf16), (hidden, f32),
                   (hidden, bf16), last]
    shapes += [((2, sz.d, sz.attnp), bf16)] * n + [((2, sz.d, sz.ffw), bf16)] * n + [own]
    vmem, hbm = pl.BlockSpec(memory_space=pltpu.VMEM), pl.BlockSpec(memory_space=pl.ANY)
    padded = sz.groups * sz.wrowsp
    scratch = [
        VMEM((n, sz.zl, sz.wrowsp, sz.attnp), bf16), VMEM((n, sz.zl, sz.wrowsp, sz.ffs), bf16),
        VMEM((n, 2, padded, sz.attnp), bf16), VMEM((n, 2, padded, sz.ffw), bf16),
        VMEM((sz.images, 2, sz.part, sz.d), bf16), VMEM((sz.images, 2, sz.part, sz.d), bf16),
        VMEM((2 * n,) + team[0], bf16),
        VMEM((n,) + head, bf16), VMEM((n,) + pair, bf16), VMEM((n,) + pair, bf16), VMEM((n,) + head, bf16),
        VMEM((n,) + hidden, f32), VMEM((n,) + hidden, bf16),
        VMEM((n + 1,) + own[0], f32), VMEM((n,) + own[0], f32), VMEM((1, sz.keys), f32),
        VMEM((2, sz.d, sz.headp), bf16), VMEM((n, 2, 8, max(sz.headp, sz.ffp)), f32),
        DMA((2, sz.images)), DMA((12 * n + 2,)), DMA((2 * n, sz.chunks, sz.fsdp, 2, sz.ctx)),
        DMA((2 * n, sz.chunks, sz.fsdp, 2, sz.ctx)), DMA((n, 2, 2, 2, sz.images)), DMA((2, n)),
    ] + team_scratch(sz, 2 * n)
    if sz.wrowsp != sz.wrows:
        scratch += [VMEM((2, sz.d, sz.attnp), bf16), VMEM((2, sz.d, sz.ffw), bf16)]
    return pl.pallas_call(
        functools.partial(forward_kernel, sz),
        out_shape=[jax.ShapeDtypeStruct(*s) for s in shapes],
        in_specs=[pl.BlockSpec(memory_space=pltpu.SMEM)] + [vmem] * (len(operands) - 1),
        out_specs=[hbm] * (len(shapes) - 1) + [vmem],
        scratch_shapes=scratch,
        compiler_params=params(1),
        name="forward",
    )(*operands)


def params(collective_id):
    return pltpu.CompilerParams(
        collective_id=collective_id, has_side_effects=True, vmem_limit_bytes=63 * 1024 * 1024
    )


class Twins:
    def __init__(self, pc, dw, got, sems, span):
        self.pc, self.dw, self.got, self.sems, self.span = pc, dw, got, sems, span
        self.count = pc.sz.d // span

    def copy(self, i):
        rows = pl.ds(pl.multiple_of(i * self.span, 128), self.span)
        return send(self.dw.at[1 - self.pc.k, rows], self.got.at[rows], self.sems.at[0, i], self.sems.at[1, i],
                    self.pc.twin)

    def put(self, core, i, pieces):
        rows = pl.ds(pl.multiple_of(i * self.span, 128), self.span)
        for at, values in pieces:
            self.dw[core, rows, at:at + values.shape[-1]] = values.astype(bf16)

    def run(self, make, jobs, between=None):
        def other(i, carry):
            self.put(1 - self.pc.k, i, make(1 - self.pc.k, i))
            self.copy(i).start()
            return carry

        def own(i, carry):
            self.put(self.pc.k, i, make(self.pc.k, i))
            jobs.at("step_grads", i)
            return carry

        def add(i, carry):
            self.copy(i).wait_recv()
            rows = pl.ds(pl.multiple_of(i * self.span, 128), self.span)
            self.dw[self.pc.k, rows, :] = (
                self.dw[self.pc.k, rows, :].astype(f32) + self.got[rows, :].astype(f32)
            ).astype(bf16)
            self.copy(i).wait_send()
            return carry

        lax.fori_loop(0, self.count, other, 0)
        if between:
            between()
        lax.fori_loop(0, self.count, own, 0)
        lax.fori_loop(0, self.count, add, 0)


def ff_backward(pc, jobs, gather, w_ref, n2_ref, pre_ref, hidden_ref, dup_ref, pg_ref, twins, scatter):
    sz = pc.sz
    dup_ref[...] = jnp.zeros_like(dup_ref)

    def feed(step, carry):
        units, tokens = gather.ready(step)

        def shard(s, partial):
            back = dot(tokens, w_ref[s, :, sz.down_at:], (1, 0))
            if sz.down_shift != sz.ff_at:
                back = pltpu.roll(back, (sz.ff_at - sz.down_shift) % sz.ffp, 1)
            pre = rows_of(pre_ref.at[s], units)
            bent = jnp.tanh(gelu_root * (pre + gelu_cubic * pre * pre * pre))
            slope = 0.5 * (1.0 + bent) + 0.5 * pre * (1.0 - bent * bent) * (
                gelu_root * (1.0 + 3.0 * gelu_cubic * pre * pre)
            )
            pre_grad = ff_lanes(sz, back * slope).astype(bf16)
            put_rows(sz, pg_ref.at[s], units, pre_grad)
            dup_ref[s] += jnp.sum(pre_grad.astype(f32), axis=0, keepdims=True)
            return partial + dot(pre_grad, w_ref[s, :, 0:sz.ffp], (1, 1))

        partial = lax.fori_loop(0, 2, shard, jnp.zeros((sz.tile, sz.d), f32))
        scatter.push(step, partial)
        jobs.at("feed", step)
        return carry

    lax.fori_loop(0, sz.steps, feed, 0)
    jobs.run("flush")

    def make(core, i):
        lanes = pl.ds(pl.multiple_of(i * twins.span, 128), twins.span)
        hidden = hidden_ref[core].reshape(sz.half, sz.ffp)
        down = dot(by_unit(sz, gather.buf[:, :, :, lanes]), hidden, (0, 0))
        pre_grad = pg_ref[core].reshape(sz.half, sz.ffp)
        up = dot(by_unit(sz, n2_ref[:, :, :, lanes]), pre_grad, (0, 0))
        over = sz.ffp - sz.down_at
        both = [(sz.down_at, up[:, sz.down_at:] + down[:, 0:over])] if over else []
        return [(0, up[:, 0:sz.down_at])] + both + [(sz.ffp, down[:, over:])]

    twins.run(make, jobs)
    jobs.run("grads")
    gather.finish()


def attn_backward(pc, jobs, gather, w_ref, n1_ref, q_ref, k_ref, v_ref, mixed_ref, valid_ref, dqv_ref,
                  o_ref, dkv_ref, kvsend_ref, kvgot_ref, stack_ref, kv_sems, twins, scatter):
    sz = pc.sz
    for s in range(2):
        unpack_out(sz, w_ref.at[s], o_ref.at[s])
    dkv_ref[...] = jnp.zeros_like(dkv_ref)
    dqv_ref[...] = jnp.zeros_like(dqv_ref)
    scale = HEAD_DIM ** (-0.5)

    def attend(step, carry):
        units, tokens = gather.ready(step)

        def shard(s, none):
            mixed_grad = dot(tokens, o_ref[s], (1, 0)).astype(bf16)
            keys = k_ref[s].reshape(sz.keys, sz.headp)
            values = v_ref[s].reshape(sz.keys, sz.headp)
            queries = rows_of(q_ref.at[s], units)
            total = jnp.zeros((sz.tile, sz.headp), f32)
            dkey, dvalue = None, None
            for head in range(sz.heads):
                q_head = head_of(queries, head)
                g_head = head_of(mixed_grad, head)
                probs = probabilities(q_head, keys, valid_ref[...])
                dprobs = dot(g_head, values, (1, 1))
                inner = jnp.sum(probs * dprobs, axis=-1, keepdims=True)
                dscores = (probs * (dprobs - inner)).astype(bf16)
                total = total + dot(dscores, head_of(keys, head), (1, 0))
                dk, dv = dot(dscores, q_head, (0, 0)), dot(probs.astype(bf16), g_head, (0, 0))
                dkey = dk if dkey is None else dkey + dk
                dvalue = dv if dvalue is None else dvalue + dv
            dkv_ref[s, 0] += dkey.reshape(2, sz.half, sz.headp)
            dkv_ref[s, 1] += dvalue.reshape(2, sz.half, sz.headp)
            dq = (scale * total).astype(bf16).astype(f32)
            dqv_ref[s, 0:1, :] += jnp.sum(dq, axis=0, keepdims=True)
            dq = dq.astype(bf16)
            for i, unit in enumerate(units):
                stack_ref[s, unit, :, 0:sz.headp] = dq[i * sz.part:(i + 1) * sz.part]
            return none

        lax.fori_loop(0, 2, shard, 0)
        jobs.at("attend", step)
        return carry

    lax.fori_loop(0, sz.steps, attend, 0)
    for s in range(2):
        kvsend_ref[s] = dkv_ref[s, :, 1 - pc.k].astype(bf16)
    moves = [Swap(pc, kvsend_ref.at[s], kvgot_ref.at[s], kv_sems.at[0, s], kv_sems.at[1, s]) for s in range(2)]
    for move in moves:
        move.start()
    gather.finish()
    jobs.run("middle")
    for move in moves:
        move.wait()

    def back_project(step, carry):
        units = scatter.units(step)

        def shard(s, partial):

            def both(kind):
                rows = [pl.ds(pl.multiple_of(unit * sz.part, sz.part), sz.part) for unit in units]
                return jnp.concatenate(
                    [dkv_ref[s, kind, pc.k, r, :] + kvgot_ref[s, kind, r, :].astype(f32) for r in rows], axis=0
                )

            dk = (scale * both(0)).astype(bf16).astype(f32)
            dv = both(1).astype(bf16).astype(f32)
            dqv_ref[s, 1:2, :] += jnp.sum(dv, axis=0, keepdims=True)
            dq = rows_of(stack_ref.at[s], units)[:, 0:sz.headp].astype(f32)
            total = jnp.pad(dq, ((0, 0), (0, sz.qkvp - sz.headp)))
            for kind, piece in ((1, dk), (2, dv)):
                start = kind * sz.wide // 128 * 128
                shift = kind * sz.wide - start
                moved = pltpu.roll(piece, shift, 1) if shift else piece
                total = total + jnp.pad(moved, ((0, 0), (start, sz.qkvp - start - sz.headp)))
            stacked = total.astype(bf16)
            put_rows(sz, stack_ref.at[s], units, stacked)
            return partial + dot(stacked, w_ref[s, :, 0:sz.qkvp], (1, 1))

        partial = lax.fori_loop(0, 2, shard, jnp.zeros((sz.tile, sz.d), f32))
        scatter.push(step, partial)
        return carry

    lax.fori_loop(0, sz.steps, back_project, 0)
    jobs.run("flush")
    o_at = 3 * sz.wide // 128 * 128
    o_shift = 3 * sz.wide - o_at

    def make(core, i):
        lanes = pl.ds(pl.multiple_of(i * twins.span, 128), twins.span)
        stacked = stack_ref[core].reshape(sz.half, sz.qkvp)
        dqkv = dot(by_unit(sz, n1_ref[:, :, :, lanes]), stacked, (0, 0))
        mixed = mixed_ref[core].reshape(sz.half, sz.headp)
        dout = dot(by_unit(sz, gather.buf[:, :, :, lanes]), mixed, (0, 0))
        if o_shift:
            dout = pltpu.roll(dout, o_shift, 1)
        total = jnp.pad(dqkv, ((0, 0), (0, sz.attnp - sz.qkvp))) + jnp.pad(
            dout, ((0, 0), (o_at, sz.attnp - o_at - sz.headp))
        )
        return [(0, total)]

    twins.run(make, jobs, scatter.flush)
    jobs.run("grads")


def backward_kernel(sz, *refs):
    n = sz.layers
    aligned = sz.wrowsp == sz.wrows
    saved = [refs[l * 11:(l + 1) * 11] for l in range(n)]
    wattn_ins, wff_ins, (cot_ref, gain_ref), outs, scratch = split_refs(
        refs[11 * n:], n, n, 2, 2 * n + 2, len(refs) - 11 * n - 2 * n - 2 - 2 * n - 2)
    attn_outs, ff_outs, (whole_ref, small_ref) = split_refs(outs, n, n, 2)
    (stream_ref, middle_ref, n1_ref, n2_ref, q_ref, k_ref, v_ref, mixed_ref, pre_ref, hidden_ref, valid_ref, out_ref,
     wattn_ref, wff_ref, gl_ref, ml_ref, pg_ref, o_ref, dkv_ref, kvsend_ref, kvgot_ref, stack_ref, dwattn_ref,
     dwff_ref, twattn_ref, twff_ref, got_attn, got_ff, dqv_ref, dup_ref, grad_ref, ends_ref, first, from_tp, from_ctx,
     from_fsdp, sum_tp, sum_ctx, share_ref, shgot_ref, lsems, wsems, esems, ysems, tsems, kv_sems, twsems,
     shsems), team, padded = split_refs(scratch, 48, 6, 0 if aligned else 2)
    bufs, (gsems, ssems) = team[:4], team[4:]
    pc = Place(sz)
    greeting = Greeting(team_peers(pc) + weight_peers(pc, True) + line_peers(pc))
    copies = Copies(lsems)
    into = [stream_ref, middle_ref, n1_ref, n2_ref, q_ref, k_ref, v_ref, mixed_ref, pre_ref, hidden_ref]

    def load(l, weights, ref, kinds):
        return [copies.start(weights[l], ref)] + [copies.start(saved[l][kind], into[kind]) for kind in kinds]

    def load_ff(l):
        return load(l, wff_ins, wff_ref, (8, 3, 9, 1))

    def load_attn(l):
        return load(l, wattn_ins, wattn_ref, (4, 5, 6, 7, 2, 0))

    out_load = copies.start(saved[0][10], out_ref)
    ff_loads, attn_loads = load_ff(n - 1), load_attn(n - 1)
    attn_loads.append(copies.start(saved[n - 1][10], valid_ref))
    own_attn, own_ff = dwattn_ref.at[pc.k], dwff_ref.at[pc.k]
    give_attn = [Give(pc, own_attn if aligned else padded[0], attn_outs[l], got_attn.at[l], wsems.at[2 * l])
                 for l in range(n)]
    give_ff = [Give(pc, own_ff if aligned else padded[1], ff_outs[l], got_ff.at[l], wsems.at[2 * l + 1], sz.ff_sent)
               for l in range(n)]

    def begin(give, dw, kind):
        def run():
            if kind == 0:
                ride(sz, own_ff, dw, 0, 4 * sz.wide - sz.ff_at)
            if not aligned:
                add_padding(sz, dw, padded[kind])
            give.run("d0 d1")

        return run

    def swap(kind, step):
        zh = (pc.zh + step) % sz.images
        return send(ends_ref.at[kind, zh], whole_ref.at[kind, pc.t, pc.zh], esems.at[kind, 0, step],
                    esems.at[kind, 1, step], (pc.f, zh * sz.zl + pc.zl, pc.t))

    def own_end(kind):
        return pltpu.make_async_copy(ends_ref.at[kind, pc.zh], whole_ref.at[kind, pc.t, pc.zh], esems.at[kind, 0, 0])

    def spread(kind, step):
        return send(whole_ref.at[kind, pc.t], whole_ref.at[kind, pc.t], ysems.at[kind, 0, step],
                    ysems.at[kind, 1, step], (pc.f, pc.c, (pc.t + step) % sz.tp))

    def spread_from(kind, step):
        back = (pc.t + sz.tp - step) % sz.tp
        return send(whole_ref.at[kind, back], whole_ref.at[kind, back], ysems.at[kind, 0, step],
                    ysems.at[kind, 1, step], (pc.f, pc.c, back))

    def swap_start(kind):
        own_end(kind).start()
        for step in range(1, sz.images):
            swap(kind, step).start()

    def spread_start(kind):
        own_end(kind).wait()
        for step in range(1, sz.images):
            swap(kind, step).wait()
        for step in range(1, sz.tp):
            spread(kind, step).start()

    def spread_wait(kind):
        for step in range(1, sz.tp):
            spread_from(kind, step).wait_recv()
            spread(kind, step).wait_send()

    def over_tp(step):
        return send(first, from_tp.at[step - 1], tsems.at[0, 0, step], tsems.at[0, 1, step],
                    (pc.f, pc.c, (pc.t + step) % sz.tp))

    def over_ctx(step):
        return send(sum_tp, from_ctx.at[step - 1], tsems.at[1, 0, step], tsems.at[1, 1, step],
                    (pc.f, pc.ctx_ahead(step), pc.t))

    def over_fsdp(step):
        return send(sum_ctx, from_fsdp.at[step - 1], tsems.at[2, 0, step], tsems.at[2, 1, step],
                    ((pc.f + step) % sz.fsdp, pc.c, pc.t))

    sum_tp[...] = jnp.zeros_like(sum_tp)
    share_ref[...] = jnp.zeros_like(share_ref)
    first[...] = jnp.zeros_like(first)
    copies.wait([out_load])
    ends_ref[0] = out_ref[...].astype(bf16)
    grad_ref[...] = cot_ref[...]
    gathers = [Gather(pc, (gl_ref, ml_ref)[i % 2], gsems.at[i], BACKWARD_TURN[1 - i % 2]) for i in range(2 * n)]
    scatters = [Scatter(pc, bufs, ssems.at[i], i % 2 == 1, i % 2 == 1 and SUM_TURN[1]) for i in range(2 * n)]
    def low_of(l, p, row):
        low = grad_ref[p].astype(bf16)
        first[l, row:row + 1, :] += jnp.sum(low.astype(f32), axis=0, keepdims=True)
        return low

    def after_ff(l, p):
        def run():
            turn = n - 1 - l
            term, dgain, dshift = norm_back(middle_ref[p], gain_ref[l, 1:2, :], scatters[2 * turn].finish(p))
            grad_ref[p] += term
            gathers[2 * turn + 1].start(p, low_of(l, p, 4))
            first[l, 1:2, :] += dgain
            first[l, 3:4, :] += dshift

        return run

    def after_attn(l, p):
        def run():
            turn = n - 1 - l
            term, dgain, dshift = norm_back(stream_ref[p], gain_ref[l, 0:1, :], scatters[2 * turn + 1].finish(p))
            grad_ref[p] += term
            if l:
                gathers[2 * turn + 2].start(p, low_of(l - 1, p, 5))
            else:
                ends_ref[1, p] = grad_ref[p].astype(bf16)
            first[l, 0:1, :] += dgain
            first[l, 2:3, :] += dshift

        return run

    greeting.wait()
    per, rest = sz.steps // sz.images, range(1, sz.images)
    span = 384 if sz.d % 384 == 0 else 128
    for p in range(sz.images):
        gathers[0].start(p, low_of(n - 1, p, 5))
    swap_start(0)
    for turn in range(n):
        l = n - 1 - turn
        start = turn == 0
        copies.wait(ff_loads)
        feed = {}
        if start:
            feed[1] = [lambda: spread_start(0)]
        else:
            after = give_attn[l + 1]
            feed.update({(p - 1) * per: [after_attn(l + 1, p)] for p in rest})
            feed[(sz.images - 2) * per] = feed[(sz.images - 2) * per] + [lambda: attn_loads.extend(load_attn(l))]
            plan(feed, None, None, GIVE_FF, None, after)
        feed[FF_OVER] = [after_ff(l, 0)] + feed.get(FF_OVER, [])
        jobs = Jobs(feed=feed, flush=([] if start else [give_ff[l + 1].finish]),
                    grads=[begin(give_ff[l], own_ff, 1)] + [after_ff(l, p) for p in rest])
        twins = Twins(pc, dwff_ref, twff_ref, twsems.at[2 * l + 1], span)
        ff_backward(pc, jobs, gathers[2 * turn], wff_ref, n2_ref, pre_ref, hidden_ref, dup_ref, pg_ref, twins,
                    scatters[2 * turn])
        for core in range(2):
            share_ref[core, 3 * l + 2:3 * l + 3, 0:sz.ffp] = dup_ref[core]
        copies.wait(attn_loads)
        del attn_loads[:]
        if l:
            ff_loads = load_ff(l - 1)
        if start:
            spread_wait(0)
        now = give_ff[l]
        jobs = Jobs(
            attend=planned(GIVE_ATTN, now),
            flush=([] if start else [give_attn[l + 1].finish]),
            step_grads={0: [after_attn(l, 0)]}, grads=[begin(give_attn[l], own_attn, 0)],
        )
        twins = Twins(pc, dwattn_ref, twattn_ref, twsems.at[2 * l], span)
        attn_backward(pc, jobs, gathers[2 * turn + 1], wattn_ref, n1_ref, q_ref, k_ref, v_ref, mixed_ref, valid_ref,
                      dqv_ref, o_ref, dkv_ref, kvsend_ref, kvgot_ref, stack_ref, kv_sems.at[l], twins,
                      scatters[2 * turn + 1])
        for core in range(2):
            share_ref[core, 3 * l:3 * l + 2, 0:sz.headp] = dqv_ref[core]
    share = Swap(pc, share_ref.at[1 - pc.k], shgot_ref, shsems.at[0], shsems.at[1])
    share.start()
    for p in rest:
        after_attn(0, p)()
    last = give_attn[0]
    swap_start(1)
    for step in range(1, sz.tp):
        over_tp(step).start()
    last.run("d2 t0")
    spread_start(1)
    last.run("t1")
    value = first[...]
    for step in range(1, sz.tp):
        over_tp(step).wait()
        value = value + from_tp[step - 1]
    sum_tp[0:n] = value
    share.wait()
    sum_tp[n + pc.zl] = share_ref[pc.k] + shgot_ref[...]
    for step in range(1, sz.ctx):
        over_ctx(step).start()
    last.run("t2")
    value = sum_tp[...]
    for step in range(1, sz.ctx):
        over_ctx(step).wait()
        value = value + from_ctx[step - 1]
    sum_ctx[...] = value
    for step in range(1, sz.fsdp):
        over_fsdp(step).start()
    value = sum_ctx[...]
    for step in range(1, sz.fsdp):
        over_fsdp(step).wait()
        value = value + from_fsdp[step - 1]
    small_ref[...] = value
    give_ff[0].finish()
    spread_wait(1)
    last.finish()


def backward_call(sz, saved, wattn, wff, cot, gains):
    n = sz.layers
    own, team = (sz.images, sz.part, sz.d), (sz.chips, sz.images, sz.part, sz.d)
    head, pair = (2, sz.units, sz.part, sz.headp), (2, 2, sz.units, sz.part, sz.headp)
    hidden = (2, sz.units, sz.part, sz.ffp)
    deep = up_to(max(6, 3 * n), 8)
    small = (n + sz.zl, deep, sz.d)
    ends = (sz.images, sz.part, sz.d)
    attn_sum, ff_sum = (sz.ctx, sz.wrowsp, sz.attnp), (sz.ctx, sz.wrowsp, sz.ffs)
    shapes = [(attn_sum, bf16)] * n + [(ff_sum, bf16)] * n + [((2, sz.tp) + ends, bf16), (small, f32)]
    vmem, hbm = pl.BlockSpec(memory_space=pltpu.VMEM), pl.BlockSpec(memory_space=pl.ANY)
    far, jumps = max(sz.tp, sz.ctx, sz.fsdp), max(sz.fsdp - 1, 1)
    scratch = [
        VMEM(own, f32), VMEM(own, f32), VMEM(team, bf16), VMEM(team, bf16),
        VMEM(head, bf16), VMEM(pair, bf16), VMEM(pair, bf16), VMEM(head, bf16), VMEM(hidden, f32), VMEM(hidden, bf16),
        VMEM((1, sz.keys), f32), VMEM(own, f32),
        VMEM((2, sz.d, sz.attnp), bf16), VMEM((2, sz.d, sz.ffw), bf16),
        VMEM(team, bf16), VMEM(team, bf16), VMEM(hidden, bf16), VMEM((2, sz.d, sz.headp), bf16),
        VMEM((2, 2, 2, sz.half, sz.headp), f32), VMEM((2, 2, sz.half, sz.headp), bf16),
        VMEM((2, 2, sz.half, sz.headp), bf16), VMEM((2, sz.units, sz.part, sz.qkvp), bf16),
        VMEM((2, sz.d, sz.attnp), bf16), VMEM((2, sz.d, sz.ffw), bf16),
        VMEM((sz.d, sz.attnp), bf16), VMEM((sz.d, sz.ffw), bf16),
        VMEM((n, jumps) + attn_sum, bf16), VMEM((n, jumps) + ff_sum, bf16),
        VMEM((2, 2, sz.headp), f32), VMEM((2, 1, sz.ffp), f32), VMEM(own, f32), VMEM((2,) + ends, bf16),
        VMEM((n, deep, sz.d), f32), VMEM((sz.tp - 1, n, deep, sz.d), f32),
        VMEM((max(sz.ctx - 1, 1),) + small, f32), VMEM((jumps,) + small, f32), VMEM(small, f32), VMEM(small, f32),
        VMEM((2, deep, sz.d), f32), VMEM((deep, sz.d), f32),
        DMA((12 * n + 2,)), DMA((2 * n, sz.chunks, sz.fsdp, 2, sz.ctx)), DMA((2, 2, sz.images)), DMA((2, 2, sz.tp)),
        DMA((3, 2, far)), DMA((n, 2, 2)), DMA((2 * n, 2, sz.d // 128)), DMA((2,)),
    ] + team_scratch(sz, 2 * n)
    if sz.wrowsp != sz.wrows:
        padded = sz.groups * sz.wrowsp
        scratch += [VMEM((padded, sz.attnp), bf16), VMEM((padded, sz.ffw), bf16)]
    operands = (*saved, *wattn, *wff, cot, gains)
    return pl.pallas_call(
        functools.partial(backward_kernel, sz),
        out_shape=[jax.ShapeDtypeStruct(*s) for s in shapes],
        in_specs=[hbm] * (len(operands) - 2) + [vmem] * 2,
        out_specs=[hbm] * (2 * n + 1) + [vmem],
        scratch_shapes=scratch,
        compiler_params=params(2),
        name="backward",
    )(*operands)


def close_kernel(sz, *refs):
    n = sz.layers
    attn_ins, ff_ins, (whole_in, small_ref), outs, scratch = split_refs(refs, n, n, 2, 11, 10)
    out_to, gin_to, gain_ref, bias_ref, qkv_to, qv_ref, wout_to, up_to_, upb_ref, down_to, resid_ref = outs
    attn_refs, ff_refs, whole_ref, out_ref, gin_ref, qkv_ref, wout_ref, up_ref, down_ref, sems = scratch
    copies = Copies(sems)
    whole_load = copies.start(whole_in, whole_ref)
    loads = [[copies.start(attn_ins[l], attn_refs.at[l]), copies.start(ff_ins[l], ff_refs.at[l])] for l in range(n)]
    arrived = [whole_load] + sum(loads, [])
    full, ff = sz.wide * sz.zl, sz.ff * sz.zl

    def summed(ref):
        return [sum(ref[zh * sz.zl + j].astype(f32) for zh in range(sz.images)) for j in range(sz.zl)]

    def join(width, count, *runs):
        total = None
        for j, halves, start, lanes, place in [(j, *run) for run in runs for j in range(sz.zl)]:
            piece = shift_lanes(halves[j], start, lanes, j * count + place, up_to(width, 128))
            total = piece if total is None else total + piece
        return total[0:sz.wrows, 0:width]

    copies.wait([whole_load])
    for image in range(sz.images):
        rows = whole_ref[0, :, image].reshape(sz.tp * sz.part, sz.d)
        out_ref[image] = rows[0:sz.rows]
        rows = whole_ref[1, :, image].reshape(sz.tp * sz.part, sz.d)
        gin_ref[image] = rows.astype(f32)[0:sz.rows]
    copies.start(out_ref, out_to)
    copies.start(gin_ref, gin_to)
    for layer in range(n):
        copies.wait(loads[layer])
        attn, hidden = summed(attn_refs.at[layer]), summed(ff_refs.at[layer])
        for kind in range(3):
            qkv_ref[layer, kind] = join(full, sz.wide, (attn, kind * sz.wide, sz.wide, 0))
        wout_ref[layer] = join(full, sz.wide, (attn, 3 * sz.wide, sz.wide, 0))
        rest = sz.ff - sz.spare
        first = [(attn, 4 * sz.wide, sz.spare, 0)] if sz.spare else []
        up_ref[layer] = join(ff, sz.ff, *first, (hidden, 0, rest, sz.spare))
        down_ref[layer] = join(ff, sz.ff, (hidden, rest, sz.ff, 0))
        for ref, to in ((qkv_ref, qkv_to), (wout_ref, wout_to), (up_ref, up_to_), (down_ref, down_to)):
            copies.start(ref.at[layer], to.at[layer])
        values = small_ref[layer]
        gain_ref[layer] = values[0:2]
        bias_ref[layer] = values[2:4]
        resid_ref[layer] = values[4:6]
        total_qv, total_up = None, None
        for half in range(sz.zl):
            values = small_ref[n + half]
            qv = shift_lanes(values, 0, sz.wide, half * sz.wide, up_to(full, 128))
            up = shift_lanes(values, sz.ff_at, sz.ff, half * sz.ff, up_to(ff, 128))
            total_qv = qv if total_qv is None else total_qv + qv
            total_up = up if total_up is None else total_up + up
        qv_ref[layer] = total_qv[3 * layer:3 * layer + 2, 0:full]
        upb_ref[layer:layer + 1, :] = total_up[3 * layer + 2:3 * layer + 3, 0:ff]
    copies.wait([i for i in range(len(copies.made)) if i not in arrived])


def close_call(sz, attn_sums, ff_sums, ends, small):
    n, full, ff = sz.layers, sz.wide * sz.zl, sz.ff * sz.zl
    tokens = (sz.images, sz.rows, sz.d)
    vec, up = ((n, 2, sz.d), f32), ((n, sz.wrows, ff), f32)
    shapes = [
        (tokens, bf16), (tokens, f32), vec, vec, ((n, 3, sz.wrows, full), f32), ((n, 2, full), f32),
        ((n, sz.wrows, full), f32), up, ((n, ff), f32), up, vec,
    ]
    vmem, hbm = pl.BlockSpec(memory_space=pltpu.VMEM), pl.BlockSpec(memory_space=pl.ANY)
    results = pl.pallas_call(
        functools.partial(close_kernel, sz),
        out_shape=[jax.ShapeDtypeStruct(*s) for s in shapes],
        in_specs=[hbm] * (2 * n + 1) + [vmem],
        out_specs=[hbm, hbm, vmem, vmem, hbm, vmem, hbm, hbm, vmem, hbm, vmem],
        scratch_shapes=[
            VMEM((n,) + attn_sums[0].shape, bf16), VMEM((n,) + ff_sums[0].shape, bf16), VMEM(ends.shape, bf16),
            *[VMEM(*shapes[i]) for i in (0, 1, 4, 6, 7, 9)], DMA((6 * n + 3,)),
        ],
        compiler_params=pltpu.CompilerParams(vmem_limit_bytes=60 * 1024 * 1024),
        name="close",
    )(*attn_sums, *ff_sums, ends, small)
    results = list(results)
    results[4] = jnp.swapaxes(results[4], 1, 2)
    return tuple(results)


def per_device(mesh, inputs, cotangent, valid_count, norm_gain, norm_bias, w_qkv, bias_qv, w_out, w_up, bias_up,
               w_down, bias_resid):
    sz = Sizes(mesh, inputs, w_qkv, w_up)
    n = sz.layers
    *made, cot = forward_call(sz, valid_count, inputs, cotangent, jnp.swapaxes(w_qkv, 1, 2), w_out, w_up,
                              w_down, norm_gain, norm_bias, bias_qv, bias_up, bias_resid)
    saved, wattn, wff = split_refs(made, 11 * n, n, n)
    *sums, ends, small = backward_call(sz, saved, wattn, wff, cot, norm_gain)
    return close_call(sz, sums[:n], sums[n:], ends, small)


def solution(mesh):
    tokens, rows = P("fsdp", "ctx", None), P(None, ("fsdp", "ctx"), "tp")
    qkv = P(None, ("fsdp", "ctx"), None, "tp")
    qv, up = P(None, None, "tp"), P(None, "tp")
    return jax.shard_map(
        functools.partial(per_device, mesh),
        mesh=mesh,
        in_specs=(tokens, tokens, P("fsdp"), P(), P(), qkv, qv, rows, rows, up, rows, P()),
        out_specs=(tokens, tokens, P(), P(), qkv, qv, rows, rows, up, rows, P()),
        check_vma=False,
    )
```
